32 devices in a mesh: seq: 8 (over z, x), row: 4 (over y, core).
Axes of the slice: x: 2, y: 2, z: 4, core: 2. Of those that a mesh axis runs over, the one named last changes fastest.
Arguments:
- tokens: bfloat16 [4, 8192, 768], P('row', 'seq'), as said below
- doc_lengths: int32 [4, 4], P('row'), may hold values from 64 to 8000, as said below
- w_qkv: bfloat16 [768, 2304], replicated, may hold values from -0.21875 to 0.21875
- w_out: bfloat16 [768, 768], replicated, may hold values from -0.21875 to 0.21875
- conv_taps: float32 [12, 33], replicated, may hold values from -0.5 to 0.5
- norm1_gain: float32 [768], replicated, may hold values from 0.25 to 1.75
- norm1_bias: float32 [768], replicated, may hold values from -1.5 to 1.5
- w_up: bfloat16 [768, 3072], replicated, may hold values from -0.21875 to 0.21875
- w_down: bfloat16 [3072, 768], replicated, may hold values from -0.109375 to 0.109375
- norm2_gain: float32 [768], replicated, may hold values from 0.25 to 1.75
- norm2_bias: float32 [768], replicated, may hold values from -1.5 to 1.5
- cotangent: bfloat16 [4, 8192, 768], P('row', 'seq'), may hold values from -6 to 6
Outputs:
- outputs: bfloat16 [4, 8192, 768], P('row', 'seq')
- grad_tokens: float32 [4, 8192, 768], P('row', 'seq')
- grad_w_qkv: float32 [768, 2304], replicated
- grad_w_out: float32 [768, 768], replicated
- grad_conv_taps: float32 [12, 33], replicated
- grad_norm1_gain: float32 [768], replicated
- grad_norm1_bias: float32 [768], replicated
- grad_w_up: float32 [768, 3072], replicated
- grad_w_down: float32 [3072, 768], replicated
- grad_norm2_gain: float32 [768], replicated
- grad_norm2_bias: float32 [768], replicated
The draws below stay inside these ranges and needn't reach their ends.
Inputs may be any that keep to these rules, and one draw needn't show every extreme that they name: `tokens`: activations of the previous layer. `doc_lengths`: each row's 4 lengths sum to 8192; every document holds at least 64 tokens, and one of them more than 7168.
All inputs are finite; a program needn't handle non-finite values.
Results may differ from the reference program's by a relative error of at most 0.014.
Values may be sent and summed in bfloat16 or wider, within the bound.
A program may use at most 320 MiB of HBM per device.

```python
import jax
import jax.numpy as jnp
from jax import lax

D = 768
HEADS = 12
HEAD = 64
FF = 3072
LMK = 64
KS = 33
NS_ITERS = 6
DOCS = 4
TOK_DEV = 1024
ROWS = 4
ROW_LEN = 8192


def draw_tokens(key, part):
    key = jax.random.fold_in(key, 11)
    keys = jax.random.split(key, 3)
    cycles = jnp.exp(jax.random.uniform(keys[0], (ROWS, 1, D), minval=0.0, maxval=jnp.log(LMK * 1.0)))
    phase = jax.random.uniform(keys[1], (ROWS, 1, D), minval=-3.14159, maxval=3.14159)
    places = jnp.arange(ROW_LEN, dtype=jnp.float32)[None, :, None] / ROW_LEN
    smooth = jnp.sin(6.2831853 * cycles * places + phase)
    rough = jnp.clip(jax.random.normal(keys[2], (ROWS, ROW_LEN, D)), -5.0, 5.0)
    return (smooth + rough).astype(jnp.bfloat16)


def draw_doc_lengths(key, part):
    key = jax.random.fold_in(key, 5)
    first_key, second_key = jax.random.split(key)
    short_lengths = jax.random.randint(first_key, (ROWS, DOCS), LMK, 2 * LMK)
    first_row = jnp.arange(ROWS, dtype=jnp.int32)[:, None] == 0
    short_lengths = jnp.where(first_row, LMK, short_lengths)
    longest = jax.random.randint(second_key, (ROWS, 1), 0, DOCS)
    chosen = jnp.arange(DOCS, dtype=jnp.int32)[None, :] == longest
    others = jnp.sum(jnp.where(chosen, 0, short_lengths), axis=1, keepdims=True)
    return jnp.where(chosen, ROW_LEN - others, short_lengths).astype(jnp.int32)


def levels(rng, shape, cuts, low, largest):
    def one(dim, parts):
        steps = jax.random.uniform(jax.random.fold_in(jax.random.fold_in(rng, 6), dim), (parts,), jnp.float32, low / len(cuts), largest / len(cuts))
        return jnp.repeat(jnp.exp(steps), shape[dim] // parts).reshape((-1,) + (1,) * (len(shape) - dim - 1))

    factor_of = one(*cuts[0])
    for cut in cuts[1:]:
        factor_of = factor_of * one(*cut)
    return factor_of


def bell_draw(rng, dims, width, reach, cuts=(), kind=jnp.bfloat16):
    loudness = levels(rng, dims, cuts, -0.22, 0.18) if cuts else 1.0
    array = jax.random.normal(rng, dims, jnp.float32) * width * loudness
    return jnp.minimum(jnp.maximum(array, -reach), reach).astype(kind)


def setup_inputs(seed: int = 0) -> dict:
    key_of = jax.random.split(jax.random.key(seed), 13)
    tokens = draw_tokens(jax.random.fold_in(key_of[12], 71), 0)
    doc_lengths = draw_doc_lengths(jax.random.fold_in(key_of[12], 71), 0)
    w_qkv = bell_draw(key_of[2], (D, 3 * D), D ** -0.5, 0.21875)
    w_out = bell_draw(key_of[3], (D, D), D ** -0.5, 0.21875)
    conv_taps = bell_draw(key_of[4], (HEADS, KS), 0.1, 0.5, (), jnp.float32)
    norm1_gain = jnp.clip(1.0 + 0.15 * jax.random.normal(key_of[5], (D,), jnp.float32), 0.25, 1.75)
    norm1_bias = bell_draw(key_of[6], (D,), 0.3, 1.5, (), jnp.float32)
    w_up = bell_draw(key_of[7], (D, FF), D ** -0.5, 0.21875)
    w_down = bell_draw(key_of[8], (FF, D), FF ** -0.5, 0.109375)
    norm2_gain = jnp.clip(1.0 + 0.15 * jax.random.normal(key_of[9], (D,), jnp.float32), 0.25, 1.75)
    norm2_bias = bell_draw(key_of[10], (D,), 0.3, 1.5, (), jnp.float32)
    cotangent = bell_draw(key_of[11], (ROWS, ROW_LEN, D), 1.0, 6.0, ((0, 4), (1, 8)))
    return dict(tokens=tokens, doc_lengths=doc_lengths, w_qkv=w_qkv, w_out=w_out, conv_taps=conv_taps, norm1_gain=norm1_gain, norm1_bias=norm1_bias, w_up=w_up, w_down=w_down, norm2_gain=norm2_gain, norm2_bias=norm2_bias, cotangent=cotangent)


HIGHEST = lax.Precision.HIGHEST
EPSILON = 1e-05
BIG_NEGATIVE = -1e+30

@jax.custom_vjp
def low(v):
    return lax.optimization_barrier(v.astype(jnp.bfloat16)).astype(jnp.float32)

@jax.custom_vjp
def low_back(v):
    return v

def low_keep(v):
    return (low(v), None)

def low_pass(kept, grad):
    return (grad,)

def back_keep(v):
    return (v, None)

def back_low(kept, grad):
    return (low(grad),)
low.defvjp(low_keep, low_pass)
low_back.defvjp(back_keep, back_low)

def layout(lengths, places):
    doc_end = jnp.cumsum(lengths)
    doc_starts = doc_end - lengths
    doc_ids = lax.optimization_barrier(jnp.sum((places[:, None] >= doc_starts[None, :]).astype(jnp.int32), axis=1)) - 1
    chosen = (doc_ids[:, None] == jnp.arange(DOCS, dtype=jnp.int32)[None, :]).astype(jnp.int32)
    doc_length = lax.optimization_barrier(jnp.sum(chosen * lengths[None, :], axis=1))
    doc_start = lax.optimization_barrier(jnp.sum(chosen * doc_starts[None, :], axis=1))
    segment = (places - doc_start) * LMK // jnp.maximum(doc_length, 1)
    return (doc_ids, doc_ids * LMK + segment)

def slot_counts(lengths):
    mark_ids = jnp.arange(DOCS * LMK, dtype=jnp.int32)
    which_doc = mark_ids // LMK
    within = mark_ids % LMK
    chosen = (which_doc[:, None] == jnp.arange(DOCS, dtype=jnp.int32)[None, :]).astype(jnp.int32)
    doc_length = lax.optimization_barrier(jnp.sum(chosen * lengths[None, :], axis=1))
    upper = ((within + 1) * doc_length + LMK - 1) // LMK
    lower = (within * doc_length + LMK - 1) // LMK
    return (upper - lower).astype(jnp.float32)

def layer_norm(inputs, gain, bias):
    average = lax.optimization_barrier(jnp.mean(inputs, axis=-1, keepdims=True))
    centered = inputs - average
    variance = lax.optimization_barrier(jnp.mean(centered * centered, axis=-1, keepdims=True))
    return centered * lax.rsqrt(variance + EPSILON) * gain + bias

def gelu(inputs):
    return 0.5 * inputs * (1.0 + lax.erf(inputs * 0.7071067811865476))

def masked_softmax(scores, allowed):
    highest = lax.optimization_barrier(jnp.max(jnp.where(allowed, scores, BIG_NEGATIVE), axis=-1, keepdims=True))
    exponent = jnp.exp(jnp.where(allowed, scores - highest, BIG_NEGATIVE))
    return exponent / lax.optimization_barrier(jnp.sum(exponent, axis=-1, keepdims=True))

def landmark_inverse(query_marks, key_marks):
    query_docs = query_marks.reshape(DOCS, LMK, HEADS, HEAD)
    key_docs = key_marks.reshape(DOCS, LMK, HEADS, HEAD)
    scores = jnp.einsum('dlhe,dmhe->dhlm', query_docs, key_docs, precision=HIGHEST) * 0.125
    highest = lax.optimization_barrier(jnp.max(scores, axis=-1, keepdims=True))
    exponent = jnp.exp(scores - highest)
    kernel_a = exponent / lax.optimization_barrier(jnp.sum(exponent, axis=-1, keepdims=True))
    scale = lax.optimization_barrier(jnp.sum(kernel_a * kernel_a, axis=(2, 3), keepdims=True))
    approx = jnp.swapaxes(kernel_a, 2, 3) / scale
    identity = jnp.eye(LMK, dtype=jnp.float32)
    for sweep in range(NS_ITERS):
        product = jnp.einsum('dhlm,dhmn->dhln', kernel_a, approx, precision=HIGHEST)
        bracket = 7.0 * identity - product
        bracket = 15.0 * identity - jnp.einsum('dhlm,dhmn->dhln', product, bracket, precision=HIGHEST)
        bracket = 13.0 * identity - jnp.einsum('dhlm,dhmn->dhln', product, bracket, precision=HIGHEST)
        approx = 0.25 * jnp.einsum('dhlm,dhmn->dhln', approx, bracket, precision=HIGHEST)
    return approx

def layer(inputs, w_qkv, w_out, conv_taps, gain1, bias1, w_up, w_down, gain2, bias2, doc_ids, slot_ids, counts):
    row_count = inputs.shape[0]
    blocks = row_count // TOK_DEV
    slot_count = DOCS * LMK
    rim_width = (KS - 1) // 2
    joined = low(low_back(jnp.dot(inputs, w_qkv, precision=HIGHEST)))
    queries = joined[:, :D]
    key_rows = joined[:, D:2 * D]
    values = joined[:, 2 * D:]
    member = (slot_ids[None, :] == jnp.arange(slot_count, dtype=jnp.int32)[:, None]).astype(jnp.float32)
    landmark_sums = low_back(jnp.dot(member, joined[:, :2 * D], precision=HIGHEST))
    landmarks = low(landmark_sums / counts[:, None])
    query_marks = landmarks[:, :D]
    key_marks = landmarks[:, D:]
    approx = landmark_inverse(query_marks, key_marks)
    mark_doc = jnp.arange(slot_count, dtype=jnp.int32) // LMK
    qm_heads = query_marks.reshape(slot_count, HEADS, HEAD)
    km_heads = key_marks.reshape(slot_count, HEADS, HEAD)
    key_blocks = key_rows.reshape(blocks, TOK_DEV, HEADS, HEAD)
    value_blocks = values.reshape(blocks, TOK_DEV, HEADS, HEAD)
    query_blocks = queries.reshape(blocks, TOK_DEV, HEADS, HEAD)
    owner_blocks = doc_ids.reshape(blocks, TOK_DEV)

    def peak_block(pieces):
        key_block, owner_block = pieces
        scores = jnp.einsum('she,the->hst', qm_heads, key_block, precision=HIGHEST) * 0.125
        allowed = (mark_doc[:, None] == owner_block[None, :])[None]
        return lax.optimization_barrier(jnp.max(jnp.where(allowed, scores, BIG_NEGATIVE), axis=2))
    maxima = lax.optimization_barrier(jnp.max(lax.map(jax.checkpoint(peak_block), (key_blocks, owner_blocks)), axis=0))

    def total_block(pieces):
        key_block, value_block, owner_block = pieces
        scores = low_back(jnp.einsum('she,the->hst', qm_heads, key_block, precision=HIGHEST) * 0.125)
        allowed = (mark_doc[:, None] == owner_block[None, :])[None]
        exponent = jnp.exp(jnp.where(allowed, scores - maxima[:, :, None], BIG_NEGATIVE))
        weighted = jnp.einsum('hst,the->she', low(exponent), value_block, precision=HIGHEST)
        return (lax.optimization_barrier(jnp.sum(exponent, axis=2)), weighted)
    block_totals, block_weighted = lax.map(jax.checkpoint(total_block), (key_blocks, value_blocks, owner_blocks))
    denominator = lax.optimization_barrier(jnp.sum(block_totals, axis=0))
    weighted = lax.optimization_barrier(jnp.sum(block_weighted, axis=0))
    mixed_values = weighted / jnp.transpose(denominator)[:, :, None]
    mixed_docs = mixed_values.reshape(DOCS, LMK, HEADS, HEAD)
    carried = low(jnp.einsum('dhlm,dmhe->dlhe', approx, mixed_docs, precision=HIGHEST).reshape(slot_count, HEADS, HEAD))

    def query_block(pieces):
        query_piece, owner_block = pieces
        scores = low_back(jnp.einsum('the,she->ths', query_piece, km_heads, precision=HIGHEST) * 0.125)
        allowed = (owner_block[:, None] == mark_doc[None, :])[:, None, :]
        kernel = low(masked_softmax(scores, allowed))
        attended = jnp.einsum('ths,she->the', kernel, carried, precision=HIGHEST)
        return low_back(attended).reshape(TOK_DEV, D)
    attended = lax.map(jax.checkpoint(query_block), (query_blocks, owner_blocks)).reshape(row_count, D)
    tap_table = jnp.repeat(jnp.transpose(conv_taps), HEAD, axis=1)
    padded = jnp.pad(values, ((rim_width, rim_width), (0, 0)))
    around_ids = jnp.pad(doc_ids, (rim_width, rim_width), constant_values=-1)
    convolved = jnp.zeros((row_count, D), jnp.float32)
    for tap_index in range(KS):
        same_doc = (around_ids[tap_index:tap_index + row_count] == doc_ids)[:, None]
        convolved = convolved + jnp.where(same_doc, tap_table[tap_index] * padded[tap_index:tap_index + row_count], 0.0)
    mixture = low(attended + convolved)
    residual1 = inputs + low_back(jnp.dot(mixture, w_out, precision=HIGHEST))
    normed1 = layer_norm(residual1, gain1, bias1)
    upward = low_back(jnp.dot(low(normed1), w_up, precision=HIGHEST))
    activated = low(gelu(upward))
    residual2 = normed1 + low_back(jnp.dot(activated, w_down, precision=HIGHEST))
    return layer_norm(residual2, gain2, bias2)

def reference(tokens, doc_lengths, w_qkv, w_out, conv_taps, norm1_gain, norm1_bias, w_up, w_down, norm2_gain, norm2_bias, cotangent):
    params = (w_qkv.astype(jnp.float32), w_out.astype(jnp.float32), conv_taps.astype(jnp.float32), norm1_gain.astype(jnp.float32), norm1_bias.astype(jnp.float32), w_up.astype(jnp.float32), w_down.astype(jnp.float32), norm2_gain.astype(jnp.float32), norm2_bias.astype(jnp.float32))
    places = jnp.arange(ROW_LEN, dtype=jnp.int32)

    def one_row(running, row_data):
        row_tokens, lengths, row_cotangent = row_data
        doc_ids, slot_ids = layout(lengths, places)
        counts = slot_counts(lengths)

        def forward(inputs, *weights):
            return layer(inputs, *weights, doc_ids, slot_ids, counts)
        result, pullback = jax.vjp(forward, row_tokens.astype(jnp.float32), *params)
        gradients = pullback(row_cotangent.astype(jnp.float32))
        summed = tuple((before + fresh for before, fresh in zip(running, gradients[1:])))
        return (summed, (result.astype(jnp.bfloat16), gradients[0]))
    start = tuple((jnp.zeros_like(weight) for weight in params))
    totals, (results, grad_inputs) = lax.scan(one_row, start, (tokens, doc_lengths, cotangent))
    return (results, grad_inputs, totals[0], totals[1], totals[2], totals[3], totals[4], totals[5], totals[6], totals[7], totals[8])
```

```python
import functools

import jax
import jax.numpy as jnp
from jax import lax
from jax.experimental import pallas as pl
from jax.experimental.pallas import tpu as pltpu
from jax.sharding import PartitionSpec as P

MESH = pl.DeviceIdType.MESH

LMK = 64
NS_ITERS = 6
DOCS = 4


HIGHEST = lax.Precision.HIGHEST
EPSILON = 1e-05
BIG_NEGATIVE = -1e30


def extended(x, sides, width):
    for axis, dim in sides:
        count, length = (lax.axis_size(axis), x.shape[dim])
        up = [(i, (i + 1) % count) for i in range(count - 1)]
        down = [(j, i) for i, j in up]
        last = lax.slice_in_dim(x, length - width, length, axis=dim)
        first = lax.slice_in_dim(x, 0, width, axis=dim)
        before = lax.ppermute(last, axis, up)
        after = lax.ppermute(first, axis, down)
        x = jnp.concatenate([before, x, after], axis=dim)
    return x


def layout(lengths, places):
    doc_end = jnp.cumsum(lengths)
    doc_starts = doc_end - lengths
    doc_ids = jnp.sum((places[:, None] >= doc_starts[None, :]).astype(jnp.int32), axis=1) - 1
    chosen = (doc_ids[:, None] == jnp.arange(DOCS, dtype=jnp.int32)[None, :]).astype(jnp.int32)
    doc_length = jnp.sum(chosen * lengths[None, :], axis=1)
    doc_start = jnp.sum(chosen * doc_starts[None, :], axis=1)
    segment = (places - doc_start) * LMK // jnp.maximum(doc_length, 1)
    return (doc_ids, doc_ids * LMK + segment)


def slot_counts(lengths):
    mark_ids = jnp.arange(DOCS * LMK, dtype=jnp.int32)
    which_doc = mark_ids // LMK
    within = mark_ids % LMK
    chosen = (which_doc[:, None] == jnp.arange(DOCS, dtype=jnp.int32)[None, :]).astype(jnp.int32)
    doc_length = jnp.sum(chosen * lengths[None, :], axis=1)
    upper = ((within + 1) * doc_length + LMK - 1) // LMK
    lower = (within * doc_length + LMK - 1) // LMK
    return (upper - lower).astype(jnp.float32)


def layer_norm(inputs, gain, bias):
    average = jnp.mean(inputs, axis=-1, keepdims=True)
    centered = inputs - average
    variance = jnp.mean(centered * centered, axis=-1, keepdims=True)
    return centered * lax.rsqrt(variance + EPSILON) * gain + bias


def gelu(inputs):
    return 0.5 * inputs * (1.0 + lax.erf(inputs * 0.7071067811865476))


def masked_softmax(scores, allowed):
    highest = jnp.max(jnp.where(allowed, scores, BIG_NEGATIVE), axis=-1, keepdims=True)
    exponent = jnp.exp(jnp.where(allowed, scores - highest, BIG_NEGATIVE))
    return exponent / jnp.sum(exponent, axis=-1, keepdims=True)


def inverse_from_scores(scores):
    highest = jnp.max(scores, axis=-1, keepdims=True)
    exponent = jnp.exp(scores - highest)
    kernel_a = exponent / jnp.sum(exponent, axis=-1, keepdims=True)
    scale = jnp.sum(kernel_a * kernel_a, axis=(2, 3), keepdims=True)
    approx = jnp.swapaxes(kernel_a, 2, 3) / scale
    identity = jnp.eye(LMK, dtype=jnp.float32)
    for sweep in range(NS_ITERS):
        product = jnp.einsum("dhlm,dhmn->dhln", kernel_a, approx, precision=HIGHEST)
        bracket = 7.0 * identity - product
        bracket = 15.0 * identity - jnp.einsum(
            "dhlm,dhmn->dhln", product, bracket, precision=HIGHEST
        )
        bracket = 13.0 * identity - jnp.einsum(
            "dhlm,dhmn->dhln", product, bracket, precision=HIGHEST
        )
        approx = 0.25 * jnp.einsum("dhlm,dhmn->dhln", approx, bracket, precision=HIGHEST)
    return approx


def split_heads(matrix, head_count):
    return matrix.reshape(matrix.shape[0], head_count, matrix.shape[1] // head_count)


def wsum_kernel(dims, gq, go, gu, gd, sm, oq, oo, ou, od, osm, own, out, r0, r1, r2, r3, smr, lsem, osem, ss, rs, sss, srs):
    s_ax, r_ax = lax.axis_index("seq"), lax.axis_index("row")
    z, x, y, c = s_ax // 2, s_ax % 2, r_ax // 2, r_ax % 2
    x1, y1 = x + (1 - c) * (1 - 2 * x), y + c * (1 - 2 * y)
    x2, y2 = x + c * (1 - 2 * x), y + (1 - c) * (1 - 2 * y)
    core_dev = (s_ax, y * 2 + (1 - c))
    d1_dev = (z * 2 + x1, y1 * 2 + c)
    d2_dev = (z * 2 + x2, y2 * 2 + c)
    z_devs = [(lax.rem(z + k, 4) * 2 + x, r_ax) for k in (1, 2, 3)]
    peers = [core_dev, d1_dev, d2_dev] + z_devs
    b1 = x * (1 - c) + y * c
    b2 = y * (1 - c) + x * c
    barrier = pltpu.get_barrier_semaphore()
    for p in peers:
        pl.semaphore_signal(barrier, inc=1, device_id=p, device_id_type=MESH)
    units = [(gq, oq, 0, i) for i in range(3)] + [(go, oo, 0, 0)]
    units = [(gd, od, i, 0) for i in range(4)] + [(gu, ou, 0, i) for i in range(4)] + [(go, oo, 0, 0)] + [(gq, oq, 0, i) for i in range(3)]
    n_units = len(units)
    W, H = 768, 384
    mine = pl.ds(pl.multiple_of(c * H, 128), H)
    other = pl.ds(pl.multiple_of((1 - c) * H, 128), H)

    def block(ref, i, j):
        return ref.at[pl.ds(i * W, W), pl.ds(j * W, W)]

    loads = []
    for u, (src, _, i, j) in enumerate(units):
        cp = pltpu.make_async_copy(block(src, i, j), own.at[u], lsem.at[u])
        cp.start()
        loads.append(cp)
    pl.semaphore_wait(barrier, len(peers))

    def remote(src, dst, u, k, dev):
        cp = pltpu.make_async_remote_copy(src_ref=src, dst_ref=dst, send_sem=ss.at[u, k], recv_sem=rs.at[u, k], device_id=dev, device_id_type=MESH)
        cp.start()
        return cp

    def rows(start, size):
        return pl.ds(pl.multiple_of(start, 16), size)

    def add_rows(dst, dst_at, a, a_at, b, b_at, n, step):
        @pl.loop(0, n, step=step)
        def _(t):
            s = a(a_at + t, step).astype(jnp.float32) + b(b_at + t, step).astype(jnp.float32)
            dst(dst_at + t, step, s.astype(jnp.bfloat16))

    pend = {}
    base1 = b1 * 384
    base2 = b1 * 384 + b2 * 192
    base3 = base2 + z * 48

    def step(u, s):
        if s == 0:
            loads[u].wait()
            pend[u, 0] = remote(own.at[u, :, other], r0.at[u], u, 0, core_dev)
        elif s == 1:
            pend[u, 0].wait_recv()

            @pl.loop(0, 768, step=64)
            def _(t):
                q = pl.ds(pl.multiple_of(t, 64), 64)
                r0[u, q, :] = (r0[u, q, :].astype(jnp.float32) + own[u, q, mine].astype(jnp.float32)).astype(jnp.bfloat16)

            pend[u, 1] = remote(r0.at[u, rows((1 - b1) * 384, 384), :], r1.at[u], u, 1, d1_dev)
        elif s == 2:
            pend[u, 1].wait_recv()

            @pl.loop(0, 384, step=64)
            def _(t):
                q = pl.ds(pl.multiple_of(t, 64), 64)
                r1[u, q, :] = (r1[u, q, :].astype(jnp.float32) + r0[u, rows(base1 + t, 64), :].astype(jnp.float32)).astype(jnp.bfloat16)

            pend[u, 2] = remote(r1.at[u, rows((1 - b2) * 192, 192), :], r2.at[u], u, 2, d2_dev)
        elif s == 3:
            pend[u, 2].wait_recv()

            @pl.loop(0, 192, step=64)
            def _(t):
                q = pl.ds(pl.multiple_of(t, 64), 64)
                r2[u, q, :] = (r2[u, q, :].astype(jnp.float32) + r1[u, rows(b2 * 192 + t, 64), :].astype(jnp.float32)).astype(jnp.bfloat16)

            for k in range(3):
                zz = lax.rem(z + k + 1, 4)
                pend[u, 3 + k] = remote(r2.at[u, rows(zz * 48, 48), :], r3.at[u, k], u, 3 + k, z_devs[k])
        elif s == 4:
            for k in range(3):
                pend[u, 3 + k].wait_recv()
            tot = r2[u, rows(z * 48, 48), :].astype(jnp.float32)
            for k in range(3):
                tot = tot + r3[u, k].astype(jnp.float32)
            out[u, rows(base3, 48), mine] = tot.astype(jnp.bfloat16)
            region = out.at[u, rows(base3, 48), mine]
            for k in range(3):
                pend[u, 6 + k] = remote(region, region, u, 6 + k, z_devs[k])
        elif s == 5:
            for k in range(3):
                pend[u, 6 + k].wait_recv()
            region = out.at[u, rows(base2, 192), mine]
            pend[u, 9] = remote(region, region, u, 9, d2_dev)
        elif s == 6:
            pend[u, 9].wait_recv()
            region = out.at[u, rows(base1, 384), mine]
            pend[u, 10] = remote(region, region, u, 10, d1_dev)
        elif s == 7:
            pend[u, 10].wait_recv()
            region = out.at[u, :, mine]
            pend[u, 11] = remote(region, region, u, 11, core_dev)
        elif s == 8:
            pend[u, 11].wait_recv()
            _, dst, i, j = units[u]
            cp = pltpu.make_async_copy(out.at[u], block(dst, i, j), osem.at[u])
            cp.start()
            pend[u, 12] = cp

    small = {}
    small_devs = [core_dev, d1_dev, d2_dev, (lax.rem(z + 2, 4) * 2 + x, r_ax), ((z + 1 - 2 * lax.rem(z, 2)) * 2 + x, r_ax)]

    def small_step(k):
        if k == 0:
            smr[0] = sm[...]
        else:
            small[k - 1].wait_recv()
            smr[k] = smr[k - 1] + smr[k + 5]
        if k < 5:
            small[k] = pltpu.make_async_remote_copy(src_ref=smr.at[k], dst_ref=smr.at[k + 6], send_sem=sss.at[k], recv_sem=srs.at[k], device_id=small_devs[k], device_id_type=MESH)
            small[k].start()
        else:
            osm[...] = smr[5]

    for tau in range(n_units + 8):
        for s in range(8, -1, -1):
            u = tau - s
            if 0 <= u < n_units:
                step(u, s)
        if tau < 6:
            small_step(tau)
    for u in range(n_units):
        for k in range(12):
            pend[u, k].wait_send()
        pend[u, 12].wait()
    for k in range(5):
        small[k].wait_send()


def weight_sums(gq, go, gu, gd, sm):
    n = 12
    bf = jnp.bfloat16
    return pl.pallas_call(
        functools.partial(wsum_kernel, None),
        out_shape=(
            jax.ShapeDtypeStruct(gq.shape, bf),
            jax.ShapeDtypeStruct(go.shape, bf),
            jax.ShapeDtypeStruct(gu.shape, bf),
            jax.ShapeDtypeStruct(gd.shape, bf),
            jax.ShapeDtypeStruct(sm.shape, sm.dtype),
        ),
        in_specs=[pl.BlockSpec(memory_space=pl.ANY)] * 4 + [pl.BlockSpec(memory_space=pltpu.VMEM)],
        out_specs=[pl.BlockSpec(memory_space=pl.ANY)] * 4 + [pl.BlockSpec(memory_space=pltpu.VMEM)],
        scratch_shapes=[
            pltpu.VMEM((n, 768, 768), bf),
            pltpu.VMEM((n, 768, 768), bf),
            pltpu.VMEM((n, 768, 384), bf),
            pltpu.VMEM((n, 384, 384), bf),
            pltpu.VMEM((n, 192, 384), bf),
            pltpu.VMEM((n, 3, 48, 384), bf),
            pltpu.VMEM((11,) + sm.shape, jnp.float32),
            pltpu.SemaphoreType.DMA((n,)),
            pltpu.SemaphoreType.DMA((n,)),
            pltpu.SemaphoreType.DMA((n, 12)),
            pltpu.SemaphoreType.DMA((n, 12)),
            pltpu.SemaphoreType.DMA((5,)),
            pltpu.SemaphoreType.DMA((5,)),
        ],
        compiler_params=pltpu.CompilerParams(collective_id=10, has_side_effects=True, vmem_limit_bytes=60 * 2**20),
        name="weight_sums",
    )(gq, go, gu, gd, sm)


def on_device(
    tokens,
    doc_lengths,
    w_qkv,
    w_out,
    conv_taps,
    norm1_gain,
    norm1_bias,
    w_up,
    w_down,
    norm2_gain,
    norm2_bias,
    cotangent,
):
    shard_len = tokens.shape[1]
    model_width = tokens.shape[2]
    head_count = conv_taps.shape[0]
    tap_count = conv_taps.shape[1]
    head_width = model_width // head_count
    slot_count = DOCS * LMK
    rim_width = (tap_count - 1) // 2
    shard_start = lax.axis_index("seq") * shard_len
    lengths = doc_lengths[0]
    doc_ids, slot_ids = layout(lengths, shard_start + jnp.arange(shard_len, dtype=jnp.int32))
    around_ids = layout(
        lengths, shard_start - rim_width + jnp.arange(shard_len + 2 * rim_width, dtype=jnp.int32)
    )[0]
    counts = slot_counts(lengths)
    mark_doc = jnp.arange(slot_count, dtype=jnp.int32) // LMK
    inputs = tokens[0]
    joined = jnp.dot(inputs, w_qkv, preferred_element_type=jnp.float32).astype(jnp.bfloat16)
    queries = joined[:, :model_width]
    key_rows = joined[:, model_width : 2 * model_width]
    values = joined[:, 2 * model_width :]
    member = (slot_ids[None, :] == jnp.arange(slot_count, dtype=jnp.int32)[:, None]).astype(
        jnp.bfloat16
    )
    partial_sums = jnp.dot(member, joined[:, : 2 * model_width], preferred_element_type=jnp.float32)
    landmark_sums = lax.psum(partial_sums, "seq")
    landmarks = (landmark_sums / counts[:, None]).astype(jnp.bfloat16)
    query_marks = landmarks[:, :model_width]
    key_marks = landmarks[:, model_width:]
    query_docs = query_marks.reshape(DOCS, LMK, head_count, head_width)
    key_docs = key_marks.reshape(DOCS, LMK, head_count, head_width)
    mark_scores = (
        jnp.einsum("dlhe,dmhe->dhlm", query_docs, key_docs, preferred_element_type=jnp.float32)
        * 0.125
    )
    approx, inverse_pull = jax.vjp(inverse_from_scores, mark_scores)
    qm_heads = split_heads(query_marks, head_count)
    km_heads = split_heads(key_marks, head_count)
    query_heads = split_heads(queries, head_count)
    key_heads = split_heads(key_rows, head_count)
    value_heads = split_heads(values, head_count)
    key_allowed = (mark_doc[:, None] == doc_ids[None, :])[None]
    scores_b = (
        jnp.einsum("she,the->hst", qm_heads, key_heads, preferred_element_type=jnp.float32) * 0.125
    )
    maxima = lax.pmax(jnp.max(jnp.where(key_allowed, scores_b, BIG_NEGATIVE), axis=2), "seq")
    exponent = jnp.exp(jnp.where(key_allowed, scores_b - maxima[:, :, None], BIG_NEGATIVE))
    weights_b = exponent.astype(jnp.bfloat16)
    weighted_part = jnp.einsum(
        "hst,the->she", weights_b, value_heads, preferred_element_type=jnp.float32
    )
    denominator, weighted = lax.psum((jnp.sum(exponent, axis=2), weighted_part), "seq")
    mixed_values = weighted / jnp.transpose(denominator)[:, :, None]
    mixed_docs = mixed_values.reshape(DOCS, LMK, head_count, -1)
    carried = (
        jnp.einsum("dhlm,dmhe->dlhe", approx, mixed_docs, precision=HIGHEST)
        .reshape(slot_count, head_count, -1)
        .astype(jnp.bfloat16)
    )
    query_allowed = (doc_ids[:, None] == mark_doc[None, :])[:, None, :]
    scores_f = (
        jnp.einsum("the,she->ths", query_heads, km_heads, preferred_element_type=jnp.float32)
        * 0.125
    )
    kernel = masked_softmax(scores_f, query_allowed)
    kernel_b = kernel.astype(jnp.bfloat16)
    attended = jnp.einsum(
        "ths,she->the", kernel_b, carried, preferred_element_type=jnp.float32
    ).reshape(shard_len, model_width)
    tap_table = jnp.repeat(jnp.transpose(conv_taps), head_width, axis=1)
    padded = extended(values, (("seq", 0),), rim_width)
    convolved = jnp.zeros((shard_len, model_width), jnp.float32)
    for tap_index in range(tap_count):
        same_doc = (around_ids[tap_index : tap_index + shard_len] == doc_ids)[:, None]
        convolved = convolved + jnp.where(
            same_doc,
            tap_table[tap_index] * padded[tap_index : tap_index + shard_len].astype(jnp.float32),
            0.0,
        )
    mixture_b = (attended + convolved).astype(jnp.bfloat16)
    residual1 = inputs.astype(jnp.float32) + jnp.dot(
        mixture_b, w_out, preferred_element_type=jnp.float32
    )
    normed1, norm1_pull = jax.vjp(layer_norm, residual1, norm1_gain, norm1_bias)
    normed1_b = normed1.astype(jnp.bfloat16)
    upward = jnp.dot(normed1_b, w_up, preferred_element_type=jnp.float32)
    activated_wide, gelu_pull = jax.vjp(gelu, upward)
    activated = activated_wide.astype(jnp.bfloat16)
    residual2 = normed1 + jnp.dot(activated, w_down, preferred_element_type=jnp.float32)
    result, norm2_pull = jax.vjp(layer_norm, residual2, norm2_gain, norm2_bias)
    delta_residual2, delta_gain2, delta_bias2 = norm2_pull(cotangent[0].astype(jnp.float32))
    delta_down = delta_residual2.astype(jnp.bfloat16)
    grad_down = jnp.dot(activated.T, delta_down, preferred_element_type=jnp.float32)
    delta_active = jnp.dot(delta_down, w_down.T, preferred_element_type=jnp.float32)
    delta_up = gelu_pull(delta_active)[0].astype(jnp.bfloat16)
    grad_up = jnp.dot(normed1_b.T, delta_up, preferred_element_type=jnp.float32)
    delta_normed1 = delta_residual2 + jnp.dot(delta_up, w_up.T, preferred_element_type=jnp.float32)
    delta_residual1, delta_gain1, delta_bias1 = norm1_pull(delta_normed1)
    delta_output = delta_residual1.astype(jnp.bfloat16)
    grad_output = jnp.dot(mixture_b.T, delta_output, preferred_element_type=jnp.float32)
    delta_mixture = jnp.dot(delta_output, w_out.T, preferred_element_type=jnp.float32)
    delta_padded = extended(delta_mixture.astype(jnp.bfloat16), (("seq", 0),), rim_width).astype(
        delta_mixture.dtype
    )
    delta_conv_values = jnp.zeros((shard_len, model_width), jnp.float32)
    tap_terms = []
    for tap_index in range(tap_count):
        same_doc = (around_ids[tap_index : tap_index + shard_len] == doc_ids)[:, None]
        mirror = 2 * rim_width - tap_index
        same_back = (around_ids[mirror : mirror + shard_len] == doc_ids)[:, None]
        delta_conv_values = delta_conv_values + jnp.where(
            same_back, tap_table[tap_index] * delta_padded[mirror : mirror + shard_len], 0.0
        )
        tap_terms.append(
            jnp.sum(
                jnp.where(
                    same_doc,
                    delta_mixture * padded[tap_index : tap_index + shard_len].astype(jnp.float32),
                    0.0,
                ),
                axis=0,
            )
        )
    grad_taps = jnp.transpose(
        jnp.sum(jnp.stack(tap_terms).reshape(tap_count, head_count, -1), axis=2)
    )
    delta_attended = split_heads(delta_mixture.astype(jnp.bfloat16), head_count)
    carried_part = jnp.einsum(
        "ths,the->she", kernel_b, delta_attended, preferred_element_type=jnp.float32
    )
    delta_kernel = jnp.einsum(
        "the,she->ths", delta_attended, carried, preferred_element_type=jnp.float32
    )
    delta_scores_f = (
        kernel * (delta_kernel - jnp.sum(kernel * delta_kernel, axis=2, keepdims=True))
    ).astype(jnp.bfloat16)
    delta_queries_f = (
        jnp.einsum("ths,she->the", delta_scores_f, km_heads, preferred_element_type=jnp.float32)
        * 0.125
    )
    keymark_part = (
        jnp.einsum("ths,the->she", delta_scores_f, query_heads, preferred_element_type=jnp.float32)
        * 0.125
    )
    delta_carried, delta_keymarks_f = lax.psum(
        (carried_part, keymark_part.reshape(slot_count, model_width)), "seq"
    )
    delta_carried_docs = delta_carried.reshape(DOCS, LMK, head_count, -1)
    delta_approx = jnp.einsum("dlhe,dmhe->dhlm", delta_carried_docs, mixed_docs, precision=HIGHEST)
    delta_mixed = jnp.einsum(
        "dhlm,dlhe->dmhe", approx, delta_carried_docs, precision=HIGHEST
    ).reshape(slot_count, head_count, -1)
    delta_mark_scores = inverse_pull(delta_approx)[0]
    key_docs_wide = key_docs.astype(jnp.float32)
    query_docs_wide = query_docs.astype(jnp.float32)
    delta_querymarks_a = (
        jnp.einsum("dhlm,dmhe->dlhe", delta_mark_scores, key_docs_wide, precision=HIGHEST) * 0.125
    ).reshape(slot_count, model_width)
    delta_keymarks_a = (
        jnp.einsum("dhlm,dlhe->dmhe", delta_mark_scores, query_docs_wide, precision=HIGHEST) * 0.125
    ).reshape(slot_count, model_width)
    scaled_grad = delta_mixed / jnp.transpose(denominator)[:, :, None]
    upper_part = scaled_grad.astype(jnp.bfloat16)
    lower_part = (scaled_grad - upper_part.astype(jnp.float32)).astype(jnp.bfloat16)
    delta_values_b = jnp.einsum(
        "hst,she->the", weights_b, upper_part, preferred_element_type=jnp.float32
    ) + jnp.einsum("hst,she->the", weights_b, lower_part, preferred_element_type=jnp.float32)
    along_values = jnp.einsum(
        "the,she->hst", value_heads, upper_part, preferred_element_type=jnp.float32
    ) + jnp.einsum("the,she->hst", value_heads, lower_part, preferred_element_type=jnp.float32)
    along_mixed = jnp.transpose(jnp.sum(scaled_grad * mixed_values, axis=2))
    delta_scores_b = (exponent * (along_values - along_mixed[:, :, None])).astype(jnp.bfloat16)
    delta_keys_b = (
        jnp.einsum("hst,she->the", delta_scores_b, qm_heads, preferred_element_type=jnp.float32)
        * 0.125
    )
    querymark_part = (
        jnp.einsum("hst,the->she", delta_scores_b, key_heads, preferred_element_type=jnp.float32)
        * 0.125
    )
    delta_querymarks_b = lax.psum(querymark_part.reshape(slot_count, model_width), "seq")
    delta_query_sums = ((delta_querymarks_a + delta_querymarks_b) / counts[:, None]).astype(
        jnp.bfloat16
    )
    delta_key_sums = ((delta_keymarks_a + delta_keymarks_f) / counts[:, None]).astype(jnp.bfloat16)
    from_marks = jnp.dot(
        member.T,
        jnp.concatenate([delta_query_sums, delta_key_sums], axis=1),
        preferred_element_type=jnp.float32,
    )
    delta_joined = jnp.concatenate(
        [
            delta_queries_f.reshape(shard_len, model_width) + from_marks[:, :model_width],
            delta_keys_b.reshape(shard_len, model_width) + from_marks[:, model_width:],
            delta_values_b.reshape(shard_len, model_width) + delta_conv_values,
        ],
        axis=1,
    ).astype(jnp.bfloat16)
    grad_joined = jnp.dot(inputs.T, delta_joined, preferred_element_type=jnp.float32)
    delta_inputs = delta_residual1 + jnp.dot(
        delta_joined, w_qkv.T, preferred_element_type=jnp.float32
    )
    norm_terms = jnp.stack([delta_gain1, delta_bias1, delta_gain2, delta_bias2])
    if lax.axis_size("seq") == 8 and lax.axis_size("row") == 4:
        bf = jnp.bfloat16
        taps_row = jnp.pad(grad_taps.reshape(1, -1), ((0, 3), (0, model_width - grad_taps.size)))
        sm = jnp.concatenate([norm_terms, taps_row], axis=0)
        tq, to, tu, td, tsm = weight_sums(grad_joined.astype(bf), grad_output.astype(bf), grad_up.astype(bf), grad_down.astype(bf), sm)
        f32 = jnp.float32
        return (
            result.astype(jnp.bfloat16)[None],
            delta_inputs[None],
            tq.astype(f32),
            to.astype(f32),
            tsm[4, : grad_taps.size].reshape(grad_taps.shape),
            tsm[0],
            tsm[1],
            tu.astype(f32),
            td.astype(f32),
            tsm[2],
            tsm[3],
        )
    taps_total, norms_total = lax.psum((grad_taps, norm_terms), ("seq", "row"))
    groups = lax.axis_size(("seq", "row"))
    summed = (
        lax.psum_scatter(
            grad_joined.reshape(groups, -1), ("seq", "row"), scatter_dimension=0, tiled=True
        ),
        lax.psum_scatter(
            grad_output.reshape(groups, -1), ("seq", "row"), scatter_dimension=0, tiled=True
        ),
        lax.psum_scatter(
            grad_up.reshape(groups, -1), ("seq", "row"), scatter_dimension=0, tiled=True
        ),
        lax.psum_scatter(
            grad_down.reshape(groups, -1), ("seq", "row"), scatter_dimension=0, tiled=True
        ),
    )
    gathered = (
        lax.all_gather(summed[0].astype(jnp.bfloat16), ("seq", "row"), axis=0, tiled=True).astype(
            jnp.float32
        ),
        lax.all_gather(summed[1].astype(jnp.bfloat16), ("seq", "row"), axis=0, tiled=True).astype(
            jnp.float32
        ),
        lax.all_gather(summed[2].astype(jnp.bfloat16), ("seq", "row"), axis=0, tiled=True).astype(
            jnp.float32
        ),
        lax.all_gather(summed[3].astype(jnp.bfloat16), ("seq", "row"), axis=0, tiled=True).astype(
            jnp.float32
        ),
    )
    return (
        result.astype(jnp.bfloat16)[None],
        delta_inputs[None],
        gathered[0].reshape(grad_joined.shape),
        gathered[1].reshape(grad_output.shape),
        taps_total,
        norms_total[0],
        norms_total[1],
        gathered[2].reshape(grad_up.shape),
        gathered[3].reshape(grad_down.shape),
        norms_total[2],
        norms_total[3],
    )


def solution(mesh):
    return jax.shard_map(
        on_device,
        mesh=mesh,
        in_specs=(
            P("row", "seq", None),
            P("row", None),
            P(),
            P(),
            P(),
            P(),
            P(),
            P(),
            P(),
            P(),
            P(),
            P("row", "seq", None),
        ),
        out_specs=(
            P("row", "seq", None),
            P("row", "seq", None),
            P(),
            P(),
            P(),
            P(),
            P(),
            P(),
            P(),
            P(),
            P(),
        ),
        check_vma=False,
    )
```

```python
import functools

import jax
import jax.numpy as jnp
from jax import lax
from jax.experimental import pallas as pl
from jax.experimental.pallas import tpu as pltpu
from jax.sharding import PartitionSpec as P

MESH = pl.DeviceIdType.MESH

LMK = 64
NS_ITERS = 6
DOCS = 4


HIGHEST = lax.Precision.HIGHEST
EPSILON = 1e-05
BIG_NEGATIVE = -1e30


def long_first(lengths):
    starts = jnp.cumsum(lengths) - lengths
    longest = jnp.argmax(lengths)
    others = jnp.arange(DOCS - 1, dtype=jnp.int32)
    others = others + (others >= longest).astype(jnp.int32)
    order = jnp.concatenate([longest.astype(jnp.int32)[None], others])
    chosen = (order[:, None] == jnp.arange(DOCS, dtype=jnp.int32)[None, :]).astype(jnp.int32)
    return jnp.sum(chosen * lengths[None, :], axis=1), jnp.sum(chosen * starts[None, :], axis=1)


def slots(lengths, starts, places):
    inside = (places[:, None] >= starts[None, :]) & (places[:, None] < (starts + lengths)[None, :])
    inside = inside.astype(jnp.int32)
    doc = jnp.sum(inside * jnp.arange(DOCS, dtype=jnp.int32)[None, :], axis=1)
    length = jnp.sum(inside * lengths[None, :], axis=1)
    start = jnp.sum(inside * starts[None, :], axis=1)
    return doc * LMK + (places - start) * LMK // jnp.maximum(length, 1)


def slot_counts(lengths):
    mark_ids = jnp.arange(DOCS * LMK, dtype=jnp.int32)
    which_doc = mark_ids // LMK
    within = mark_ids % LMK
    chosen = (which_doc[:, None] == jnp.arange(DOCS, dtype=jnp.int32)[None, :]).astype(jnp.int32)
    doc_length = jnp.sum(chosen * lengths[None, :], axis=1)
    upper = ((within + 1) * doc_length + LMK - 1) // LMK
    lower = (within * doc_length + LMK - 1) // LMK
    return (upper - lower).astype(jnp.float32)


def layer_norm(inputs, gain, bias):
    average = jnp.mean(inputs, axis=-1, keepdims=True)
    centered = inputs - average
    variance = jnp.mean(centered * centered, axis=-1, keepdims=True)
    return centered * lax.rsqrt(variance + EPSILON) * gain + bias


def gelu(inputs):
    return 0.5 * inputs * (1.0 + lax.erf(inputs * 0.7071067811865476))


F32, BF16 = jnp.float32, jnp.bfloat16
GROUP = 256
PAIR = 128
PAIRS = 6
SMALL = DOCS - 1
WINDOW = 256
VMEM = pltpu.VMEM


def dot(a, b, dims=((1,), (0,)), precision=None):
    return lax.dot_general(a, b, (dims, ((), ())), preferred_element_type=F32, precision=precision)


NT, TN = ((1,), (1,)), ((0,), (0,))


def head_mask(width):
    rows = lax.broadcasted_iota(jnp.int32, (width, width), 0)
    lanes = lax.broadcasted_iota(jnp.int32, (width, width), 1)
    return (rows // LMK) == (lanes // LMK)


def blocks_of(side, width):
    tiled = jnp.concatenate([side] * (width // LMK), axis=0)
    return jnp.where(head_mask(width), tiled, jnp.zeros_like(tiled))


def side_of(full, width):
    full = jnp.where(head_mask(width), full, 0.0)
    return sum(full[i * LMK : (i + 1) * LMK] for i in range(width // LMK))


def flipped(side, width):
    return side_of(jnp.transpose(blocks_of(side, width)), width)


def head_ones(width):
    return jnp.where(head_mask(width), 1.0, 0.0).astype(F32)


def column_of(row, width):
    slots = lax.broadcasted_iota(jnp.int32, (LMK, width), 0)
    lanes = lax.broadcasted_iota(jnp.int32, (LMK, width), 1)
    picked = jnp.where(slots == lanes % LMK, jnp.broadcast_to(row, (LMK, width)), 0.0)
    return dot(picked, head_ones(width), precision=HIGHEST)


def row_of(side, width):
    return dot(jnp.ones((8, width), F32), blocks_of(side, width), NT, precision=HIGHEST)


def halves(x):
    high = x.astype(BF16)
    return high, (x - high.astype(F32)).astype(BF16)


def product3(a, b, dims):
    high, low = halves(a)
    b_high, b_low = halves(b)
    rows = a.shape[0]
    both = dot(jnp.concatenate([high, low], axis=0), b_high, dims)
    return both[:rows] + both[rows:] + dot(high, b_low, dims)


def mul(a, b, width):
    return product3(a, blocks_of(b, width), ((1,), (0,)))


def mul_nt(a, b, width):
    return product3(a, blocks_of(b, width), NT)


def side_eye(width):
    slots = lax.broadcasted_iota(jnp.int32, (LMK, width), 0)
    lanes = lax.broadcasted_iota(jnp.int32, (LMK, width), 1)
    return jnp.where(slots == lanes % LMK, 1.0, 0.0).astype(F32)


def head_total(side, width):
    columns = jnp.broadcast_to(jnp.sum(side, axis=0, keepdims=True), (8, width))
    return dot(columns, head_ones(width), precision=HIGHEST)[:1]


def head_max(scores, width):
    out = []
    for i in range(width // PAIR):
        part = scores[:, i * PAIR : (i + 1) * PAIR]
        left = lax.broadcasted_iota(jnp.int32, part.shape, 1) < LMK
        low = jnp.max(jnp.where(left, part, BIG_NEGATIVE), axis=1, keepdims=True)
        high = jnp.max(jnp.where(left, BIG_NEGATIVE, part), axis=1, keepdims=True)
        out.append(jnp.where(left, low, high))
    return out[0] if len(out) == 1 else jnp.concatenate(out, axis=1)


def inverse_forward(qm, km, save, width):
    scores = dot(qm, blocks_of(km, width), NT) * 0.125
    exponent = jnp.exp(scores - head_max(scores, width))
    kernel_a = exponent / dot(exponent, head_ones(width), precision=HIGHEST)
    scale = head_total(kernel_a * kernel_a, width)
    approx = flipped(kernel_a, width) / scale
    eye = side_eye(width)
    save(3 * NS_ITERS + 1, kernel_a)
    for sweep in range(NS_ITERS):
        product = mul(kernel_a, approx, width)
        square = mul(product, product, width)
        cube = mul(square, product, width)
        poly = 3.25 * eye - 3.75 * product + 1.75 * square - 0.25 * cube
        save(3 * sweep, approx)
        save(3 * sweep + 1, product)
        save(3 * sweep + 2, poly)
        approx = mul(approx, poly, width)
    save(3 * NS_ITERS, approx)
    return approx


def inverse_backward(d_approx, saved, width):
    kernel_a = saved(3 * NS_ITERS + 1)
    kernel_at = flipped(kernel_a, width)
    d_kernel = jnp.zeros_like(kernel_a)
    for sweep in reversed(range(NS_ITERS)):
        approx, product, poly = saved(3 * sweep), saved(3 * sweep + 1), saved(3 * sweep + 2)
        product_t = flipped(product, width)
        d_poly = mul(flipped(approx, width), d_approx, width)
        d_next = mul_nt(d_approx, poly, width)
        right = mul_nt(d_poly, product, width)
        both = right + mul(product_t, d_poly, width)
        d_product = -3.75 * d_poly + 1.75 * both - 0.25 * (mul_nt(right, product, width) + mul(product_t, both, width))
        d_kernel = d_kernel + mul_nt(d_product, approx, width)
        d_approx = d_next + mul(kernel_at, d_product, width)
    first = saved(0)
    scale = head_total(kernel_a * kernel_a, width)
    d_scale = -head_total(d_approx * first, width) / scale
    d_kernel = d_kernel + flipped(d_approx, width) / scale + 2.0 * kernel_a * d_scale
    inner = dot(d_kernel * kernel_a, head_ones(width), precision=HIGHEST)
    return kernel_a * (d_kernel - inner)


def stacked(side):
    return blocks_of(side, GROUP)


def joint(ref):
    return jnp.concatenate([ref[0], ref[1]], axis=1)


def write_pairs(ref, at, value):
    ref[0, at, :] = value[:, :PAIR]
    ref[1, at, :] = value[:, PAIR:]


LONG_SPEC = pl.BlockSpec((2, LMK, PAIR), lambda g: (g, 0, 0))
ROW_SPEC = pl.BlockSpec((2, 8, PAIR), lambda g: (g, 0, 0))
SMALL_SPEC = pl.BlockSpec((SMALL, None, LMK, GROUP), lambda g: (0, g, 0, 0))
SMALL_ROW_SPEC = pl.BlockSpec((SMALL, None, 8, GROUP), lambda g: (0, g, 0, 0))
TOP = slice(0, LMK)


def for_docs(info, total, body):
    def inside(doc, size, start):
        rows = lax.broadcasted_iota(jnp.int32, (size, 1), 0) + start
        return (rows >= info[2 * doc]) & (rows < info[2 * doc + 1])

    body(0, total, 0, inside(0, total, 0))
    for doc in range(1, DOCS):
        low, high = info[2 * doc], info[2 * doc + 1]
        start = jnp.minimum(low // 16 * 16, total - WINDOW)

        @pl.when((high > low) & (high - start <= WINDOW))
        def _():
            at = pl.multiple_of(start, 16)
            body(doc, WINDOW, at, inside(doc, WINDOW, at))

        @pl.when(high - start > WINDOW)
        def _():
            body(doc, total, 0, inside(doc, total, 0))


def mix_kernel(info, keys, values, qm, qms, exps, part, parts, stats):
    parts[...] = jnp.zeros_like(parts)
    stats[...] = jnp.zeros_like(stats)
    part[...] = jnp.zeros_like(part)

    def body(doc, size, start, inside):
        rows = pl.ds(start, size)
        marks = stacked(joint(qm) if doc == 0 else qms[doc - 1])
        scores = jnp.where(inside, dot(keys[rows, :], marks, NT) * 0.125, BIG_NEGATIVE)
        top = jnp.max(scores, axis=0, keepdims=True)
        wide = jnp.exp(scores - top)
        narrow = wide.astype(BF16)
        weighted = side_of(dot(narrow, values[rows, :], TN), GROUP)
        total = jnp.sum(wide, axis=0, keepdims=True)
        if doc == 0:
            exps[...] = narrow
            write_pairs(part, TOP, weighted)
            write_pairs(part, slice(LMK, LMK + 1), top)
            write_pairs(part, slice(LMK + 1, LMK + 2), total)
        else:
            exps[rows, :] = jnp.where(inside, narrow, exps[rows, :])
            parts[doc - 1] = weighted
            stats[doc - 1, 0:1, :] = top
            stats[doc - 1, 1:2, :] = total

    for_docs(info, exps.shape[0], body)


def mix(info, joined, qm, qms):
    total, width = joined.shape[0], joined.shape[1] // 3
    groups = width // GROUP
    return pl.pallas_call(
        mix_kernel,
        grid=(groups,),
        in_specs=[
            pl.BlockSpec(memory_space=pltpu.SMEM),
            pl.BlockSpec((total, GROUP), lambda g: (0, groups + g)),
            pl.BlockSpec((total, GROUP), lambda g: (0, 2 * groups + g)),
            LONG_SPEC,
            SMALL_SPEC,
        ],
        out_specs=[
            pl.BlockSpec((total, GROUP), lambda g: (0, g)),
            pl.BlockSpec((2, LMK + 8, PAIR), lambda g: (g, 0, 0)),
            SMALL_SPEC,
            SMALL_ROW_SPEC,
        ],
        out_shape=[
            jax.ShapeDtypeStruct((total, width), BF16),
            jax.ShapeDtypeStruct((PAIRS, LMK + 8, PAIR), F32),
            jax.ShapeDtypeStruct((SMALL, groups, LMK, GROUP), F32),
            jax.ShapeDtypeStruct((SMALL, groups, 8, GROUP), F32),
        ],
        compiler_params=pltpu.CompilerParams(vmem_limit_bytes=48 * 2**20),
        name="mix",
    )(info, joined, joined, qm, qms)


TOEP = 160
BLK = 128


def band(taps, reverse_unused=None):
    wide = jnp.broadcast_to(taps, (BLK, 256))
    return pltpu.roll(wide, 0, 1, stride=1, stride_axis=0)[:, :TOEP].astype(BF16)


def bands(taps, group):
    heads = GROUP // LMK
    return jnp.concatenate([band(taps[pl.ds(group * heads + i, 1), :]) for i in range(heads)], axis=0)


def head_rows(stack):
    lanes = lax.broadcasted_iota(jnp.int32, (BLK, GROUP), 1) // LMK
    out = stack[:BLK]
    for i in range(1, GROUP // LMK):
        out = jnp.where(lanes == i, stack[i * BLK : (i + 1) * BLK], out)
    return out


def padded_rows(before, here, after, pad):
    total = here.shape[0]
    pad[0:16, :] = before
    pad[16 : total + 16, :] = here[...]
    pad[total + 16 : total + 32, :] = after


def doc_windows(info, total, body):
    def member(doc, start):
        rows = lax.broadcasted_iota(jnp.int32, (TOEP, 1), 0) + start - 16
        low, high = (info[8], info[9]) if doc == 0 else (info[2 * doc], info[2 * doc + 1])
        return (rows >= low) & (rows < high)

    for doc in range(DOCS):
        low, high = info[2 * doc], info[2 * doc + 1]

        @pl.loop(low // BLK, jnp.where(high > low, (high + BLK - 1) // BLK, low // BLK))
        def _(b):
            start = pl.multiple_of(b * BLK, BLK)
            body(doc, start, member(doc, start))


def attend_kernel(info, queries, values, halo, taps, km, car, kms, cars, kern, mixture, pad, att):
    total = queries.shape[0]
    group = pl.program_id(0)
    ones = head_ones(GROUP).astype(BF16)

    def body(doc, size, start, inside):
        rows = pl.ds(start, size)
        marks = stacked(joint(km) if doc == 0 else kms[doc - 1])
        scores = dot(queries[rows, :], marks, NT) * 0.125
        exponent = jnp.exp(scores - head_max(scores, GROUP))
        kernel = (exponent / dot(exponent.astype(BF16), ones)).astype(BF16)
        carried = stacked(joint(car) if doc == 0 else cars[doc - 1])
        attended = dot(kernel, carried)
        if doc == 0:
            kern[...] = kernel
            att[...] = attended
        else:
            kern[rows, :] = jnp.where(inside, kernel, kern[rows, :])
            att[rows, :] = jnp.where(inside, attended, att[rows, :])

    for_docs(info, total, body)
    padded_rows(halo[0], values, halo[1], pad)
    tape = bands(taps, group)

    def conv(doc, start, inside):
        window = jnp.where(inside, pad[pl.ds(start, TOEP), :], jnp.zeros((), BF16))
        out = head_rows(dot(tape, window))
        rows = pl.ds(start, BLK)
        here = inside[16 : 16 + BLK]
        new = (att[rows, :] + out).astype(BF16)
        if doc == 0:
            mixture[rows, :] = new
        else:
            mixture[rows, :] = jnp.where(here, new, mixture[rows, :])

    doc_windows(info, total, conv)


def attend(info, joined, halo, taps, km, car, kms, cars):
    total, width = joined.shape[0], joined.shape[1] // 3
    groups = width // GROUP
    col = pl.BlockSpec((total, GROUP), lambda g: (0, g))
    mark, marks = LONG_SPEC, SMALL_SPEC
    return pl.pallas_call(
        attend_kernel,
        grid=(groups,),
        in_specs=[
            pl.BlockSpec(memory_space=pltpu.SMEM),
            col,
            pl.BlockSpec((total, GROUP), lambda g: (0, 2 * groups + g)),
            pl.BlockSpec((2, 16, GROUP), lambda g: (0, 0, g)),
            pl.BlockSpec(taps.shape, lambda g: (0, 0)),
            mark,
            mark,
            marks,
            marks,
        ],
        out_specs=[col, col],
        out_shape=[jax.ShapeDtypeStruct((total, width), BF16)] * 2,
        scratch_shapes=[VMEM((total + 32, GROUP), BF16), VMEM((total, GROUP), F32)],
        compiler_params=pltpu.CompilerParams(vmem_limit_bytes=48 * 2**20),
        name="attend",
    )(info, joined, joined, halo, taps, km, car, kms, cars)


def back_f_kernel(info, queries, dmix, kern, km, car, kms, cars, dq, part, parts):
    parts[...] = jnp.zeros_like(parts)
    ones = head_ones(GROUP).astype(BF16)

    def body(doc, size, start, inside):
        rows = pl.ds(start, size)
        zero = jnp.zeros((), BF16)
        marks = stacked(joint(km) if doc == 0 else kms[doc - 1])
        carried = stacked(joint(car) if doc == 0 else cars[doc - 1])
        datt = dmix[rows, :]
        kernel = jnp.where(inside, kern[rows, :], zero)
        d_carried = side_of(dot(kernel, datt, TN), GROUP)
        d_kernel = dot(datt, carried, NT)
        wide = kernel.astype(F32)
        weighed = wide * d_kernel
        high = weighed.astype(BF16)
        low = (weighed - high.astype(F32)).astype(BF16)
        inner = dot(high, ones) + dot(low, ones)
        d_scores = (weighed - wide * inner).astype(BF16)
        d_queries = dot(d_scores, marks) * 0.125
        d_marks = side_of(dot(d_scores, queries[rows, :], TN), GROUP) * 0.125
        if doc == 0:
            dq[...] = d_queries
            write_pairs(part, TOP, d_carried)
            write_pairs(part, slice(LMK, 2 * LMK), d_marks)
        else:
            dq[rows, :] = jnp.where(inside, d_queries, dq[rows, :])
            parts[0, doc - 1] = d_carried
            parts[1, doc - 1] = d_marks

    for_docs(info, dq.shape[0], body)


def back_f(info, joined, dmix, kern, km, car, kms, cars):
    total, width = dmix.shape
    groups = width // GROUP
    col = pl.BlockSpec((total, GROUP), lambda g: (0, g))
    mark, marks = LONG_SPEC, SMALL_SPEC
    return pl.pallas_call(
        back_f_kernel,
        grid=(groups,),
        in_specs=[pl.BlockSpec(memory_space=pltpu.SMEM), col, col, col, mark, mark, marks, marks],
        out_specs=[
            col,
            pl.BlockSpec((2, 2 * LMK, PAIR), lambda g: (g, 0, 0)),
            pl.BlockSpec((2, SMALL, None, LMK, GROUP), lambda g: (0, 0, g, 0, 0)),
        ],
        out_shape=[
            jax.ShapeDtypeStruct((total, width), F32),
            jax.ShapeDtypeStruct((PAIRS, 2 * LMK, PAIR), F32),
            jax.ShapeDtypeStruct((2, SMALL, groups, LMK, GROUP), F32),
        ],
        compiler_params=pltpu.CompilerParams(vmem_limit_bytes=48 * 2**20),
        name="back_f",
    )(info, joined, dmix, kern, km, car, kms, cars)


def back_b_kernel(info, keys, values, halo, exps, factor, sc, along, scs, alongs, qm, qms, taps, dmix, dhalo, dk, dv, part, parts, dtaps, pad, dpad, acc):
    total = keys.shape[0]
    group = pl.program_id(0)
    parts[...] = jnp.zeros_like(parts)

    def body(doc, size, start, inside):
        rows = pl.ds(start, size)
        scaled = stacked(joint(sc) if doc == 0 else scs[doc - 1])
        marks = stacked(joint(qm) if doc == 0 else qms[doc - 1])
        wide = jnp.where(inside, exps[rows, :].astype(F32), 0.0)
        if doc == 0:
            wide = wide * factor[0:1, :]
        shift = joint(along)[0:1, :] if doc == 0 else alongs[doc - 1, 0:1, :]
        d_values = dot(wide.astype(BF16), scaled)
        reach = dot(values[rows, :], scaled, NT)
        d_scores = (wide * (reach - shift)).astype(BF16)
        d_keys = dot(d_scores, marks) * 0.125
        d_marks = side_of(dot(d_scores, keys[rows, :], TN), GROUP) * 0.125
        if doc == 0:
            dk[...] = d_keys
            dv[...] = d_values
            write_pairs(part, TOP, d_marks)
        else:
            dk[rows, :] = jnp.where(inside, d_keys, dk[rows, :])
            dv[rows, :] = jnp.where(inside, d_values, dv[rows, :])
            parts[doc - 1] = d_marks

    for_docs(info, total, body)
    padded_rows(halo[0], values, halo[1], pad)
    padded_rows(dhalo[0], dmix, dhalo[1], dpad)
    tape = bands(taps, group)
    acc[...] = jnp.zeros_like(acc)

    def conv(doc, start, inside):
        zero = jnp.zeros((), BF16)
        rows = pl.ds(start, BLK)
        here = inside[16 : 16 + BLK]
        out = head_rows(dot(tape, jnp.where(inside, dpad[pl.ds(start, TOEP), :], zero)))
        dv[rows, :] = dv[rows, :] + jnp.where(here, out, 0.0)
        window = jnp.where(inside, pad[pl.ds(start, TOEP), :], zero)
        mine = jnp.where(here, dmix[rows, :], zero)
        lanes = lax.broadcasted_iota(jnp.int32, (BLK, GROUP), 1) // LMK
        spread = jnp.concatenate([jnp.where(lanes == i, mine, zero) for i in range(GROUP // LMK)], axis=0)
        acc[:, :TOEP] = acc[:, :TOEP] + dot(spread, window, NT)

    doc_windows(info, total, conv)
    rows = lax.broadcasted_iota(jnp.int32, (BLK, BLK), 0)
    lanes = lax.broadcasted_iota(jnp.int32, (BLK, BLK), 1)
    reverse = jnp.where(rows + lanes == BLK - 1, 1.0, 0.0).astype(F32)
    for i in range(GROUP // LMK):
        square = dot(reverse, acc[i * BLK : (i + 1) * BLK, :], precision=HIGHEST)
        turned = pltpu.roll(square, 0, 1, stride=1, stride_axis=0)
        dtaps[0, i : i + 1, :] = jnp.sum(turned, axis=0, keepdims=True)


def back_b(info, joined, halo, exps, factor, sc, along, scs, alongs, qm, qms, taps, dmix, dhalo):
    total, width = dmix.shape
    groups = width // GROUP
    heads = GROUP // LMK
    col = pl.BlockSpec((total, GROUP), lambda g: (0, g))
    mark, marks = LONG_SPEC, SMALL_SPEC
    row = pl.BlockSpec((8, GROUP), lambda g: (0, g))
    edge = pl.BlockSpec((2, 16, GROUP), lambda g: (0, 0, g))
    return pl.pallas_call(
        back_b_kernel,
        grid=(groups,),
        in_specs=[
            pl.BlockSpec(memory_space=pltpu.SMEM),
            pl.BlockSpec((total, GROUP), lambda g: (0, groups + g)),
            pl.BlockSpec((total, GROUP), lambda g: (0, 2 * groups + g)),
            edge,
            col,
            row,
            mark,
            ROW_SPEC,
            marks,
            SMALL_ROW_SPEC,
            mark,
            marks,
            pl.BlockSpec(taps.shape, lambda g: (0, 0)),
            col,
            edge,
        ],
        out_specs=[col, col, mark, marks, pl.BlockSpec((1, heads, 256), lambda g: (g, 0, 0))],
        out_shape=[
            jax.ShapeDtypeStruct((total, width), F32),
            jax.ShapeDtypeStruct((total, width), F32),
            jax.ShapeDtypeStruct((PAIRS, LMK, PAIR), F32),
            jax.ShapeDtypeStruct((SMALL, groups, LMK, GROUP), F32),
            jax.ShapeDtypeStruct((groups, heads, 256), F32),
        ],
        scratch_shapes=[VMEM((total + 32, GROUP), BF16), VMEM((total + 32, GROUP), BF16), VMEM((heads * BLK, 256), F32)],
        compiler_params=pltpu.CompilerParams(vmem_limit_bytes=48 * 2**20),
        name="back_b",
    )(info, joined, joined, halo, exps, factor, sc, along, scs, alongs, qm, qms, taps, dmix, dhalo)


class Ring:
    def __init__(self, count):
        self.count = count
        self.me = lax.axis_index("seq")
        self.row = lax.axis_index("row")
        self.steps = range(1, count)

    def ahead(self, k):
        return lax.rem(self.me + k, self.count)

    def enter(self):
        barrier = pltpu.get_barrier_semaphore()
        for k in self.steps:
            pl.semaphore_signal(barrier, inc=1, device_id=(self.ahead(k), self.row), device_id_type=MESH)
        pl.semaphore_wait(barrier, self.count - 1)

    def copy(self, src, dst, send, recv, to):
        return pltpu.make_async_remote_copy(src_ref=src, dst_ref=dst, send_sem=send, recv_sem=recv, device_id=(to, self.row), device_id_type=MESH)

    def scatter(self, pieces, landing, send, recv, first, owners):
        for k in self.steps:
            to = self.ahead(k)

            @pl.when((to >= first) & (to < first + owners))
            def _():
                self.copy(pieces(to - first), landing.at[k - 1], send.at[k - 1], recv.at[k - 1], to).start()

        def arrived():
            for k in self.steps:
                self.copy(pieces(0), landing.at[k - 1], send.at[k - 1], recv.at[k - 1], self.ahead(k)).wait_recv()

        def sent():
            for k in self.steps:
                to = self.ahead(k)

                @pl.when((to >= first) & (to < first + owners))
                def _():
                    self.copy(pieces(to - first), landing.at[k - 1], send.at[k - 1], recv.at[k - 1], to).wait_send()

        return arrived, sent

    def share(self, held, send, recv, first):
        piece = self.me - first
        for k in self.steps:
            self.copy(held.at[piece], held.at[piece], send.at[k - 1], recv.at[piece], self.ahead(k)).start()

    def share_sent(self, held, send, recv, first):
        piece = self.me - first
        for k in self.steps:
            self.copy(held.at[piece], held.at[piece], send.at[k - 1], recv.at[piece], self.ahead(k)).wait_send()

    def shared(self, held, send, recv, first, owners):
        for p in range(owners):

            @pl.when(self.me != first + p)
            def _():
                self.copy(held.at[p], held.at[p], send.at[0], recv.at[p], self.ahead(1)).wait_recv()


    def edges_start(self, here, landing, send, recv):
        @pl.when(self.me > 0)
        def _():
            self.copy(here.at[0], landing.at[1], send.at[0], recv.at[1], self.me - 1).start()

        @pl.when(self.me < self.count - 1)
        def _():
            self.copy(here.at[1], landing.at[0], send.at[1], recv.at[0], self.me + 1).start()

    def edges_wait(self, here, landing, send, recv, out):
        out[...] = jnp.zeros_like(out)

        @pl.when(self.me > 0)
        def _():
            done = self.copy(here.at[0], landing.at[0], send.at[0], recv.at[0], self.me - 1)
            done.wait_recv()
            done.wait_send()
            out[0] = landing[0]

        @pl.when(self.me < self.count - 1)
        def _():
            done = self.copy(here.at[1], landing.at[1], send.at[1], recv.at[1], self.me + 1)
            done.wait_recv()
            done.wait_send()
            out[1] = landing[1]


OWNERS = 8
DMA = pltpu.SemaphoreType.DMA


def marks_kernel(count, part, counts, edge, qm, km, halo, landing, held, hland, ss, rs, gs, gr, es, er):
    ring = Ring(count)
    ring.enter()
    ring.edges_start(edge, hland, es, er)
    each = LMK // OWNERS
    arrived, sent = ring.scatter(lambda o: part.at[pl.ds(pl.multiple_of(o * each, each), each), :], landing, ss, rs, 0, OWNERS)

    @pl.when(ring.me < OWNERS)
    def _():
        arrived()
        at = pl.ds(pl.multiple_of(ring.me * each, each), each)
        total = part[at, :]
        for k in ring.steps:
            total = total + landing[k - 1]
        total = total / counts[at, 0:1]
        half = total.shape[1] // 2
        held[ring.me, 0:each, :] = total[:, :half].astype(BF16)
        held[ring.me, each : 2 * each, :] = total[:, half:].astype(BF16)
        ring.share(held, gs, gr, 0)

    ring.shared(held, gs, gr, 0, OWNERS)
    wide = [held[o].astype(F32) for o in range(OWNERS)]
    query = jnp.concatenate([w[:each] for w in wide], axis=0).astype(BF16)
    key = jnp.concatenate([w[each:] for w in wide], axis=0).astype(BF16)
    for p in range(PAIRS):
        qm[p] = query[:, p * PAIR : (p + 1) * PAIR]
        km[p] = key[:, p * PAIR : (p + 1) * PAIR]
    ring.edges_wait(edge, hland, es, er, halo)
    sent()

    @pl.when(ring.me < OWNERS)
    def _():
        ring.share_sent(held, gs, gr, 0)


def remote_params(cid):
    return pltpu.CompilerParams(collective_id=cid, has_side_effects=True, vmem_limit_bytes=56 * 2**20)


def in_vmem(n):
    return [pl.BlockSpec(memory_space=VMEM)] * n


def all_marks(count, part, counts, edge):
    width = part.shape[1]
    each = LMK // OWNERS
    return pl.pallas_call(
        functools.partial(marks_kernel, count),
        in_specs=in_vmem(3),
        out_specs=in_vmem(3),
        out_shape=[jax.ShapeDtypeStruct((PAIRS, LMK, PAIR), BF16)] * 2 + [jax.ShapeDtypeStruct(edge.shape, BF16)],
        scratch_shapes=[
            VMEM((count - 1, each, width), F32),
            VMEM((OWNERS, 2 * each, width // 2), BF16),
            VMEM(edge.shape, BF16),
            DMA((count - 1,)),
            DMA((count - 1,)),
            DMA((count - 1,)),
            DMA((OWNERS,)),
            DMA((2,)),
            DMA((2,)),
        ],
        compiler_params=remote_params(1),
        name="all_marks",
    )(part, counts, edge)


SAVES = 3 * NS_ITERS + 2
GROUPS = 3


def ends(ring):
    return (ring.me == 0) | (ring.me == ring.count - 1)


def owner_of_pair(ring):
    return (ring.me >= 1) & (ring.me <= PAIRS)


def pair_of(ring):
    return jnp.clip(ring.me - 1, 0, PAIRS - 1)


def small_cases(body):
    @pl.loop(0, SMALL * GROUPS)
    def _(i):
        body(i // GROUPS, lax.rem(i, GROUPS), i)


def carry_kernel(count, part, qm, km, qms, kms, wsm, stsm, car, stat, saved, mixed, cars, saveds, mixeds, landing, cheld, sheld, ss, rs, cs, cr, ts, tr):
    ring = Ring(count)
    ring.enter()
    arrived, sent = ring.scatter(lambda p: part.at[p], landing, ss, rs, 1, PAIRS)

    @pl.when(owner_of_pair(ring))
    def _():
        pair = pair_of(ring)

        def save(i, value):
            saved[i] = value

        inverse = inverse_forward(qm[pair], km[pair], save, PAIR)
        arrived()
        pieces = [part[pair]] + [landing[k - 1] for k in ring.steps]
        top = pieces[0][LMK : LMK + 1]
        for piece in pieces[1:]:
            top = jnp.maximum(top, piece[LMK : LMK + 1])
        weighted = jnp.zeros((LMK, PAIR), F32)
        total = jnp.zeros((1, PAIR), F32)
        for piece in pieces:
            share = jnp.exp(piece[LMK : LMK + 1] - top)
            weighted = weighted + piece[:LMK] * column_of(share, PAIR)
            total = total + piece[LMK + 1 : LMK + 2] * share
        mean = weighted / column_of(total, PAIR)
        mixed[...] = mean
        cheld[pair] = mul(inverse, mean, PAIR).astype(BF16)
        sheld[pair] = jnp.concatenate([top, total, jnp.zeros((6, PAIR), F32)], axis=0)
        ring.share(cheld, cs, cr, 1)
        ring.share(sheld, ts, tr, 1)

    @pl.when(ends(ring))
    def _():
        def case(doc, group, i):
            def save(j, value):
                saveds[i, j] = value

            inverse = inverse_forward(qms[i], kms[i], save, GROUP)
            total = jnp.maximum(stsm[i, 1:2, :], 1e-30)
            mean = wsm[i] / column_of(total, GROUP)
            mixeds[i] = mean
            cars[i] = mul(inverse, mean, GROUP).astype(BF16)

        small_cases(case)

    ring.shared(cheld, cs, cr, 1, PAIRS)
    ring.shared(sheld, ts, tr, 1, PAIRS)
    car[...] = cheld[...]
    stat[...] = sheld[...]
    sent()

    @pl.when(owner_of_pair(ring))
    def _():
        ring.share_sent(cheld, cs, cr, 1)
        ring.share_sent(sheld, ts, tr, 1)


CASES = SMALL * GROUPS


def carry(count, part, qm, km, qms, kms, wsm, stsm):
    return pl.pallas_call(
        functools.partial(carry_kernel, count),
        in_specs=in_vmem(7),
        out_specs=in_vmem(7),
        out_shape=[
            jax.ShapeDtypeStruct((PAIRS, LMK, PAIR), BF16),
            jax.ShapeDtypeStruct((PAIRS, 8, PAIR), F32),
            jax.ShapeDtypeStruct((SAVES, LMK, PAIR), F32),
            jax.ShapeDtypeStruct((LMK, PAIR), F32),
            jax.ShapeDtypeStruct((CASES, LMK, GROUP), BF16),
            jax.ShapeDtypeStruct((CASES, SAVES, LMK, GROUP), F32),
            jax.ShapeDtypeStruct((CASES, LMK, GROUP), F32),
        ],
        scratch_shapes=[
            VMEM((count - 1, LMK + 8, PAIR), F32),
            VMEM((PAIRS, LMK, PAIR), BF16),
            VMEM((PAIRS, 8, PAIR), F32),
            DMA((count - 1,)),
            DMA((count - 1,)),
            DMA((count - 1,)),
            DMA((PAIRS,)),
            DMA((count - 1,)),
            DMA((PAIRS,)),
        ],
        compiler_params=remote_params(2),
        name="carry",
    )(part, qm, km, qms, kms, wsm, stsm)


def spread_grad(d_carried, inverse, mixed, total, width):
    d_mixed = mul(flipped(inverse, width), d_carried, width)
    scaled = (d_mixed / column_of(total, width)).astype(BF16)
    along = row_of(scaled.astype(F32) * mixed, width)
    return scaled, along


def spread_kernel(count, part, stat, saved, mixed, dcs, stsm, saveds, mixeds, edge, sc, along, dtot, scs, alongs, halo, landing, sheld, aheld, hland, ss, rs, cs, cr, ts, tr, es, er):
    ring = Ring(count)
    ring.enter()
    arrived, sent = ring.scatter(lambda p: part.at[p], landing, ss, rs, 1, PAIRS)
    ring.edges_start(edge, hland, es, er)

    @pl.when(owner_of_pair(ring))
    def _():
        pair = pair_of(ring)
        arrived()
        total = part[pair]
        for k in ring.steps:
            total = total + landing[k - 1]
        dtot[...] = total
        scaled, reach = spread_grad(total[:LMK], saved[...], mixed[...], stat[pair, 1:2, :], PAIR)
        sheld[pair] = scaled
        aheld[pair] = reach
        ring.share(sheld, cs, cr, 1)
        ring.share(aheld, ts, tr, 1)

    @pl.when(ends(ring))
    def _():
        def case(doc, group, i):
            total = jnp.maximum(stsm[i, 1:2, :], 1e-30)
            scaled, reach = spread_grad(dcs[i], saveds[i], mixeds[i], total, GROUP)
            scs[i] = scaled
            alongs[i] = reach

        small_cases(case)

    ring.shared(sheld, cs, cr, 1, PAIRS)
    ring.shared(aheld, ts, tr, 1, PAIRS)
    sc[...] = sheld[...]
    along[...] = aheld[...]
    ring.edges_wait(edge, hland, es, er, halo)
    sent()

    @pl.when(owner_of_pair(ring))
    def _():
        ring.share_sent(sheld, cs, cr, 1)
        ring.share_sent(aheld, ts, tr, 1)


def spread(count, part, stat, saved, mixed, dcs, stsm, saveds, mixeds, edge):
    return pl.pallas_call(
        functools.partial(spread_kernel, count),
        in_specs=in_vmem(9),
        out_specs=in_vmem(6),
        out_shape=[
            jax.ShapeDtypeStruct((PAIRS, LMK, PAIR), BF16),
            jax.ShapeDtypeStruct((PAIRS, 8, PAIR), F32),
            jax.ShapeDtypeStruct((2 * LMK, PAIR), F32),
            jax.ShapeDtypeStruct((CASES, LMK, GROUP), BF16),
            jax.ShapeDtypeStruct((CASES, 8, GROUP), F32),
            jax.ShapeDtypeStruct(edge.shape, BF16),
        ],
        scratch_shapes=[
            VMEM((count - 1, 2 * LMK, PAIR), F32),
            VMEM((PAIRS, LMK, PAIR), BF16),
            VMEM((PAIRS, 8, PAIR), F32),
            VMEM(edge.shape, BF16),
            DMA((count - 1,)),
            DMA((count - 1,)),
            DMA((count - 1,)),
            DMA((PAIRS,)),
            DMA((count - 1,)),
            DMA((PAIRS,)),
            DMA((2,)),
            DMA((2,)),
        ],
        compiler_params=remote_params(3),
        name="spread",
    )(part, stat, saved, mixed, dcs, stsm, saveds, mixeds, edge)


def mark_grads(d_carried, mixed, saved, qm, km, width):
    d_inverse = mul_nt(d_carried, mixed, width)
    d_scores = inverse_backward(d_inverse, saved, width) * 0.125
    d_query = mul(d_scores, km.astype(F32), width)
    d_key = mul(flipped(d_scores, width), qm.astype(F32), width)
    return d_query, d_key


def sums_kernel(count, part, dtot, saved, mixed, qm, km, counts, dqs, dcs, dks, saveds, mixeds, qms, kms, dsum, dsums, landing, held, ss, rs, cs, cr):
    ring = Ring(count)
    ring.enter()
    arrived, sent = ring.scatter(lambda p: part.at[p], landing, ss, rs, 1, PAIRS)

    @pl.when(owner_of_pair(ring))
    def _():
        pair = pair_of(ring)
        d_query, d_key = mark_grads(dtot[:LMK], mixed[...], lambda i: saved[i], qm[pair], km[pair], PAIR)
        arrived()
        total = part[pair]
        for k in ring.steps:
            total = total + landing[k - 1]
        held[pair, :LMK, :] = ((d_query + total) / counts[0, :, 0:1]).astype(BF16)
        held[pair, LMK:, :] = ((d_key + dtot[LMK:]) / counts[0, :, 0:1]).astype(BF16)
        ring.share(held, cs, cr, 1)

    @pl.when(ends(ring))
    def _():
        def case(doc, group, i):
            d_query, d_key = mark_grads(dcs[i], mixeds[i], lambda j: saveds[i, j], qms[i], kms[i], GROUP)
            dsums[i, :LMK, :] = ((d_query + dqs[i]) / counts[1 + doc, :, 0:1]).astype(BF16)
            dsums[i, LMK:, :] = ((d_key + dks[i]) / counts[1 + doc, :, 0:1]).astype(BF16)

        small_cases(case)

    ring.shared(held, cs, cr, 1, PAIRS)
    dsum[...] = held[...]
    sent()

    @pl.when(owner_of_pair(ring))
    def _():
        ring.share_sent(held, cs, cr, 1)


def mark_sums(count, part, dtot, saved, mixed, qm, km, counts, dqs, dcs, dks, saveds, mixeds, qms, kms):
    return pl.pallas_call(
        functools.partial(sums_kernel, count),
        in_specs=in_vmem(14),
        out_specs=in_vmem(2),
        out_shape=[jax.ShapeDtypeStruct((PAIRS, 2 * LMK, PAIR), BF16), jax.ShapeDtypeStruct((CASES, 2 * LMK, GROUP), BF16)],
        scratch_shapes=[
            VMEM((count - 1, LMK, PAIR), F32),
            VMEM((PAIRS, 2 * LMK, PAIR), BF16),
            DMA((count - 1,)),
            DMA((count - 1,)),
            DMA((count - 1,)),
            DMA((PAIRS,)),
        ],
        compiler_params=remote_params(4),
        name="mark_sums",
    )(part, dtot, saved, mixed, qm, km, counts, dqs, dcs, dks, saveds, mixeds, qms, kms)


def wsum_kernel(dims, gq, go, gu, gd, sm, oq, oo, ou, od, osm, own, out, r0, r1, r2, r3, smr, lsem, osem, ss, rs, sss, srs):
    s_ax, r_ax = lax.axis_index("seq"), lax.axis_index("row")
    z, x, y, c = s_ax // 2, s_ax % 2, r_ax // 2, r_ax % 2
    x1, y1 = x + (1 - c) * (1 - 2 * x), y + c * (1 - 2 * y)
    x2, y2 = x + c * (1 - 2 * x), y + (1 - c) * (1 - 2 * y)
    core_dev = (s_ax, y * 2 + (1 - c))
    d1_dev = (z * 2 + x1, y1 * 2 + c)
    d2_dev = (z * 2 + x2, y2 * 2 + c)
    z_devs = [(lax.rem(z + k, 4) * 2 + x, r_ax) for k in (1, 2, 3)]
    peers = [core_dev, d1_dev, d2_dev] + z_devs
    b1 = x * (1 - c) + y * c
    b2 = y * (1 - c) + x * c
    barrier = pltpu.get_barrier_semaphore()
    for p in peers:
        pl.semaphore_signal(barrier, inc=1, device_id=p, device_id_type=MESH)
    units = [(gq, oq, 0, i) for i in range(3)] + [(go, oo, 0, 0)]
    units = [(gd, od, i, 0) for i in range(4)] + [(gu, ou, 0, i) for i in range(4)] + [(go, oo, 0, 0)] + [(gq, oq, 0, i) for i in range(3)]
    n_units = len(units)
    W, H = 768, 384
    mine = pl.ds(pl.multiple_of(c * H, 128), H)
    other = pl.ds(pl.multiple_of((1 - c) * H, 128), H)

    def block(ref, i, j):
        return ref.at[pl.ds(i * W, W), pl.ds(j * W, W)]

    loads = []
    for u, (src, _, i, j) in enumerate(units):
        cp = pltpu.make_async_copy(block(src, i, j), own.at[u], lsem.at[u])
        cp.start()
        loads.append(cp)
    pl.semaphore_wait(barrier, len(peers))

    def remote(src, dst, u, k, dev):
        cp = pltpu.make_async_remote_copy(src_ref=src, dst_ref=dst, send_sem=ss.at[u, k], recv_sem=rs.at[u, k], device_id=dev, device_id_type=MESH)
        cp.start()
        return cp

    def rows(start, size):
        return pl.ds(pl.multiple_of(start, 16), size)

    def add_rows(dst, dst_at, a, a_at, b, b_at, n, step):
        @pl.loop(0, n, step=step)
        def _(t):
            s = a(a_at + t, step).astype(jnp.float32) + b(b_at + t, step).astype(jnp.float32)
            dst(dst_at + t, step, s.astype(jnp.bfloat16))

    pend = {}
    base1 = b1 * 384
    base2 = b1 * 384 + b2 * 192
    base3 = base2 + z * 48

    def step(u, s):
        if s == 0:
            loads[u].wait()
            pend[u, 0] = remote(own.at[u, :, other], r0.at[u], u, 0, core_dev)
        elif s == 1:
            pend[u, 0].wait_recv()

            @pl.loop(0, 768, step=64)
            def _(t):
                q = pl.ds(pl.multiple_of(t, 64), 64)
                r0[u, q, :] = (r0[u, q, :].astype(jnp.float32) + own[u, q, mine].astype(jnp.float32)).astype(jnp.bfloat16)

            pend[u, 1] = remote(r0.at[u, rows((1 - b1) * 384, 384), :], r1.at[u], u, 1, d1_dev)
        elif s == 2:
            pend[u, 1].wait_recv()

            @pl.loop(0, 384, step=64)
            def _(t):
                q = pl.ds(pl.multiple_of(t, 64), 64)
                r1[u, q, :] = (r1[u, q, :].astype(jnp.float32) + r0[u, rows(base1 + t, 64), :].astype(jnp.float32)).astype(jnp.bfloat16)

            pend[u, 2] = remote(r1.at[u, rows((1 - b2) * 192, 192), :], r2.at[u], u, 2, d2_dev)
        elif s == 3:
            pend[u, 2].wait_recv()

            @pl.loop(0, 192, step=64)
            def _(t):
                q = pl.ds(pl.multiple_of(t, 64), 64)
                r2[u, q, :] = (r2[u, q, :].astype(jnp.float32) + r1[u, rows(b2 * 192 + t, 64), :].astype(jnp.float32)).astype(jnp.bfloat16)

            for k in range(3):
                zz = lax.rem(z + k + 1, 4)
                pend[u, 3 + k] = remote(r2.at[u, rows(zz * 48, 48), :], r3.at[u, k], u, 3 + k, z_devs[k])
        elif s == 4:
            for k in range(3):
                pend[u, 3 + k].wait_recv()
            tot = r2[u, rows(z * 48, 48), :].astype(jnp.float32)
            for k in range(3):
                tot = tot + r3[u, k].astype(jnp.float32)
            out[u, rows(base3, 48), mine] = tot.astype(jnp.bfloat16)
            region = out.at[u, rows(base3, 48), mine]
            for k in range(3):
                pend[u, 6 + k] = remote(region, region, u, 6 + k, z_devs[k])
        elif s == 5:
            for k in range(3):
                pend[u, 6 + k].wait_recv()
            region = out.at[u, rows(base2, 192), mine]
            pend[u, 9] = remote(region, region, u, 9, d2_dev)
        elif s == 6:
            pend[u, 9].wait_recv()
            region = out.at[u, rows(base1, 384), mine]
            pend[u, 10] = remote(region, region, u, 10, d1_dev)
        elif s == 7:
            pend[u, 10].wait_recv()
            region = out.at[u, :, mine]
            pend[u, 11] = remote(region, region, u, 11, core_dev)
        elif s == 8:
            pend[u, 11].wait_recv()
            _, dst, i, j = units[u]
            cp = pltpu.make_async_copy(out.at[u], block(dst, i, j), osem.at[u])
            cp.start()
            pend[u, 12] = cp

    small = {}
    small_devs = [core_dev, d1_dev, d2_dev, (lax.rem(z + 2, 4) * 2 + x, r_ax), ((z + 1 - 2 * lax.rem(z, 2)) * 2 + x, r_ax)]

    def small_step(k):
        if k == 0:
            smr[0] = sm[...]
        else:
            small[k - 1].wait_recv()
            smr[k] = smr[k - 1] + smr[k + 5]
        if k < 5:
            small[k] = pltpu.make_async_remote_copy(src_ref=smr.at[k], dst_ref=smr.at[k + 6], send_sem=sss.at[k], recv_sem=srs.at[k], device_id=small_devs[k], device_id_type=MESH)
            small[k].start()
        else:
            osm[...] = smr[5]

    for tau in range(n_units + 8):
        for s in range(8, -1, -1):
            u = tau - s
            if 0 <= u < n_units:
                step(u, s)
        if tau < 6:
            small_step(tau)
    for u in range(n_units):
        for k in range(12):
            pend[u, k].wait_send()
        pend[u, 12].wait()
    for k in range(5):
        small[k].wait_send()


def weight_sums(gq, go, gu, gd, sm):
    n = 12
    bf = jnp.bfloat16
    return pl.pallas_call(
        functools.partial(wsum_kernel, None),
        out_shape=(
            jax.ShapeDtypeStruct(gq.shape, bf),
            jax.ShapeDtypeStruct(go.shape, bf),
            jax.ShapeDtypeStruct(gu.shape, bf),
            jax.ShapeDtypeStruct(gd.shape, bf),
            jax.ShapeDtypeStruct(sm.shape, sm.dtype),
        ),
        in_specs=[pl.BlockSpec(memory_space=pl.ANY)] * 4 + [pl.BlockSpec(memory_space=pltpu.VMEM)],
        out_specs=[pl.BlockSpec(memory_space=pl.ANY)] * 4 + [pl.BlockSpec(memory_space=pltpu.VMEM)],
        scratch_shapes=[
            pltpu.VMEM((n, 768, 768), bf),
            pltpu.VMEM((n, 768, 768), bf),
            pltpu.VMEM((n, 768, 384), bf),
            pltpu.VMEM((n, 384, 384), bf),
            pltpu.VMEM((n, 192, 384), bf),
            pltpu.VMEM((n, 3, 48, 384), bf),
            pltpu.VMEM((11,) + sm.shape, jnp.float32),
            pltpu.SemaphoreType.DMA((n,)),
            pltpu.SemaphoreType.DMA((n,)),
            pltpu.SemaphoreType.DMA((n, 12)),
            pltpu.SemaphoreType.DMA((n, 12)),
            pltpu.SemaphoreType.DMA((5,)),
            pltpu.SemaphoreType.DMA((5,)),
        ],
        compiler_params=pltpu.CompilerParams(collective_id=10, has_side_effects=True, vmem_limit_bytes=60 * 2**20),
        name="weight_sums",
    )(gq, go, gu, gd, sm)


def on_device(
    tokens,
    doc_lengths,
    w_qkv,
    w_out,
    conv_taps,
    norm1_gain,
    norm1_bias,
    w_up,
    w_down,
    norm2_gain,
    norm2_bias,
    cotangent,
):
    shard_len = tokens.shape[1]
    model_width = tokens.shape[2]
    head_count, tap_count = conv_taps.shape
    slot_count = DOCS * LMK
    rim = (tap_count - 1) // 2
    count = lax.axis_size("seq")
    shard_start = lax.axis_index("seq") * shard_len
    lengths, starts = long_first(doc_lengths[0])
    low, high = starts - shard_start, starts + lengths - shard_start
    inside = jnp.stack([jnp.clip(low, 0, shard_len), jnp.clip(high, 0, shard_len)], axis=1).reshape(-1)
    info = jnp.concatenate([inside, low[:1], high[:1], jnp.zeros(6, jnp.int32)])
    slot_ids = slots(lengths, starts, shard_start + jnp.arange(shard_len, dtype=jnp.int32))
    counts = slot_counts(lengths)
    inputs = tokens[0]
    joined = jnp.dot(inputs, w_qkv, preferred_element_type=F32).astype(BF16)
    member = (slot_ids[None, :] == jnp.arange(slot_count, dtype=jnp.int32)[:, None]).astype(BF16)
    slot_sums = jnp.dot(member, joined[:, : 2 * model_width], preferred_element_type=F32)
    wide_counts = jnp.broadcast_to(counts.reshape(DOCS, LMK, 1), (DOCS, LMK, PAIR))
    edge = jnp.stack([joined[:rim, 2 * model_width :], joined[-rim:, 2 * model_width :]])
    qm, km, halo = all_marks(count, slot_sums[:LMK], wide_counts[0], edge)
    small = (slot_sums[LMK:] / counts[LMK:, None]).astype(BF16)
    small = small.reshape(SMALL, LMK, 2, GROUPS, GROUP).transpose(2, 0, 3, 1, 4)
    qms, kms = small[0], small[1]

    def cases(x):
        return x.reshape((CASES,) + x.shape[2:])

    def grouped(x):
        return x.reshape((SMALL, GROUPS) + x.shape[1:])

    exps, part, wsm, stsm = mix(info, joined, qm, qms)
    carried, stat, saved, mixed, cars, saveds, mixeds = carry(count, part, qm, km, cases(qms), cases(kms), cases(wsm), cases(stsm))
    taps = jnp.pad(conv_taps, ((0, 0), (0, 256 - tap_count)))
    taps_back = jnp.pad(conv_taps[:, ::-1], ((0, 0), (0, 256 - tap_count)))
    kernel_b, mixture_b = attend(info, joined, halo, taps, km, carried, kms, grouped(cars))
    residual1 = inputs.astype(jnp.float32) + jnp.dot(
        mixture_b, w_out, preferred_element_type=jnp.float32
    )
    normed1, norm1_pull = jax.vjp(layer_norm, residual1, norm1_gain, norm1_bias)
    normed1_b = normed1.astype(jnp.bfloat16)
    upward = jnp.dot(normed1_b, w_up, preferred_element_type=jnp.float32)
    activated_wide, gelu_pull = jax.vjp(gelu, upward)
    activated = activated_wide.astype(jnp.bfloat16)
    residual2 = normed1 + jnp.dot(activated, w_down, preferred_element_type=jnp.float32)
    result, norm2_pull = jax.vjp(layer_norm, residual2, norm2_gain, norm2_bias)
    delta_residual2, delta_gain2, delta_bias2 = norm2_pull(cotangent[0].astype(jnp.float32))
    delta_down = delta_residual2.astype(jnp.bfloat16)
    grad_down = jnp.dot(activated.T, delta_down, preferred_element_type=jnp.float32)
    delta_active = jnp.dot(delta_down, w_down.T, preferred_element_type=jnp.float32)
    delta_up = gelu_pull(delta_active)[0].astype(jnp.bfloat16)
    grad_up = jnp.dot(normed1_b.T, delta_up, preferred_element_type=jnp.float32)
    delta_normed1 = delta_residual2 + jnp.dot(delta_up, w_up.T, preferred_element_type=jnp.float32)
    delta_residual1, delta_gain1, delta_bias1 = norm1_pull(delta_normed1)
    delta_output = delta_residual1.astype(jnp.bfloat16)
    grad_output = jnp.dot(mixture_b.T, delta_output, preferred_element_type=jnp.float32)
    delta_mixture = jnp.dot(delta_output, w_out.T, preferred_element_type=jnp.float32)
    delta_mix = delta_mixture.astype(BF16)
    dq, part_f, small_f = back_f(info, joined, delta_mix, kernel_b, km, carried, kms, grouped(cars))
    delta_edge = jnp.stack([delta_mix[:rim], delta_mix[-rim:]])
    scaled, along, dtot, scs, alongs, delta_halo = spread(
        count, part_f, stat, saved[3 * NS_ITERS], mixed, cases(small_f[0]), cases(stsm), saveds[:, 3 * NS_ITERS], mixeds, delta_edge
    )
    factor = jnp.exp(part[:, LMK] - stat[:, 0]).reshape(1, model_width)
    factor = jnp.broadcast_to(factor, (8, model_width))
    dk, dv, part_b, small_b, dtaps = back_b(
        info, joined, halo, exps, factor, scaled, along, grouped(scs), grouped(alongs), qm, qms, taps_back, delta_mix, delta_halo
    )
    grad_taps = dtaps.reshape(head_count, 256)[:, BLK - 1 : BLK - 1 + tap_count]
    dsum, dsums = mark_sums(
        count, part_b, dtot, saved, mixed, qm, km, wide_counts, cases(small_b), cases(small_f[0]), cases(small_f[1]), saveds, mixeds, cases(qms), cases(kms)
    )
    long_sums = dsum.reshape(PAIRS, 2, LMK, PAIR).transpose(2, 1, 0, 3).reshape(LMK, 2 * model_width)
    here = (lax.axis_index("seq") == 0) | (lax.axis_index("seq") == count - 1)
    dsums = jnp.where(here, dsums, jnp.zeros((), BF16))
    small_sums = dsums.reshape(SMALL, GROUPS, 2, LMK, GROUP).transpose(0, 3, 2, 1, 4).reshape(SMALL * LMK, 2 * model_width)
    from_marks = jnp.dot(member.T, jnp.concatenate([long_sums, small_sums], axis=0), preferred_element_type=F32)
    delta_joined = jnp.concatenate([dq + from_marks[:, :model_width], dk + from_marks[:, model_width:], dv], axis=1).astype(BF16)
    grad_joined = jnp.dot(inputs.T, delta_joined, preferred_element_type=F32)
    delta_inputs = delta_residual1 + jnp.dot(delta_joined, w_qkv.T, preferred_element_type=F32)
    norm_terms = jnp.stack([delta_gain1, delta_bias1, delta_gain2, delta_bias2])
    if lax.axis_size("seq") == 8 and lax.axis_size("row") == 4:
        bf = jnp.bfloat16
        taps_row = jnp.pad(grad_taps.reshape(1, -1), ((0, 3), (0, model_width - grad_taps.size)))
        sm = jnp.concatenate([norm_terms, taps_row], axis=0)
        tq, to, tu, td, tsm = weight_sums(grad_joined.astype(bf), grad_output.astype(bf), grad_up.astype(bf), grad_down.astype(bf), sm)
        f32 = jnp.float32
        return (
            result.astype(jnp.bfloat16)[None],
            delta_inputs[None],
            tq.astype(f32),
            to.astype(f32),
            tsm[4, : grad_taps.size].reshape(grad_taps.shape),
            tsm[0],
            tsm[1],
            tu.astype(f32),
            td.astype(f32),
            tsm[2],
            tsm[3],
        )
    taps_total, norms_total = lax.psum((grad_taps, norm_terms), ("seq", "row"))
    groups = lax.axis_size(("seq", "row"))
    summed = (
        lax.psum_scatter(
            grad_joined.reshape(groups, -1), ("seq", "row"), scatter_dimension=0, tiled=True
        ),
        lax.psum_scatter(
            grad_output.reshape(groups, -1), ("seq", "row"), scatter_dimension=0, tiled=True
        ),
        lax.psum_scatter(
            grad_up.reshape(groups, -1), ("seq", "row"), scatter_dimension=0, tiled=True
        ),
        lax.psum_scatter(
            grad_down.reshape(groups, -1), ("seq", "row"), scatter_dimension=0, tiled=True
        ),
    )
    gathered = (
        lax.all_gather(summed[0].astype(jnp.bfloat16), ("seq", "row"), axis=0, tiled=True).astype(
            jnp.float32
        ),
        lax.all_gather(summed[1].astype(jnp.bfloat16), ("seq", "row"), axis=0, tiled=True).astype(
            jnp.float32
        ),
        lax.all_gather(summed[2].astype(jnp.bfloat16), ("seq", "row"), axis=0, tiled=True).astype(
            jnp.float32
        ),
        lax.all_gather(summed[3].astype(jnp.bfloat16), ("seq", "row"), axis=0, tiled=True).astype(
            jnp.float32
        ),
    )
    return (
        result.astype(jnp.bfloat16)[None],
        delta_inputs[None],
        gathered[0].reshape(grad_joined.shape),
        gathered[1].reshape(grad_output.shape),
        taps_total,
        norms_total[0],
        norms_total[1],
        gathered[2].reshape(grad_up.shape),
        gathered[3].reshape(grad_down.shape),
        norms_total[2],
        norms_total[3],
    )


def solution(mesh):
    return jax.shard_map(
        on_device,
        mesh=mesh,
        in_specs=(
            P("row", "seq", None),
            P("row", None),
            P(),
            P(),
            P(),
            P(),
            P(),
            P(),
            P(),
            P(),
            P(),
            P("row", "seq", None),
        ),
        out_specs=(
            P("row", "seq", None),
            P("row", "seq", None),
            P(),
            P(),
            P(),
            P(),
            P(),
            P(),
            P(),
            P(),
            P(),
        ),
        check_vma=False,
    )
```

```python
import functools

import jax
import jax.numpy as jnp
from jax import lax
from jax.experimental import pallas as pl
from jax.experimental.pallas import tpu as pltpu
from jax.sharding import PartitionSpec as P

MESH = pl.DeviceIdType.MESH

LMK = 64
NS_ITERS = 6
DOCS = 4


HIGHEST = lax.Precision.HIGHEST
EPSILON = 1e-05
BIG_NEGATIVE = -1e30


def layer_norm(inputs, gain, bias):
    average = jnp.mean(inputs, axis=-1, keepdims=True)
    centered = inputs - average
    variance = jnp.mean(centered * centered, axis=-1, keepdims=True)
    return centered * lax.rsqrt(variance + EPSILON) * gain + bias


def gelu(inputs):
    return 0.5 * inputs * (1.0 + lax.erf(inputs * 0.7071067811865476))


F32, BF16 = jnp.float32, jnp.bfloat16
GROUP = 256
PAIR = 128
PAIRS = 6
SMALL = DOCS - 1
GROUPS = 3
WINDOW = 256
VMEM = pltpu.VMEM


def dot(a, b, dims=((1,), (0,)), precision=None):
    return lax.dot_general(a, b, (dims, ((), ())), preferred_element_type=F32, precision=precision)


NT, TN = ((1,), (1,)), ((0,), (0,))


def head_mask(width):
    rows = lax.broadcasted_iota(jnp.int32, (width, width), 0)
    lanes = lax.broadcasted_iota(jnp.int32, (width, width), 1)
    return (rows // LMK) == (lanes // LMK)


def blocks_of(side, width):
    tiled = jnp.concatenate([side] * (width // LMK), axis=0)
    return jnp.where(head_mask(width), tiled, jnp.zeros_like(tiled))


def side_of(full, width):
    full = jnp.where(head_mask(width), full, 0.0)
    return sum(full[i * LMK : (i + 1) * LMK] for i in range(width // LMK))


def flipped(side, width):
    return side_of(jnp.transpose(blocks_of(side, width)), width)


def head_ones(width):
    return jnp.where(head_mask(width), 1.0, 0.0).astype(F32)


def column_of(row, width):
    slots = lax.broadcasted_iota(jnp.int32, (LMK, width), 0)
    lanes = lax.broadcasted_iota(jnp.int32, (LMK, width), 1)
    picked = jnp.where(slots == lanes % LMK, jnp.broadcast_to(row, (LMK, width)), 0.0)
    return dot(picked, head_ones(width), precision=HIGHEST)


def row_of(side, width):
    return dot(jnp.ones((8, width), F32), blocks_of(side, width), NT, precision=HIGHEST)


def halves(x):
    high = x.astype(BF16)
    return high, (x - high.astype(F32)).astype(BF16)


def product3(a, b, dims, width):
    high, low = halves(a)
    b_high, b_low = halves(b)
    rows = a.shape[0]
    both = dot(jnp.concatenate([high, low], axis=0), blocks_of(b_high, width), dims)
    return both[:rows] + both[rows:] + dot(high, blocks_of(b_low, width), dims)


def mul(a, b, width):
    return product3(a, b, ((1,), (0,)), width)


def mul_nt(a, b, width):
    return product3(a, b, NT, width)


def each(f, *lists):
    return [f(*items) for items in zip(*lists)]


def side_eye(width):
    slots = lax.broadcasted_iota(jnp.int32, (LMK, width), 0)
    lanes = lax.broadcasted_iota(jnp.int32, (LMK, width), 1)
    return jnp.where(slots == lanes % LMK, 1.0, 0.0).astype(F32)


def head_total(side, width):
    columns = jnp.broadcast_to(jnp.sum(side, axis=0, keepdims=True), (8, width))
    return dot(columns, head_ones(width), precision=HIGHEST)[:1]


def head_max(scores, width):
    out = []
    for i in range(width // PAIR):
        part = scores[:, i * PAIR : (i + 1) * PAIR]
        left = lax.broadcasted_iota(jnp.int32, part.shape, 1) < LMK
        low = jnp.max(jnp.where(left, part, BIG_NEGATIVE), axis=1, keepdims=True)
        high = jnp.max(jnp.where(left, BIG_NEGATIVE, part), axis=1, keepdims=True)
        out.append(jnp.where(left, low, high))
    return out[0] if len(out) == 1 else jnp.concatenate(out, axis=1)


def inverse_forward(qm, km, save, width):
    ones = head_ones(width)

    def begin(q, k):
        scores = dot(q, blocks_of(k, width), NT) * 0.125
        exponent = jnp.exp(scores - head_max(scores, width))
        return exponent / dot(exponent, ones, precision=HIGHEST)

    kernel_a = each(begin, qm, km)
    approx = each(lambda a: flipped(a, width) / head_total(a * a, width), kernel_a)
    eye = side_eye(width)
    for j, a in enumerate(kernel_a):
        save(3 * NS_ITERS + 1, j, a)

    def sweep(i, approx):
        product = each(lambda a, x: mul(a, x, width), kernel_a, approx)
        square = each(lambda p: mul(p, p, width), product)
        cube = each(lambda s, p: mul(s, p, width), square, product)
        poly = each(lambda p, s, c: 3.25 * eye - 3.75 * p + 1.75 * s - 0.25 * c, product, square, cube)
        for j in range(len(approx)):
            save(3 * i, j, approx[j])
            save(3 * i + 1, j, product[j])
            save(3 * i + 2, j, poly[j])
        return tuple(each(lambda x, q: mul(x, q, width), approx, poly))

    approx = lax.fori_loop(0, NS_ITERS, sweep, tuple(approx))
    for j, x in enumerate(approx):
        save(3 * NS_ITERS, j, x)
    return list(approx)


def backward_step(d_approx, d_kernel, kernel_at, approx, product, poly, width):
    product_t = each(lambda p: flipped(p, width), product)
    d_poly = each(lambda x, d: mul(flipped(x, width), d, width), approx, d_approx)
    d_next = each(lambda d, q: mul_nt(d, q, width), d_approx, poly)
    right = each(lambda d, p: mul_nt(d, p, width), d_poly, product)
    left = each(lambda p, d: mul(p, d, width), product_t, d_poly)
    both = each(lambda r, x: r + x, right, left)
    third = each(lambda r, p: mul_nt(r, p, width), right, product)
    fourth = each(lambda p, b: mul(p, b, width), product_t, both)
    d_product = each(lambda d, b, t, f: -3.75 * d + 1.75 * b - 0.25 * (t + f), d_poly, both, third, fourth)
    d_kernel = each(lambda k, d, x: k + mul_nt(d, x, width), d_kernel, d_product, approx)
    d_approx = each(lambda n, a, d: n + mul(a, d, width), d_next, kernel_at, d_product)
    return d_approx, d_kernel


def backward_end(d_approx, d_kernel, kernel_a, first, width):
    scale = head_total(kernel_a * kernel_a, width)
    d_scale = -head_total(d_approx * first, width) / scale
    d_kernel = d_kernel + flipped(d_approx, width) / scale + 2.0 * kernel_a * d_scale
    inner = dot(d_kernel * kernel_a, head_ones(width), precision=HIGHEST)
    return kernel_a * (d_kernel - inner)


def stacked(side):
    return blocks_of(side, GROUP)


def doc_table(lens, total):
    shard_start = lax.axis_index("seq") * total
    lengths = [lens[0, i] for i in range(DOCS)]
    starts = [-shard_start]
    for i in range(DOCS - 1):
        starts.append(starts[i] + lengths[i])
    best, size, start = jnp.int32(0), lengths[0], starts[0]
    for i in range(1, DOCS):
        more = lengths[i] > size
        best, size, start = jnp.where(more, i, best), jnp.where(more, lengths[i], size), jnp.where(more, starts[i], start)
    sizes, begins = [size], [start]
    for i in range(DOCS - 1):
        later = best <= i
        sizes.append(jnp.where(later, lengths[i + 1], lengths[i]))
        begins.append(jnp.where(later, starts[i + 1], starts[i]))
    return sizes, begins


def doc_ranges(lens, total):
    sizes, begins = doc_table(lens, total)
    info = []
    for size, begin in zip(sizes, begins):
        info += [jnp.clip(begin, 0, total), jnp.clip(begin + size, 0, total)]
    return info + [begins[0], begins[0] + sizes[0]]


def slot_bounds(lens, total, shape, axis):
    sizes, begins = doc_table(lens, total)
    slot = lax.broadcasted_iota(jnp.int32, shape, axis)
    doc, within = slot // LMK, slot % LMK
    size, begin = jnp.full(shape, sizes[0]), jnp.full(shape, begins[0])
    for d in range(1, DOCS):
        size, begin = jnp.where(doc == d, sizes[d], size), jnp.where(doc == d, begins[d], begin)
    return begin + (within * size + LMK - 1) // LMK, begin + ((within + 1) * size + LMK - 1) // LMK


def project_kernel(lens, inputs, weight, joined, sums, small, edge, counts):
    total = inputs.shape[0]
    block = pl.program_id(0)
    out = dot(inputs[...], weight[...]).astype(BF16)
    joined[...] = out

    @pl.when(block < 2 * GROUPS)
    def _():
        low, high = slot_bounds(lens, total, (DOCS * LMK, 1), 0)
        rows = lax.broadcasted_iota(jnp.int32, (DOCS * LMK, total), 1)
        member = jnp.where((rows >= low) & (rows < high), 1.0, 0.0).astype(BF16)
        slot_sums = dot(member, out)
        size = (high - low).astype(F32)
        sums[...] = slot_sums[:LMK]
        small[0] = (slot_sums[LMK:] / size[LMK:]).astype(BF16).reshape(SMALL, LMK, GROUP)
        counts[...] = jnp.broadcast_to(size, (DOCS * LMK, PAIR)).reshape(DOCS, LMK, PAIR)

    @pl.when(block >= 2 * GROUPS)
    def _():
        edge[0] = out[:16]
        edge[1] = out[total - 16 :]


def project(lens, inputs, weight):
    total, depth = inputs.shape
    width = weight.shape[1]
    half = 2 * GROUPS - 1

    return pl.pallas_call(
        project_kernel,
        grid=(width // GROUP,),
        in_specs=[
            pl.BlockSpec(memory_space=pltpu.SMEM),
            pl.BlockSpec((total, depth), lambda j: (0, 0)),
            pl.BlockSpec((depth, GROUP), lambda j: (0, j)),
        ],
        out_specs=[
            pl.BlockSpec((total, GROUP), lambda j: (0, j)),
            pl.BlockSpec((LMK, GROUP), lambda j: (0, jnp.minimum(j, half))),
            pl.BlockSpec((1, SMALL, None, LMK, GROUP), lambda j: (jnp.minimum(j, half) // GROUPS, 0, lax.rem(jnp.minimum(j, half), GROUPS), 0, 0)),
            pl.BlockSpec((2, 16, GROUP), lambda j: (0, 0, jnp.maximum(j - 2 * GROUPS, 0))),
            pl.BlockSpec((DOCS, LMK, PAIR), lambda j: (0, 0, 0)),
        ],
        out_shape=[
            jax.ShapeDtypeStruct((total, width), BF16),
            jax.ShapeDtypeStruct((LMK, 2 * GROUPS * GROUP), F32),
            jax.ShapeDtypeStruct((2, SMALL, GROUPS, LMK, GROUP), BF16),
            jax.ShapeDtypeStruct((2, 16, GROUPS * GROUP), BF16),
            jax.ShapeDtypeStruct((DOCS, LMK, PAIR), F32),
        ],
        compiler_params=pltpu.CompilerParams(vmem_limit_bytes=48 * 2**20),
        name="project",
    )(lens, inputs, weight)


def join_kernel(lens, inputs, dq, dk, dv, dsum, dsums, tu, td, to, joined, grad, gu, gd, go, flip):
    total = inputs.shape[0]
    block = pl.program_id(0)

    @pl.when(block == 0)
    def _():
        flip[...] = jnp.transpose(inputs[...])

    @pl.when(block < 2 * GROUPS)
    def _():
        low, high = slot_bounds(lens, total, (1, DOCS * LMK), 1)
        rows = lax.broadcasted_iota(jnp.int32, (total, DOCS * LMK), 0)
        member = jnp.where((rows >= low) & (rows < high), 1.0, 0.0).astype(BF16)
        sums = jnp.concatenate([joint(dsum)] + [dsums[d] for d in range(SMALL)], axis=0)
        from_marks = dot(member, sums)

        @pl.when(block < GROUPS)
        def _():
            joined[...] = (from_marks + dq[...]).astype(BF16)

        @pl.when(block >= GROUPS)
        def _():
            joined[...] = (from_marks + dk[...]).astype(BF16)

    @pl.when(block >= 2 * GROUPS)
    def _():
        joined[...] = dv[...].astype(BF16)

    grad[...] = dot(flip[...], joined[...]).astype(BF16)

    @pl.when(block < JOIN_PARTS)
    def _():
        gu[...] = tu[...].astype(F32)
        gd[...] = td[...].astype(F32)
        go[...] = to[...].astype(F32)


JOIN_PARTS = 8


def join(lens, inputs, dq, dk, dv, dsum, dsums, tu, td, to):
    total, depth = inputs.shape
    width = 3 * dq.shape[1]
    half = 2 * GROUPS - 1

    def part(x):
        return pl.BlockSpec((x.shape[0] // JOIN_PARTS, x.shape[1]), lambda j: (jnp.minimum(j, JOIN_PARTS - 1), 0))

    def third(i):
        return pl.BlockSpec((total, GROUP), lambda j: (0, jnp.clip(j - i * GROUPS, 0, GROUPS - 1)))

    return pl.pallas_call(
        join_kernel,
        grid=(width // GROUP,),
        in_specs=[
            pl.BlockSpec(memory_space=pltpu.SMEM),
            pl.BlockSpec((total, depth), lambda j: (0, 0)),
            third(0),
            third(1),
            third(2),
            pl.BlockSpec((2, LMK, PAIR), lambda j: (lax.rem(jnp.minimum(j, half), GROUPS), jnp.minimum(j, half) // GROUPS, 0)),
            pl.BlockSpec((SMALL, None, LMK, GROUP), lambda j: (0, lax.rem(jnp.minimum(j, half), GROUPS), jnp.minimum(j, half) // GROUPS, 0)),
            part(tu),
            part(td),
            part(to),
        ],
        out_specs=[
            pl.BlockSpec((total, GROUP), lambda j: (0, j)),
            pl.BlockSpec((depth, GROUP), lambda j: (0, j)),
            part(tu),
            part(td),
            part(to),
        ],
        out_shape=[
            jax.ShapeDtypeStruct((total, width), BF16),
            jax.ShapeDtypeStruct((depth, width), BF16),
            jax.ShapeDtypeStruct(tu.shape, F32),
            jax.ShapeDtypeStruct(td.shape, F32),
            jax.ShapeDtypeStruct(to.shape, F32),
        ],
        scratch_shapes=[VMEM((depth, total), BF16)],
        compiler_params=pltpu.CompilerParams(vmem_limit_bytes=56 * 2**20),
        name="join",
    )(lens, inputs, dq, dk, dv, dsum, dsums, tu, td, to)


def joint(ref):
    return jnp.concatenate([ref[0], ref[1]], axis=1)


def write_pairs(ref, at, value):
    ref[0, at, :] = value[:, :PAIR]
    ref[1, at, :] = value[:, PAIR:]


LONG_SPEC = pl.BlockSpec((2, LMK, PAIR), lambda g: (g, 0, 0))
ROW_SPEC = pl.BlockSpec((2, 8, PAIR), lambda g: (g, 0, 0))
SMALL_SPEC = pl.BlockSpec((SMALL, None, LMK, GROUP), lambda g: (0, g, 0, 0))
SMALL_ROW_SPEC = pl.BlockSpec((SMALL, None, 8, GROUP), lambda g: (0, g, 0, 0))
TOP = slice(0, LMK)


def for_docs(info, total, body):
    def inside(doc, size, start):
        rows = lax.broadcasted_iota(jnp.int32, (size, 1), 0) + start
        return (rows >= info[2 * doc]) & (rows < info[2 * doc + 1])

    body(0, total, 0, inside(0, total, 0))
    for doc in range(1, DOCS):
        low, high = info[2 * doc], info[2 * doc + 1]
        start = jnp.minimum(low // 16 * 16, total - WINDOW)

        @pl.when((high > low) & (high - start <= WINDOW))
        def _():
            at = pl.multiple_of(start, 16)
            body(doc, WINDOW, at, inside(doc, WINDOW, at))

        @pl.when(high - start > WINDOW)
        def _():
            body(doc, total, 0, inside(doc, total, 0))


def mix_kernel(lens, keys, values, qm, qms, exps, part, parts, stats):
    info = doc_ranges(lens, exps.shape[0])
    parts[...] = jnp.zeros_like(parts)
    stats[...] = jnp.zeros_like(stats)
    part[...] = jnp.zeros_like(part)

    def body(doc, size, start, inside):
        rows = pl.ds(start, size)
        marks = stacked(joint(qm) if doc == 0 else qms[doc - 1])
        scores = jnp.where(inside, dot(keys[rows, :], marks, NT) * 0.125, BIG_NEGATIVE)
        top = jnp.max(scores, axis=0, keepdims=True)
        wide = jnp.exp(scores - top)
        narrow = wide.astype(BF16)
        weighted = side_of(dot(narrow, values[rows, :], TN), GROUP)
        total = jnp.sum(wide, axis=0, keepdims=True)
        if doc == 0:
            exps[...] = narrow
            write_pairs(part, TOP, weighted)
            write_pairs(part, slice(LMK, LMK + 1), top)
            write_pairs(part, slice(LMK + 1, LMK + 2), total)
        else:
            exps[rows, :] = jnp.where(inside, narrow, exps[rows, :])
            parts[doc - 1] = weighted
            stats[doc - 1, 0:1, :] = top
            stats[doc - 1, 1:2, :] = total

    for_docs(info, exps.shape[0], body)


def mix(lens, joined, qm, qms):
    total, width = joined.shape[0], joined.shape[1] // 3
    groups = width // GROUP
    return pl.pallas_call(
        mix_kernel,
        grid=(groups,),
        in_specs=[
            pl.BlockSpec(memory_space=pltpu.SMEM),
            pl.BlockSpec((total, GROUP), lambda g: (0, groups + g)),
            pl.BlockSpec((total, GROUP), lambda g: (0, 2 * groups + g)),
            LONG_SPEC,
            SMALL_SPEC,
        ],
        out_specs=[
            pl.BlockSpec((total, GROUP), lambda g: (0, g)),
            pl.BlockSpec((2, LMK + 8, PAIR), lambda g: (g, 0, 0)),
            SMALL_SPEC,
            SMALL_ROW_SPEC,
        ],
        out_shape=[
            jax.ShapeDtypeStruct((total, width), BF16),
            jax.ShapeDtypeStruct((PAIRS, LMK + 8, PAIR), F32),
            jax.ShapeDtypeStruct((SMALL, groups, LMK, GROUP), F32),
            jax.ShapeDtypeStruct((SMALL, groups, 8, GROUP), F32),
        ],
        compiler_params=pltpu.CompilerParams(vmem_limit_bytes=48 * 2**20),
        name="mix",
    )(lens, joined, joined, qm, qms)


TOEP = 160
BLK = 128


def band(taps, reverse_unused=None):
    wide = jnp.broadcast_to(taps, (BLK, 256))
    return pltpu.roll(wide, 0, 1, stride=1, stride_axis=0)[:, :TOEP].astype(BF16)


def bands(taps, group):
    heads = GROUP // LMK
    return jnp.concatenate([band(taps[pl.ds(group * heads + i, 1), :]) for i in range(heads)], axis=0)


def head_rows(stack):
    lanes = lax.broadcasted_iota(jnp.int32, (BLK, GROUP), 1) // LMK
    out = stack[:BLK]
    for i in range(1, GROUP // LMK):
        out = jnp.where(lanes == i, stack[i * BLK : (i + 1) * BLK], out)
    return out


def padded_rows(before, here, after, pad):
    total = here.shape[0]
    pad[0:16, :] = before
    pad[16 : total + 16, :] = here[...]
    pad[total + 16 : total + 32, :] = after


def doc_windows(info, total, body):
    def member(doc, start):
        rows = lax.broadcasted_iota(jnp.int32, (TOEP, 1), 0) + start - 16
        low, high = (info[8], info[9]) if doc == 0 else (info[2 * doc], info[2 * doc + 1])
        return (rows >= low) & (rows < high)

    for doc in range(DOCS):
        low, high = info[2 * doc], info[2 * doc + 1]

        @pl.loop(low // BLK, jnp.where(high > low, (high + BLK - 1) // BLK, low // BLK))
        def _(b):
            start = pl.multiple_of(b * BLK, BLK)
            body(doc, start, member(doc, start))


def attend_kernel(lens, queries, values, halo, taps, km, car, kms, cars, kern, mixture, pad, att):
    total = queries.shape[0]
    info = doc_ranges(lens, total)
    group = pl.program_id(0)
    ones = head_ones(GROUP).astype(BF16)

    def body(doc, size, start, inside):
        rows = pl.ds(start, size)
        marks = stacked(joint(km) if doc == 0 else kms[doc - 1])
        scores = dot(queries[rows, :], marks, NT) * 0.125
        exponent = jnp.exp(scores - head_max(scores, GROUP))
        kernel = (exponent / dot(exponent.astype(BF16), ones)).astype(BF16)
        carried = stacked(joint(car) if doc == 0 else cars[doc - 1])
        attended = dot(kernel, carried)
        if doc == 0:
            kern[...] = kernel
            att[...] = attended
        else:
            kern[rows, :] = jnp.where(inside, kernel, kern[rows, :])
            att[rows, :] = jnp.where(inside, attended, att[rows, :])

    for_docs(info, total, body)
    padded_rows(halo[0], values, halo[1], pad)
    tape = bands(taps, group)

    def conv(doc, start, inside):
        window = jnp.where(inside, pad[pl.ds(start, TOEP), :], jnp.zeros((), BF16))
        out = head_rows(dot(tape, window))
        rows = pl.ds(start, BLK)
        here = inside[16 : 16 + BLK]
        new = (att[rows, :] + out).astype(BF16)
        if doc == 0:
            mixture[rows, :] = new
        else:
            mixture[rows, :] = jnp.where(here, new, mixture[rows, :])

    doc_windows(info, total, conv)


def attend(lens, joined, halo, taps, km, car, kms, cars):
    total, width = joined.shape[0], joined.shape[1] // 3
    groups = width // GROUP
    col = pl.BlockSpec((total, GROUP), lambda g: (0, g))
    mark, marks = LONG_SPEC, SMALL_SPEC
    return pl.pallas_call(
        attend_kernel,
        grid=(groups,),
        in_specs=[
            pl.BlockSpec(memory_space=pltpu.SMEM),
            col,
            pl.BlockSpec((total, GROUP), lambda g: (0, 2 * groups + g)),
            pl.BlockSpec((2, 16, GROUP), lambda g: (0, 0, g)),
            pl.BlockSpec(taps.shape, lambda g: (0, 0)),
            mark,
            mark,
            marks,
            marks,
        ],
        out_specs=[col, col],
        out_shape=[jax.ShapeDtypeStruct((total, width), BF16)] * 2,
        scratch_shapes=[VMEM((total + 32, GROUP), BF16), VMEM((total, GROUP), F32)],
        compiler_params=pltpu.CompilerParams(vmem_limit_bytes=48 * 2**20),
        name="attend",
    )(lens, joined, joined, halo, taps, km, car, kms, cars)


def back_f_kernel(lens, queries, dmix, kern, km, car, kms, cars, dq, part, parts):
    info = doc_ranges(lens, dq.shape[0])
    parts[...] = jnp.zeros_like(parts)
    ones = head_ones(GROUP).astype(BF16)

    def body(doc, size, start, inside):
        rows = pl.ds(start, size)
        zero = jnp.zeros((), BF16)
        marks = stacked(joint(km) if doc == 0 else kms[doc - 1])
        carried = stacked(joint(car) if doc == 0 else cars[doc - 1])
        datt = dmix[rows, :]
        kernel = jnp.where(inside, kern[rows, :], zero)
        d_carried = side_of(dot(kernel, datt, TN), GROUP)
        d_kernel = dot(datt, carried, NT)
        wide = kernel.astype(F32)
        weighed = wide * d_kernel
        high = weighed.astype(BF16)
        low = (weighed - high.astype(F32)).astype(BF16)
        inner = dot(high, ones) + dot(low, ones)
        d_scores = (weighed - wide * inner).astype(BF16)
        d_queries = dot(d_scores, marks) * 0.125
        d_marks = side_of(dot(d_scores, queries[rows, :], TN), GROUP) * 0.125
        if doc == 0:
            dq[...] = d_queries
            write_pairs(part, TOP, d_carried)
            write_pairs(part, slice(LMK, 2 * LMK), d_marks)
        else:
            dq[rows, :] = jnp.where(inside, d_queries, dq[rows, :])
            parts[0, doc - 1] = d_carried
            parts[1, doc - 1] = d_marks

    for_docs(info, dq.shape[0], body)


def back_f(lens, joined, dmix, kern, km, car, kms, cars):
    total, width = dmix.shape
    groups = width // GROUP
    col = pl.BlockSpec((total, GROUP), lambda g: (0, g))
    mark, marks = LONG_SPEC, SMALL_SPEC
    return pl.pallas_call(
        back_f_kernel,
        grid=(groups,),
        in_specs=[pl.BlockSpec(memory_space=pltpu.SMEM), col, col, col, mark, mark, marks, marks],
        out_specs=[
            col,
            pl.BlockSpec((2, 2 * LMK, PAIR), lambda g: (g, 0, 0)),
            pl.BlockSpec((2, SMALL, None, LMK, GROUP), lambda g: (0, 0, g, 0, 0)),
        ],
        out_shape=[
            jax.ShapeDtypeStruct((total, width), F32),
            jax.ShapeDtypeStruct((PAIRS, 2 * LMK, PAIR), F32),
            jax.ShapeDtypeStruct((2, SMALL, groups, LMK, GROUP), F32),
        ],
        compiler_params=pltpu.CompilerParams(vmem_limit_bytes=48 * 2**20),
        name="back_f",
    )(lens, joined, dmix, kern, km, car, kms, cars)


def back_b_kernel(lens, keys, values, halo, exps, factor, sc, along, scs, alongs, qm, qms, taps, dmix, dhalo, dk, dv, part, parts, dtaps, pad, dpad, acc):
    total = keys.shape[0]
    info = doc_ranges(lens, total)
    group = pl.program_id(0)
    parts[...] = jnp.zeros_like(parts)

    def body(doc, size, start, inside):
        rows = pl.ds(start, size)
        scaled = stacked(joint(sc) if doc == 0 else scs[doc - 1])
        marks = stacked(joint(qm) if doc == 0 else qms[doc - 1])
        wide = jnp.where(inside, exps[rows, :].astype(F32), 0.0)
        if doc == 0:
            wide = wide * factor[0:1, :]
        shift = joint(along)[0:1, :] if doc == 0 else alongs[doc - 1, 0:1, :]
        d_values = dot(wide.astype(BF16), scaled)
        reach = dot(values[rows, :], scaled, NT)
        d_scores = (wide * (reach - shift)).astype(BF16)
        d_keys = dot(d_scores, marks) * 0.125
        d_marks = side_of(dot(d_scores, keys[rows, :], TN), GROUP) * 0.125
        if doc == 0:
            dk[...] = d_keys
            dv[...] = d_values
            write_pairs(part, TOP, d_marks)
        else:
            dk[rows, :] = jnp.where(inside, d_keys, dk[rows, :])
            dv[rows, :] = jnp.where(inside, d_values, dv[rows, :])
            parts[doc - 1] = d_marks

    for_docs(info, total, body)
    padded_rows(halo[0], values, halo[1], pad)
    padded_rows(dhalo[0], dmix, dhalo[1], dpad)
    tape = bands(taps, group)
    acc[...] = jnp.zeros_like(acc)

    def conv(doc, start, inside):
        zero = jnp.zeros((), BF16)
        rows = pl.ds(start, BLK)
        here = inside[16 : 16 + BLK]
        out = head_rows(dot(tape, jnp.where(inside, dpad[pl.ds(start, TOEP), :], zero)))
        dv[rows, :] = dv[rows, :] + jnp.where(here, out, 0.0)
        window = jnp.where(inside, pad[pl.ds(start, TOEP), :], zero)
        mine = jnp.where(here, dmix[rows, :], zero)
        lanes = lax.broadcasted_iota(jnp.int32, (BLK, GROUP), 1) // LMK
        spread = jnp.concatenate([jnp.where(lanes == i, mine, zero) for i in range(GROUP // LMK)], axis=0)
        acc[:, :TOEP] = acc[:, :TOEP] + dot(spread, window, NT)

    doc_windows(info, total, conv)
    rows = lax.broadcasted_iota(jnp.int32, (BLK, BLK), 0)
    lanes = lax.broadcasted_iota(jnp.int32, (BLK, BLK), 1)
    reverse = jnp.where(rows + lanes == BLK - 1, 1.0, 0.0).astype(F32)
    for i in range(GROUP // LMK):
        square = dot(reverse, acc[i * BLK : (i + 1) * BLK, :], precision=HIGHEST)
        turned = pltpu.roll(square, 0, 1, stride=1, stride_axis=0)
        dtaps[0, i : i + 1, :] = jnp.sum(turned, axis=0, keepdims=True)


def back_b(lens, joined, halo, exps, factor, sc, along, scs, alongs, qm, qms, taps, dmix, dhalo):
    total, width = dmix.shape
    groups = width // GROUP
    heads = GROUP // LMK
    col = pl.BlockSpec((total, GROUP), lambda g: (0, g))
    mark, marks = LONG_SPEC, SMALL_SPEC
    row = pl.BlockSpec((8, GROUP), lambda g: (0, g))
    edge = pl.BlockSpec((2, 16, GROUP), lambda g: (0, 0, g))
    return pl.pallas_call(
        back_b_kernel,
        grid=(groups,),
        in_specs=[
            pl.BlockSpec(memory_space=pltpu.SMEM),
            pl.BlockSpec((total, GROUP), lambda g: (0, groups + g)),
            pl.BlockSpec((total, GROUP), lambda g: (0, 2 * groups + g)),
            edge,
            col,
            row,
            mark,
            ROW_SPEC,
            marks,
            SMALL_ROW_SPEC,
            mark,
            marks,
            pl.BlockSpec(taps.shape, lambda g: (0, 0)),
            col,
            edge,
        ],
        out_specs=[col, col, mark, marks, pl.BlockSpec((1, heads, 256), lambda g: (g, 0, 0))],
        out_shape=[
            jax.ShapeDtypeStruct((total, width), F32),
            jax.ShapeDtypeStruct((total, width), F32),
            jax.ShapeDtypeStruct((PAIRS, LMK, PAIR), F32),
            jax.ShapeDtypeStruct((SMALL, groups, LMK, GROUP), F32),
            jax.ShapeDtypeStruct((groups, heads, 256), F32),
        ],
        scratch_shapes=[VMEM((total + 32, GROUP), BF16), VMEM((total + 32, GROUP), BF16), VMEM((heads * BLK, 256), F32)],
        compiler_params=pltpu.CompilerParams(vmem_limit_bytes=48 * 2**20),
        name="back_b",
    )(lens, joined, joined, halo, exps, factor, sc, along, scs, alongs, qm, qms, taps, dmix, dhalo)


class Ring:
    def __init__(self, count):
        self.count = count
        self.me = lax.axis_index("seq")
        self.row = lax.axis_index("row")
        self.steps = range(1, count)

    def ahead(self, k):
        return lax.rem(self.me + k, self.count)

    def enter(self, others=()):
        barrier = pltpu.get_barrier_semaphore()
        for to in [(self.ahead(k), self.row) for k in self.steps] + list(others):
            pl.semaphore_signal(barrier, inc=1, device_id=to, device_id_type=MESH)
        pl.semaphore_wait(barrier, self.count - 1 + len(others))

    def copy(self, src, dst, send, recv, to):
        return pltpu.make_async_remote_copy(src_ref=src, dst_ref=dst, send_sem=send, recv_sem=recv, device_id=(to, self.row), device_id_type=MESH)

    def scatter(self, pieces, landing, send, recv, first, owners):
        for k in self.steps:
            to = self.ahead(k)

            @pl.when((to >= first) & (to < first + owners))
            def _():
                self.copy(pieces(to - first), landing.at[k - 1], send.at[k - 1], recv.at[k - 1], to).start()

        def arrived():
            for k in self.steps:
                self.copy(pieces(0), landing.at[k - 1], send.at[k - 1], recv.at[k - 1], self.ahead(k)).wait_recv()

        def sent():
            for k in self.steps:
                to = self.ahead(k)

                @pl.when((to >= first) & (to < first + owners))
                def _():
                    self.copy(pieces(to - first), landing.at[k - 1], send.at[k - 1], recv.at[k - 1], to).wait_send()

        return arrived, sent

    def share(self, held, send, recv, first):
        piece = self.me - first
        for k in self.steps:
            self.copy(held.at[piece], held.at[piece], send.at[k - 1], recv.at[piece], self.ahead(k)).start()

    def share_sent(self, held, send, recv, first):
        piece = self.me - first
        for k in self.steps:
            self.copy(held.at[piece], held.at[piece], send.at[k - 1], recv.at[piece], self.ahead(k)).wait_send()

    def shared(self, held, send, recv, first, owners):
        for p in range(owners):

            @pl.when(self.me != first + p)
            def _():
                self.copy(held.at[p], held.at[p], send.at[0], recv.at[p], self.ahead(1)).wait_recv()


    def edges_start(self, here, landing, send, recv):
        @pl.when(self.me > 0)
        def _():
            self.copy(here.at[0], landing.at[1], send.at[0], recv.at[1], self.me - 1).start()

        @pl.when(self.me < self.count - 1)
        def _():
            self.copy(here.at[1], landing.at[0], send.at[1], recv.at[0], self.me + 1).start()

    def edges_wait(self, here, landing, send, recv, out):
        out[...] = jnp.zeros_like(out)

        @pl.when(self.me > 0)
        def _():
            done = self.copy(here.at[0], landing.at[0], send.at[0], recv.at[0], self.me - 1)
            done.wait_recv()
            done.wait_send()
            out[0] = landing[0]

        @pl.when(self.me < self.count - 1)
        def _():
            done = self.copy(here.at[1], landing.at[1], send.at[1], recv.at[1], self.me + 1)
            done.wait_recv()
            done.wait_send()
            out[1] = landing[1]


OWNERS = 8
DMA = pltpu.SemaphoreType.DMA
SAVES = 3 * NS_ITERS + 2
CASES = SMALL * GROUPS
EARLY = 2


def ends(ring):
    return (ring.me == 0) | (ring.me == ring.count - 1)


def owner_of_pair(ring):
    return (ring.me >= 1) & (ring.me <= PAIRS)


def pair_of(ring):
    return jnp.clip(ring.me - 1, 0, PAIRS - 1)


def remote_params(cid):
    return pltpu.CompilerParams(collective_id=cid, has_side_effects=True, vmem_limit_bytes=60 * 2**20)


def in_vmem(n):
    return [pl.BlockSpec(memory_space=VMEM)] * n


ANY_SPEC = pl.BlockSpec(memory_space=pl.ANY)


def small_forward(doc, at, qms, kms, held, invs):
    def save(i, j, value):
        held[at, j, i] = value

    inverse = inverse_forward([qms[doc, g] for g in range(GROUPS)], [kms[doc, g] for g in range(GROUPS)], save, GROUP)
    for g in range(GROUPS):
        invs[at, g] = inverse[g]


def marks_kernel(count, part, counts, edge, small, qm, km, halo, saved, invs, landing, held, hland, sheld, ss, rs, gs, gr, es, er, hs):
    ring = Ring(count)
    ring.enter()
    ring.edges_start(edge, hland, es, er)
    each_ = LMK // OWNERS
    arrived, sent = ring.scatter(lambda o: part.at[pl.ds(pl.multiple_of(o * each_, each_), each_), :], landing, ss, rs, 0, OWNERS)
    keep = [pltpu.make_async_copy(sheld.at[d], saved.at[d], hs.at[d]) for d in range(EARLY)]

    @pl.when(ring.me < OWNERS)
    def _():
        arrived()
        at = pl.ds(pl.multiple_of(ring.me * each_, each_), each_)
        total = part[at, :]
        for k in ring.steps:
            total = total + landing[k - 1]
        total = total / counts[0, at, 0:1]
        half = total.shape[1] // 2
        held[ring.me, 0:each_, :] = total[:, :half].astype(BF16)
        held[ring.me, each_ : 2 * each_, :] = total[:, half:].astype(BF16)
        ring.share(held, gs, gr, 0)

    @pl.when(ends(ring))
    def _():
        @pl.loop(0, EARLY)
        def _(d):
            small_forward(d, d, small.at[0], small.at[1], sheld, invs)

        for copy in keep:
            copy.start()

    ring.shared(held, gs, gr, 0, OWNERS)
    wide = [held[o].astype(F32) for o in range(OWNERS)]
    query = jnp.concatenate([w[:each_] for w in wide], axis=0).astype(BF16)
    key = jnp.concatenate([w[each_:] for w in wide], axis=0).astype(BF16)
    for p in range(PAIRS):
        qm[p] = query[:, p * PAIR : (p + 1) * PAIR]
        km[p] = key[:, p * PAIR : (p + 1) * PAIR]
    ring.edges_wait(edge, hland, es, er, halo)
    sent()

    @pl.when(ring.me < OWNERS)
    def _():
        ring.share_sent(held, gs, gr, 0)

    @pl.when(ends(ring))
    def _():
        for copy in keep:
            copy.wait()


def all_marks(count, part, counts, edge, small):
    width = part.shape[1]
    each_ = LMK // OWNERS
    return pl.pallas_call(
        functools.partial(marks_kernel, count),
        in_specs=in_vmem(4),
        out_specs=in_vmem(3) + [ANY_SPEC] + in_vmem(1),
        out_shape=[jax.ShapeDtypeStruct((PAIRS, LMK, PAIR), BF16)] * 2
        + [
            jax.ShapeDtypeStruct(edge.shape, BF16),
            jax.ShapeDtypeStruct((EARLY, GROUPS, SAVES, LMK, GROUP), F32),
            jax.ShapeDtypeStruct((EARLY, GROUPS, LMK, GROUP), F32),
        ],
        scratch_shapes=[
            VMEM((count - 1, each_, width), F32),
            VMEM((OWNERS, 2 * each_, width // 2), BF16),
            VMEM(edge.shape, BF16),
            VMEM((EARLY, GROUPS, SAVES, LMK, GROUP), F32),
            DMA((count - 1,)),
            DMA((count - 1,)),
            DMA((count - 1,)),
            DMA((OWNERS,)),
            DMA((2,)),
            DMA((2,)),
            DMA((EARLY,)),
        ],
        compiler_params=remote_params(1),
        name="all_marks",
    )(part, counts, edge, small)


def carry_kernel(count, part, qm, km, small, wsm, stsm, invs, car, stat, saved, inv, mixed, cars, saveds, inv2, mixeds, landing, cheld, sheld, sk, ss, rs, cs, cr, ts, tr, hs):
    ring = Ring(count)
    ring.enter()
    arrived, sent = ring.scatter(lambda p: part.at[p], landing, ss, rs, 1, PAIRS)
    keep = pltpu.make_async_copy(sk, saveds, hs.at[0])

    @pl.when(owner_of_pair(ring))
    def _():
        pair = pair_of(ring)

        def save(i, j, value):
            saved[i] = value

        inverse = inverse_forward([qm[pair]], [km[pair]], save, PAIR)[0]
        inv[...] = inverse
        arrived()
        pieces = [part[pair]] + [landing[k - 1] for k in ring.steps]
        top = pieces[0][LMK : LMK + 1]
        for piece in pieces[1:]:
            top = jnp.maximum(top, piece[LMK : LMK + 1])
        weighted = jnp.zeros((LMK, PAIR), F32)
        total = jnp.zeros((1, PAIR), F32)
        for piece in pieces:
            share = jnp.exp(piece[LMK : LMK + 1] - top)
            weighted = weighted + piece[:LMK] * column_of(share, PAIR)
            total = total + piece[LMK + 1 : LMK + 2] * share
        mean = weighted / column_of(total, PAIR)
        mixed[...] = mean
        cheld[pair] = mul(inverse, mean, PAIR).astype(BF16)
        sheld[pair] = jnp.concatenate([top, total, jnp.zeros((6, PAIR), F32)], axis=0)
        ring.share(cheld, cs, cr, 1)
        ring.share(sheld, ts, tr, 1)

    @pl.when(ends(ring))
    def _():
        @pl.loop(0, SMALL - EARLY)
        def _(d):
            small_forward(d + EARLY, d, small.at[0], small.at[1], sk, inv2)

        keep.start()

        def finish(doc, inverse):
            for g in range(GROUPS):
                total = jnp.maximum(stsm[doc, g, 1:2, :], 1e-30)
                mean = wsm[doc, g] / column_of(total, GROUP)
                mixeds[doc, g] = mean
                cars[doc, g] = mul(inverse[g], mean, GROUP).astype(BF16)

        for d in range(SMALL):
            finish(d, [invs[d, g] if d < EARLY else inv2[d - EARLY, g] for g in range(GROUPS)])

    ring.shared(cheld, cs, cr, 1, PAIRS)
    ring.shared(sheld, ts, tr, 1, PAIRS)
    car[...] = cheld[...]
    stat[...] = sheld[...]
    sent()

    @pl.when(owner_of_pair(ring))
    def _():
        ring.share_sent(cheld, cs, cr, 1)
        ring.share_sent(sheld, ts, tr, 1)

    @pl.when(ends(ring))
    def _():
        keep.wait()


def carry(count, part, qm, km, small, wsm, stsm, invs):
    late = SMALL - EARLY
    return pl.pallas_call(
        functools.partial(carry_kernel, count),
        in_specs=in_vmem(7),
        out_specs=in_vmem(6) + [ANY_SPEC] + in_vmem(2),
        out_shape=[
            jax.ShapeDtypeStruct((PAIRS, LMK, PAIR), BF16),
            jax.ShapeDtypeStruct((PAIRS, 8, PAIR), F32),
            jax.ShapeDtypeStruct((SAVES, LMK, PAIR), F32),
            jax.ShapeDtypeStruct((LMK, PAIR), F32),
            jax.ShapeDtypeStruct((LMK, PAIR), F32),
            jax.ShapeDtypeStruct((SMALL, GROUPS, LMK, GROUP), BF16),
            jax.ShapeDtypeStruct((late, GROUPS, SAVES, LMK, GROUP), F32),
            jax.ShapeDtypeStruct((late, GROUPS, LMK, GROUP), F32),
            jax.ShapeDtypeStruct((SMALL, GROUPS, LMK, GROUP), F32),
        ],
        scratch_shapes=[
            VMEM((count - 1, LMK + 8, PAIR), F32),
            VMEM((PAIRS, LMK, PAIR), BF16),
            VMEM((PAIRS, 8, PAIR), F32),
            VMEM((late, GROUPS, SAVES, LMK, GROUP), F32),
            DMA((count - 1,)),
            DMA((count - 1,)),
            DMA((count - 1,)),
            DMA((PAIRS,)),
            DMA((count - 1,)),
            DMA((PAIRS,)),
            DMA((1,)),
        ],
        compiler_params=remote_params(2),
        name="carry",
    )(part, qm, km, small, wsm, stsm, invs)


def spread_grad(d_carried, inverse, mixed, total, width):
    d_mixed = mul(flipped(inverse, width), d_carried, width)
    scaled = (d_mixed / column_of(total, width)).astype(BF16)
    along = row_of(scaled.astype(F32) * mixed, width)
    return scaled, along


def spread_kernel(count, part, stat, inv, mixed, smallf, stsm, invs, inv2, mixeds, edge, sc, along, dtot, scs, alongs, halo, landing, sheld, aheld, hland, ss, rs, cs, cr, ts, tr, es, er):
    ring = Ring(count)
    ring.enter()
    arrived, sent = ring.scatter(lambda p: part.at[p], landing, ss, rs, 1, PAIRS)
    ring.edges_start(edge, hland, es, er)

    @pl.when(owner_of_pair(ring))
    def _():
        pair = pair_of(ring)
        arrived()
        total = part[pair]
        for k in ring.steps:
            total = total + landing[k - 1]
        dtot[...] = total
        scaled, reach = spread_grad(total[:LMK], inv[...], mixed[...], stat[pair, 1:2, :], PAIR)
        sheld[pair] = scaled
        aheld[pair] = reach
        ring.share(sheld, cs, cr, 1)
        ring.share(aheld, ts, tr, 1)

    @pl.when(ends(ring))
    def _():
        for d in range(SMALL):
            for g in range(GROUPS):
                total = jnp.maximum(stsm[d, g, 1:2, :], 1e-30)
                inverse = invs[d, g] if d < EARLY else inv2[d - EARLY, g]
                scaled, reach = spread_grad(smallf[0, d, g], inverse, mixeds[d, g], total, GROUP)
                scs[d, g] = scaled
                alongs[d, g] = reach

    ring.shared(sheld, cs, cr, 1, PAIRS)
    ring.shared(aheld, ts, tr, 1, PAIRS)
    sc[...] = sheld[...]
    along[...] = aheld[...]
    ring.edges_wait(edge, hland, es, er, halo)
    sent()

    @pl.when(owner_of_pair(ring))
    def _():
        ring.share_sent(sheld, cs, cr, 1)
        ring.share_sent(aheld, ts, tr, 1)


def spread(count, part, stat, inv, mixed, smallf, stsm, invs, inv2, mixeds, edge):
    return pl.pallas_call(
        functools.partial(spread_kernel, count),
        in_specs=in_vmem(10),
        out_specs=in_vmem(6),
        out_shape=[
            jax.ShapeDtypeStruct((PAIRS, LMK, PAIR), BF16),
            jax.ShapeDtypeStruct((PAIRS, 8, PAIR), F32),
            jax.ShapeDtypeStruct((2 * LMK, PAIR), F32),
            jax.ShapeDtypeStruct((SMALL, GROUPS, LMK, GROUP), BF16),
            jax.ShapeDtypeStruct((SMALL, GROUPS, 8, GROUP), F32),
            jax.ShapeDtypeStruct(edge.shape, BF16),
        ],
        scratch_shapes=[
            VMEM((count - 1, 2 * LMK, PAIR), F32),
            VMEM((PAIRS, LMK, PAIR), BF16),
            VMEM((PAIRS, 8, PAIR), F32),
            VMEM(edge.shape, BF16),
            DMA((count - 1,)),
            DMA((count - 1,)),
            DMA((count - 1,)),
            DMA((PAIRS,)),
            DMA((count - 1,)),
            DMA((PAIRS,)),
            DMA((2,)),
            DMA((2,)),
        ],
        compiler_params=remote_params(3),
        name="spread",
    )(part, stat, inv, mixed, smallf, stsm, invs, inv2, mixeds, edge)


class Sums:
    STEPS = 9

    def __init__(self, units, width, own, out, r0, r1, r2, r3, lsem, osem, ss, rs):
        self.units, self.width = units, width
        self.own, self.out, self.r0, self.r1, self.r2, self.r3 = own, out, r0, r1, r2, r3
        self.lsem, self.osem, self.ss, self.rs = lsem, osem, ss, rs
        s_ax, r_ax = lax.axis_index("seq"), lax.axis_index("row")
        z, x, y, c = s_ax // 2, lax.rem(s_ax, 2), r_ax // 2, lax.rem(r_ax, 2)
        x1, y1 = x + (1 - c) * (1 - 2 * x), y + c * (1 - 2 * y)
        x2, y2 = x + c * (1 - 2 * x), y + (1 - c) * (1 - 2 * y)
        self.z = z
        self.core = (s_ax, y * 2 + (1 - c))
        self.first = (z * 2 + x1, y1 * 2 + c)
        self.second = (z * 2 + x2, y2 * 2 + c)
        self.line = [(lax.rem(z + k, 4) * 2 + x, r_ax) for k in (1, 2, 3)]
        self.others = [self.core, self.first, self.second] + self.line
        self.b1 = x * (1 - c) + y * c
        self.b2 = y * (1 - c) + x * c
        self.mine = pl.ds(pl.multiple_of(c * width, 128), width)
        self.theirs = pl.ds(pl.multiple_of((1 - c) * width, 128), width)
        self.fly = (self.core, self.first, self.second) + tuple(self.line) + tuple(self.line) + (self.second, self.first, self.core)

    def block(self, ref, i, j):
        return ref.at[pl.ds(i * 768, 768), pl.ds(j * 2 * self.width, 2 * self.width)]

    def load(self):
        for u, (src, _, i, j) in enumerate(self.units):
            pltpu.make_async_copy(self.block(src, i, j), self.own.at[u], self.lsem.at[u]).start()

    def rows(self, start, size):
        return pl.ds(pl.multiple_of(start, 16), size)

    def copies(self, u):
        out, line = self.out, [lax.rem(self.z + k, 4) for k in (1, 2, 3)]
        base1, base2 = self.b1 * 384, self.b1 * 384 + self.b2 * 192
        last = out.at[u, self.rows(base2 + self.z * 48, 48), self.mine]
        pairs = [
            (self.own.at[u, :, self.theirs], self.r0.at[u]),
            (self.r0.at[u, self.rows((1 - self.b1) * 384, 384), :], self.r1.at[u]),
            (self.r1.at[u, self.rows((1 - self.b2) * 192, 192), :], self.r2.at[u]),
        ]
        pairs += [(self.r2.at[u, self.rows(line[k] * 48, 48), :], self.r3.at[u, k]) for k in range(3)]
        pairs += [(last, last)] * 3
        for region in (out.at[u, self.rows(base2, 192), self.mine], out.at[u, self.rows(base1, 384), self.mine], out.at[u, :, self.mine]):
            pairs.append((region, region))
        return pairs

    def copy(self, u, k):
        src, dst = self.copies(u)[k]
        return pltpu.make_async_remote_copy(src_ref=src, dst_ref=dst, send_sem=self.ss.at[u, k], recv_sem=self.rs.at[u, k], device_id=self.fly[k], device_id_type=MESH)

    def add(self, u, here, start, there, size):
        @pl.loop(0, size, step=64)
        def _(t):
            q = self.rows(t, 64)
            here[u, q, :] = (here[u, q, :].astype(F32) + there(self.rows(start + t, 64)).astype(F32)).astype(BF16)

    def advance(self, u, s):
        if s == 0:
            pltpu.make_async_copy(self.own.at[u], self.own.at[u], self.lsem.at[u]).wait()
            self.copy(u, 0).start()
        elif s == 1:
            self.copy(u, 0).wait_recv()
            self.add(u, self.r0, 0, lambda q: self.own[u, q, self.mine], 768)
            self.copy(u, 1).start()
        elif s == 2:
            self.copy(u, 1).wait_recv()
            self.add(u, self.r1, self.b1 * 384, lambda q: self.r0[u, q, :], 384)
            self.copy(u, 2).start()
        elif s == 3:
            self.copy(u, 2).wait_recv()
            self.add(u, self.r2, self.b2 * 192, lambda q: self.r1[u, q, :], 192)
            for k in range(3):
                self.copy(u, 3 + k).start()
        elif s == 4:
            for k in range(3):
                self.copy(u, 3 + k).wait_recv()
            total = self.r2[u, self.rows(self.z * 48, 48), :].astype(F32)
            for k in range(3):
                total = total + self.r3[u, k].astype(F32)
            self.out[u, self.rows(self.b1 * 384 + self.b2 * 192 + self.z * 48, 48), self.mine] = total.astype(BF16)
            for k in range(3):
                self.copy(u, 6 + k).start()
        elif s == 5:
            for k in range(3):
                self.copy(u, 6 + k).wait_recv()
            self.copy(u, 9).start()
        elif s in (6, 7):
            self.copy(u, s + 3).wait_recv()
            self.copy(u, s + 4).start()
        else:
            self.copy(u, 11).wait_recv()

    def step(self, tau):
        for s in range(self.STEPS - 1, -1, -1):
            u = tau - s

            @pl.when((u >= 0) & (u < len(self.units)))
            def _():
                self.advance(jnp.clip(u, 0, len(self.units) - 1), s)

    def finish(self):
        copies = []
        for u, (_, dst, i, j) in enumerate(self.units):
            copies.append(pltpu.make_async_copy(self.out.at[u], self.block(dst, i, j), self.osem.at[u]))
            copies[-1].start()

        @pl.loop(0, len(self.units))
        def _(u):
            for k in range(12):
                self.copy(u, k).wait_send()

        for copy in copies:
            copy.wait()


def sums_scratch(n, width):
    return [
        VMEM((n, 768, 2 * width), BF16),
        VMEM((n, 768, 2 * width), BF16),
        VMEM((n, 768, width), BF16),
        VMEM((n, 384, width), BF16),
        VMEM((n, 192, width), BF16),
        VMEM((n, 3, 48, width), BF16),
        DMA((n,)),
        DMA((n,)),
        DMA((n, 12)),
        DMA((n, 12)),
    ]


N_SUMS = 10


def small_all(values, smr, sss, srs, sums, k):
    z = sums.z
    s_ax, r_ax = lax.axis_index("seq"), lax.axis_index("row")
    x = lax.rem(s_ax, 2)
    partners = [sums.core, sums.first, sums.second, (lax.rem(z + 2, 4) * 2 + x, r_ax), ((z + 1 - 2 * lax.rem(z, 2)) * 2 + x, r_ax)]

    def copy(i):
        return pltpu.make_async_remote_copy(src_ref=smr.at[i], dst_ref=smr.at[i + 6], send_sem=sss.at[i], recv_sem=srs.at[i], device_id=partners[i], device_id_type=MESH)

    if k == 0:
        smr[0] = values[...]
    else:
        copy(k - 1).wait_recv()
        smr[k] = smr[k - 1] + smr[k + 5]
    if k < 5:
        copy(k).start()
    else:
        for i in range(5):
            copy(i).wait_send()


def sums_kernel(count, wide, *refs):
    (part, dtot, saved, mixed, qm, km, counts, smallb, smallf, save_a, save_b, mixeds, marks, gd, gu, go, sm), refs = refs[:17], refs[17:]
    (dsum, dsums, td, tu, to, osm), refs = refs[:6], refs[6:]
    (landing, held, keep, da, dk, kt, la, lk, lt, smr), refs = refs[:10], refs[10:]
    scratch, refs = refs[:N_SUMS], refs[N_SUMS:]
    ss, rs, cs, cr, hs, sss, srs = refs
    ring = Ring(count)
    if wide:
        units = [(gd, td, i, 0) for i in range(4)] + [(gu, tu, 0, i) for i in range(4)] + [(go, to, 0, 0)]
        sums = Sums(units, 384, *scratch)
        sums.load()
        ring.enter(sums.others)
    else:
        ring.enter()
    arrived, sent = ring.scatter(lambda p: part.at[p], landing, ss, rs, 1, PAIRS)
    fetch = [pltpu.make_async_copy(save_a, keep.at[pl.ds(0, EARLY)], hs.at[0]), pltpu.make_async_copy(save_b, keep.at[pl.ds(EARLY, SMALL - EARLY)], hs.at[1])]
    owner, end = owner_of_pair(ring), ends(ring)
    pair = pair_of(ring)
    last = 3 * NS_ITERS + 1

    @pl.when(end)
    def _():
        for copy in fetch:
            copy.start()
        for copy in fetch:
            copy.wait()

    @pl.when(jnp.logical_not(end))
    def _():
        dsums[...] = jnp.zeros_like(dsums)

    @pl.loop(0, NS_ITERS * SMALL)
    def _(tau):
        if wide:
            sums.step(tau)
            for k in range(6):

                @pl.when(tau == k)
                def _():
                    small_all(sm, smr, sss, srs, sums, k)

        doc, turn = tau // NS_ITERS, lax.rem(tau, NS_ITERS)
        back = NS_ITERS - 1 - turn

        @pl.when(owner & (tau == 0))
        def _():
            la[...] = mul_nt(dtot[:LMK], mixed[...], PAIR)
            lk[...] = jnp.zeros_like(lk)
            lt[...] = flipped(saved[last], PAIR)

        @pl.when(owner & (tau < NS_ITERS))
        def _():
            a, b = backward_step([la[...]], [lk[...]], [lt[...]], [saved[3 * back]], [saved[3 * back + 1]], [saved[3 * back + 2]], PAIR)
            la[...] = a[0]
            lk[...] = b[0]

        @pl.when(owner & (tau == NS_ITERS - 1))
        def _():
            d_scores = backward_end(la[...], lk[...], saved[last], saved[0], PAIR) * 0.125
            d_query = mul(d_scores, km[pair].astype(F32), PAIR)
            d_key = mul(flipped(d_scores, PAIR), qm[pair].astype(F32), PAIR)
            arrived()
            total = part[pair]
            for k in ring.steps:
                total = total + landing[k - 1]
            held[pair, :LMK, :] = ((d_query + total) / counts[0, :, 0:1]).astype(BF16)
            held[pair, LMK:, :] = ((d_key + dtot[LMK:]) / counts[0, :, 0:1]).astype(BF16)
            ring.share(held, cs, cr, 1)

        @pl.when(end & (turn == 0))
        def _():
            for g in range(GROUPS):
                da[g] = mul_nt(smallf[0, doc, g], mixeds[doc, g], GROUP)
                dk[g] = jnp.zeros((LMK, GROUP), F32)
                kt[g] = flipped(keep[doc, g, last], GROUP)

        @pl.when(end)
        def _():
            rows = range(GROUPS)
            iterates = [[keep[doc, g, 3 * back + i] for g in rows] for i in range(3)]
            a, b = backward_step([da[g] for g in rows], [dk[g] for g in rows], [kt[g] for g in rows], *iterates, GROUP)
            for g in rows:
                da[g] = a[g]
                dk[g] = b[g]

        @pl.when(end & (turn == NS_ITERS - 1))
        def _():
            for g in range(GROUPS):
                d_scores = backward_end(da[g], dk[g], keep[doc, g, last], keep[doc, g, 0], GROUP) * 0.125
                d_query = mul(d_scores, marks[1, doc, g].astype(F32), GROUP)
                d_key = mul(flipped(d_scores, GROUP), marks[0, doc, g].astype(F32), GROUP)
                size = counts[1 + doc, :, 0:1]
                dsums[doc, g, :LMK, :] = ((d_query + smallb[doc, g]) / size).astype(BF16)
                dsums[doc, g, LMK:, :] = ((d_key + smallf[1, doc, g]) / size).astype(BF16)

    ring.shared(held, cs, cr, 1, PAIRS)
    dsum[...] = held[...]
    sent()

    @pl.when(owner)
    def _():
        ring.share_sent(held, cs, cr, 1)

    if wide:
        sums.finish()
        osm[...] = smr[5]
    else:
        osm[...] = sm[...]


def mark_sums(count, wide, part, dtot, saved, mixed, qm, km, counts, smallb, smallf, save_a, save_b, mixeds, marks, gd, gu, go, sm):
    shape = jax.ShapeDtypeStruct
    return pl.pallas_call(
        functools.partial(sums_kernel, count, wide),
        in_specs=in_vmem(9) + [ANY_SPEC] * 2 + in_vmem(2) + [ANY_SPEC] * 3 + in_vmem(1),
        out_specs=in_vmem(2) + [ANY_SPEC] * 3 + in_vmem(1),
        out_shape=[
            shape((PAIRS, 2 * LMK, PAIR), BF16),
            shape((SMALL, GROUPS, 2 * LMK, GROUP), BF16),
            shape(gd.shape, BF16),
            shape(gu.shape, BF16),
            shape(go.shape, BF16),
            shape(sm.shape, F32),
        ],
        scratch_shapes=[
            VMEM((count - 1, LMK, PAIR), F32),
            VMEM((PAIRS, 2 * LMK, PAIR), BF16),
            VMEM((SMALL, GROUPS, SAVES, LMK, GROUP), F32),
            VMEM((GROUPS, LMK, GROUP), F32),
            VMEM((GROUPS, LMK, GROUP), F32),
            VMEM((GROUPS, LMK, GROUP), F32),
            VMEM((LMK, PAIR), F32),
            VMEM((LMK, PAIR), F32),
            VMEM((LMK, PAIR), F32),
            VMEM((11,) + sm.shape, F32),
        ]
        + sums_scratch(9 if wide else 1, 384 if wide else 128)
        + [
            DMA((count - 1,)),
            DMA((count - 1,)),
            DMA((count - 1,)),
            DMA((PAIRS,)),
            DMA((2,)),
            DMA((5,)),
            DMA((5,)),
        ],
        compiler_params=remote_params(4),
        name="mark_sums",
    )(part, dtot, saved, mixed, qm, km, counts, smallb, smallf, save_a, save_b, mixeds, marks, gd, gu, go, sm)


LAST_WIDTH = 384


def last_kernel(gq, dj, w, tq, dx, *scratch):
    units = [(gq, tq, 0, i) for i in range(gq.shape[1] // (2 * LAST_WIDTH))]
    sums = Sums(units, LAST_WIDTH, *scratch)
    sums.load()
    barrier = pltpu.get_barrier_semaphore()
    for to in sums.others:
        pl.semaphore_signal(barrier, inc=1, device_id=to, device_id_type=MESH)
    pl.semaphore_wait(barrier, len(sums.others))
    taus = len(units) + Sums.STEPS - 1
    total = dj.shape[0]
    chunk = 128

    @pl.loop(0, taus)
    def _(tau):
        sums.step(tau)

        @pl.when(tau < total // chunk)
        def _():
            rows = pl.ds(pl.multiple_of(jnp.minimum(tau, total // chunk - 1) * chunk, chunk), chunk)
            dx[rows, :] = dot(dj[rows, :], w[...], NT)

    sums.finish()


def last_sums(gq, dj, w):
    n = gq.shape[1] // (2 * LAST_WIDTH)
    return pl.pallas_call(
        last_kernel,
        in_specs=[ANY_SPEC] + in_vmem(2),
        out_specs=[ANY_SPEC] + in_vmem(1),
        out_shape=[jax.ShapeDtypeStruct(gq.shape, BF16), jax.ShapeDtypeStruct((dj.shape[0], w.shape[0]), F32)],
        scratch_shapes=sums_scratch(n, LAST_WIDTH),
        compiler_params=remote_params(5),
        name="last_sums",
    )(gq, dj, w)


def over_all(*grads):
    out = []
    for g in grads:
        part = lax.psum_scatter(g.astype(F32).reshape(lax.axis_size(("seq", "row")), -1), ("seq", "row"), scatter_dimension=0, tiled=True)
        out.append(lax.all_gather(part.astype(BF16), ("seq", "row"), axis=0, tiled=True).reshape(g.shape))
    return out


def on_device(
    tokens,
    doc_lengths,
    w_qkv,
    w_out,
    conv_taps,
    norm1_gain,
    norm1_bias,
    w_up,
    w_down,
    norm2_gain,
    norm2_bias,
    cotangent,
):
    model_width = tokens.shape[2]
    head_count, tap_count = conv_taps.shape
    rim = (tap_count - 1) // 2
    count = lax.axis_size("seq")
    wide = count == 8 and lax.axis_size("row") == 4
    inputs = tokens[0]
    joined, slot_sums, small, edge, counts = project(doc_lengths, inputs, w_qkv)
    qm, km, halo, save_a, invs = all_marks(count, slot_sums, counts, edge, small)
    exps, part, wsm, stsm = mix(doc_lengths, joined, qm, small[0])
    carried, stat, saved, inv, mixed, cars, save_b, inv2, mixeds = carry(count, part, qm, km, small, wsm, stsm, invs)
    taps = jnp.pad(conv_taps, ((0, 0), (0, 256 - tap_count)))
    taps_back = jnp.pad(conv_taps[:, ::-1], ((0, 0), (0, 256 - tap_count)))
    kernel_b, mixture_b = attend(doc_lengths, joined, halo, taps, km, carried, small[1], cars)
    residual1 = inputs.astype(jnp.float32) + jnp.dot(
        mixture_b, w_out, preferred_element_type=jnp.float32
    )
    normed1, norm1_pull = jax.vjp(layer_norm, residual1, norm1_gain, norm1_bias)
    normed1_b = normed1.astype(jnp.bfloat16)
    upward = jnp.dot(normed1_b, w_up, preferred_element_type=jnp.float32)
    activated_wide, gelu_pull = jax.vjp(gelu, upward)
    activated = activated_wide.astype(jnp.bfloat16)
    residual2 = normed1 + jnp.dot(activated, w_down, preferred_element_type=jnp.float32)
    result, norm2_pull = jax.vjp(layer_norm, residual2, norm2_gain, norm2_bias)
    delta_residual2, delta_gain2, delta_bias2 = norm2_pull(cotangent[0].astype(jnp.float32))
    delta_down = delta_residual2.astype(jnp.bfloat16)
    grad_down = jnp.dot(activated.T, delta_down, preferred_element_type=jnp.float32)
    delta_active = jnp.dot(delta_down, w_down.T, preferred_element_type=jnp.float32)
    delta_up = gelu_pull(delta_active)[0].astype(jnp.bfloat16)
    grad_up = jnp.dot(normed1_b.T, delta_up, preferred_element_type=jnp.float32)
    delta_normed1 = delta_residual2 + jnp.dot(delta_up, w_up.T, preferred_element_type=jnp.float32)
    delta_residual1, delta_gain1, delta_bias1 = norm1_pull(delta_normed1)
    delta_output = delta_residual1.astype(jnp.bfloat16)
    grad_output = jnp.dot(mixture_b.T, delta_output, preferred_element_type=jnp.float32)
    delta_mixture = jnp.dot(delta_output, w_out.T, preferred_element_type=jnp.float32)
    delta_mix = delta_mixture.astype(BF16)
    dq, part_f, small_f = back_f(doc_lengths, joined, delta_mix, kernel_b, km, carried, small[1], cars)
    delta_edge = jnp.stack([delta_mix[:rim], delta_mix[-rim:]])
    scaled, along, dtot, scs, alongs, delta_halo = spread(count, part_f, stat, inv, mixed, small_f, stsm, invs, inv2, mixeds, delta_edge)
    factor = jnp.exp(part[:, LMK] - stat[:, 0]).reshape(1, model_width)
    factor = jnp.broadcast_to(factor, (8, model_width))
    dk, dv, part_b, small_b, dtaps = back_b(
        doc_lengths, joined, halo, exps, factor, scaled, along, scs, alongs, qm, small[0], taps_back, delta_mix, delta_halo
    )
    grad_taps = dtaps.reshape(head_count, 256)[:, BLK - 1 : BLK - 1 + tap_count]
    taps_row = jnp.pad(grad_taps.reshape(1, -1), ((0, 3), (0, model_width - grad_taps.size)))
    norm_terms = jnp.concatenate([jnp.stack([delta_gain1, delta_bias1, delta_gain2, delta_bias2]), taps_row], axis=0)
    grad_down, grad_up, grad_output = grad_down.astype(BF16), grad_up.astype(BF16), grad_output.astype(BF16)
    dsum, dsums, td, tu, to, tsm = mark_sums(
        count, wide, part_b, dtot, saved, mixed, qm, km, counts, small_b, small_f, save_a, save_b, mixeds, small, grad_down, grad_up, grad_output, norm_terms
    )
    if not wide:
        td, tu, to = over_all(grad_down, grad_up, grad_output)
        tsm = lax.psum(norm_terms, ("seq", "row"))
    delta_joined, grad_joined, total_up, total_down, total_output = join(doc_lengths, inputs, dq, dk, dv, dsum, dsums, tu, td, to)
    if wide:
        tq, from_joined = last_sums(grad_joined, delta_joined, w_qkv)
    else:
        (tq,) = over_all(grad_joined)
        from_joined = dot(delta_joined, w_qkv, NT)
    return (
        result.astype(BF16)[None],
        (delta_residual1 + from_joined)[None],
        tq.astype(F32),
        total_output,
        tsm[4, : grad_taps.size].reshape(grad_taps.shape),
        tsm[0],
        tsm[1],
        total_up,
        total_down,
        tsm[2],
        tsm[3],
    )


def solution(mesh):
    return jax.shard_map(
        on_device,
        mesh=mesh,
        in_specs=(
            P("row", "seq", None),
            P("row", None),
            P(),
            P(),
            P(),
            P(),
            P(),
            P(),
            P(),
            P(),
            P(),
            P("row", "seq", None),
        ),
        out_specs=(
            P("row", "seq", None),
            P("row", "seq", None),
            P(),
            P(),
            P(),
            P(),
            P(),
            P(),
            P(),
            P(),
            P(),
        ),
        check_vma=False,
    )
```

```python
import functools

import jax
import jax.numpy as jnp
from jax import lax
from jax.experimental import pallas as pl
from jax.experimental.pallas import tpu as pltpu
from jax.sharding import PartitionSpec as P

MESH = pl.DeviceIdType.MESH

LMK = 64
NS_ITERS = 6
DOCS = 4


HIGHEST = lax.Precision.HIGHEST
EPSILON = 1e-05
BIG_NEGATIVE = -1e30


def layer_norm(inputs, gain, bias):
    average = jnp.mean(inputs, axis=-1, keepdims=True)
    centered = inputs - average
    variance = jnp.mean(centered * centered, axis=-1, keepdims=True)
    return centered * lax.rsqrt(variance + EPSILON) * gain + bias


def gelu(inputs):
    return 0.5 * inputs * (1.0 + lax.erf(inputs * 0.7071067811865476))


F32, BF16 = jnp.float32, jnp.bfloat16
GROUP = 256
PAIR = 128
PAIRS = 6
SMALL = DOCS - 1
GROUPS = 3
WINDOW = 256
VMEM = pltpu.VMEM


def dot(a, b, dims=((1,), (0,)), precision=None):
    return lax.dot_general(a, b, (dims, ((), ())), preferred_element_type=F32, precision=precision)


NT, TN = ((1,), (1,)), ((0,), (0,))


def head_mask(width):
    rows = lax.broadcasted_iota(jnp.int32, (width, width), 0)
    lanes = lax.broadcasted_iota(jnp.int32, (width, width), 1)
    return (rows // LMK) == (lanes // LMK)


def blocks_of(side, width):
    tiled = jnp.concatenate([side] * (width // LMK), axis=0)
    return jnp.where(head_mask(width), tiled, jnp.zeros_like(tiled))


def side_of(full, width):
    full = jnp.where(head_mask(width), full, 0.0)
    return sum(full[i * LMK : (i + 1) * LMK] for i in range(width // LMK))


def flipped(side, width):
    return side_of(jnp.transpose(blocks_of(side, width)), width)


def head_ones(width):
    return jnp.where(head_mask(width), 1.0, 0.0).astype(F32)


def column_of(row, width):
    slots = lax.broadcasted_iota(jnp.int32, (LMK, width), 0)
    lanes = lax.broadcasted_iota(jnp.int32, (LMK, width), 1)
    picked = jnp.where(slots == lanes % LMK, jnp.broadcast_to(row, (LMK, width)), 0.0)
    return dot(picked, head_ones(width), precision=HIGHEST)


def row_of(side, width):
    return dot(jnp.ones((8, width), F32), blocks_of(side, width), NT, precision=HIGHEST)


def halves(x):
    high = x.astype(BF16)
    return high, (x - high.astype(F32)).astype(BF16)


def product3(a, b, dims, width):
    high, low = halves(a)
    b_high, b_low = halves(b)
    rows = a.shape[0]
    both = dot(jnp.concatenate([high, low], axis=0), blocks_of(b_high, width), dims)
    return both[:rows] + both[rows:] + dot(high, blocks_of(b_low, width), dims)


def mul(a, b, width):
    return product3(a, b, ((1,), (0,)), width)


def mul_nt(a, b, width):
    return product3(a, b, NT, width)


def each(f, *lists):
    return [f(*items) for items in zip(*lists)]


def side_eye(width):
    slots = lax.broadcasted_iota(jnp.int32, (LMK, width), 0)
    lanes = lax.broadcasted_iota(jnp.int32, (LMK, width), 1)
    return jnp.where(slots == lanes % LMK, 1.0, 0.0).astype(F32)


def head_total(side, width):
    columns = jnp.broadcast_to(jnp.sum(side, axis=0, keepdims=True), (8, width))
    return dot(columns, head_ones(width), precision=HIGHEST)[:1]


def head_max(scores, width):
    out = []
    for i in range(width // PAIR):
        part = scores[:, i * PAIR : (i + 1) * PAIR]
        left = lax.broadcasted_iota(jnp.int32, part.shape, 1) < LMK
        low = jnp.max(jnp.where(left, part, BIG_NEGATIVE), axis=1, keepdims=True)
        high = jnp.max(jnp.where(left, BIG_NEGATIVE, part), axis=1, keepdims=True)
        out.append(jnp.where(left, low, high))
    return out[0] if len(out) == 1 else jnp.concatenate(out, axis=1)


def inverse_forward(qm, km, save, width):
    ones = head_ones(width)

    def begin(q, k):
        scores = dot(q, blocks_of(k, width), NT) * 0.125
        exponent = jnp.exp(scores - head_max(scores, width))
        return exponent / dot(exponent, ones, precision=HIGHEST)

    kernel_a = each(begin, qm, km)
    approx = each(lambda a: flipped(a, width) / head_total(a * a, width), kernel_a)
    eye = side_eye(width)
    for j, a in enumerate(kernel_a):
        save(3 * NS_ITERS + 1, j, a)

    def sweep(i, approx):
        product = each(lambda a, x: mul(a, x, width), kernel_a, approx)
        square = each(lambda p: mul(p, p, width), product)
        cube = each(lambda s, p: mul(s, p, width), square, product)
        poly = each(lambda p, s, c: 3.25 * eye - 3.75 * p + 1.75 * s - 0.25 * c, product, square, cube)
        for j in range(len(approx)):
            save(3 * i, j, approx[j])
            save(3 * i + 1, j, product[j])
            save(3 * i + 2, j, poly[j])
        return tuple(each(lambda x, q: mul(x, q, width), approx, poly))

    approx = lax.fori_loop(0, NS_ITERS, sweep, tuple(approx))
    for j, x in enumerate(approx):
        save(3 * NS_ITERS, j, x)
    return list(approx)


def backward_step(d_approx, d_kernel, kernel_at, approx, product, poly, width):
    product_t = each(lambda p: flipped(p, width), product)
    d_poly = each(lambda x, d: mul(flipped(x, width), d, width), approx, d_approx)
    d_next = each(lambda d, q: mul_nt(d, q, width), d_approx, poly)
    right = each(lambda d, p: mul_nt(d, p, width), d_poly, product)
    left = each(lambda p, d: mul(p, d, width), product_t, d_poly)
    both = each(lambda r, x: r + x, right, left)
    third = each(lambda r, p: mul_nt(r, p, width), right, product)
    fourth = each(lambda p, b: mul(p, b, width), product_t, both)
    d_product = each(lambda d, b, t, f: -3.75 * d + 1.75 * b - 0.25 * (t + f), d_poly, both, third, fourth)
    d_kernel = each(lambda k, d, x: k + mul_nt(d, x, width), d_kernel, d_product, approx)
    d_approx = each(lambda n, a, d: n + mul(a, d, width), d_next, kernel_at, d_product)
    return d_approx, d_kernel


def backward_end(d_approx, d_kernel, kernel_a, first, width):
    scale = head_total(kernel_a * kernel_a, width)
    d_scale = -head_total(d_approx * first, width) / scale
    d_kernel = d_kernel + flipped(d_approx, width) / scale + 2.0 * kernel_a * d_scale
    inner = dot(d_kernel * kernel_a, head_ones(width), precision=HIGHEST)
    return kernel_a * (d_kernel - inner)


def stacked(side):
    return blocks_of(side, GROUP)


def doc_table(lens, total):
    shard_start = lax.axis_index("seq") * total
    lengths = [lens[0, i] for i in range(DOCS)]
    starts = [-shard_start]
    for i in range(DOCS - 1):
        starts.append(starts[i] + lengths[i])
    best, size, start = jnp.int32(0), lengths[0], starts[0]
    for i in range(1, DOCS):
        more = lengths[i] > size
        best, size, start = jnp.where(more, i, best), jnp.where(more, lengths[i], size), jnp.where(more, starts[i], start)
    sizes, begins = [size], [start]
    for i in range(DOCS - 1):
        later = best <= i
        sizes.append(jnp.where(later, lengths[i + 1], lengths[i]))
        begins.append(jnp.where(later, starts[i + 1], starts[i]))
    return sizes, begins


def doc_ranges(lens, total):
    sizes, begins = doc_table(lens, total)
    info = []
    for size, begin in zip(sizes, begins):
        info += [jnp.clip(begin, 0, total), jnp.clip(begin + size, 0, total)]
    return info + [begins[0], begins[0] + sizes[0]]


def slot_bounds(lens, total, shape, axis):
    sizes, begins = doc_table(lens, total)
    slot = lax.broadcasted_iota(jnp.int32, shape, axis)
    doc, within = slot // LMK, slot % LMK
    size, begin = jnp.full(shape, sizes[0]), jnp.full(shape, begins[0])
    for d in range(1, DOCS):
        size, begin = jnp.where(doc == d, sizes[d], size), jnp.where(doc == d, begins[d], begin)
    return begin + (within * size + LMK - 1) // LMK, begin + ((within + 1) * size + LMK - 1) // LMK


def project_kernel(lens, inputs, weight, joined, sums, small, edge, counts):
    total = inputs.shape[0]
    block = pl.program_id(0)
    out = dot(inputs[...], weight[...]).astype(BF16)
    joined[...] = out

    @pl.when(block < 2 * GROUPS)
    def _():
        low, high = slot_bounds(lens, total, (DOCS * LMK, 1), 0)
        rows = lax.broadcasted_iota(jnp.int32, (DOCS * LMK, total), 1)
        member = jnp.where((rows >= low) & (rows < high), 1.0, 0.0).astype(BF16)
        slot_sums = dot(member, out)
        size = (high - low).astype(F32)
        sums[...] = slot_sums[:LMK]
        small[0] = (slot_sums[LMK:] / size[LMK:]).astype(BF16).reshape(SMALL, LMK, GROUP)
        counts[...] = jnp.broadcast_to(size, (DOCS * LMK, PAIR)).reshape(DOCS, LMK, PAIR)

    @pl.when(block >= 2 * GROUPS)
    def _():
        edge[0] = out[:16]
        edge[1] = out[total - 16 :]


def project(lens, inputs, weight):
    total, depth = inputs.shape
    width = weight.shape[1]
    half = 2 * GROUPS - 1

    return pl.pallas_call(
        project_kernel,
        grid=(width // GROUP,),
        in_specs=[
            pl.BlockSpec(memory_space=pltpu.SMEM),
            pl.BlockSpec((total, depth), lambda j: (0, 0)),
            pl.BlockSpec((depth, GROUP), lambda j: (0, j)),
        ],
        out_specs=[
            pl.BlockSpec((total, GROUP), lambda j: (0, j)),
            pl.BlockSpec((LMK, GROUP), lambda j: (0, jnp.minimum(j, half))),
            pl.BlockSpec((1, SMALL, None, LMK, GROUP), lambda j: (jnp.minimum(j, half) // GROUPS, 0, lax.rem(jnp.minimum(j, half), GROUPS), 0, 0)),
            pl.BlockSpec((2, 16, GROUP), lambda j: (0, 0, jnp.maximum(j - 2 * GROUPS, 0))),
            pl.BlockSpec((DOCS, LMK, PAIR), lambda j: (0, 0, 0)),
        ],
        out_shape=[
            jax.ShapeDtypeStruct((total, width), BF16),
            jax.ShapeDtypeStruct((LMK, 2 * GROUPS * GROUP), F32),
            jax.ShapeDtypeStruct((2, SMALL, GROUPS, LMK, GROUP), BF16),
            jax.ShapeDtypeStruct((2, 16, GROUPS * GROUP), BF16),
            jax.ShapeDtypeStruct((DOCS, LMK, PAIR), F32),
        ],
        compiler_params=pltpu.CompilerParams(vmem_limit_bytes=62 * 2**20),
        name="project",
    )(lens, inputs, weight)


def joint(ref):
    return jnp.concatenate([ref[0], ref[1]], axis=1)


def write_pairs(ref, at, value):
    ref[0, at, :] = value[:, :PAIR]
    ref[1, at, :] = value[:, PAIR:]


LONG_SPEC = pl.BlockSpec((2, LMK, PAIR), lambda g: (g, 0, 0))
ROW_SPEC = pl.BlockSpec((2, 8, PAIR), lambda g: (g, 0, 0))
SMALL_SPEC = pl.BlockSpec((SMALL, None, LMK, GROUP), lambda g: (0, g, 0, 0))
SMALL_ROW_SPEC = pl.BlockSpec((SMALL, None, 8, GROUP), lambda g: (0, g, 0, 0))
TOP = slice(0, LMK)


def for_docs(info, total, body):
    def inside(doc, size, start):
        rows = lax.broadcasted_iota(jnp.int32, (size, 1), 0) + start
        return (rows >= info[2 * doc]) & (rows < info[2 * doc + 1])

    body(0, total, 0, inside(0, total, 0))
    for doc in range(1, DOCS):
        low, high = info[2 * doc], info[2 * doc + 1]
        start = jnp.minimum(low // 16 * 16, total - WINDOW)

        @pl.when((high > low) & (high - start <= WINDOW))
        def _():
            at = pl.multiple_of(start, 16)
            body(doc, WINDOW, at, inside(doc, WINDOW, at))

        @pl.when(high - start > WINDOW)
        def _():
            body(doc, total, 0, inside(doc, total, 0))


def mix_kernel(lens, keys, values, qm, qms, exps, part, parts, stats):
    info = doc_ranges(lens, exps.shape[0])
    parts[...] = jnp.zeros_like(parts)
    stats[...] = jnp.zeros_like(stats)
    part[...] = jnp.zeros_like(part)

    def body(doc, size, start, inside):
        rows = pl.ds(start, size)
        marks = stacked(joint(qm) if doc == 0 else qms[doc - 1])
        scores = jnp.where(inside, dot(keys[rows, :], marks, NT) * 0.125, BIG_NEGATIVE)
        top = jnp.max(scores, axis=0, keepdims=True)
        wide = jnp.exp(scores - top)
        narrow = wide.astype(BF16)
        weighted = side_of(dot(narrow, values[rows, :], TN), GROUP)
        total = jnp.sum(wide, axis=0, keepdims=True)
        if doc == 0:
            exps[...] = narrow
            write_pairs(part, TOP, weighted)
            write_pairs(part, slice(LMK, LMK + 1), top)
            write_pairs(part, slice(LMK + 1, LMK + 2), total)
        else:
            exps[rows, :] = jnp.where(inside, narrow, exps[rows, :])
            parts[doc - 1] = weighted
            stats[doc - 1, 0:1, :] = top
            stats[doc - 1, 1:2, :] = total

    for_docs(info, exps.shape[0], body)


def mix(lens, joined, qm, qms):
    total, width = joined.shape[0], joined.shape[1] // 3
    groups = width // GROUP
    return pl.pallas_call(
        mix_kernel,
        grid=(groups,),
        in_specs=[
            pl.BlockSpec(memory_space=pltpu.SMEM),
            pl.BlockSpec((total, GROUP), lambda g: (0, groups + g)),
            pl.BlockSpec((total, GROUP), lambda g: (0, 2 * groups + g)),
            LONG_SPEC,
            SMALL_SPEC,
        ],
        out_specs=[
            pl.BlockSpec((total, GROUP), lambda g: (0, g)),
            pl.BlockSpec((2, LMK + 8, PAIR), lambda g: (g, 0, 0)),
            SMALL_SPEC,
            SMALL_ROW_SPEC,
        ],
        out_shape=[
            jax.ShapeDtypeStruct((total, width), BF16),
            jax.ShapeDtypeStruct((PAIRS, LMK + 8, PAIR), F32),
            jax.ShapeDtypeStruct((SMALL, groups, LMK, GROUP), F32),
            jax.ShapeDtypeStruct((SMALL, groups, 8, GROUP), F32),
        ],
        compiler_params=pltpu.CompilerParams(vmem_limit_bytes=62 * 2**20),
        name="mix",
    )(lens, joined, joined, qm, qms)


TOEP = 160
BLK = 128


def band(taps, reverse_unused=None):
    wide = jnp.broadcast_to(taps, (BLK, 256))
    return pltpu.roll(wide, 0, 1, stride=1, stride_axis=0)[:, :TOEP].astype(BF16)


def bands(taps, group):
    heads = GROUP // LMK
    return jnp.concatenate([band(taps[pl.ds(group * heads + i, 1), :]) for i in range(heads)], axis=0)


def head_rows(stack):
    lanes = lax.broadcasted_iota(jnp.int32, (BLK, GROUP), 1) // LMK
    out = stack[:BLK]
    for i in range(1, GROUP // LMK):
        out = jnp.where(lanes == i, stack[i * BLK : (i + 1) * BLK], out)
    return out


def padded_rows(before, here, after, pad):
    total = here.shape[0]
    pad[0:16, :] = before
    pad[16 : total + 16, :] = here[...]
    pad[total + 16 : total + 32, :] = after


def doc_windows(info, total, body):
    def member(doc, start):
        rows = lax.broadcasted_iota(jnp.int32, (TOEP, 1), 0) + start - 16
        low, high = (info[8], info[9]) if doc == 0 else (info[2 * doc], info[2 * doc + 1])
        return (rows >= low) & (rows < high)

    for doc in range(DOCS):
        low, high = info[2 * doc], info[2 * doc + 1]

        @pl.loop(low // BLK, jnp.where(high > low, (high + BLK - 1) // BLK, low // BLK))
        def _(b):
            start = pl.multiple_of(b * BLK, BLK)
            body(doc, start, member(doc, start))


def attend_kernel(lens, queries, values, halo, taps, km, car, kms, cars, kern, mixture, pad, att):
    total = queries.shape[0]
    info = doc_ranges(lens, total)
    group = pl.program_id(0)
    ones = head_ones(GROUP).astype(BF16)

    def body(doc, size, start, inside):
        rows = pl.ds(start, size)
        marks = stacked(joint(km) if doc == 0 else kms[doc - 1])
        scores = dot(queries[rows, :], marks, NT) * 0.125
        exponent = jnp.exp(scores - head_max(scores, GROUP))
        kernel = (exponent / dot(exponent.astype(BF16), ones)).astype(BF16)
        carried = stacked(joint(car) if doc == 0 else cars[doc - 1])
        attended = dot(kernel, carried)
        if doc == 0:
            kern[...] = kernel
            att[...] = attended
        else:
            kern[rows, :] = jnp.where(inside, kernel, kern[rows, :])
            att[rows, :] = jnp.where(inside, attended, att[rows, :])

    for_docs(info, total, body)
    padded_rows(halo[0], values, halo[1], pad)
    tape = bands(taps, group)

    def conv(doc, start, inside):
        window = jnp.where(inside, pad[pl.ds(start, TOEP), :], jnp.zeros((), BF16))
        out = head_rows(dot(tape, window))
        rows = pl.ds(start, BLK)
        here = inside[16 : 16 + BLK]
        new = (att[rows, :] + out).astype(BF16)
        if doc == 0:
            mixture[rows, :] = new
        else:
            mixture[rows, :] = jnp.where(here, new, mixture[rows, :])

    doc_windows(info, total, conv)


def attend(lens, joined, halo, taps, km, car, kms, cars):
    total, width = joined.shape[0], joined.shape[1] // 3
    groups = width // GROUP
    col = pl.BlockSpec((total, GROUP), lambda g: (0, g))
    mark, marks = LONG_SPEC, SMALL_SPEC
    return pl.pallas_call(
        attend_kernel,
        grid=(groups,),
        in_specs=[
            pl.BlockSpec(memory_space=pltpu.SMEM),
            col,
            pl.BlockSpec((total, GROUP), lambda g: (0, 2 * groups + g)),
            pl.BlockSpec((2, 16, GROUP), lambda g: (0, 0, g)),
            pl.BlockSpec(taps.shape, lambda g: (0, 0)),
            mark,
            mark,
            marks,
            marks,
        ],
        out_specs=[col, col],
        out_shape=[jax.ShapeDtypeStruct((total, width), BF16)] * 2,
        scratch_shapes=[VMEM((total + 32, GROUP), BF16), VMEM((total, GROUP), F32)],
        compiler_params=pltpu.CompilerParams(vmem_limit_bytes=62 * 2**20),
        name="attend",
    )(lens, joined, joined, halo, taps, km, car, kms, cars)


def back_f_kernel(lens, queries, dmix, kern, km, car, kms, cars, dq, part, parts):
    info = doc_ranges(lens, dq.shape[0])
    parts[...] = jnp.zeros_like(parts)
    ones = head_ones(GROUP).astype(BF16)

    def body(doc, size, start, inside):
        rows = pl.ds(start, size)
        zero = jnp.zeros((), BF16)
        marks = stacked(joint(km) if doc == 0 else kms[doc - 1])
        carried = stacked(joint(car) if doc == 0 else cars[doc - 1])
        datt = dmix[rows, :]
        kernel = jnp.where(inside, kern[rows, :], zero)
        d_carried = side_of(dot(kernel, datt, TN), GROUP)
        d_kernel = dot(datt, carried, NT)
        wide = kernel.astype(F32)
        weighed = wide * d_kernel
        high = weighed.astype(BF16)
        low = (weighed - high.astype(F32)).astype(BF16)
        inner = dot(high, ones) + dot(low, ones)
        d_scores = (weighed - wide * inner).astype(BF16)
        d_queries = dot(d_scores, marks) * 0.125
        d_marks = side_of(dot(d_scores, queries[rows, :], TN), GROUP) * 0.125
        if doc == 0:
            dq[...] = d_queries.astype(BF16)
            write_pairs(part, TOP, d_carried)
            write_pairs(part, slice(LMK, 2 * LMK), d_marks)
        else:
            dq[rows, :] = jnp.where(inside, d_queries.astype(BF16), dq[rows, :])
            parts[0, doc - 1] = d_carried
            parts[1, doc - 1] = d_marks

    for_docs(info, dq.shape[0], body)


def back_f(lens, joined, dmix, kern, km, car, kms, cars):
    total, width = dmix.shape
    groups = width // GROUP
    col = pl.BlockSpec((total, GROUP), lambda g: (0, g))
    mark, marks = LONG_SPEC, SMALL_SPEC
    return pl.pallas_call(
        back_f_kernel,
        grid=(groups,),
        in_specs=[pl.BlockSpec(memory_space=pltpu.SMEM), col, col, col, mark, mark, marks, marks],
        out_specs=[
            col,
            pl.BlockSpec((2, 2 * LMK, PAIR), lambda g: (g, 0, 0)),
            pl.BlockSpec((2, SMALL, None, LMK, GROUP), lambda g: (0, 0, g, 0, 0)),
        ],
        out_shape=[
            jax.ShapeDtypeStruct((total, width), BF16),
            jax.ShapeDtypeStruct((PAIRS, 2 * LMK, PAIR), F32),
            jax.ShapeDtypeStruct((2, SMALL, groups, LMK, GROUP), F32),
        ],
        compiler_params=pltpu.CompilerParams(vmem_limit_bytes=62 * 2**20),
        name="back_f",
    )(lens, joined, dmix, kern, km, car, kms, cars)


def back_b_kernel(lens, keys, values, halo, exps, factor, sc, along, scs, alongs, qm, qms, taps, dmix, dhalo, dk, dv, part, parts, dtaps, pad, dpad, acc, dval):
    total = keys.shape[0]
    info = doc_ranges(lens, total)
    group = pl.program_id(0)
    parts[...] = jnp.zeros_like(parts)

    def body(doc, size, start, inside):
        rows = pl.ds(start, size)
        scaled = stacked(joint(sc) if doc == 0 else scs[doc - 1])
        marks = stacked(joint(qm) if doc == 0 else qms[doc - 1])
        wide = jnp.where(inside, exps[rows, :].astype(F32), 0.0)
        if doc == 0:
            wide = wide * factor[0:1, :]
        shift = joint(along)[0:1, :] if doc == 0 else alongs[doc - 1, 0:1, :]
        d_values = dot(wide.astype(BF16), scaled)
        reach = dot(values[rows, :], scaled, NT)
        d_scores = (wide * (reach - shift)).astype(BF16)
        d_keys = dot(d_scores, marks) * 0.125
        d_marks = side_of(dot(d_scores, keys[rows, :], TN), GROUP) * 0.125
        if doc == 0:
            dk[...] = d_keys.astype(BF16)
            dval[...] = d_values
            write_pairs(part, TOP, d_marks)
        else:
            dk[rows, :] = jnp.where(inside, d_keys.astype(BF16), dk[rows, :])
            dval[rows, :] = jnp.where(inside, d_values, dval[rows, :])
            parts[doc - 1] = d_marks

    for_docs(info, total, body)
    padded_rows(halo[0], values, halo[1], pad)
    padded_rows(dhalo[0], dmix, dhalo[1], dpad)
    tape = bands(taps, group)
    acc[...] = jnp.zeros_like(acc)

    def conv(doc, start, inside):
        zero = jnp.zeros((), BF16)
        rows = pl.ds(start, BLK)
        here = inside[16 : 16 + BLK]
        out = head_rows(dot(tape, jnp.where(inside, dpad[pl.ds(start, TOEP), :], zero)))
        dval[rows, :] = dval[rows, :] + jnp.where(here, out, 0.0)
        window = jnp.where(inside, pad[pl.ds(start, TOEP), :], zero)
        mine = jnp.where(here, dmix[rows, :], zero)
        lanes = lax.broadcasted_iota(jnp.int32, (BLK, GROUP), 1) // LMK
        spread = jnp.concatenate([jnp.where(lanes == i, mine, zero) for i in range(GROUP // LMK)], axis=0)
        acc[:, :TOEP] = acc[:, :TOEP] + dot(spread, window, NT)

    doc_windows(info, total, conv)
    dv[...] = dval[...].astype(BF16)
    rows = lax.broadcasted_iota(jnp.int32, (BLK, BLK), 0)
    lanes = lax.broadcasted_iota(jnp.int32, (BLK, BLK), 1)
    reverse = jnp.where(rows + lanes == BLK - 1, 1.0, 0.0).astype(F32)
    for i in range(GROUP // LMK):
        square = dot(reverse, acc[i * BLK : (i + 1) * BLK, :], precision=HIGHEST)
        turned = pltpu.roll(square, 0, 1, stride=1, stride_axis=0)
        dtaps[0, i : i + 1, :] = jnp.sum(turned, axis=0, keepdims=True)


def back_b(lens, joined, halo, exps, factor, sc, along, scs, alongs, qm, qms, taps, dmix, dhalo):
    total, width = dmix.shape
    groups = width // GROUP
    heads = GROUP // LMK
    col = pl.BlockSpec((total, GROUP), lambda g: (0, g))
    mark, marks = LONG_SPEC, SMALL_SPEC
    row = pl.BlockSpec((8, GROUP), lambda g: (0, g))
    edge = pl.BlockSpec((2, 16, GROUP), lambda g: (0, 0, g))
    return pl.pallas_call(
        back_b_kernel,
        grid=(groups,),
        in_specs=[
            pl.BlockSpec(memory_space=pltpu.SMEM),
            pl.BlockSpec((total, GROUP), lambda g: (0, groups + g)),
            pl.BlockSpec((total, GROUP), lambda g: (0, 2 * groups + g)),
            edge,
            col,
            row,
            mark,
            ROW_SPEC,
            marks,
            SMALL_ROW_SPEC,
            mark,
            marks,
            pl.BlockSpec(taps.shape, lambda g: (0, 0)),
            col,
            edge,
        ],
        out_specs=[col, col, mark, marks, pl.BlockSpec((1, heads, 256), lambda g: (g, 0, 0))],
        out_shape=[
            jax.ShapeDtypeStruct((total, width), BF16),
            jax.ShapeDtypeStruct((total, width), BF16),
            jax.ShapeDtypeStruct((PAIRS, LMK, PAIR), F32),
            jax.ShapeDtypeStruct((SMALL, groups, LMK, GROUP), F32),
            jax.ShapeDtypeStruct((groups, heads, 256), F32),
        ],
        scratch_shapes=[VMEM((total + 32, GROUP), BF16), VMEM((total + 32, GROUP), BF16), VMEM((heads * BLK, 256), F32), VMEM((total, GROUP), F32)],
        compiler_params=pltpu.CompilerParams(vmem_limit_bytes=62 * 2**20),
        name="back_b",
    )(lens, joined, joined, halo, exps, factor, sc, along, scs, alongs, qm, qms, taps, dmix, dhalo)


class Ring:
    def __init__(self, count):
        self.count = count
        self.me = lax.axis_index("seq")
        self.row = lax.axis_index("row")
        self.steps = range(1, count)

    def ahead(self, k):
        return lax.rem(self.me + k, self.count)

    def enter(self, others=()):
        barrier = pltpu.get_barrier_semaphore()
        for to in [(self.ahead(k), self.row) for k in self.steps] + list(others):
            pl.semaphore_signal(barrier, inc=1, device_id=to, device_id_type=MESH)
        pl.semaphore_wait(barrier, self.count - 1 + len(others))

    def copy(self, src, dst, send, recv, to):
        return pltpu.make_async_remote_copy(src_ref=src, dst_ref=dst, send_sem=send, recv_sem=recv, device_id=(to, self.row), device_id_type=MESH)

    def scatter(self, pieces, landing, send, recv, first, owners):
        for k in self.steps:
            to = self.ahead(k)

            @pl.when((to >= first) & (to < first + owners))
            def _():
                self.copy(pieces(to - first), landing.at[k - 1], send.at[k - 1], recv.at[k - 1], to).start()

        def arrived():
            for k in self.steps:
                self.copy(pieces(0), landing.at[k - 1], send.at[k - 1], recv.at[k - 1], self.ahead(k)).wait_recv()

        def sent():
            for k in self.steps:
                to = self.ahead(k)

                @pl.when((to >= first) & (to < first + owners))
                def _():
                    self.copy(pieces(to - first), landing.at[k - 1], send.at[k - 1], recv.at[k - 1], to).wait_send()

        return arrived, sent

    def share(self, held, send, recv, first):
        piece = self.me - first
        for k in self.steps:
            self.copy(held.at[piece], held.at[piece], send.at[k - 1], recv.at[piece], self.ahead(k)).start()

    def share_sent(self, held, send, recv, first):
        piece = self.me - first
        for k in self.steps:
            self.copy(held.at[piece], held.at[piece], send.at[k - 1], recv.at[piece], self.ahead(k)).wait_send()

    def shared(self, held, send, recv, first, owners):
        for p in range(owners):

            @pl.when(self.me != first + p)
            def _():
                self.copy(held.at[p], held.at[p], send.at[0], recv.at[p], self.ahead(1)).wait_recv()


    def edges_start(self, here, landing, send, recv):
        @pl.when(self.me > 0)
        def _():
            self.copy(here.at[0], landing.at[1], send.at[0], recv.at[1], self.me - 1).start()

        @pl.when(self.me < self.count - 1)
        def _():
            self.copy(here.at[1], landing.at[0], send.at[1], recv.at[0], self.me + 1).start()

    def edges_wait(self, here, landing, send, recv, out):
        out[...] = jnp.zeros_like(out)

        @pl.when(self.me > 0)
        def _():
            done = self.copy(here.at[0], landing.at[0], send.at[0], recv.at[0], self.me - 1)
            done.wait_recv()
            done.wait_send()
            out[0] = landing[0]

        @pl.when(self.me < self.count - 1)
        def _():
            done = self.copy(here.at[1], landing.at[1], send.at[1], recv.at[1], self.me + 1)
            done.wait_recv()
            done.wait_send()
            out[1] = landing[1]


OWNERS = 8
DMA = pltpu.SemaphoreType.DMA
SAVES = 3 * NS_ITERS + 2
CASES = SMALL * GROUPS
EARLY = 2


def ends(ring):
    return (ring.me == 0) | (ring.me == ring.count - 1)


def owner_of_pair(ring):
    return (ring.me >= 1) & (ring.me <= PAIRS)


def pair_of(ring):
    return jnp.clip(ring.me - 1, 0, PAIRS - 1)


def remote_params(cid):
    return pltpu.CompilerParams(collective_id=cid, has_side_effects=True, vmem_limit_bytes=62 * 2**20)


def in_vmem(n):
    return [pl.BlockSpec(memory_space=VMEM)] * n


ANY_SPEC = pl.BlockSpec(memory_space=pl.ANY)


def small_forward(doc, at, qms, kms, held, invs):
    def save(i, j, value):
        held[at, j, i] = value

    inverse = inverse_forward([qms[doc, g] for g in range(GROUPS)], [kms[doc, g] for g in range(GROUPS)], save, GROUP)
    for g in range(GROUPS):
        invs[at, g] = inverse[g]


def marks_kernel(count, part, counts, edge, small, qm, km, halo, saved, invs, landing, held, hland, sheld, ss, rs, gs, gr, es, er, hs):
    ring = Ring(count)
    ring.enter()
    ring.edges_start(edge, hland, es, er)
    each_ = LMK // OWNERS
    arrived, sent = ring.scatter(lambda o: part.at[pl.ds(pl.multiple_of(o * each_, each_), each_), :], landing, ss, rs, 0, OWNERS)
    keep = [pltpu.make_async_copy(sheld.at[d], saved.at[d], hs.at[d]) for d in range(EARLY)]

    @pl.when(ring.me < OWNERS)
    def _():
        arrived()
        at = pl.ds(pl.multiple_of(ring.me * each_, each_), each_)
        total = part[at, :]
        for k in ring.steps:
            total = total + landing[k - 1]
        total = total / counts[0, at, 0:1]
        half = total.shape[1] // 2
        held[ring.me, 0:each_, :] = total[:, :half].astype(BF16)
        held[ring.me, each_ : 2 * each_, :] = total[:, half:].astype(BF16)
        ring.share(held, gs, gr, 0)

    @pl.when(ends(ring))
    def _():
        @pl.loop(0, EARLY)
        def _(d):
            small_forward(d, d, small.at[0], small.at[1], sheld, invs)

        for copy in keep:
            copy.start()

    ring.shared(held, gs, gr, 0, OWNERS)
    wide = [held[o].astype(F32) for o in range(OWNERS)]
    query = jnp.concatenate([w[:each_] for w in wide], axis=0).astype(BF16)
    key = jnp.concatenate([w[each_:] for w in wide], axis=0).astype(BF16)
    for p in range(PAIRS):
        qm[p] = query[:, p * PAIR : (p + 1) * PAIR]
        km[p] = key[:, p * PAIR : (p + 1) * PAIR]
    ring.edges_wait(edge, hland, es, er, halo)
    sent()

    @pl.when(ring.me < OWNERS)
    def _():
        ring.share_sent(held, gs, gr, 0)

    @pl.when(ends(ring))
    def _():
        for copy in keep:
            copy.wait()


def all_marks(count, part, counts, edge, small):
    width = part.shape[1]
    each_ = LMK // OWNERS
    return pl.pallas_call(
        functools.partial(marks_kernel, count),
        in_specs=in_vmem(4),
        out_specs=in_vmem(3) + [ANY_SPEC] + in_vmem(1),
        out_shape=[jax.ShapeDtypeStruct((PAIRS, LMK, PAIR), BF16)] * 2
        + [
            jax.ShapeDtypeStruct(edge.shape, BF16),
            jax.ShapeDtypeStruct((EARLY, GROUPS, SAVES, LMK, GROUP), F32),
            jax.ShapeDtypeStruct((EARLY, GROUPS, LMK, GROUP), F32),
        ],
        scratch_shapes=[
            VMEM((count - 1, each_, width), F32),
            VMEM((OWNERS, 2 * each_, width // 2), BF16),
            VMEM(edge.shape, BF16),
            VMEM((EARLY, GROUPS, SAVES, LMK, GROUP), F32),
            DMA((count - 1,)),
            DMA((count - 1,)),
            DMA((count - 1,)),
            DMA((OWNERS,)),
            DMA((2,)),
            DMA((2,)),
            DMA((EARLY,)),
        ],
        compiler_params=remote_params(1),
        name="all_marks",
    )(part, counts, edge, small)


def carry_kernel(count, part, qm, km, small, wsm, stsm, invs, car, stat, saved, inv, mixed, cars, saveds, inv2, mixeds, landing, cheld, sheld, sk, ss, rs, cs, cr, ts, tr, hs):
    ring = Ring(count)
    ring.enter()
    arrived, sent = ring.scatter(lambda p: part.at[p], landing, ss, rs, 1, PAIRS)
    keep = pltpu.make_async_copy(sk, saveds, hs.at[0])

    @pl.when(owner_of_pair(ring))
    def _():
        pair = pair_of(ring)

        def save(i, j, value):
            saved[i] = value

        inverse = inverse_forward([qm[pair]], [km[pair]], save, PAIR)[0]
        inv[...] = inverse
        arrived()
        pieces = [part[pair]] + [landing[k - 1] for k in ring.steps]
        top = pieces[0][LMK : LMK + 1]
        for piece in pieces[1:]:
            top = jnp.maximum(top, piece[LMK : LMK + 1])
        weighted = jnp.zeros((LMK, PAIR), F32)
        total = jnp.zeros((1, PAIR), F32)
        for piece in pieces:
            share = jnp.exp(piece[LMK : LMK + 1] - top)
            weighted = weighted + piece[:LMK] * column_of(share, PAIR)
            total = total + piece[LMK + 1 : LMK + 2] * share
        mean = weighted / column_of(total, PAIR)
        mixed[...] = mean
        cheld[pair] = mul(inverse, mean, PAIR).astype(BF16)
        sheld[pair] = jnp.concatenate([top, total, jnp.zeros((6, PAIR), F32)], axis=0)
        ring.share(cheld, cs, cr, 1)
        ring.share(sheld, ts, tr, 1)

    @pl.when(ends(ring))
    def _():
        @pl.loop(0, SMALL - EARLY)
        def _(d):
            small_forward(d + EARLY, d, small.at[0], small.at[1], sk, inv2)

        keep.start()

        def finish(doc, inverse):
            for g in range(GROUPS):
                total = jnp.maximum(stsm[doc, g, 1:2, :], 1e-30)
                mean = wsm[doc, g] / column_of(total, GROUP)
                mixeds[doc, g] = mean
                cars[doc, g] = mul(inverse[g], mean, GROUP).astype(BF16)

        for d in range(SMALL):
            finish(d, [invs[d, g] if d < EARLY else inv2[d - EARLY, g] for g in range(GROUPS)])

    ring.shared(cheld, cs, cr, 1, PAIRS)
    ring.shared(sheld, ts, tr, 1, PAIRS)
    car[...] = cheld[...]
    stat[...] = sheld[...]
    sent()

    @pl.when(owner_of_pair(ring))
    def _():
        ring.share_sent(cheld, cs, cr, 1)
        ring.share_sent(sheld, ts, tr, 1)

    @pl.when(ends(ring))
    def _():
        keep.wait()


def carry(count, part, qm, km, small, wsm, stsm, invs):
    late = SMALL - EARLY
    return pl.pallas_call(
        functools.partial(carry_kernel, count),
        in_specs=in_vmem(7),
        out_specs=in_vmem(6) + [ANY_SPEC] + in_vmem(2),
        out_shape=[
            jax.ShapeDtypeStruct((PAIRS, LMK, PAIR), BF16),
            jax.ShapeDtypeStruct((PAIRS, 8, PAIR), F32),
            jax.ShapeDtypeStruct((SAVES, LMK, PAIR), F32),
            jax.ShapeDtypeStruct((LMK, PAIR), F32),
            jax.ShapeDtypeStruct((LMK, PAIR), F32),
            jax.ShapeDtypeStruct((SMALL, GROUPS, LMK, GROUP), BF16),
            jax.ShapeDtypeStruct((late, GROUPS, SAVES, LMK, GROUP), F32),
            jax.ShapeDtypeStruct((late, GROUPS, LMK, GROUP), F32),
            jax.ShapeDtypeStruct((SMALL, GROUPS, LMK, GROUP), F32),
        ],
        scratch_shapes=[
            VMEM((count - 1, LMK + 8, PAIR), F32),
            VMEM((PAIRS, LMK, PAIR), BF16),
            VMEM((PAIRS, 8, PAIR), F32),
            VMEM((late, GROUPS, SAVES, LMK, GROUP), F32),
            DMA((count - 1,)),
            DMA((count - 1,)),
            DMA((count - 1,)),
            DMA((PAIRS,)),
            DMA((count - 1,)),
            DMA((PAIRS,)),
            DMA((1,)),
        ],
        compiler_params=remote_params(2),
        name="carry",
    )(part, qm, km, small, wsm, stsm, invs)


def spread_grad(d_carried, inverse, mixed, total, width):
    d_mixed = mul(flipped(inverse, width), d_carried, width)
    scaled = (d_mixed / column_of(total, width)).astype(BF16)
    along = row_of(scaled.astype(F32) * mixed, width)
    return scaled, along


def spread_kernel(count, part, stat, inv, mixed, smallf, stsm, invs, inv2, mixeds, edge, sc, along, dtot, scs, alongs, halo, landing, sheld, aheld, hland, ss, rs, cs, cr, ts, tr, es, er):
    ring = Ring(count)
    ring.enter()
    arrived, sent = ring.scatter(lambda p: part.at[p], landing, ss, rs, 1, PAIRS)
    ring.edges_start(edge, hland, es, er)

    @pl.when(owner_of_pair(ring))
    def _():
        pair = pair_of(ring)
        arrived()
        total = part[pair]
        for k in ring.steps:
            total = total + landing[k - 1]
        dtot[...] = total
        scaled, reach = spread_grad(total[:LMK], inv[...], mixed[...], stat[pair, 1:2, :], PAIR)
        sheld[pair] = scaled
        aheld[pair] = reach
        ring.share(sheld, cs, cr, 1)
        ring.share(aheld, ts, tr, 1)

    @pl.when(ends(ring))
    def _():
        for d in range(SMALL):
            for g in range(GROUPS):
                total = jnp.maximum(stsm[d, g, 1:2, :], 1e-30)
                inverse = invs[d, g] if d < EARLY else inv2[d - EARLY, g]
                scaled, reach = spread_grad(smallf[0, d, g], inverse, mixeds[d, g], total, GROUP)
                scs[d, g] = scaled
                alongs[d, g] = reach

    ring.shared(sheld, cs, cr, 1, PAIRS)
    ring.shared(aheld, ts, tr, 1, PAIRS)
    sc[...] = sheld[...]
    along[...] = aheld[...]
    ring.edges_wait(edge, hland, es, er, halo)
    sent()

    @pl.when(owner_of_pair(ring))
    def _():
        ring.share_sent(sheld, cs, cr, 1)
        ring.share_sent(aheld, ts, tr, 1)


def spread(count, part, stat, inv, mixed, smallf, stsm, invs, inv2, mixeds, edge):
    return pl.pallas_call(
        functools.partial(spread_kernel, count),
        in_specs=in_vmem(10),
        out_specs=in_vmem(6),
        out_shape=[
            jax.ShapeDtypeStruct((PAIRS, LMK, PAIR), BF16),
            jax.ShapeDtypeStruct((PAIRS, 8, PAIR), F32),
            jax.ShapeDtypeStruct((2 * LMK, PAIR), F32),
            jax.ShapeDtypeStruct((SMALL, GROUPS, LMK, GROUP), BF16),
            jax.ShapeDtypeStruct((SMALL, GROUPS, 8, GROUP), F32),
            jax.ShapeDtypeStruct(edge.shape, BF16),
        ],
        scratch_shapes=[
            VMEM((count - 1, 2 * LMK, PAIR), F32),
            VMEM((PAIRS, LMK, PAIR), BF16),
            VMEM((PAIRS, 8, PAIR), F32),
            VMEM(edge.shape, BF16),
            DMA((count - 1,)),
            DMA((count - 1,)),
            DMA((count - 1,)),
            DMA((PAIRS,)),
            DMA((count - 1,)),
            DMA((PAIRS,)),
            DMA((2,)),
            DMA((2,)),
        ],
        compiler_params=remote_params(3),
        name="spread",
    )(part, stat, inv, mixed, smallf, stsm, invs, inv2, mixeds, edge)


UNIT = 256
ACROSS = UNIT // 2
TURNS = (0, 1, 3, 5, 7, 9, 11, 13, 14)


class Sums:
    STEPS = 9

    def __init__(self, count, own, out, r0, r1, r2, r3, osem, ss, rs):
        self.count = count
        self.own, self.out, self.r0, self.r1, self.r2, self.r3 = own, out, r0, r1, r2, r3
        self.osem, self.ss, self.rs = osem, ss, rs
        s_ax, r_ax = lax.axis_index("seq"), lax.axis_index("row")
        z, x, y, c = s_ax // 2, lax.rem(s_ax, 2), r_ax // 2, lax.rem(r_ax, 2)
        x1, y1 = x + (1 - c) * (1 - 2 * x), y + c * (1 - 2 * y)
        x2, y2 = x + c * (1 - 2 * x), y + (1 - c) * (1 - 2 * y)
        self.z = z
        self.core = (s_ax, y * 2 + (1 - c))
        self.first = (z * 2 + x1, y1 * 2 + c)
        self.second = (z * 2 + x2, y2 * 2 + c)
        self.line = [(lax.rem(z + k, 4) * 2 + x, r_ax) for k in (1, 2, 3)]
        self.others = [self.core, self.first, self.second] + self.line
        self.b1 = x * (1 - c) + y * c
        self.b2 = y * (1 - c) + x * c
        self.mine, self.theirs = c, 1 - c
        self.fly = (self.core, self.first, self.second) + tuple(self.line) + tuple(self.line) + (self.second, self.first, self.core)

    def rows(self, start, size):
        return pl.ds(pl.multiple_of(start, 16), size)

    def copies(self, u):
        out, line = self.out, [lax.rem(self.z + k, 4) for k in (1, 2, 3)]
        base1, base2 = self.b1 * 384, self.b1 * 384 + self.b2 * 192
        last = self.r2.at[u, self.rows(self.z * 48, 48), :]
        place = out.at[u, self.mine, self.rows(base2 + self.z * 48, 48), :]
        pairs = [
            (self.own.at[u, self.theirs], self.r0.at[u]),
            (self.r0.at[u, self.rows((1 - self.b1) * 384, 384), :], self.r1.at[u]),
            (self.r1.at[u, self.rows((1 - self.b2) * 192, 192), :], self.r2.at[u]),
        ]
        pairs += [(self.r2.at[u, self.rows(line[k] * 48, 48), :], self.r3.at[u, k]) for k in range(3)]
        pairs += [(last, place)] * 3
        for region in (out.at[u, self.mine, self.rows(base2, 192), :], out.at[u, self.mine, self.rows(base1, 384), :], out.at[u, self.mine]):
            pairs.append((region, region))
        return pairs

    def copy(self, u, k):
        src, dst = self.copies(u)[k]
        return pltpu.make_async_remote_copy(src_ref=src, dst_ref=dst, send_sem=self.ss.at[u, k], recv_sem=self.rs.at[u, k], device_id=self.fly[k], device_id_type=MESH)

    def keep(self, u):
        src, dst = self.copies(u)[6]
        return pltpu.make_async_copy(src, dst, self.osem.at[u])

    def add(self, u, here, start, there, size):
        @pl.loop(0, size, step=192)
        def _(t):
            q = self.rows(t, 192)
            here[u, q, :] = (here[u, q, :].astype(F32) + there(self.rows(start + t, 192)).astype(F32)).astype(BF16)

    def advance(self, u, s):
        if s == 0:
            self.copy(u, 0).start()
        elif s == 1:
            self.copy(u, 0).wait_recv()
            self.add(u, self.r0, 0, lambda q: self.own[u, self.mine, q, :], 768)
            self.copy(u, 1).start()
        elif s == 2:
            self.copy(u, 1).wait_recv()
            self.add(u, self.r1, self.b1 * 384, lambda q: self.r0[u, q, :], 384)
            self.copy(u, 2).start()
        elif s == 3:
            self.copy(u, 2).wait_recv()
            self.add(u, self.r2, self.b2 * 192, lambda q: self.r1[u, q, :], 192)
            for k in range(3):
                self.copy(u, 3 + k).start()
        elif s == 4:
            for k in range(3):
                self.copy(u, 3 + k).wait_recv()
            total = self.r2[u, self.rows(self.z * 48, 48), :].astype(F32)
            for k in range(3):
                total = total + self.r3[u, k].astype(F32)
            self.r2[u, self.rows(self.z * 48, 48), :] = total.astype(BF16)
            self.keep(u).start()
            for k in range(3):
                self.copy(u, 6 + k).start()
        elif s == 5:
            for k in range(3):
                self.copy(u, 6 + k).wait_recv()
            self.keep(u).wait()
            self.copy(u, 9).start()
        elif s in (6, 7):
            self.copy(u, s + 3).wait_recv()
            self.copy(u, s + 4).start()
        else:
            self.copy(u, 11).wait_recv()

    def taus(self):
        return self.count + TURNS[-1]

    def step(self, tau, steps):
        for s in steps:
            u = tau - TURNS[s]

            @pl.when((u >= 0) & (u < self.count))
            def _():
                self.advance(jnp.clip(u, 0, self.count - 1), s)

    def finish(self):
        @pl.loop(0, self.count)
        def _(u):
            for k in range(12):
                self.copy(u, k).wait_send()


def small_all(values, smr, sss, srs, sums, k):
    z = sums.z
    s_ax, r_ax = lax.axis_index("seq"), lax.axis_index("row")
    x = lax.rem(s_ax, 2)
    partners = [sums.core, sums.first, sums.second, (lax.rem(z + 2, 4) * 2 + x, r_ax), ((z + 1 - 2 * lax.rem(z, 2)) * 2 + x, r_ax)]

    def copy(i):
        return pltpu.make_async_remote_copy(src_ref=smr.at[i], dst_ref=smr.at[i + 6], send_sem=sss.at[i], recv_sem=srs.at[i], device_id=partners[i], device_id_type=MESH)

    if k == 0:
        smr[0] = values[...]
    else:
        copy(k - 1).wait_recv()
        smr[k] = smr[k - 1] + smr[k + 5]
    if k < 5:
        copy(k).start()
    else:
        for i in range(5):
            copy(i).wait_send()


MARK_TAUS = NS_ITERS * SMALL


def marks_backward(ring, tau, arrived, part, dtot, saved, mixed, qm, km, counts, smallb, smallf, save_a, save_b, mixeds, marks, landing, held, dsums, keep, da, dk, kt, la, lk, lt, cs, cr, hs):
    owner, end = owner_of_pair(ring), ends(ring)
    pair = pair_of(ring)
    last = 3 * NS_ITERS + 1
    doc, turn = jnp.minimum(tau // NS_ITERS, SMALL - 1), lax.rem(tau, NS_ITERS)
    back = NS_ITERS - 1 - turn

    @pl.when(owner & (tau == 0))
    def _():
        la[...] = mul_nt(dtot[:LMK], mixed[...], PAIR)
        lk[...] = jnp.zeros_like(lk)
        lt[...] = flipped(saved[last], PAIR)

    @pl.when(owner & (tau < NS_ITERS))
    def _():
        a, b = backward_step([la[...]], [lk[...]], [lt[...]], [saved[3 * back]], [saved[3 * back + 1]], [saved[3 * back + 2]], PAIR)
        la[...] = a[0]
        lk[...] = b[0]

    @pl.when(owner & (tau == NS_ITERS - 1))
    def _():
        d_scores = backward_end(la[...], lk[...], saved[last], saved[0], PAIR) * 0.125
        d_query = mul(d_scores, km[pair].astype(F32), PAIR)
        d_key = mul(flipped(d_scores, PAIR), qm[pair].astype(F32), PAIR)
        arrived()
        total = part[pair]
        for k in ring.steps:
            total = total + landing[k - 1]
        held[pair, :LMK, :] = ((d_query + total) / counts[0, :, 0:1]).astype(BF16)
        held[pair, LMK:, :] = ((d_key + dtot[LMK:]) / counts[0, :, 0:1]).astype(BF16)
        ring.share(held, cs, cr, 1)

    work = end & (tau < MARK_TAUS)

    @pl.when(work & (turn == 0))
    def _():
        @pl.when(doc < EARLY)
        def _():
            copy = pltpu.make_async_copy(save_a.at[jnp.minimum(doc, EARLY - 1)], keep, hs.at[0])
            copy.start()
            copy.wait()

        @pl.when(doc >= EARLY)
        def _():
            copy = pltpu.make_async_copy(save_b.at[jnp.maximum(doc - EARLY, 0)], keep, hs.at[0])
            copy.start()
            copy.wait()

        for g in range(GROUPS):
            da[g] = mul_nt(smallf[0, doc, g], mixeds[doc, g], GROUP)
            dk[g] = jnp.zeros((LMK, GROUP), F32)
            kt[g] = flipped(keep[g, last], GROUP)

    @pl.when(work)
    def _():
        rows = range(GROUPS)
        iterates = [[keep[g, 3 * back + i] for g in rows] for i in range(3)]
        a, b = backward_step([da[g] for g in rows], [dk[g] for g in rows], [kt[g] for g in rows], *iterates, GROUP)
        for g in rows:
            da[g] = a[g]
            dk[g] = b[g]

    @pl.when(work & (turn == NS_ITERS - 1))
    def _():
        for g in range(GROUPS):
            d_scores = backward_end(da[g], dk[g], keep[g, last], keep[g, 0], GROUP) * 0.125
            d_query = mul(d_scores, marks[1, doc, g].astype(F32), GROUP)
            d_key = mul(flipped(d_scores, GROUP), marks[0, doc, g].astype(F32), GROUP)
            size = counts[1 + doc, :, 0:1]
            dsums[doc, g, :LMK, :] = ((d_query + smallb[doc, g]) / size).astype(BF16)
            dsums[doc, g, LMK:, :] = ((d_key + smallf[1, doc, g]) / size).astype(BF16)


N_MARKS = 13
MARKS_SPECS = in_vmem(9) + [ANY_SPEC] * 2 + in_vmem(2)
N_WORK = 12


def marks_work(count):
    return [
        VMEM((count - 1, LMK, PAIR), F32),
        VMEM((PAIRS, 2 * LMK, PAIR), BF16),
        VMEM((SMALL, GROUPS, 2 * LMK, GROUP), BF16),
        VMEM((GROUPS, SAVES, LMK, GROUP), F32),
        VMEM((GROUPS, LMK, GROUP), F32),
        VMEM((GROUPS, LMK, GROUP), F32),
        VMEM((GROUPS, LMK, GROUP), F32),
        VMEM((LMK, PAIR), F32),
        VMEM((LMK, PAIR), F32),
        VMEM((LMK, PAIR), F32),
        DMA((count - 1,)),
        DMA((PAIRS,)),
        DMA((1,)),
        DMA((count - 1,)),
        DMA((count - 1,)),
    ]


def finish_marks(ring, held, cs, cr, sent):
    sent()

    @pl.when(owner_of_pair(ring))
    def _():
        ring.share_sent(held, cs, cr, 1)


def sums_kernel(count, *refs):
    args, (dsum, dsums_out), work = refs[:N_MARKS], refs[N_MARKS : N_MARKS + 2], refs[N_MARKS + 2 :]
    (landing, held, dsums), rest, (ss, rs) = work[:3], work[3:13], work[13:]
    cs, cr = rest[7], rest[8]
    ring = Ring(count)
    ring.enter()
    arrived, sent = ring.scatter(lambda p: args[0].at[p], landing, ss, rs, 1, PAIRS)
    dsums[...] = jnp.zeros_like(dsums)

    @pl.loop(0, MARK_TAUS)
    def _(tau):
        marks_backward(ring, tau, arrived, *args, landing, held, dsums, *rest)

    ring.shared(held, cs, cr, 1, PAIRS)
    dsum[...] = held[...]
    dsums_out[...] = dsums[...]
    finish_marks(ring, held, cs, cr, sent)


def mark_sums(count, *args):
    shape = jax.ShapeDtypeStruct
    return pl.pallas_call(
        functools.partial(sums_kernel, count),
        in_specs=MARKS_SPECS,
        out_specs=in_vmem(2),
        out_shape=[shape((PAIRS, 2 * LMK, PAIR), BF16), shape((SMALL, GROUPS, 2 * LMK, GROUP), BF16)],
        scratch_shapes=marks_work(count),
        compiler_params=remote_params(4),
        name="mark_sums",
    )(*args)


BLOCKS = 3 * GROUPS


FIRST = (0, 12, 24, 27, 36)


def finale_kernel(count, *refs):
    args, refs = refs[:N_MARKS], refs[N_MARKS:]
    (lens, inputs, dq, dk, dv, w, ddown, act, normed, dup, mixture, dout, sm), refs = refs[:13], refs[13:]
    (out, dx, osm), refs = refs[:3], refs[3:]
    work, refs = refs[:15], refs[15:]
    (own, r0, r1, r2, r3, dj, flip, left, right, member, table, smr), refs = refs[:12], refs[12:]
    osem, gs, gr, sss, srs, jsem, fsem, bsem = refs
    (landing, held, dsums), rest, (ss, rs) = work[:3], work[3:13], work[13:]
    cs, cr = rest[7], rest[8]
    total = inputs.shape[0]
    ring = Ring(count)
    before = FIRST[3]
    sums = Sums(FIRST[4], own, out, r0, r1, r2, r3, osem, gs, gr)
    lefts, rights = (ddown, normed, mixture, inputs), (act, dup, dout)

    def fetch_left(i):
        return pltpu.make_async_copy(lefts[i], left, fsem.at[0])

    def fetch_right(i, u):
        columns = pl.ds(pl.multiple_of((u - FIRST[i]) * UNIT, 128), UNIT)
        return pltpu.make_async_copy(rights[i].at[:, columns], right.at[lax.rem(u, 2)], bsem.at[lax.rem(u, 2)])

    fetch_left(0).start()
    fetch_right(0, 0).start()
    joined = [pltpu.make_async_copy(src, dj.at[:, pl.ds(i * GROUPS * GROUP, GROUPS * GROUP)], jsem.at[i]) for i, src in enumerate((dq, dk, dv))]
    for copy in joined:
        copy.start()
    ring.enter(sums.others)
    arrived, sent = ring.scatter(lambda p: args[0].at[p], landing, ss, rs, 1, PAIRS)
    dsums[...] = jnp.zeros_like(dsums)
    chunk = 128

    def keep(u, grad):
        own[u, 0] = grad[:, :ACROSS]
        own[u, 1] = grad[:, ACROSS:]

    def make(tau):
        for i in range(4):

            @pl.when(tau == FIRST[i])
            def _():
                fetch_left(i).wait()
                flip[...] = jnp.transpose(left[...])
                if i < 3:
                    fetch_left(i + 1).start()

        for i in range(3):

            @pl.when((tau + 1 >= FIRST[i]) & (tau + 1 < FIRST[i + 1]))
            def _():
                fetch_right(i, jnp.clip(tau + 1, FIRST[i], FIRST[i + 1] - 1)).start()

        @pl.when(tau < before)
        def _():
            u = jnp.minimum(tau, before - 1)
            pltpu.make_async_copy(act.at[:, pl.ds(0, UNIT)], right.at[lax.rem(u, 2)], bsem.at[lax.rem(u, 2)]).wait()
            keep(u, dot(flip[...], right[lax.rem(u, 2)]).astype(BF16))

        @pl.when(tau == before)
        def _():
            ring.shared(held, cs, cr, 1, PAIRS)
            for half in range(2):
                for g in range(GROUPS):
                    at = slice(half * LMK, (half + 1) * LMK)
                    table[half * GROUPS + g, :LMK, :PAIR] = held[2 * g, at, :]
                    table[half * GROUPS + g, :LMK, PAIR:] = held[2 * g + 1, at, :]
                    for d in range(SMALL):
                        table[half * GROUPS + g, (d + 1) * LMK : (d + 2) * LMK, :] = dsums[d, g, at, :]

        @pl.when((tau >= before) & (tau < FIRST[4]))
        def _():
            b = jnp.clip(tau - before, 0, BLOCKS - 1)
            columns = pl.ds(pl.multiple_of(b * GROUP, 128), GROUP)

            @pl.when(b < 2 * GROUPS)
            def _():
                from_marks = dot(member[...], table[jnp.minimum(b, 2 * GROUPS - 1)])
                dj[:, columns] = (dj[:, columns].astype(F32) + from_marks).astype(BF16)

            keep(before + b, dot(flip[...], dj[:, columns]).astype(BF16))

    @pl.loop(0, sums.taus())
    def _(tau):
        sums.step(tau, range(8, 0, -1))
        make(tau)
        sums.step(tau, (0,))
        for k in range(6):

            @pl.when(tau == k)
            def _():
                small_all(sm, smr, sss, srs, sums, k)

        marks_backward(ring, tau, arrived, *args, landing, held, dsums, *rest)

        @pl.when(tau == MARK_TAUS)
        def _():
            low, high = slot_bounds(lens, total, (1, DOCS * LMK), 1)
            rows = lax.broadcasted_iota(jnp.int32, (total, DOCS * LMK), 0)
            member[...] = jnp.where((rows >= low) & (rows < high), 1.0, 0.0).astype(BF16)
            for copy in joined:
                copy.wait()

        @pl.when((tau >= FIRST[4]) & (tau < FIRST[4] + total // chunk))
        def _():
            rows = pl.ds(pl.multiple_of(jnp.clip(tau - FIRST[4], 0, total // chunk - 1) * chunk, chunk), chunk)
            dx[rows, :] = dot(dj[rows, :], w[...], NT)

    finish_marks(ring, held, cs, cr, sent)
    sums.finish()
    osm[...] = smr[5]


def finale(count, marks_args, lens, inputs, dq, dk, dv, w, ddown, act, normed, dup, mixture, dout, sm):
    n = FIRST[4]
    total, depth = inputs.shape
    width = w.shape[1]
    shape = jax.ShapeDtypeStruct
    return pl.pallas_call(
        functools.partial(finale_kernel, count),
        in_specs=MARKS_SPECS + [pl.BlockSpec(memory_space=pltpu.SMEM)] + [ANY_SPEC] * 4 + in_vmem(1) + [ANY_SPEC] * 6 + in_vmem(1),
        out_specs=[ANY_SPEC] + in_vmem(2),
        out_shape=[shape((n, 2, 768, ACROSS), BF16), shape((total, depth), F32), shape(sm.shape, F32)],
        scratch_shapes=marks_work(count)
        + [
            VMEM((n, 2, 768, ACROSS), BF16),
            VMEM((n, 768, ACROSS), BF16),
            VMEM((n, 384, ACROSS), BF16),
            VMEM((n, 192, ACROSS), BF16),
            VMEM((n, 3, 48, ACROSS), BF16),
            VMEM((total, width), BF16),
            VMEM((depth, total), BF16),
            VMEM((total, depth), BF16),
            VMEM((2, total, UNIT), BF16),
            VMEM((total, DOCS * LMK), BF16),
            VMEM((2 * GROUPS, DOCS * LMK, GROUP), BF16),
            VMEM((11,) + sm.shape, F32),
            DMA((n,)),
            DMA((n, 12)),
            DMA((n, 12)),
            DMA((5,)),
            DMA((5,)),
            DMA((3,)),
            DMA((1,)),
            DMA((2,)),
        ],
        compiler_params=pltpu.CompilerParams(collective_id=5, has_side_effects=True, vmem_limit_bytes=62 * 2**20),
        name="finale",
    )(*marks_args, lens, inputs, dq, dk, dv, w, ddown, act, normed, dup, mixture, dout, sm)


TRIPLE = 3


def widen_kernel(units, dx, residual, gd, gu, go, gq, grad):
    i = pl.program_id(0)
    value = [jnp.concatenate([units[k, 0], units[k, 1]], axis=1).astype(F32) for k in range(TRIPLE)]

    @pl.when(i < 4)
    def _():
        for k in range(TRIPLE):
            gd[k * UNIT : (k + 1) * UNIT, :] = jnp.transpose(value[k])

    for ref, first, end in ((gu, 4, 8), (go, 8, 9), (gq, 9, 12)):

        @pl.when((i >= first) & (i < end))
        def _():
            for k in range(TRIPLE):
                ref[:, k * UNIT : (k + 1) * UNIT] = value[k]

    @pl.when(i < 8)
    def _():
        grad[...] = residual[...] + dx[...]


def widen(units, dx, residual):
    n, _, side, half = units.shape
    shape = jax.ShapeDtypeStruct
    total, depth = dx.shape

    def place(first, last, down):
        def index(i):
            b = jnp.clip(i, first, last) - first
            return (b, 0) if down else (0, b)

        return pl.BlockSpec((side, side), index)

    part = pl.BlockSpec((total // 8, depth), lambda i: (jnp.minimum(i, 7), 0))
    return pl.pallas_call(
        widen_kernel,
        grid=(n // TRIPLE,),
        in_specs=[pl.BlockSpec((TRIPLE, 2, side, half), lambda i: (i, 0, 0, 0)), part, part],
        out_specs=[place(0, 3, True), place(4, 7, False), place(8, 8, True), place(9, 11, False), part],
        out_shape=[shape((4 * side, side), F32), shape((side, 4 * side), F32), shape((side, side), F32), shape((side, 3 * side), F32), shape(dx.shape, F32)],
        compiler_params=pltpu.CompilerParams(vmem_limit_bytes=62 * 2**20),
        name="widen",
    )(units, dx, residual)


def member_of(doc_lengths, total):
    low, high = slot_bounds(doc_lengths, total, (1, DOCS * LMK), 1)
    rows = jnp.arange(total, dtype=jnp.int32)[:, None]
    return ((rows >= low) & (rows < high)).astype(BF16)


def over_all(*grads):
    out = []
    for g in grads:
        part = lax.psum_scatter(g.astype(F32).reshape(lax.axis_size(("seq", "row")), -1), ("seq", "row"), scatter_dimension=0, tiled=True)
        out.append(lax.all_gather(part.astype(BF16), ("seq", "row"), axis=0, tiled=True).reshape(g.shape))
    return out


def on_device(
    tokens,
    doc_lengths,
    w_qkv,
    w_out,
    conv_taps,
    norm1_gain,
    norm1_bias,
    w_up,
    w_down,
    norm2_gain,
    norm2_bias,
    cotangent,
):
    model_width = tokens.shape[2]
    head_count, tap_count = conv_taps.shape
    rim = (tap_count - 1) // 2
    count = lax.axis_size("seq")
    wide = count == 8 and lax.axis_size("row") == 4
    inputs = tokens[0]
    joined, slot_sums, small, edge, counts = project(doc_lengths, inputs, w_qkv)
    qm, km, halo, save_a, invs = all_marks(count, slot_sums, counts, edge, small)
    exps, part, wsm, stsm = mix(doc_lengths, joined, qm, small[0])
    carried, stat, saved, inv, mixed, cars, save_b, inv2, mixeds = carry(count, part, qm, km, small, wsm, stsm, invs)
    taps = jnp.pad(conv_taps, ((0, 0), (0, 256 - tap_count)))
    taps_back = jnp.pad(conv_taps[:, ::-1], ((0, 0), (0, 256 - tap_count)))
    kernel_b, mixture_b = attend(doc_lengths, joined, halo, taps, km, carried, small[1], cars)
    residual1 = inputs.astype(jnp.float32) + jnp.dot(
        mixture_b, w_out, preferred_element_type=jnp.float32
    )
    normed1, norm1_pull = jax.vjp(layer_norm, residual1, norm1_gain, norm1_bias)
    normed1_b = normed1.astype(jnp.bfloat16)
    upward = jnp.dot(normed1_b, w_up, preferred_element_type=jnp.float32)
    activated_wide, gelu_pull = jax.vjp(gelu, upward)
    activated = activated_wide.astype(jnp.bfloat16)
    residual2 = normed1 + jnp.dot(activated, w_down, preferred_element_type=jnp.float32)
    result, norm2_pull = jax.vjp(layer_norm, residual2, norm2_gain, norm2_bias)
    delta_residual2, delta_gain2, delta_bias2 = norm2_pull(cotangent[0].astype(jnp.float32))
    delta_down = delta_residual2.astype(jnp.bfloat16)
    delta_active = jnp.dot(delta_down, w_down.T, preferred_element_type=jnp.float32)
    delta_up = gelu_pull(delta_active)[0].astype(jnp.bfloat16)
    delta_normed1 = delta_residual2 + jnp.dot(delta_up, w_up.T, preferred_element_type=jnp.float32)
    delta_residual1, delta_gain1, delta_bias1 = norm1_pull(delta_normed1)
    delta_output = delta_residual1.astype(jnp.bfloat16)
    delta_mixture = jnp.dot(delta_output, w_out.T, preferred_element_type=jnp.float32)
    delta_mix = delta_mixture.astype(BF16)
    dq, part_f, small_f = back_f(doc_lengths, joined, delta_mix, kernel_b, km, carried, small[1], cars)
    delta_edge = jnp.stack([delta_mix[:rim], delta_mix[-rim:]])
    scaled, along, dtot, scs, alongs, delta_halo = spread(count, part_f, stat, inv, mixed, small_f, stsm, invs, inv2, mixeds, delta_edge)
    factor = jnp.exp(part[:, LMK] - stat[:, 0]).reshape(1, model_width)
    factor = jnp.broadcast_to(factor, (8, model_width))
    dk, dv, part_b, small_b, dtaps = back_b(
        doc_lengths, joined, halo, exps, factor, scaled, along, scs, alongs, qm, small[0], taps_back, delta_mix, delta_halo
    )
    grad_taps = dtaps.reshape(head_count, 256)[:, BLK - 1 : BLK - 1 + tap_count]
    taps_row = jnp.pad(grad_taps.reshape(1, -1), ((0, 3), (0, model_width - grad_taps.size)))
    norm_terms = jnp.concatenate([jnp.stack([delta_gain1, delta_bias1, delta_gain2, delta_bias2]), taps_row], axis=0)
    marks_args = (part_b, dtot, saved, mixed, qm, km, counts, small_b, small_f, save_a, save_b, mixeds, small)
    if wide:
        units, from_joined, tsm = finale(
            count, marks_args, doc_lengths, inputs, dq, dk, dv, w_qkv, delta_down, activated, normed1_b, delta_up, mixture_b, delta_output, norm_terms
        )
        total_down, total_up, total_output, total_joined, delta_inputs = widen(units, from_joined, delta_residual1)
    else:
        dsum, dsums = mark_sums(count, *marks_args)
        long_sums = dsum.reshape(PAIRS, 2, LMK, PAIR).transpose(2, 1, 0, 3).reshape(LMK, 2 * model_width)
        small_sums = dsums.reshape(SMALL, GROUPS, 2, LMK, GROUP).transpose(0, 3, 2, 1, 4).reshape(SMALL * LMK, 2 * model_width)
        from_marks = jnp.dot(member_of(doc_lengths, inputs.shape[0]), jnp.concatenate([long_sums, small_sums], axis=0), preferred_element_type=F32)
        delta_joined = jnp.concatenate([dq, dk, dv], axis=1) + jnp.pad(from_marks, ((0, 0), (0, model_width)))
        delta_joined = delta_joined.astype(BF16)
        grad_down = jnp.dot(activated.T, delta_down, preferred_element_type=F32)
        grad_up = jnp.dot(normed1_b.T, delta_up, preferred_element_type=F32)
        grad_output = jnp.dot(mixture_b.T, delta_output, preferred_element_type=F32)
        grad_joined = jnp.dot(inputs.T, delta_joined, preferred_element_type=F32)
        total_down, total_up, total_output, total_joined = over_all(grad_down, grad_up, grad_output, grad_joined)
        tsm = lax.psum(norm_terms, ("seq", "row"))
        delta_inputs = delta_residual1 + dot(delta_joined, w_qkv, NT)
    return (
        result.astype(BF16)[None],
        delta_inputs[None],
        total_joined.astype(F32),
        total_output.astype(F32),
        tsm[4, : grad_taps.size].reshape(grad_taps.shape),
        tsm[0],
        tsm[1],
        total_up.astype(F32),
        total_down.astype(F32),
        tsm[2],
        tsm[3],
    )


def solution(mesh):
    return jax.shard_map(
        on_device,
        mesh=mesh,
        in_specs=(
            P("row", "seq", None),
            P("row", None),
            P(),
            P(),
            P(),
            P(),
            P(),
            P(),
            P(),
            P(),
            P(),
            P("row", "seq", None),
        ),
        out_specs=(
            P("row", "seq", None),
            P("row", "seq", None),
            P(),
            P(),
            P(),
            P(),
            P(),
            P(),
            P(),
            P(),
            P(),
        ),
        check_vma=False,
    )
```

```python
import functools

import jax
import jax.numpy as jnp
from jax import lax
from jax.experimental import pallas as pl
from jax.experimental.pallas import tpu as pltpu
from jax.sharding import PartitionSpec as P

MESH = pl.DeviceIdType.MESH

LMK = 64
NS_ITERS = 6
DOCS = 4


HIGHEST = lax.Precision.HIGHEST
EPSILON = 1e-05
BIG_NEGATIVE = -1e30


F32, BF16 = jnp.float32, jnp.bfloat16
GROUP = 256
PAIR = 128
PAIRS = 6
SMALL = DOCS - 1
GROUPS = 3
WINDOW = 256
VMEM = pltpu.VMEM


def dot(a, b, dims=((1,), (0,)), precision=None):
    return lax.dot_general(a, b, (dims, ((), ())), preferred_element_type=F32, precision=precision)


NT, TN = ((1,), (1,)), ((0,), (0,))


def head_mask(width):
    rows = lax.broadcasted_iota(jnp.int32, (width, width), 0)
    lanes = lax.broadcasted_iota(jnp.int32, (width, width), 1)
    return (rows // LMK) == (lanes // LMK)


def blocks_of(side, width):
    tiled = jnp.concatenate([side] * (width // LMK), axis=0)
    return jnp.where(head_mask(width), tiled, jnp.zeros_like(tiled))


def side_of(full, width):
    full = jnp.where(head_mask(width), full, 0.0)
    return sum(full[i * LMK : (i + 1) * LMK] for i in range(width // LMK))


def flipped(side, width):
    return side_of(jnp.transpose(blocks_of(side, width)), width)


def head_ones(width):
    return jnp.where(head_mask(width), 1.0, 0.0).astype(F32)


def column_of(row, width):
    slots = lax.broadcasted_iota(jnp.int32, (LMK, width), 0)
    lanes = lax.broadcasted_iota(jnp.int32, (LMK, width), 1)
    picked = jnp.where(slots == lanes % LMK, jnp.broadcast_to(row, (LMK, width)), 0.0)
    return dot(picked, head_ones(width), precision=HIGHEST)


def row_of(side, width):
    return dot(jnp.ones((8, width), F32), blocks_of(side, width), NT, precision=HIGHEST)


def halves(x):
    high = x.astype(BF16)
    return high, (x - high.astype(F32)).astype(BF16)


def product3(a, b, dims, width):
    high, low = halves(a)
    b_high, b_low = halves(b)
    rows = a.shape[0]
    both = dot(jnp.concatenate([high, low], axis=0), blocks_of(b_high, width), dims)
    return both[:rows] + both[rows:] + dot(high, blocks_of(b_low, width), dims)


def mul(a, b, width):
    return product3(a, b, ((1,), (0,)), width)


def mul_nt(a, b, width):
    return product3(a, b, NT, width)


def each(f, *lists):
    return [f(*items) for items in zip(*lists)]


def side_eye(width):
    slots = lax.broadcasted_iota(jnp.int32, (LMK, width), 0)
    lanes = lax.broadcasted_iota(jnp.int32, (LMK, width), 1)
    return jnp.where(slots == lanes % LMK, 1.0, 0.0).astype(F32)


def head_total(side, width):
    columns = jnp.broadcast_to(jnp.sum(side, axis=0, keepdims=True), (8, width))
    return dot(columns, head_ones(width), precision=HIGHEST)[:1]


def head_max(scores, width):
    out = []
    for i in range(width // PAIR):
        part = scores[:, i * PAIR : (i + 1) * PAIR]
        left = lax.broadcasted_iota(jnp.int32, part.shape, 1) < LMK
        low = jnp.max(jnp.where(left, part, BIG_NEGATIVE), axis=1, keepdims=True)
        high = jnp.max(jnp.where(left, BIG_NEGATIVE, part), axis=1, keepdims=True)
        out.append(jnp.where(left, low, high))
    return out[0] if len(out) == 1 else jnp.concatenate(out, axis=1)


def inverse_forward(qm, km, save, width):
    ones = head_ones(width)

    def begin(q, k):
        scores = dot(q, blocks_of(k, width), NT) * 0.125
        exponent = jnp.exp(scores - head_max(scores, width))
        return exponent / dot(exponent, ones, precision=HIGHEST)

    kernel_a = each(begin, qm, km)
    approx = each(lambda a: flipped(a, width) / head_total(a * a, width), kernel_a)
    eye = side_eye(width)
    for j, a in enumerate(kernel_a):
        save(3 * NS_ITERS + 1, j, a)

    def sweep(i, approx):
        product = each(lambda a, x: mul(a, x, width), kernel_a, approx)
        square = each(lambda p: mul(p, p, width), product)
        cube = each(lambda s, p: mul(s, p, width), square, product)
        poly = each(lambda p, s, c: 3.25 * eye - 3.75 * p + 1.75 * s - 0.25 * c, product, square, cube)
        for j in range(len(approx)):
            save(3 * i, j, approx[j])
            save(3 * i + 1, j, product[j])
            save(3 * i + 2, j, poly[j])
        return tuple(each(lambda x, q: mul(x, q, width), approx, poly))

    approx = lax.fori_loop(0, NS_ITERS, sweep, tuple(approx))
    for j, x in enumerate(approx):
        save(3 * NS_ITERS, j, x)
    return list(approx)


def backward_step(d_approx, d_kernel, kernel_at, approx, product, poly, width):
    product_t = each(lambda p: flipped(p, width), product)
    d_poly = each(lambda x, d: mul(flipped(x, width), d, width), approx, d_approx)
    d_next = each(lambda d, q: mul_nt(d, q, width), d_approx, poly)
    right = each(lambda d, p: mul_nt(d, p, width), d_poly, product)
    left = each(lambda p, d: mul(p, d, width), product_t, d_poly)
    both = each(lambda r, x: r + x, right, left)
    third = each(lambda r, p: mul_nt(r, p, width), right, product)
    fourth = each(lambda p, b: mul(p, b, width), product_t, both)
    d_product = each(lambda d, b, t, f: -3.75 * d + 1.75 * b - 0.25 * (t + f), d_poly, both, third, fourth)
    d_kernel = each(lambda k, d, x: k + mul_nt(d, x, width), d_kernel, d_product, approx)
    d_approx = each(lambda n, a, d: n + mul(a, d, width), d_next, kernel_at, d_product)
    return d_approx, d_kernel


def backward_end(d_approx, d_kernel, kernel_a, first, width):
    scale = head_total(kernel_a * kernel_a, width)
    d_scale = -head_total(d_approx * first, width) / scale
    d_kernel = d_kernel + flipped(d_approx, width) / scale + 2.0 * kernel_a * d_scale
    inner = dot(d_kernel * kernel_a, head_ones(width), precision=HIGHEST)
    return kernel_a * (d_kernel - inner)


def stacked(side):
    return blocks_of(side, GROUP)


def doc_table(lens, total):
    shard_start = lax.axis_index("seq") * total
    lengths = [lens[0, i] for i in range(DOCS)]
    starts = [-shard_start]
    for i in range(DOCS - 1):
        starts.append(starts[i] + lengths[i])
    best, size, start = jnp.int32(0), lengths[0], starts[0]
    for i in range(1, DOCS):
        more = lengths[i] > size
        best, size, start = jnp.where(more, i, best), jnp.where(more, lengths[i], size), jnp.where(more, starts[i], start)
    sizes, begins = [size], [start]
    for i in range(DOCS - 1):
        later = best <= i
        sizes.append(jnp.where(later, lengths[i + 1], lengths[i]))
        begins.append(jnp.where(later, starts[i + 1], starts[i]))
    return sizes, begins


def doc_ranges(lens, total):
    sizes, begins = doc_table(lens, total)
    info = []
    for size, begin in zip(sizes, begins):
        info += [jnp.clip(begin, 0, total), jnp.clip(begin + size, 0, total)]
    return info + [begins[0], begins[0] + sizes[0]]


def slot_bounds(lens, total, shape, axis):
    sizes, begins = doc_table(lens, total)
    slot = lax.broadcasted_iota(jnp.int32, shape, axis)
    doc, within = slot // LMK, slot % LMK
    size, begin = jnp.full(shape, sizes[0]), jnp.full(shape, begins[0])
    for d in range(1, DOCS):
        size, begin = jnp.where(doc == d, sizes[d], size), jnp.where(doc == d, begins[d], begin)
    return begin + (within * size + LMK - 1) // LMK, begin + ((within + 1) * size + LMK - 1) // LMK


def project_kernel(lens, inputs, weight, joined, sums, small, edge, counts):
    total = inputs.shape[0]
    block = pl.program_id(0)
    out = dot(inputs[...], weight[...]).astype(BF16)
    joined[...] = out

    @pl.when(block < 2 * GROUPS)
    def _():
        low, high = slot_bounds(lens, total, (DOCS * LMK, 1), 0)
        rows = lax.broadcasted_iota(jnp.int32, (DOCS * LMK, total), 1)
        member = jnp.where((rows >= low) & (rows < high), 1.0, 0.0).astype(BF16)
        slot_sums = dot(member, out)
        size = (high - low).astype(F32)
        sums[...] = slot_sums[:LMK]
        small[0] = (slot_sums[LMK:] / size[LMK:]).astype(BF16).reshape(SMALL, LMK, GROUP)
        counts[...] = jnp.broadcast_to(size, (DOCS * LMK, PAIR)).reshape(DOCS, LMK, PAIR)

    @pl.when(block >= 2 * GROUPS)
    def _():
        edge[0] = out[:16]
        edge[1] = out[total - 16 :]


def project(lens, inputs, weight):
    total, depth = inputs.shape
    width = weight.shape[1]
    half = 2 * GROUPS - 1

    return pl.pallas_call(
        project_kernel,
        grid=(width // GROUP,),
        in_specs=[
            pl.BlockSpec(memory_space=pltpu.SMEM),
            pl.BlockSpec((total, depth), lambda j: (0, 0)),
            pl.BlockSpec((depth, GROUP), lambda j: (0, j)),
        ],
        out_specs=[
            pl.BlockSpec((total, GROUP), lambda j: (0, j)),
            pl.BlockSpec((LMK, GROUP), lambda j: (0, jnp.minimum(j, half))),
            pl.BlockSpec((1, SMALL, None, LMK, GROUP), lambda j: (jnp.minimum(j, half) // GROUPS, 0, lax.rem(jnp.minimum(j, half), GROUPS), 0, 0)),
            pl.BlockSpec((2, 16, GROUP), lambda j: (0, 0, jnp.maximum(j - 2 * GROUPS, 0))),
            pl.BlockSpec((DOCS, LMK, PAIR), lambda j: (0, 0, 0)),
        ],
        out_shape=[
            jax.ShapeDtypeStruct((total, width), BF16),
            jax.ShapeDtypeStruct((LMK, 2 * GROUPS * GROUP), F32),
            jax.ShapeDtypeStruct((2, SMALL, GROUPS, LMK, GROUP), BF16),
            jax.ShapeDtypeStruct((2, 16, GROUPS * GROUP), BF16),
            jax.ShapeDtypeStruct((DOCS, LMK, PAIR), F32),
        ],
        compiler_params=pltpu.CompilerParams(vmem_limit_bytes=62 * 2**20),
        name="project",
    )(lens, inputs, weight)


def joint(ref):
    return jnp.concatenate([ref[0], ref[1]], axis=1)


def write_pairs(ref, at, value):
    ref[0, at, :] = value[:, :PAIR]
    ref[1, at, :] = value[:, PAIR:]


LONG_SPEC = pl.BlockSpec((2, LMK, PAIR), lambda g: (g, 0, 0))
ROW_SPEC = pl.BlockSpec((2, 8, PAIR), lambda g: (g, 0, 0))
SMALL_SPEC = pl.BlockSpec((SMALL, None, LMK, GROUP), lambda g: (0, g, 0, 0))
SMALL_ROW_SPEC = pl.BlockSpec((SMALL, None, 8, GROUP), lambda g: (0, g, 0, 0))
TOP = slice(0, LMK)


def half_spec(half):
    return pl.BlockSpec((None, SMALL, None, LMK, GROUP), lambda g: (half, 0, g, 0, 0))


def for_docs(info, total, body):
    def inside(doc, size, start):
        rows = lax.broadcasted_iota(jnp.int32, (size, 1), 0) + start
        return (rows >= info[2 * doc]) & (rows < info[2 * doc + 1])

    body(0, total, 0, inside(0, total, 0))
    for doc in range(1, DOCS):
        low, high = info[2 * doc], info[2 * doc + 1]
        start = jnp.minimum(low // 16 * 16, total - WINDOW)

        @pl.when((high > low) & (high - start <= WINDOW))
        def _():
            at = pl.multiple_of(start, 16)
            body(doc, WINDOW, at, inside(doc, WINDOW, at))

        @pl.when(high - start > WINDOW)
        def _():
            body(doc, total, 0, inside(doc, total, 0))


def mix_kernel(lens, keys, values, qm, qms, exps, part, parts, stats):
    info = doc_ranges(lens, exps.shape[0])
    parts[...] = jnp.zeros_like(parts)
    stats[...] = jnp.zeros_like(stats)
    part[...] = jnp.zeros_like(part)

    def body(doc, size, start, inside):
        rows = pl.ds(start, size)
        marks = stacked(joint(qm) if doc == 0 else qms[doc - 1])
        scores = jnp.where(inside, dot(keys[rows, :], marks, NT) * 0.125, BIG_NEGATIVE)
        top = jnp.max(scores, axis=0, keepdims=True)
        wide = jnp.exp(scores - top)
        narrow = wide.astype(BF16)
        weighted = side_of(dot(narrow, values[rows, :], TN), GROUP)
        total = jnp.sum(wide, axis=0, keepdims=True)
        if doc == 0:
            exps[...] = narrow
            write_pairs(part, TOP, weighted)
            write_pairs(part, slice(LMK, LMK + 1), top)
            write_pairs(part, slice(LMK + 1, LMK + 2), total)
        else:
            exps[rows, :] = jnp.where(inside, narrow, exps[rows, :])
            parts[doc - 1] = weighted
            stats[doc - 1, 0:1, :] = top
            stats[doc - 1, 1:2, :] = total

    for_docs(info, exps.shape[0], body)


def mix(lens, joined, qm, qms):
    total, width = joined.shape[0], joined.shape[1] // 3
    groups = width // GROUP
    return pl.pallas_call(
        mix_kernel,
        grid=(groups,),
        in_specs=[
            pl.BlockSpec(memory_space=pltpu.SMEM),
            pl.BlockSpec((total, GROUP), lambda g: (0, groups + g)),
            pl.BlockSpec((total, GROUP), lambda g: (0, 2 * groups + g)),
            LONG_SPEC,
            half_spec(0),
        ],
        out_specs=[
            pl.BlockSpec((total, GROUP), lambda g: (0, g)),
            pl.BlockSpec((2, LMK + 8, PAIR), lambda g: (g, 0, 0)),
            SMALL_SPEC,
            SMALL_ROW_SPEC,
        ],
        out_shape=[
            jax.ShapeDtypeStruct((total, width), BF16),
            jax.ShapeDtypeStruct((PAIRS, LMK + 8, PAIR), F32),
            jax.ShapeDtypeStruct((SMALL, groups, LMK, GROUP), F32),
            jax.ShapeDtypeStruct((SMALL, groups, 8, GROUP), F32),
        ],
        compiler_params=pltpu.CompilerParams(vmem_limit_bytes=62 * 2**20),
        name="mix",
    )(lens, joined, joined, qm, qms)


TOEP = 160
BLK = 128


def widened(taps, backward):
    count = taps.shape[1]
    rows = lax.broadcasted_iota(jnp.int32, (count, 256), 0)
    lanes = lax.broadcasted_iota(jnp.int32, (count, 256), 1)
    place = rows + lanes == count - 1 if backward else rows == lanes
    return dot(taps[...], jnp.where(place, 1.0, 0.0).astype(F32), precision=HIGHEST)


def band(taps):
    wide = jnp.broadcast_to(taps, (BLK, 256))
    return pltpu.roll(wide, 0, 1, stride=1, stride_axis=0)[:, :TOEP].astype(BF16)


def bands(taps, group):
    heads = GROUP // LMK
    return jnp.concatenate([band(taps[pl.ds(group * heads + i, 1), :]) for i in range(heads)], axis=0)


def head_rows(stack):
    lanes = lax.broadcasted_iota(jnp.int32, (BLK, GROUP), 1) // LMK
    out = stack[:BLK]
    for i in range(1, GROUP // LMK):
        out = jnp.where(lanes == i, stack[i * BLK : (i + 1) * BLK], out)
    return out


def padded_rows(before, here, after, pad):
    total = here.shape[0]
    pad[0:16, :] = before
    pad[16 : total + 16, :] = here[...]
    pad[total + 16 : total + 32, :] = after


def doc_windows(info, total, body):
    def member(doc, start):
        rows = lax.broadcasted_iota(jnp.int32, (TOEP, 1), 0) + start - 16
        low, high = (info[8], info[9]) if doc == 0 else (info[2 * doc], info[2 * doc + 1])
        return (rows >= low) & (rows < high)

    for doc in range(DOCS):
        low, high = info[2 * doc], info[2 * doc + 1]

        @pl.loop(low // BLK, jnp.where(high > low, (high + BLK - 1) // BLK, low // BLK))
        def _(b):
            start = pl.multiple_of(b * BLK, BLK)
            body(doc, start, member(doc, start))


def attend_kernel(lens, queries, values, halo, taps, km, car, kms, cars, kern, mixture, pad, att, tap_rows):
    total = queries.shape[0]
    info = doc_ranges(lens, total)
    group = pl.program_id(0)
    ones = head_ones(GROUP).astype(BF16)

    def body(doc, size, start, inside):
        rows = pl.ds(start, size)
        marks = stacked(joint(km) if doc == 0 else kms[doc - 1])
        scores = dot(queries[rows, :], marks, NT) * 0.125
        exponent = jnp.exp(scores - head_max(scores, GROUP))
        kernel = (exponent / dot(exponent.astype(BF16), ones)).astype(BF16)
        carried = stacked(joint(car) if doc == 0 else cars[doc - 1])
        attended = dot(kernel, carried)
        if doc == 0:
            kern[...] = kernel
            att[...] = attended
        else:
            kern[rows, :] = jnp.where(inside, kernel, kern[rows, :])
            att[rows, :] = jnp.where(inside, attended, att[rows, :])

    for_docs(info, total, body)
    padded_rows(halo[0], values, halo[1], pad)
    tap_rows[...] = widened(taps, False)
    tape = bands(tap_rows, group)

    def conv(doc, start, inside):
        window = jnp.where(inside, pad[pl.ds(start, TOEP), :], jnp.zeros((), BF16))
        out = head_rows(dot(tape, window))
        rows = pl.ds(start, BLK)
        here = inside[16 : 16 + BLK]
        new = (att[rows, :] + out).astype(BF16)
        if doc == 0:
            mixture[rows, :] = new
        else:
            mixture[rows, :] = jnp.where(here, new, mixture[rows, :])

    doc_windows(info, total, conv)


def attend(lens, joined, halo, taps, km, car, kms, cars):
    total, width = joined.shape[0], joined.shape[1] // 3
    groups = width // GROUP
    col = pl.BlockSpec((total, GROUP), lambda g: (0, g))
    mark, marks = LONG_SPEC, SMALL_SPEC
    return pl.pallas_call(
        attend_kernel,
        grid=(groups,),
        in_specs=[
            pl.BlockSpec(memory_space=pltpu.SMEM),
            col,
            pl.BlockSpec((total, GROUP), lambda g: (0, 2 * groups + g)),
            pl.BlockSpec((2, 16, GROUP), lambda g: (0, 0, g)),
            pl.BlockSpec(taps.shape, lambda g: (0, 0)),
            mark,
            mark,
            half_spec(1),
            marks,
        ],
        out_specs=[col, col],
        out_shape=[jax.ShapeDtypeStruct((total, width), BF16)] * 2,
        scratch_shapes=[VMEM((total + 32, GROUP), BF16), VMEM((total, GROUP), F32), VMEM((taps.shape[0], 256), F32)],
        compiler_params=pltpu.CompilerParams(vmem_limit_bytes=62 * 2**20),
        name="attend",
    )(lens, joined, joined, halo, taps, km, car, kms, cars)


ROWS = 512
HALF = 256
PART = 1536
DENSE_TERMS = 8


def normalize(x):
    average = jnp.mean(x, axis=-1, keepdims=True)
    centered = x - average
    scale = lax.rsqrt(jnp.mean(centered * centered, axis=-1, keepdims=True) + EPSILON)
    return centered * scale, scale


def normalize_back(grad, gain, unit, scale):
    n = grad * gain
    return scale * (n - jnp.mean(n, axis=-1, keepdims=True) - unit * jnp.mean(n * unit, axis=-1, keepdims=True))


def column_sums(x):
    return jnp.sum(x, axis=0, keepdims=True)


def dense_kernel(mix_ref, inputs, cot, g1, b1, g2, b2, w_out, w_up, w_down, out, act, dup, ddown, normed, dout, dmix, dres, terms, edge, v_out, v_up, v_down, slope, wsem):
    step = pl.program_id(0)
    parts = w_up.shape[1] // PART
    loads = [pltpu.make_async_copy(w_out, v_out, wsem.at[0])]
    for c in range(parts):
        at = pl.ds(c * PART, PART)
        loads.append(pltpu.make_async_copy(w_up.at[:, at], v_up.at[c], wsem.at[1 + 2 * c]))
        loads.append(pltpu.make_async_copy(w_down.at[at, :], v_down.at[c], wsem.at[2 + 2 * c]))

    @pl.when(step == 0)
    def _():
        for load in loads:
            load.start()
        for load in loads:
            load.wait()
        terms[...] = jnp.zeros_like(terms)

    gain1, bias1, gain2, bias2 = (x[...].reshape(1, -1) for x in (g1, b1, g2, b2))

    def chain(half, first):
        r = slice(half * HALF, (half + 1) * HALF)
        unit1, scale1 = normalize(inputs[r, :].astype(F32) + dot(mix_ref[r, :], v_out[...]))
        n1 = unit1 * gain1 + bias1
        n1_low = n1.astype(BF16)
        normed[r, :] = n1_low
        yield
        total = n1
        for c in range(parts):
            at = slice(c * PART, (c + 1) * PART)
            up = dot(n1_low, v_up[c])
            share = 0.5 * (1.0 + lax.erf(up * 0.7071067811865476))
            active = (up * share).astype(BF16)
            act[r, at] = active
            slope[r, at] = share + up * (jnp.exp(-0.5 * up * up) * 0.3989422804014327)
            total = total + dot(active, v_down[c])
        yield
        unit2, scale2 = normalize(total)
        out[r, :] = (unit2 * gain2 + bias2).astype(BF16)
        grad = cot[r, :].astype(F32)
        terms[2:3, :] += column_sums(grad * unit2)
        terms[3:4, :] += column_sums(grad)
        d_total = normalize_back(grad, gain2, unit2, scale2)
        low = d_total.astype(BF16)
        ddown[r, :] = low
        yield
        for c in range(parts):
            at = slice(c * PART, (c + 1) * PART)
            d_up = (dot(low, v_down[c], NT) * slope[r, at]).astype(BF16)
            dup[r, at] = d_up
            d_total = d_total + dot(d_up, v_up[c], NT)
        yield
        terms[0:1, :] += column_sums(d_total * unit1)
        terms[1:2, :] += column_sums(d_total)
        d_first = normalize_back(d_total, gain1, unit1, scale1)
        dres[r, :] = d_first
        low = d_first.astype(BF16)
        dout[r, :] = low
        dmix[r, :] = dot(low, v_out[...], NT).astype(BF16)

    ahead, behind = chain(0, True), chain(1, False)
    next(ahead)
    for _ in range(4):
        next(ahead, None)
        next(behind)
    next(behind, None)

    @pl.when(step == 0)
    def _():
        edge[0] = dmix[:16, :]

    @pl.when(step == pl.num_programs(0) - 1)
    def _():
        edge[1] = dmix[ROWS - 16 :, :]


def dense(mixture, inputs, cot, gains, w_out, w_up, w_down):
    total, width = mixture.shape
    wide = w_up.shape[1]
    parts = wide // PART
    row = pl.BlockSpec((ROWS, width), lambda i: (i, 0))
    long_row = pl.BlockSpec((ROWS, wide), lambda i: (i, 0))
    shape = jax.ShapeDtypeStruct
    return pl.pallas_call(
        dense_kernel,
        grid=(total // ROWS,),
        in_specs=[row, row, row] + [pl.BlockSpec((width,), lambda i: (0,))] * 4 + [pl.BlockSpec(memory_space=pl.ANY)] * 3,
        out_specs=[row, long_row, long_row, row, row, row, row, row]
        + [pl.BlockSpec((DENSE_TERMS, width), lambda i: (0, 0)), pl.BlockSpec((2, 16, width), lambda i: (0, 0, 0))],
        out_shape=[
            shape((total, width), BF16),
            shape((total, wide), BF16),
            shape((total, wide), BF16),
            shape((total, width), BF16),
            shape((total, width), BF16),
            shape((total, width), BF16),
            shape((total, width), BF16),
            shape((total, width), F32),
            shape((DENSE_TERMS, width), F32),
            shape((2, 16, width), BF16),
        ],
        scratch_shapes=[
            VMEM((width, width), BF16),
            VMEM((parts, width, PART), BF16),
            VMEM((parts, PART, width), BF16),
            VMEM((ROWS, wide), F32),
            pltpu.SemaphoreType.DMA((1 + 2 * parts,)),
        ],
        compiler_params=pltpu.CompilerParams(vmem_limit_bytes=62 * 2**20),
        name="dense",
    )(mixture, inputs, cot, *gains, w_out, w_up, w_down)


def back_f_kernel(lens, queries, dmix, kern, km, car, kms, cars, dq, part, parts):
    info = doc_ranges(lens, dq.shape[0])
    parts[...] = jnp.zeros_like(parts)
    ones = head_ones(GROUP).astype(BF16)

    def body(doc, size, start, inside):
        rows = pl.ds(start, size)
        zero = jnp.zeros((), BF16)
        marks = stacked(joint(km) if doc == 0 else kms[doc - 1])
        carried = stacked(joint(car) if doc == 0 else cars[doc - 1])
        datt = dmix[rows, :]
        kernel = jnp.where(inside, kern[rows, :], zero)
        d_carried = side_of(dot(kernel, datt, TN), GROUP)
        d_kernel = dot(datt, carried, NT)
        wide = kernel.astype(F32)
        weighed = wide * d_kernel
        high = weighed.astype(BF16)
        low = (weighed - high.astype(F32)).astype(BF16)
        inner = dot(high, ones) + dot(low, ones)
        d_scores = (weighed - wide * inner).astype(BF16)
        d_queries = dot(d_scores, marks) * 0.125
        d_marks = side_of(dot(d_scores, queries[rows, :], TN), GROUP) * 0.125
        if doc == 0:
            dq[...] = d_queries.astype(BF16)
            write_pairs(part, TOP, d_carried)
            write_pairs(part, slice(LMK, 2 * LMK), d_marks)
        else:
            dq[rows, :] = jnp.where(inside, d_queries.astype(BF16), dq[rows, :])
            parts[0, doc - 1] = d_carried
            parts[1, doc - 1] = d_marks

    for_docs(info, dq.shape[0], body)


def back_f(lens, joined, dmix, kern, km, car, kms, cars):
    total, width = dmix.shape
    groups = width // GROUP
    col = pl.BlockSpec((total, GROUP), lambda g: (0, g))
    mark, marks = LONG_SPEC, SMALL_SPEC
    return pl.pallas_call(
        back_f_kernel,
        grid=(groups,),
        in_specs=[pl.BlockSpec(memory_space=pltpu.SMEM), col, col, col, mark, mark, half_spec(1), marks],
        out_specs=[
            col,
            pl.BlockSpec((2, 2 * LMK, PAIR), lambda g: (g, 0, 0)),
            pl.BlockSpec((2, SMALL, None, LMK, GROUP), lambda g: (0, 0, g, 0, 0)),
        ],
        out_shape=[
            jax.ShapeDtypeStruct((total, width), BF16),
            jax.ShapeDtypeStruct((PAIRS, 2 * LMK, PAIR), F32),
            jax.ShapeDtypeStruct((2, SMALL, groups, LMK, GROUP), F32),
        ],
        compiler_params=pltpu.CompilerParams(vmem_limit_bytes=62 * 2**20),
        name="back_f",
    )(lens, joined, dmix, kern, km, car, kms, cars)


def back_b_kernel(lens, keys, values, halo, exps, local, stat, sc, along, scs, alongs, qm, qms, taps, dmix, dhalo, dk, dv, part, parts, dtaps, pad, dpad, acc, dval, tap_rows):
    total = keys.shape[0]
    info = doc_ranges(lens, total)
    group = pl.program_id(0)
    parts[...] = jnp.zeros_like(parts)

    def body(doc, size, start, inside):
        rows = pl.ds(start, size)
        scaled = stacked(joint(sc) if doc == 0 else scs[doc - 1])
        marks = stacked(joint(qm) if doc == 0 else qms[doc - 1])
        wide = jnp.where(inside, exps[rows, :].astype(F32), 0.0)
        if doc == 0:
            top = jnp.concatenate([local[0, LMK : LMK + 1], local[1, LMK : LMK + 1]], axis=1)
            wide = wide * jnp.exp(top - joint(stat)[0:1, :])
        shift = joint(along)[0:1, :] if doc == 0 else alongs[doc - 1, 0:1, :]
        d_values = dot(wide.astype(BF16), scaled)
        reach = dot(values[rows, :], scaled, NT)
        d_scores = (wide * (reach - shift)).astype(BF16)
        d_keys = dot(d_scores, marks) * 0.125
        d_marks = side_of(dot(d_scores, keys[rows, :], TN), GROUP) * 0.125
        if doc == 0:
            dk[...] = d_keys.astype(BF16)
            dval[...] = d_values
            write_pairs(part, TOP, d_marks)
        else:
            dk[rows, :] = jnp.where(inside, d_keys.astype(BF16), dk[rows, :])
            dval[rows, :] = jnp.where(inside, d_values, dval[rows, :])
            parts[doc - 1] = d_marks

    for_docs(info, total, body)
    padded_rows(halo[0], values, halo[1], pad)
    padded_rows(dhalo[0], dmix, dhalo[1], dpad)
    tap_rows[...] = widened(taps, True)
    tape = bands(tap_rows, group)
    acc[...] = jnp.zeros_like(acc)

    def conv(doc, start, inside):
        zero = jnp.zeros((), BF16)
        rows = pl.ds(start, BLK)
        here = inside[16 : 16 + BLK]
        out = head_rows(dot(tape, jnp.where(inside, dpad[pl.ds(start, TOEP), :], zero)))
        dval[rows, :] = dval[rows, :] + jnp.where(here, out, 0.0)
        window = jnp.where(inside, pad[pl.ds(start, TOEP), :], zero)
        mine = jnp.where(here, dmix[rows, :], zero)
        lanes = lax.broadcasted_iota(jnp.int32, (BLK, GROUP), 1) // LMK
        spread = jnp.concatenate([jnp.where(lanes == i, mine, zero) for i in range(GROUP // LMK)], axis=0)
        acc[:, :TOEP] = acc[:, :TOEP] + dot(spread, window, NT)

    doc_windows(info, total, conv)
    dv[...] = dval[...].astype(BF16)
    rows = lax.broadcasted_iota(jnp.int32, (BLK, BLK), 0)
    lanes = lax.broadcasted_iota(jnp.int32, (BLK, BLK), 1)
    reverse = jnp.where(rows + lanes == BLK - 1, 1.0, 0.0).astype(F32)
    for i in range(GROUP // LMK):
        square = dot(reverse, acc[i * BLK : (i + 1) * BLK, :], precision=HIGHEST)
        turned = pltpu.roll(square, 0, 1, stride=1, stride_axis=0)
        dtaps[0, i : i + 1, :] = jnp.sum(turned, axis=0, keepdims=True)


def back_b(lens, joined, halo, exps, local, stat, sc, along, scs, alongs, qm, qms, taps, dmix, dhalo):
    total, width = dmix.shape
    groups = width // GROUP
    heads = GROUP // LMK
    col = pl.BlockSpec((total, GROUP), lambda g: (0, g))
    mark, marks = LONG_SPEC, SMALL_SPEC
    edge = pl.BlockSpec((2, 16, GROUP), lambda g: (0, 0, g))
    return pl.pallas_call(
        back_b_kernel,
        grid=(groups,),
        in_specs=[
            pl.BlockSpec(memory_space=pltpu.SMEM),
            pl.BlockSpec((total, GROUP), lambda g: (0, groups + g)),
            pl.BlockSpec((total, GROUP), lambda g: (0, 2 * groups + g)),
            edge,
            col,
            pl.BlockSpec((2, LMK + 8, PAIR), lambda g: (g, 0, 0)),
            ROW_SPEC,
            mark,
            ROW_SPEC,
            marks,
            SMALL_ROW_SPEC,
            mark,
            half_spec(0),
            pl.BlockSpec(taps.shape, lambda g: (0, 0)),
            col,
            edge,
        ],
        out_specs=[col, col, mark, marks, pl.BlockSpec((1, heads, 256), lambda g: (g, 0, 0))],
        out_shape=[
            jax.ShapeDtypeStruct((total, width), BF16),
            jax.ShapeDtypeStruct((total, width), BF16),
            jax.ShapeDtypeStruct((PAIRS, LMK, PAIR), F32),
            jax.ShapeDtypeStruct((SMALL, groups, LMK, GROUP), F32),
            jax.ShapeDtypeStruct((groups, heads, 256), F32),
        ],
        scratch_shapes=[VMEM((total + 32, GROUP), BF16), VMEM((total + 32, GROUP), BF16), VMEM((heads * BLK, 256), F32), VMEM((total, GROUP), F32), VMEM((taps.shape[0], 256), F32)],
        compiler_params=pltpu.CompilerParams(vmem_limit_bytes=62 * 2**20),
        name="back_b",
    )(lens, joined, joined, halo, exps, local, stat, sc, along, scs, alongs, qm, qms, taps, dmix, dhalo)


class Ring:
    def __init__(self, count):
        self.count = count
        self.me = lax.axis_index("seq")
        self.row = lax.axis_index("row")
        self.steps = range(1, count)

    def ahead(self, k):
        return lax.rem(self.me + k, self.count)

    def enter(self, others=()):
        barrier = pltpu.get_barrier_semaphore()
        for to in [(self.ahead(k), self.row) for k in self.steps] + list(others):
            pl.semaphore_signal(barrier, inc=1, device_id=to, device_id_type=MESH)
        pl.semaphore_wait(barrier, self.count - 1 + len(others))

    def copy(self, src, dst, send, recv, to):
        return pltpu.make_async_remote_copy(src_ref=src, dst_ref=dst, send_sem=send, recv_sem=recv, device_id=(to, self.row), device_id_type=MESH)

    def scatter(self, pieces, landing, send, recv, first, owners):
        for k in self.steps:
            to = self.ahead(k)

            @pl.when((to >= first) & (to < first + owners))
            def _():
                self.copy(pieces(to - first), landing.at[k - 1], send.at[k - 1], recv.at[k - 1], to).start()

        def arrived():
            for k in self.steps:
                self.copy(pieces(0), landing.at[k - 1], send.at[k - 1], recv.at[k - 1], self.ahead(k)).wait_recv()

        def sent():
            for k in self.steps:
                to = self.ahead(k)

                @pl.when((to >= first) & (to < first + owners))
                def _():
                    self.copy(pieces(to - first), landing.at[k - 1], send.at[k - 1], recv.at[k - 1], to).wait_send()

        return arrived, sent

    def share(self, held, send, recv, first):
        piece = self.me - first
        for k in self.steps:
            self.copy(held.at[piece], held.at[piece], send.at[k - 1], recv.at[piece], self.ahead(k)).start()

    def share_sent(self, held, send, recv, first):
        piece = self.me - first
        for k in self.steps:
            self.copy(held.at[piece], held.at[piece], send.at[k - 1], recv.at[piece], self.ahead(k)).wait_send()

    def shared(self, held, send, recv, first, owners):
        for p in range(owners):

            @pl.when(self.me != first + p)
            def _():
                self.copy(held.at[p], held.at[p], send.at[0], recv.at[p], self.ahead(1)).wait_recv()


    def edges_start(self, here, landing, send, recv):
        @pl.when(self.me > 0)
        def _():
            self.copy(here.at[0], landing.at[1], send.at[0], recv.at[1], self.me - 1).start()

        @pl.when(self.me < self.count - 1)
        def _():
            self.copy(here.at[1], landing.at[0], send.at[1], recv.at[0], self.me + 1).start()

    def edges_wait(self, here, landing, send, recv, out):
        out[...] = jnp.zeros_like(out)

        @pl.when(self.me > 0)
        def _():
            done = self.copy(here.at[0], landing.at[0], send.at[0], recv.at[0], self.me - 1)
            done.wait_recv()
            done.wait_send()
            out[0] = landing[0]

        @pl.when(self.me < self.count - 1)
        def _():
            done = self.copy(here.at[1], landing.at[1], send.at[1], recv.at[1], self.me + 1)
            done.wait_recv()
            done.wait_send()
            out[1] = landing[1]


OWNERS = 8
DMA = pltpu.SemaphoreType.DMA
SAVES = 3 * NS_ITERS + 2
CASES = SMALL * GROUPS
EARLY = 2


def ends(ring):
    return (ring.me == 0) | (ring.me == ring.count - 1)


def owner_of_pair(ring):
    return (ring.me >= 1) & (ring.me <= PAIRS)


def pair_of(ring):
    return jnp.clip(ring.me - 1, 0, PAIRS - 1)


def remote_params(cid):
    return pltpu.CompilerParams(collective_id=cid, has_side_effects=True, vmem_limit_bytes=62 * 2**20)


def in_vmem(n):
    return [pl.BlockSpec(memory_space=VMEM)] * n


ANY_SPEC = pl.BlockSpec(memory_space=pl.ANY)


def small_forward(doc, at, qms, kms, held, invs):
    def save(i, j, value):
        held[at, j, i] = value

    inverse = inverse_forward([qms[doc, g] for g in range(GROUPS)], [kms[doc, g] for g in range(GROUPS)], save, GROUP)
    for g in range(GROUPS):
        invs[at, g] = inverse[g]


def marks_kernel(count, part, counts, edge, small, qm, km, halo, saved, invs, landing, held, hland, sheld, ss, rs, gs, gr, es, er, hs):
    ring = Ring(count)
    ring.enter()
    ring.edges_start(edge, hland, es, er)
    each_ = LMK // OWNERS
    arrived, sent = ring.scatter(lambda o: part.at[pl.ds(pl.multiple_of(o * each_, each_), each_), :], landing, ss, rs, 0, OWNERS)
    keep = [pltpu.make_async_copy(sheld.at[d], saved.at[d], hs.at[d]) for d in range(EARLY)]

    @pl.when(ring.me < OWNERS)
    def _():
        arrived()
        at = pl.ds(pl.multiple_of(ring.me * each_, each_), each_)
        total = part[at, :]
        for k in ring.steps:
            total = total + landing[k - 1]
        total = total / counts[0, at, 0:1]
        half = total.shape[1] // 2
        held[ring.me, 0:each_, :] = total[:, :half].astype(BF16)
        held[ring.me, each_ : 2 * each_, :] = total[:, half:].astype(BF16)
        ring.share(held, gs, gr, 0)

    @pl.when(ends(ring))
    def _():
        @pl.loop(0, EARLY)
        def _(d):
            small_forward(d, d, small.at[0], small.at[1], sheld, invs)

        for copy in keep:
            copy.start()

    ring.shared(held, gs, gr, 0, OWNERS)
    wide = [held[o].astype(F32) for o in range(OWNERS)]
    query = jnp.concatenate([w[:each_] for w in wide], axis=0).astype(BF16)
    key = jnp.concatenate([w[each_:] for w in wide], axis=0).astype(BF16)
    for p in range(PAIRS):
        qm[p] = query[:, p * PAIR : (p + 1) * PAIR]
        km[p] = key[:, p * PAIR : (p + 1) * PAIR]
    ring.edges_wait(edge, hland, es, er, halo)
    sent()

    @pl.when(ring.me < OWNERS)
    def _():
        ring.share_sent(held, gs, gr, 0)

    @pl.when(ends(ring))
    def _():
        for copy in keep:
            copy.wait()


def all_marks(count, part, counts, edge, small):
    width = part.shape[1]
    each_ = LMK // OWNERS
    return pl.pallas_call(
        functools.partial(marks_kernel, count),
        in_specs=in_vmem(4),
        out_specs=in_vmem(3) + [ANY_SPEC] + in_vmem(1),
        out_shape=[jax.ShapeDtypeStruct((PAIRS, LMK, PAIR), BF16)] * 2
        + [
            jax.ShapeDtypeStruct(edge.shape, BF16),
            jax.ShapeDtypeStruct((EARLY, GROUPS, SAVES, LMK, GROUP), F32),
            jax.ShapeDtypeStruct((EARLY, GROUPS, LMK, GROUP), F32),
        ],
        scratch_shapes=[
            VMEM((count - 1, each_, width), F32),
            VMEM((OWNERS, 2 * each_, width // 2), BF16),
            VMEM(edge.shape, BF16),
            VMEM((EARLY, GROUPS, SAVES, LMK, GROUP), F32),
            DMA((count - 1,)),
            DMA((count - 1,)),
            DMA((count - 1,)),
            DMA((OWNERS,)),
            DMA((2,)),
            DMA((2,)),
            DMA((EARLY,)),
        ],
        compiler_params=remote_params(1),
        name="all_marks",
    )(part, counts, edge, small)


def carry_kernel(count, part, qm, km, small, wsm, stsm, invs, car, stat, saved, inv, mixed, cars, saveds, inv2, mixeds, landing, cheld, sheld, sk, ss, rs, cs, cr, ts, tr, hs):
    ring = Ring(count)
    ring.enter()
    arrived, sent = ring.scatter(lambda p: part.at[p], landing, ss, rs, 1, PAIRS)
    keep = pltpu.make_async_copy(sk, saveds, hs.at[0])

    @pl.when(owner_of_pair(ring))
    def _():
        pair = pair_of(ring)

        def save(i, j, value):
            saved[i] = value

        inverse = inverse_forward([qm[pair]], [km[pair]], save, PAIR)[0]
        inv[...] = inverse
        arrived()
        pieces = [part[pair]] + [landing[k - 1] for k in ring.steps]
        top = pieces[0][LMK : LMK + 1]
        for piece in pieces[1:]:
            top = jnp.maximum(top, piece[LMK : LMK + 1])
        weighted = jnp.zeros((LMK, PAIR), F32)
        total = jnp.zeros((1, PAIR), F32)
        for piece in pieces:
            share = jnp.exp(piece[LMK : LMK + 1] - top)
            weighted = weighted + piece[:LMK] * column_of(share, PAIR)
            total = total + piece[LMK + 1 : LMK + 2] * share
        mean = weighted / column_of(total, PAIR)
        mixed[...] = mean
        cheld[pair] = mul(inverse, mean, PAIR).astype(BF16)
        sheld[pair] = jnp.concatenate([top, total, jnp.zeros((6, PAIR), F32)], axis=0)
        ring.share(cheld, cs, cr, 1)
        ring.share(sheld, ts, tr, 1)

    @pl.when(ends(ring))
    def _():
        @pl.loop(0, SMALL - EARLY)
        def _(d):
            small_forward(d + EARLY, d, small.at[0], small.at[1], sk, inv2)

        keep.start()

        def finish(doc, inverse):
            for g in range(GROUPS):
                total = jnp.maximum(stsm[doc, g, 1:2, :], 1e-30)
                mean = wsm[doc, g] / column_of(total, GROUP)
                mixeds[doc, g] = mean
                cars[doc, g] = mul(inverse[g], mean, GROUP).astype(BF16)

        for d in range(SMALL):
            finish(d, [invs[d, g] if d < EARLY else inv2[d - EARLY, g] for g in range(GROUPS)])

    ring.shared(cheld, cs, cr, 1, PAIRS)
    ring.shared(sheld, ts, tr, 1, PAIRS)
    car[...] = cheld[...]
    stat[...] = sheld[...]
    sent()

    @pl.when(owner_of_pair(ring))
    def _():
        ring.share_sent(cheld, cs, cr, 1)
        ring.share_sent(sheld, ts, tr, 1)

    @pl.when(ends(ring))
    def _():
        keep.wait()


def carry(count, part, qm, km, small, wsm, stsm, invs):
    late = SMALL - EARLY
    return pl.pallas_call(
        functools.partial(carry_kernel, count),
        in_specs=in_vmem(7),
        out_specs=in_vmem(6) + [ANY_SPEC] + in_vmem(2),
        out_shape=[
            jax.ShapeDtypeStruct((PAIRS, LMK, PAIR), BF16),
            jax.ShapeDtypeStruct((PAIRS, 8, PAIR), F32),
            jax.ShapeDtypeStruct((SAVES, LMK, PAIR), F32),
            jax.ShapeDtypeStruct((LMK, PAIR), F32),
            jax.ShapeDtypeStruct((LMK, PAIR), F32),
            jax.ShapeDtypeStruct((SMALL, GROUPS, LMK, GROUP), BF16),
            jax.ShapeDtypeStruct((late, GROUPS, SAVES, LMK, GROUP), F32),
            jax.ShapeDtypeStruct((late, GROUPS, LMK, GROUP), F32),
            jax.ShapeDtypeStruct((SMALL, GROUPS, LMK, GROUP), F32),
        ],
        scratch_shapes=[
            VMEM((count - 1, LMK + 8, PAIR), F32),
            VMEM((PAIRS, LMK, PAIR), BF16),
            VMEM((PAIRS, 8, PAIR), F32),
            VMEM((late, GROUPS, SAVES, LMK, GROUP), F32),
            DMA((count - 1,)),
            DMA((count - 1,)),
            DMA((count - 1,)),
            DMA((PAIRS,)),
            DMA((count - 1,)),
            DMA((PAIRS,)),
            DMA((1,)),
        ],
        compiler_params=remote_params(2),
        name="carry",
    )(part, qm, km, small, wsm, stsm, invs)


def spread_grad(d_carried, inverse, mixed, total, width):
    d_mixed = mul(flipped(inverse, width), d_carried, width)
    scaled = (d_mixed / column_of(total, width)).astype(BF16)
    along = row_of(scaled.astype(F32) * mixed, width)
    return scaled, along


def spread_kernel(count, part, stat, inv, mixed, smallf, stsm, invs, inv2, mixeds, edge, sc, along, dtot, scs, alongs, halo, landing, sheld, aheld, hland, ss, rs, cs, cr, ts, tr, es, er):
    ring = Ring(count)
    ring.enter()
    arrived, sent = ring.scatter(lambda p: part.at[p], landing, ss, rs, 1, PAIRS)
    ring.edges_start(edge, hland, es, er)

    @pl.when(owner_of_pair(ring))
    def _():
        pair = pair_of(ring)
        arrived()
        total = part[pair]
        for k in ring.steps:
            total = total + landing[k - 1]
        dtot[...] = total
        scaled, reach = spread_grad(total[:LMK], inv[...], mixed[...], stat[pair, 1:2, :], PAIR)
        sheld[pair] = scaled
        aheld[pair] = reach
        ring.share(sheld, cs, cr, 1)
        ring.share(aheld, ts, tr, 1)

    @pl.when(ends(ring))
    def _():
        for d in range(SMALL):
            for g in range(GROUPS):
                total = jnp.maximum(stsm[d, g, 1:2, :], 1e-30)
                inverse = invs[d, g] if d < EARLY else inv2[d - EARLY, g]
                scaled, reach = spread_grad(smallf[0, d, g], inverse, mixeds[d, g], total, GROUP)
                scs[d, g] = scaled
                alongs[d, g] = reach

    ring.shared(sheld, cs, cr, 1, PAIRS)
    ring.shared(aheld, ts, tr, 1, PAIRS)
    sc[...] = sheld[...]
    along[...] = aheld[...]
    ring.edges_wait(edge, hland, es, er, halo)
    sent()

    @pl.when(owner_of_pair(ring))
    def _():
        ring.share_sent(sheld, cs, cr, 1)
        ring.share_sent(aheld, ts, tr, 1)


def spread(count, part, stat, inv, mixed, smallf, stsm, invs, inv2, mixeds, edge):
    return pl.pallas_call(
        functools.partial(spread_kernel, count),
        in_specs=in_vmem(10),
        out_specs=in_vmem(6),
        out_shape=[
            jax.ShapeDtypeStruct((PAIRS, LMK, PAIR), BF16),
            jax.ShapeDtypeStruct((PAIRS, 8, PAIR), F32),
            jax.ShapeDtypeStruct((2 * LMK, PAIR), F32),
            jax.ShapeDtypeStruct((SMALL, GROUPS, LMK, GROUP), BF16),
            jax.ShapeDtypeStruct((SMALL, GROUPS, 8, GROUP), F32),
            jax.ShapeDtypeStruct(edge.shape, BF16),
        ],
        scratch_shapes=[
            VMEM((count - 1, 2 * LMK, PAIR), F32),
            VMEM((PAIRS, LMK, PAIR), BF16),
            VMEM((PAIRS, 8, PAIR), F32),
            VMEM(edge.shape, BF16),
            DMA((count - 1,)),
            DMA((count - 1,)),
            DMA((count - 1,)),
            DMA((PAIRS,)),
            DMA((count - 1,)),
            DMA((PAIRS,)),
            DMA((2,)),
            DMA((2,)),
        ],
        compiler_params=remote_params(3),
        name="spread",
    )(part, stat, inv, mixed, smallf, stsm, invs, inv2, mixeds, edge)


UNIT = 256
ACROSS = UNIT // 2
TURNS = (0, 1, 3, 5, 7, 9, 11, 13, 14)


class Sums:
    STEPS = 9

    def __init__(self, count, own, out, r0, r1, r2, r3, osem, ss, rs):
        self.count = count
        self.own, self.out, self.r0, self.r1, self.r2, self.r3 = own, out, r0, r1, r2, r3
        self.osem, self.ss, self.rs = osem, ss, rs
        s_ax, r_ax = lax.axis_index("seq"), lax.axis_index("row")
        z, x, y, c = s_ax // 2, lax.rem(s_ax, 2), r_ax // 2, lax.rem(r_ax, 2)
        x1, y1 = x + (1 - c) * (1 - 2 * x), y + c * (1 - 2 * y)
        x2, y2 = x + c * (1 - 2 * x), y + (1 - c) * (1 - 2 * y)
        self.z = z
        self.core = (s_ax, y * 2 + (1 - c))
        self.first = (z * 2 + x1, y1 * 2 + c)
        self.second = (z * 2 + x2, y2 * 2 + c)
        self.line = [(lax.rem(z + k, 4) * 2 + x, r_ax) for k in (1, 2, 3)]
        self.others = [self.core, self.first, self.second] + self.line
        self.b1 = x * (1 - c) + y * c
        self.b2 = y * (1 - c) + x * c
        self.mine, self.theirs = c, 1 - c
        self.fly = (self.core, self.first, self.second) + tuple(self.line) + tuple(self.line) + (self.second, self.first, self.core)

    def rows(self, start, size):
        return pl.ds(pl.multiple_of(start, 16), size)

    def copies(self, u):
        out, line = self.out, [lax.rem(self.z + k, 4) for k in (1, 2, 3)]
        base1, base2 = self.b1 * 384, self.b1 * 384 + self.b2 * 192
        last = self.r2.at[u, self.rows(self.z * 48, 48), :]
        place = out.at[u, self.mine, self.rows(base2 + self.z * 48, 48), :]
        pairs = [
            (self.own.at[u, self.theirs], self.r0.at[u]),
            (self.r0.at[u, self.rows((1 - self.b1) * 384, 384), :], self.r1.at[u]),
            (self.r1.at[u, self.rows((1 - self.b2) * 192, 192), :], self.r2.at[u]),
        ]
        pairs += [(self.r2.at[u, self.rows(line[k] * 48, 48), :], self.r3.at[u, k]) for k in range(3)]
        pairs += [(last, place)] * 3
        for region in (out.at[u, self.mine, self.rows(base2, 192), :], out.at[u, self.mine, self.rows(base1, 384), :], out.at[u, self.mine]):
            pairs.append((region, region))
        return pairs

    def copy(self, u, k):
        src, dst = self.copies(u)[k]
        return pltpu.make_async_remote_copy(src_ref=src, dst_ref=dst, send_sem=self.ss.at[u, k], recv_sem=self.rs.at[u, k], device_id=self.fly[k], device_id_type=MESH)

    def keep(self, u):
        src, dst = self.copies(u)[6]
        return pltpu.make_async_copy(src, dst, self.osem.at[u])

    def add(self, u, here, start, there, size):
        @pl.loop(0, size, step=192)
        def _(t):
            q = self.rows(t, 192)
            here[u, q, :] = (here[u, q, :].astype(F32) + there(self.rows(start + t, 192)).astype(F32)).astype(BF16)

    def advance(self, u, s):
        if s == 0:
            self.copy(u, 0).start()
        elif s == 1:
            self.copy(u, 0).wait_recv()
            self.add(u, self.r0, 0, lambda q: self.own[u, self.mine, q, :], 768)
            self.copy(u, 1).start()
        elif s == 2:
            self.copy(u, 1).wait_recv()
            self.add(u, self.r1, self.b1 * 384, lambda q: self.r0[u, q, :], 384)
            self.copy(u, 2).start()
        elif s == 3:
            self.copy(u, 2).wait_recv()
            self.add(u, self.r2, self.b2 * 192, lambda q: self.r1[u, q, :], 192)
            for k in range(3):
                self.copy(u, 3 + k).start()
        elif s == 4:
            for k in range(3):
                self.copy(u, 3 + k).wait_recv()
            total = self.r2[u, self.rows(self.z * 48, 48), :].astype(F32)
            for k in range(3):
                total = total + self.r3[u, k].astype(F32)
            self.r2[u, self.rows(self.z * 48, 48), :] = total.astype(BF16)
            self.keep(u).start()
            for k in range(3):
                self.copy(u, 6 + k).start()
        elif s == 5:
            for k in range(3):
                self.copy(u, 6 + k).wait_recv()
            self.keep(u).wait()
            self.copy(u, 9).start()
        elif s in (6, 7):
            self.copy(u, s + 3).wait_recv()
            self.copy(u, s + 4).start()
        else:
            self.copy(u, 11).wait_recv()

    def taus(self):
        return self.count + TURNS[-1]

    def step(self, tau, steps):
        for s in steps:
            u = tau - TURNS[s]

            @pl.when((u >= 0) & (u < self.count))
            def _():
                self.advance(jnp.clip(u, 0, self.count - 1), s)

    def finish(self):
        @pl.loop(0, self.count)
        def _(u):
            for k in range(12):
                self.copy(u, k).wait_send()


def small_all(values, smr, sss, srs, sums, k):
    z = sums.z
    s_ax, r_ax = lax.axis_index("seq"), lax.axis_index("row")
    x = lax.rem(s_ax, 2)
    partners = [sums.core, sums.first, sums.second, (lax.rem(z + 2, 4) * 2 + x, r_ax), ((z + 1 - 2 * lax.rem(z, 2)) * 2 + x, r_ax)]

    def copy(i):
        return pltpu.make_async_remote_copy(src_ref=smr.at[i], dst_ref=smr.at[i + 6], send_sem=sss.at[i], recv_sem=srs.at[i], device_id=partners[i], device_id_type=MESH)

    if k == 0:
        terms, taps = values
        smr[0] = jnp.zeros(smr.shape[1:], F32)
        smr[0, 0:4, :] = terms[0:4, :]
        for g in range(GROUPS):
            smr[0, 8:12, g * GROUP : (g + 1) * GROUP] = taps[g]
    else:
        copy(k - 1).wait_recv()
        smr[k] = smr[k - 1] + smr[k + 5]
    if k < 5:
        copy(k).start()
    else:
        for i in range(5):
            copy(i).wait_send()


MARK_TAUS = NS_ITERS * SMALL


def marks_backward(ring, tau, arrived, part, dtot, saved, mixed, qm, km, counts, smallb, smallf, save_a, save_b, mixeds, marks, landing, held, dsums, keep, da, dk, kt, la, lk, lt, cs, cr, hs):
    owner, end = owner_of_pair(ring), ends(ring)
    pair = pair_of(ring)
    last = 3 * NS_ITERS + 1
    doc, turn = jnp.minimum(tau // NS_ITERS, SMALL - 1), lax.rem(tau, NS_ITERS)
    back = NS_ITERS - 1 - turn

    @pl.when(owner & (tau == 0))
    def _():
        la[...] = mul_nt(dtot[:LMK], mixed[...], PAIR)
        lk[...] = jnp.zeros_like(lk)
        lt[...] = flipped(saved[last], PAIR)

    @pl.when(owner & (tau < NS_ITERS))
    def _():
        a, b = backward_step([la[...]], [lk[...]], [lt[...]], [saved[3 * back]], [saved[3 * back + 1]], [saved[3 * back + 2]], PAIR)
        la[...] = a[0]
        lk[...] = b[0]

    @pl.when(owner & (tau == NS_ITERS - 1))
    def _():
        d_scores = backward_end(la[...], lk[...], saved[last], saved[0], PAIR) * 0.125
        d_query = mul(d_scores, km[pair].astype(F32), PAIR)
        d_key = mul(flipped(d_scores, PAIR), qm[pair].astype(F32), PAIR)
        arrived()
        total = part[pair]
        for k in ring.steps:
            total = total + landing[k - 1]
        held[pair, :LMK, :] = ((d_query + total) / counts[0, :, 0:1]).astype(BF16)
        held[pair, LMK:, :] = ((d_key + dtot[LMK:]) / counts[0, :, 0:1]).astype(BF16)
        ring.share(held, cs, cr, 1)

    work = end & (tau < MARK_TAUS)

    @pl.when(work & (turn == 0))
    def _():
        @pl.when(doc < EARLY)
        def _():
            copy = pltpu.make_async_copy(save_a.at[jnp.minimum(doc, EARLY - 1)], keep, hs.at[0])
            copy.start()
            copy.wait()

        @pl.when(doc >= EARLY)
        def _():
            copy = pltpu.make_async_copy(save_b.at[jnp.maximum(doc - EARLY, 0)], keep, hs.at[0])
            copy.start()
            copy.wait()

        for g in range(GROUPS):
            da[g] = mul_nt(smallf[0, doc, g], mixeds[doc, g], GROUP)
            dk[g] = jnp.zeros((LMK, GROUP), F32)
            kt[g] = flipped(keep[g, last], GROUP)

    @pl.when(work)
    def _():
        rows = range(GROUPS)
        iterates = [[keep[g, 3 * back + i] for g in rows] for i in range(3)]
        a, b = backward_step([da[g] for g in rows], [dk[g] for g in rows], [kt[g] for g in rows], *iterates, GROUP)
        for g in rows:
            da[g] = a[g]
            dk[g] = b[g]

    @pl.when(work & (turn == NS_ITERS - 1))
    def _():
        for g in range(GROUPS):
            d_scores = backward_end(da[g], dk[g], keep[g, last], keep[g, 0], GROUP) * 0.125
            d_query = mul(d_scores, marks[1, doc, g].astype(F32), GROUP)
            d_key = mul(flipped(d_scores, GROUP), marks[0, doc, g].astype(F32), GROUP)
            size = counts[1 + doc, :, 0:1]
            dsums[doc, g, :LMK, :] = ((d_query + smallb[doc, g]) / size).astype(BF16)
            dsums[doc, g, LMK:, :] = ((d_key + smallf[1, doc, g]) / size).astype(BF16)


N_MARKS = 13
MARKS_SPECS = in_vmem(9) + [ANY_SPEC] * 2 + in_vmem(2)
N_WORK = 12


def marks_work(count):
    return [
        VMEM((count - 1, LMK, PAIR), F32),
        VMEM((PAIRS, 2 * LMK, PAIR), BF16),
        VMEM((SMALL, GROUPS, 2 * LMK, GROUP), BF16),
        VMEM((GROUPS, SAVES, LMK, GROUP), F32),
        VMEM((GROUPS, LMK, GROUP), F32),
        VMEM((GROUPS, LMK, GROUP), F32),
        VMEM((GROUPS, LMK, GROUP), F32),
        VMEM((LMK, PAIR), F32),
        VMEM((LMK, PAIR), F32),
        VMEM((LMK, PAIR), F32),
        DMA((count - 1,)),
        DMA((PAIRS,)),
        DMA((1,)),
        DMA((count - 1,)),
        DMA((count - 1,)),
    ]


def finish_marks(ring, held, cs, cr, sent):
    sent()

    @pl.when(owner_of_pair(ring))
    def _():
        ring.share_sent(held, cs, cr, 1)


def sums_kernel(count, *refs):
    args, (dsum, dsums_out), work = refs[:N_MARKS], refs[N_MARKS : N_MARKS + 2], refs[N_MARKS + 2 :]
    (landing, held, dsums), rest, (ss, rs) = work[:3], work[3:13], work[13:]
    cs, cr = rest[7], rest[8]
    ring = Ring(count)
    ring.enter()
    arrived, sent = ring.scatter(lambda p: args[0].at[p], landing, ss, rs, 1, PAIRS)
    dsums[...] = jnp.zeros_like(dsums)

    @pl.loop(0, MARK_TAUS)
    def _(tau):
        marks_backward(ring, tau, arrived, *args, landing, held, dsums, *rest)

    ring.shared(held, cs, cr, 1, PAIRS)
    dsum[...] = held[...]
    dsums_out[...] = dsums[...]
    finish_marks(ring, held, cs, cr, sent)


def mark_sums(count, *args):
    shape = jax.ShapeDtypeStruct
    return pl.pallas_call(
        functools.partial(sums_kernel, count),
        in_specs=MARKS_SPECS,
        out_specs=in_vmem(2),
        out_shape=[shape((PAIRS, 2 * LMK, PAIR), BF16), shape((SMALL, GROUPS, 2 * LMK, GROUP), BF16)],
        scratch_shapes=marks_work(count),
        compiler_params=remote_params(4),
        name="mark_sums",
    )(*args)


BLOCKS = 3 * GROUPS


FIRST = (0, 12, 24, 27, 36)


def finale_kernel(count, *refs):
    args, refs = refs[:N_MARKS], refs[N_MARKS:]
    (lens, inputs, dq, dk, dv, w, ddown, act, normed, dup, mixture, dout, *sm), refs = refs[:14], refs[14:]
    (out, dx, osm), refs = refs[:3], refs[3:]
    work, refs = refs[:15], refs[15:]
    (own, r0, r1, r2, r3, dj, flip, left, right, member, table, smr, wide), refs = refs[:13], refs[13:]
    osem, gs, gr, sss, srs, jsem, fsem, bsem, wsem = refs
    (landing, held, dsums), rest, (ss, rs) = work[:3], work[3:13], work[13:]
    cs, cr = rest[7], rest[8]
    total = inputs.shape[0]
    ring = Ring(count)
    before = FIRST[3]
    sums = Sums(FIRST[4], own, out, r0, r1, r2, r3, osem, gs, gr)
    lefts, rights = (ddown, normed, mixture, inputs), (act, dup, dout)

    def fetch_left(i):
        return pltpu.make_async_copy(lefts[i], left, fsem.at[0])

    def fetch_right(i, u):
        columns = pl.ds(pl.multiple_of((u - FIRST[i]) * UNIT, 128), UNIT)
        return pltpu.make_async_copy(rights[i].at[:, columns], right.at[lax.rem(u, 2)], bsem.at[lax.rem(u, 2)])

    fetch_left(0).start()
    fetch_right(0, 0).start()
    joined = [pltpu.make_async_copy(src, dj.at[:, pl.ds(i * GROUPS * GROUP, GROUPS * GROUP)], jsem.at[i]) for i, src in enumerate((dq, dk, dv))]
    for copy in joined:
        copy.start()
    ring.enter(sums.others)
    arrived, sent = ring.scatter(lambda p: args[0].at[p], landing, ss, rs, 1, PAIRS)
    dsums[...] = jnp.zeros_like(dsums)
    weight = pltpu.make_async_copy(w, wide, wsem.at[0])
    weight.start()

    def keep(u, grad):
        own[u, 0] = grad[:, :ACROSS]
        own[u, 1] = grad[:, ACROSS:]

    def make(tau):
        for i in range(4):

            @pl.when(tau == FIRST[i])
            def _():
                fetch_left(i).wait()
                flip[...] = jnp.transpose(left[...])
                if i < 3:
                    fetch_left(i + 1).start()

        for i in range(3):

            @pl.when((tau + 1 >= FIRST[i]) & (tau + 1 < FIRST[i + 1]))
            def _():
                fetch_right(i, jnp.clip(tau + 1, FIRST[i], FIRST[i + 1] - 1)).start()

        @pl.when(tau < before)
        def _():
            u = jnp.minimum(tau, before - 1)
            pltpu.make_async_copy(act.at[:, pl.ds(0, UNIT)], right.at[lax.rem(u, 2)], bsem.at[lax.rem(u, 2)]).wait()
            keep(u, dot(flip[...], right[lax.rem(u, 2)]).astype(BF16))

        @pl.when(tau == before)
        def _():
            ring.shared(held, cs, cr, 1, PAIRS)
            for half in range(2):
                for g in range(GROUPS):
                    at = slice(half * LMK, (half + 1) * LMK)
                    table[half * GROUPS + g, :LMK, :PAIR] = held[2 * g, at, :]
                    table[half * GROUPS + g, :LMK, PAIR:] = held[2 * g + 1, at, :]
                    for d in range(SMALL):
                        table[half * GROUPS + g, (d + 1) * LMK : (d + 2) * LMK, :] = dsums[d, g, at, :]

        @pl.when((tau >= before) & (tau < FIRST[4]))
        def _():
            b = jnp.clip(tau - before, 0, BLOCKS - 1)
            columns = pl.ds(pl.multiple_of(b * GROUP, 128), GROUP)

            @pl.when(b < 2 * GROUPS)
            def _():
                from_marks = dot(member[...], table[jnp.minimum(b, 2 * GROUPS - 1)])
                dj[:, columns] = (dj[:, columns].astype(F32) + from_marks).astype(BF16)

            keep(before + b, dot(flip[...], dj[:, columns]).astype(BF16))

    @pl.loop(0, sums.taus())
    def _(tau):
        sums.step(tau, range(8, 0, -1))
        make(tau)
        sums.step(tau, (0,))
        for k in range(6):

            @pl.when(tau == 4 * k + 3)
            def _():
                small_all(sm, smr, sss, srs, sums, k)

        marks_backward(ring, tau, arrived, *args, landing, held, dsums, *rest)

        @pl.when(tau == MARK_TAUS)
        def _():
            low, high = slot_bounds(lens, total, (1, DOCS * LMK), 1)
            rows = lax.broadcasted_iota(jnp.int32, (total, DOCS * LMK), 0)
            member[...] = jnp.where((rows >= low) & (rows < high), 1.0, 0.0).astype(BF16)
            for copy in joined:
                copy.wait()

        for k in range(GROUPS):

            @pl.when(tau == FIRST[4] + 2 * k + 1)
            def _():
                if k == 0:
                    weight.wait()
                columns = slice(k * GROUP, (k + 1) * GROUP)
                dx[:, columns] = dot(dj[...], wide[columns, :], NT)

    finish_marks(ring, held, cs, cr, sent)
    sums.finish()
    osm[...] = smr[5]


def finale(count, marks_args, lens, inputs, dq, dk, dv, w, ddown, act, normed, dup, mixture, dout, terms, dtaps):
    n = FIRST[4]
    total, depth = inputs.shape
    width = w.shape[1]
    shape = jax.ShapeDtypeStruct
    return pl.pallas_call(
        functools.partial(finale_kernel, count),
        in_specs=MARKS_SPECS + [pl.BlockSpec(memory_space=pltpu.SMEM)] + [ANY_SPEC] * 11 + in_vmem(2),
        out_specs=[ANY_SPEC] + in_vmem(2),
        out_shape=[shape((n, 2, 768, ACROSS), BF16), shape((total, depth), F32), shape((16, depth), F32)],
        scratch_shapes=marks_work(count)
        + [
            VMEM((n, 2, 768, ACROSS), BF16),
            VMEM((n, 768, ACROSS), BF16),
            VMEM((n, 384, ACROSS), BF16),
            VMEM((n, 192, ACROSS), BF16),
            VMEM((n, 3, 48, ACROSS), BF16),
            VMEM((total, width), BF16),
            VMEM((depth, total), BF16),
            VMEM((total, depth), BF16),
            VMEM((2, total, UNIT), BF16),
            VMEM((total, DOCS * LMK), BF16),
            VMEM((2 * GROUPS, DOCS * LMK, GROUP), BF16),
            VMEM((11, 16, depth), F32),
            VMEM(w.shape, BF16),
            DMA((n,)),
            DMA((n, 12)),
            DMA((n, 12)),
            DMA((5,)),
            DMA((5,)),
            DMA((3,)),
            DMA((1,)),
            DMA((2,)),
            DMA((1,)),
        ],
        compiler_params=pltpu.CompilerParams(collective_id=5, has_side_effects=True, vmem_limit_bytes=62 * 2**20),
        name="finale",
    )(*marks_args, lens, inputs, dq, dk, dv, w, ddown, act, normed, dup, mixture, dout, terms, dtaps)


TRIPLE = 3


def widen_kernel(units, dx, residual, little, gd, gu, go, gq, grad, g1, b1, g2, b2, gtaps):
    i = pl.program_id(0)

    @pl.when(i == 0)
    def _():
        for k, ref in enumerate((g1, b1, g2, b2)):
            ref[...] = little[k, :]
        heads = GROUP // LMK
        for h in range(gtaps.shape[0]):
            row = little[8 + h % heads : 9 + h % heads, h // heads * GROUP : (h // heads + 1) * GROUP]
            gtaps[h : h + 1, :] = pltpu.roll(row, GROUP - BLK + 1, 1)[:, : gtaps.shape[1]]

    value = [jnp.concatenate([units[k, 0], units[k, 1]], axis=1).astype(F32) for k in range(TRIPLE)]

    @pl.when(i < 4)
    def _():
        for k in range(TRIPLE):
            gd[k * UNIT : (k + 1) * UNIT, :] = jnp.transpose(value[k])

    for ref, first, end in ((gu, 4, 8), (go, 8, 9), (gq, 9, 12)):

        @pl.when((i >= first) & (i < end))
        def _():
            for k in range(TRIPLE):
                ref[:, k * UNIT : (k + 1) * UNIT] = value[k]

    @pl.when(i < 8)
    def _():
        grad[...] = residual[...] + dx[...]


def widen(units, dx, residual, little, taps):
    n, _, side, half = units.shape
    shape = jax.ShapeDtypeStruct
    total, depth = dx.shape

    def place(first, last, down):
        def index(i):
            b = jnp.clip(i, first, last) - first
            return (b, 0) if down else (0, b)

        return pl.BlockSpec((side, side), index)

    part = pl.BlockSpec((total // 8, depth), lambda i: (jnp.minimum(i, 7), 0))
    return pl.pallas_call(
        widen_kernel,
        grid=(n // TRIPLE,),
        in_specs=[pl.BlockSpec((TRIPLE, 2, side, half), lambda i: (i, 0, 0, 0)), part, part, pl.BlockSpec(little.shape, lambda i: (0, 0))],
        out_specs=[place(0, 3, True), place(4, 7, False), place(8, 8, True), place(9, 11, False), part] + [pl.BlockSpec((depth,), lambda i: (0,))] * 4 + [pl.BlockSpec(taps, lambda i: (0, 0))],
        out_shape=[shape((4 * side, side), F32), shape((side, 4 * side), F32), shape((side, side), F32), shape((side, 3 * side), F32), shape(dx.shape, F32)] + [shape((depth,), F32)] * 4 + [shape(taps, F32)],
        compiler_params=pltpu.CompilerParams(vmem_limit_bytes=62 * 2**20),
        name="widen",
    )(units, dx, residual, little)


def member_of(doc_lengths, total):
    low, high = slot_bounds(doc_lengths, total, (1, DOCS * LMK), 1)
    rows = jnp.arange(total, dtype=jnp.int32)[:, None]
    return ((rows >= low) & (rows < high)).astype(BF16)


def over_all(*grads):
    out = []
    for g in grads:
        part = lax.psum_scatter(g.astype(F32).reshape(lax.axis_size(("seq", "row")), -1), ("seq", "row"), scatter_dimension=0, tiled=True)
        out.append(lax.all_gather(part.astype(BF16), ("seq", "row"), axis=0, tiled=True).reshape(g.shape))
    return out


def on_device(
    tokens,
    doc_lengths,
    w_qkv,
    w_out,
    conv_taps,
    norm1_gain,
    norm1_bias,
    w_up,
    w_down,
    norm2_gain,
    norm2_bias,
    cotangent,
):
    model_width = tokens.shape[2]
    head_count, tap_count = conv_taps.shape
    rim = (tap_count - 1) // 2
    count = lax.axis_size("seq")
    wide = count == 8 and lax.axis_size("row") == 4
    inputs = tokens[0]
    joined, slot_sums, small, edge, counts = project(doc_lengths, inputs, w_qkv)
    qm, km, halo, save_a, invs = all_marks(count, slot_sums, counts, edge, small)
    exps, part, wsm, stsm = mix(doc_lengths, joined, qm, small)
    carried, stat, saved, inv, mixed, cars, save_b, inv2, mixeds = carry(count, part, qm, km, small, wsm, stsm, invs)
    kernel_b, mixture_b = attend(doc_lengths, joined, halo, conv_taps, km, carried, small, cars)
    gains = (norm1_gain, norm1_bias, norm2_gain, norm2_bias)
    result, activated, delta_up, delta_down, normed1_b, delta_output, delta_mix, delta_residual1, norm_sums, delta_edge = dense(
        mixture_b, inputs, cotangent[0], gains, w_out, w_up, w_down
    )
    dq, part_f, small_f = back_f(doc_lengths, joined, delta_mix, kernel_b, km, carried, small, cars)
    scaled, along, dtot, scs, alongs, delta_halo = spread(count, part_f, stat, inv, mixed, small_f, stsm, invs, inv2, mixeds, delta_edge)
    dk, dv, part_b, small_b, dtaps = back_b(
        doc_lengths, joined, halo, exps, part, stat, scaled, along, scs, alongs, qm, small, conv_taps, delta_mix, delta_halo
    )
    marks_args = (part_b, dtot, saved, mixed, qm, km, counts, small_b, small_f, save_a, save_b, mixeds, small)
    if wide:
        units, from_joined, tsm = finale(
            count, marks_args, doc_lengths, inputs, dq, dk, dv, w_qkv, delta_down, activated, normed1_b, delta_up, mixture_b, delta_output, norm_sums, dtaps
        )
        total_down, total_up, total_output, total_joined, delta_inputs, *norms, total_taps = widen(units, from_joined, delta_residual1, tsm, conv_taps.shape)
    else:
        dsum, dsums = mark_sums(count, *marks_args)
        long_sums = dsum.reshape(PAIRS, 2, LMK, PAIR).transpose(2, 1, 0, 3).reshape(LMK, 2 * model_width)
        small_sums = dsums.reshape(SMALL, GROUPS, 2, LMK, GROUP).transpose(0, 3, 2, 1, 4).reshape(SMALL * LMK, 2 * model_width)
        from_marks = jnp.dot(member_of(doc_lengths, inputs.shape[0]), jnp.concatenate([long_sums, small_sums], axis=0), preferred_element_type=F32)
        delta_joined = jnp.concatenate([dq, dk, dv], axis=1) + jnp.pad(from_marks, ((0, 0), (0, model_width)))
        delta_joined = delta_joined.astype(BF16)
        grad_down = jnp.dot(activated.T, delta_down, preferred_element_type=F32)
        grad_up = jnp.dot(normed1_b.T, delta_up, preferred_element_type=F32)
        grad_output = jnp.dot(mixture_b.T, delta_output, preferred_element_type=F32)
        grad_joined = jnp.dot(inputs.T, delta_joined, preferred_element_type=F32)
        total_down, total_up, total_output, total_joined = over_all(grad_down, grad_up, grad_output, grad_joined)
        taps = dtaps.reshape(head_count, GROUP)[:, BLK - 1 : BLK - 1 + tap_count]
        norms, total_taps = lax.psum((norm_sums[:4], taps), ("seq", "row"))
        delta_inputs = delta_residual1 + dot(delta_joined, w_qkv, NT)
    return (
        result[None],
        delta_inputs[None],
        total_joined.astype(F32),
        total_output.astype(F32),
        total_taps,
        norms[0],
        norms[1],
        total_up.astype(F32),
        total_down.astype(F32),
        norms[2],
        norms[3],
    )


def solution(mesh):
    return jax.shard_map(
        on_device,
        mesh=mesh,
        in_specs=(
            P("row", "seq", None),
            P("row", None),
            P(),
            P(),
            P(),
            P(),
            P(),
            P(),
            P(),
            P(),
            P(),
            P("row", "seq", None),
        ),
        out_specs=(
            P("row", "seq", None),
            P("row", "seq", None),
            P(),
            P(),
            P(),
            P(),
            P(),
            P(),
            P(),
            P(),
            P(),
        ),
        check_vma=False,
    )
```

```python
import functools

import jax
import jax.numpy as jnp
from jax import lax
from jax.experimental import pallas as pl
from jax.experimental.pallas import tpu as pltpu
from jax.sharding import PartitionSpec as P

MESH = pl.DeviceIdType.MESH

LMK = 64
NS_ITERS = 6
DOCS = 4


HIGHEST = lax.Precision.HIGHEST
EPSILON = 1e-05
BIG_NEGATIVE = -1e30


F32, BF16 = jnp.float32, jnp.bfloat16
GROUP = 256
PAIR = 128
PAIRS = 6
SMALL = DOCS - 1
GROUPS = 3
WINDOW = 256
VMEM = pltpu.VMEM


def dot(a, b, dims=((1,), (0,)), precision=None):
    return lax.dot_general(a, b, (dims, ((), ())), preferred_element_type=F32, precision=precision)


NT, TN = ((1,), (1,)), ((0,), (0,))


def head_mask(width):
    rows = lax.broadcasted_iota(jnp.int32, (width, width), 0)
    lanes = lax.broadcasted_iota(jnp.int32, (width, width), 1)
    return (rows // LMK) == (lanes // LMK)


def blocks_of(side, width):
    tiled = jnp.concatenate([side] * (width // LMK), axis=0)
    return jnp.where(head_mask(width), tiled, jnp.zeros_like(tiled))


def side_of(full, width):
    full = jnp.where(head_mask(width), full, 0.0)
    return sum(full[i * LMK : (i + 1) * LMK] for i in range(width // LMK))


def flipped(side, width):
    return side_of(jnp.transpose(blocks_of(side, width)), width)


def head_ones(width):
    return jnp.where(head_mask(width), 1.0, 0.0).astype(F32)


def column_of(row, width):
    slots = lax.broadcasted_iota(jnp.int32, (LMK, width), 0)
    lanes = lax.broadcasted_iota(jnp.int32, (LMK, width), 1)
    picked = jnp.where(slots == lanes % LMK, jnp.broadcast_to(row, (LMK, width)), 0.0)
    return dot(picked, head_ones(width), precision=HIGHEST)


def row_of(side, width):
    return dot(jnp.ones((8, width), F32), blocks_of(side, width), NT, precision=HIGHEST)


def halves(x):
    high = x.astype(BF16)
    return high, (x - high.astype(F32)).astype(BF16)


def product3(a, b, dims, width):
    high, low = halves(a)
    b_high, b_low = halves(b)
    rows = a.shape[0]
    both = dot(jnp.concatenate([high, low], axis=0), blocks_of(b_high, width), dims)
    return both[:rows] + both[rows:] + dot(high, blocks_of(b_low, width), dims)


def mul(a, b, width):
    return product3(a, b, ((1,), (0,)), width)


def mul_nt(a, b, width):
    return product3(a, b, NT, width)


def each(f, *lists):
    return [f(*items) for items in zip(*lists)]


def side_eye(width):
    slots = lax.broadcasted_iota(jnp.int32, (LMK, width), 0)
    lanes = lax.broadcasted_iota(jnp.int32, (LMK, width), 1)
    return jnp.where(slots == lanes % LMK, 1.0, 0.0).astype(F32)


def head_total(side, width):
    columns = jnp.broadcast_to(jnp.sum(side, axis=0, keepdims=True), (8, width))
    return dot(columns, head_ones(width), precision=HIGHEST)[:1]


def head_max(scores, width):
    out = []
    for i in range(width // PAIR):
        part = scores[:, i * PAIR : (i + 1) * PAIR]
        left = lax.broadcasted_iota(jnp.int32, part.shape, 1) < LMK
        low = jnp.max(jnp.where(left, part, BIG_NEGATIVE), axis=1, keepdims=True)
        high = jnp.max(jnp.where(left, BIG_NEGATIVE, part), axis=1, keepdims=True)
        out.append(jnp.where(left, low, high))
    return out[0] if len(out) == 1 else jnp.concatenate(out, axis=1)


def inverse_forward(qm, km, save, width):
    ones = head_ones(width)

    def begin(q, k):
        scores = dot(q, blocks_of(k, width), NT) * 0.125
        exponent = jnp.exp(scores - head_max(scores, width))
        return exponent / dot(exponent, ones, precision=HIGHEST)

    kernel_a = each(begin, qm, km)
    approx = each(lambda a: flipped(a, width) / head_total(a * a, width), kernel_a)
    eye = side_eye(width)
    for j, a in enumerate(kernel_a):
        save(3 * NS_ITERS + 1, j, a)

    def sweep(i, approx):
        product = each(lambda a, x: mul(a, x, width), kernel_a, approx)
        square = each(lambda p: mul(p, p, width), product)
        cube = each(lambda s, p: mul(s, p, width), square, product)
        poly = each(lambda p, s, c: 3.25 * eye - 3.75 * p + 1.75 * s - 0.25 * c, product, square, cube)
        for j in range(len(approx)):
            save(3 * i, j, approx[j])
            save(3 * i + 1, j, product[j])
            save(3 * i + 2, j, poly[j])
        return tuple(each(lambda x, q: mul(x, q, width), approx, poly))

    approx = lax.fori_loop(0, NS_ITERS, sweep, tuple(approx))
    for j, x in enumerate(approx):
        save(3 * NS_ITERS, j, x)
    return list(approx)


def backward_step(d_approx, d_kernel, kernel_at, approx, product, poly, width):
    product_t = each(lambda p: flipped(p, width), product)
    d_poly = each(lambda x, d: mul(flipped(x, width), d, width), approx, d_approx)
    d_next = each(lambda d, q: mul_nt(d, q, width), d_approx, poly)
    right = each(lambda d, p: mul_nt(d, p, width), d_poly, product)
    left = each(lambda p, d: mul(p, d, width), product_t, d_poly)
    both = each(lambda r, x: r + x, right, left)
    third = each(lambda r, p: mul_nt(r, p, width), right, product)
    fourth = each(lambda p, b: mul(p, b, width), product_t, both)
    d_product = each(lambda d, b, t, f: -3.75 * d + 1.75 * b - 0.25 * (t + f), d_poly, both, third, fourth)
    d_kernel = each(lambda k, d, x: k + mul_nt(d, x, width), d_kernel, d_product, approx)
    d_approx = each(lambda n, a, d: n + mul(a, d, width), d_next, kernel_at, d_product)
    return d_approx, d_kernel


def backward_end(d_approx, d_kernel, kernel_a, first, width):
    scale = head_total(kernel_a * kernel_a, width)
    d_scale = -head_total(d_approx * first, width) / scale
    d_kernel = d_kernel + flipped(d_approx, width) / scale + 2.0 * kernel_a * d_scale
    inner = dot(d_kernel * kernel_a, head_ones(width), precision=HIGHEST)
    return kernel_a * (d_kernel - inner)


def stacked(side):
    return blocks_of(side, GROUP)


def doc_table(lens, total):
    shard_start = lax.axis_index("seq") * total
    lengths = [lens[0, i] for i in range(DOCS)]
    starts = [-shard_start]
    for i in range(DOCS - 1):
        starts.append(starts[i] + lengths[i])
    best, size, start = jnp.int32(0), lengths[0], starts[0]
    for i in range(1, DOCS):
        more = lengths[i] > size
        best, size, start = jnp.where(more, i, best), jnp.where(more, lengths[i], size), jnp.where(more, starts[i], start)
    sizes, begins = [size], [start]
    for i in range(DOCS - 1):
        later = best <= i
        sizes.append(jnp.where(later, lengths[i + 1], lengths[i]))
        begins.append(jnp.where(later, starts[i + 1], starts[i]))
    return sizes, begins


def doc_ranges(lens, total):
    sizes, begins = doc_table(lens, total)
    info = []
    for size, begin in zip(sizes, begins):
        info += [jnp.clip(begin, 0, total), jnp.clip(begin + size, 0, total)]
    return info + [begins[0], begins[0] + sizes[0]]


def slot_bounds(lens, total, shape, axis):
    sizes, begins = doc_table(lens, total)
    slot = lax.broadcasted_iota(jnp.int32, shape, axis)
    doc, within = slot // LMK, slot % LMK
    size, begin = jnp.full(shape, sizes[0]), jnp.full(shape, begins[0])
    for d in range(1, DOCS):
        size, begin = jnp.where(doc == d, sizes[d], size), jnp.where(doc == d, begins[d], begin)
    return begin + (within * size + LMK - 1) // LMK, begin + ((within + 1) * size + LMK - 1) // LMK


def project_kernel(lens, inputs, weight, joined, sums, small, edge, counts):
    total = inputs.shape[0]
    block = pl.program_id(0)
    out = dot(inputs[...], weight[...]).astype(BF16)
    joined[...] = out

    @pl.when(block < 2 * GROUPS)
    def _():
        low, high = slot_bounds(lens, total, (DOCS * LMK, 1), 0)
        rows = lax.broadcasted_iota(jnp.int32, (DOCS * LMK, total), 1)
        member = jnp.where((rows >= low) & (rows < high), 1.0, 0.0).astype(BF16)
        slot_sums = dot(member, out)
        size = (high - low).astype(F32)
        sums[...] = slot_sums[:LMK]
        small[0] = (slot_sums[LMK:] / size[LMK:]).astype(BF16).reshape(SMALL, LMK, GROUP)
        counts[...] = jnp.broadcast_to(size, (DOCS * LMK, PAIR)).reshape(DOCS, LMK, PAIR)

    @pl.when(block >= 2 * GROUPS)
    def _():
        edge[0] = out[:16]
        edge[1] = out[total - 16 :]


def project(lens, inputs, weight):
    total, depth = inputs.shape
    width = weight.shape[1]
    half = 2 * GROUPS - 1

    return pl.pallas_call(
        project_kernel,
        grid=(width // GROUP,),
        in_specs=[
            pl.BlockSpec(memory_space=pltpu.SMEM),
            pl.BlockSpec((total, depth), lambda j: (0, 0)),
            pl.BlockSpec((depth, GROUP), lambda j: (0, j)),
        ],
        out_specs=[
            pl.BlockSpec((total, GROUP), lambda j: (0, j)),
            pl.BlockSpec((LMK, GROUP), lambda j: (0, jnp.minimum(j, half))),
            pl.BlockSpec((1, SMALL, None, LMK, GROUP), lambda j: (jnp.minimum(j, half) // GROUPS, 0, lax.rem(jnp.minimum(j, half), GROUPS), 0, 0)),
            pl.BlockSpec((2, 16, GROUP), lambda j: (0, 0, jnp.maximum(j - 2 * GROUPS, 0))),
            pl.BlockSpec((DOCS, LMK, PAIR), lambda j: (0, 0, 0)),
        ],
        out_shape=[
            jax.ShapeDtypeStruct((total, width), BF16),
            jax.ShapeDtypeStruct((LMK, 2 * GROUPS * GROUP), F32),
            jax.ShapeDtypeStruct((2, SMALL, GROUPS, LMK, GROUP), BF16),
            jax.ShapeDtypeStruct((2, 16, GROUPS * GROUP), BF16),
            jax.ShapeDtypeStruct((DOCS, LMK, PAIR), F32),
        ],
        compiler_params=pltpu.CompilerParams(vmem_limit_bytes=62 * 2**20),
        name="project",
    )(lens, inputs, weight)


def joint(ref):
    return jnp.concatenate([ref[0], ref[1]], axis=1)


def write_pairs(ref, at, value):
    ref[0, at, :] = value[:, :PAIR]
    ref[1, at, :] = value[:, PAIR:]


LONG_SPEC = pl.BlockSpec((2, LMK, PAIR), lambda g: (g, 0, 0))
ROW_SPEC = pl.BlockSpec((2, 8, PAIR), lambda g: (g, 0, 0))
SMALL_SPEC = pl.BlockSpec((SMALL, None, LMK, GROUP), lambda g: (0, g, 0, 0))
SMALL_ROW_SPEC = pl.BlockSpec((SMALL, None, 8, GROUP), lambda g: (0, g, 0, 0))
TOP = slice(0, LMK)


def half_spec(half):
    return pl.BlockSpec((None, SMALL, None, LMK, GROUP), lambda g: (half, 0, g, 0, 0))


def for_docs(info, total, body):
    def inside(doc, size, start):
        rows = lax.broadcasted_iota(jnp.int32, (size, 1), 0) + start
        return (rows >= info[2 * doc]) & (rows < info[2 * doc + 1])

    body(0, total, 0, inside(0, total, 0))
    for doc in range(1, DOCS):
        low, high = info[2 * doc], info[2 * doc + 1]
        start = jnp.minimum(low // 16 * 16, total - WINDOW)

        @pl.when((high > low) & (high - start <= WINDOW))
        def _():
            at = pl.multiple_of(start, 16)
            body(doc, WINDOW, at, inside(doc, WINDOW, at))

        @pl.when(high - start > WINDOW)
        def _():
            body(doc, total, 0, inside(doc, total, 0))


def mix_kernel(lens, keys, values, qm, qms, exps, part, parts, stats):
    info = doc_ranges(lens, exps.shape[0])
    parts[...] = jnp.zeros_like(parts)
    stats[...] = jnp.zeros_like(stats)
    part[...] = jnp.zeros_like(part)

    def body(doc, size, start, inside):
        rows = pl.ds(start, size)
        marks = stacked(joint(qm) if doc == 0 else qms[doc - 1])
        scores = jnp.where(inside, dot(keys[rows, :], marks, NT) * 0.125, BIG_NEGATIVE)
        top = jnp.max(scores, axis=0, keepdims=True)
        wide = jnp.exp(scores - top)
        narrow = wide.astype(BF16)
        weighted = side_of(dot(narrow, values[rows, :], TN), GROUP)
        total = jnp.sum(wide, axis=0, keepdims=True)
        if doc == 0:
            exps[...] = narrow
            write_pairs(part, TOP, weighted)
            write_pairs(part, slice(LMK, LMK + 1), top)
            write_pairs(part, slice(LMK + 1, LMK + 2), total)
        else:
            exps[rows, :] = jnp.where(inside, narrow, exps[rows, :])
            parts[doc - 1] = weighted
            stats[doc - 1, 0:1, :] = top
            stats[doc - 1, 1:2, :] = total

    for_docs(info, exps.shape[0], body)


def mix(lens, joined, qm, qms):
    total, width = joined.shape[0], joined.shape[1] // 3
    groups = width // GROUP
    return pl.pallas_call(
        mix_kernel,
        grid=(groups,),
        in_specs=[
            pl.BlockSpec(memory_space=pltpu.SMEM),
            pl.BlockSpec((total, GROUP), lambda g: (0, groups + g)),
            pl.BlockSpec((total, GROUP), lambda g: (0, 2 * groups + g)),
            LONG_SPEC,
            half_spec(0),
        ],
        out_specs=[
            pl.BlockSpec((total, GROUP), lambda g: (0, g)),
            pl.BlockSpec((2, LMK + 8, PAIR), lambda g: (g, 0, 0)),
            SMALL_SPEC,
            SMALL_ROW_SPEC,
        ],
        out_shape=[
            jax.ShapeDtypeStruct((total, width), BF16),
            jax.ShapeDtypeStruct((PAIRS, LMK + 8, PAIR), F32),
            jax.ShapeDtypeStruct((SMALL, groups, LMK, GROUP), F32),
            jax.ShapeDtypeStruct((SMALL, groups, 8, GROUP), F32),
        ],
        compiler_params=pltpu.CompilerParams(vmem_limit_bytes=62 * 2**20),
        name="mix",
    )(lens, joined, joined, qm, qms)


TOEP = 160
BLK = 128


def widened(taps, backward):
    count = taps.shape[1]
    rows = lax.broadcasted_iota(jnp.int32, (count, 256), 0)
    lanes = lax.broadcasted_iota(jnp.int32, (count, 256), 1)
    place = rows + lanes == count - 1 if backward else rows == lanes
    return dot(taps[...], jnp.where(place, 1.0, 0.0).astype(F32), precision=HIGHEST)


def band(taps):
    wide = jnp.broadcast_to(taps, (BLK, 256))
    return pltpu.roll(wide, 0, 1, stride=1, stride_axis=0)[:, :TOEP].astype(BF16)


def bands(taps, group):
    heads = GROUP // LMK
    return jnp.concatenate([band(taps[pl.ds(group * heads + i, 1), :]) for i in range(heads)], axis=0)


def head_rows(stack):
    lanes = lax.broadcasted_iota(jnp.int32, (BLK, GROUP), 1) // LMK
    out = stack[:BLK]
    for i in range(1, GROUP // LMK):
        out = jnp.where(lanes == i, stack[i * BLK : (i + 1) * BLK], out)
    return out


def padded_rows(before, here, after, pad):
    total = here.shape[0]
    pad[0:16, :] = before
    pad[16 : total + 16, :] = here[...]
    pad[total + 16 : total + 32, :] = after


def doc_windows(info, total, body):
    def member(doc, start):
        rows = lax.broadcasted_iota(jnp.int32, (TOEP, 1), 0) + start - 16
        low, high = (info[8], info[9]) if doc == 0 else (info[2 * doc], info[2 * doc + 1])
        return (rows >= low) & (rows < high)

    for doc in range(DOCS):
        low, high = info[2 * doc], info[2 * doc + 1]

        @pl.loop(low // BLK, jnp.where(high > low, (high + BLK - 1) // BLK, low // BLK))
        def _(b):
            start = pl.multiple_of(b * BLK, BLK)
            body(doc, start, member(doc, start))


def attend_kernel(lens, queries, values, halo, taps, km, car, kms, cars, kern, mixture, pad, att, tap_rows):
    total = queries.shape[0]
    info = doc_ranges(lens, total)
    group = pl.program_id(0)
    ones = head_ones(GROUP).astype(BF16)

    def body(doc, size, start, inside):
        rows = pl.ds(start, size)
        marks = stacked(joint(km) if doc == 0 else kms[doc - 1])
        scores = dot(queries[rows, :], marks, NT) * 0.125
        exponent = jnp.exp(scores - head_max(scores, GROUP))
        kernel = (exponent / dot(exponent.astype(BF16), ones)).astype(BF16)
        carried = stacked(joint(car) if doc == 0 else cars[doc - 1])
        attended = dot(kernel, carried)
        if doc == 0:
            kern[...] = kernel
            att[...] = attended
        else:
            kern[rows, :] = jnp.where(inside, kernel, kern[rows, :])
            att[rows, :] = jnp.where(inside, attended, att[rows, :])

    for_docs(info, total, body)
    padded_rows(halo[0], values, halo[1], pad)
    tap_rows[...] = widened(taps, False)
    tape = bands(tap_rows, group)

    def conv(doc, start, inside):
        window = jnp.where(inside, pad[pl.ds(start, TOEP), :], jnp.zeros((), BF16))
        out = head_rows(dot(tape, window))
        rows = pl.ds(start, BLK)
        here = inside[16 : 16 + BLK]
        new = (att[rows, :] + out).astype(BF16)
        if doc == 0:
            mixture[rows, :] = new
        else:
            mixture[rows, :] = jnp.where(here, new, mixture[rows, :])

    doc_windows(info, total, conv)


def attend(lens, joined, halo, taps, km, car, kms, cars):
    total, width = joined.shape[0], joined.shape[1] // 3
    groups = width // GROUP
    col = pl.BlockSpec((total, GROUP), lambda g: (0, g))
    mark, marks = LONG_SPEC, SMALL_SPEC
    return pl.pallas_call(
        attend_kernel,
        grid=(groups,),
        in_specs=[
            pl.BlockSpec(memory_space=pltpu.SMEM),
            col,
            pl.BlockSpec((total, GROUP), lambda g: (0, 2 * groups + g)),
            pl.BlockSpec((2, 16, GROUP), lambda g: (0, 0, g)),
            pl.BlockSpec(taps.shape, lambda g: (0, 0)),
            mark,
            mark,
            half_spec(1),
            marks,
        ],
        out_specs=[col, col],
        out_shape=[jax.ShapeDtypeStruct((total, width), BF16)] * 2,
        scratch_shapes=[VMEM((total + 32, GROUP), BF16), VMEM((total, GROUP), F32), VMEM((taps.shape[0], 256), F32)],
        compiler_params=pltpu.CompilerParams(vmem_limit_bytes=62 * 2**20),
        name="attend",
    )(lens, joined, joined, halo, taps, km, car, kms, cars)


ROWS = 512
HALF = 256
PART = 1536
DENSE_TERMS = 8


def normalize(x):
    average = jnp.mean(x, axis=-1, keepdims=True)
    centered = x - average
    scale = lax.rsqrt(jnp.mean(centered * centered, axis=-1, keepdims=True) + EPSILON)
    return centered * scale, scale


def normalize_back(grad, gain, unit, scale):
    n = grad * gain
    return scale * (n - jnp.mean(n, axis=-1, keepdims=True) - unit * jnp.mean(n * unit, axis=-1, keepdims=True))


def column_sums(x):
    return jnp.sum(x, axis=0, keepdims=True)


def dense_kernel(mix_ref, inputs, cot, g1, b1, g2, b2, w_out, w_up, w_down, out, act, dup, ddown, normed, dout, dmix, dres, terms, edge, v_out, v_up, v_down, slope, wsem):
    step = pl.program_id(0)
    parts = w_up.shape[1] // PART
    loads = [pltpu.make_async_copy(w_out, v_out, wsem.at[0])]
    for c in range(parts):
        at = pl.ds(c * PART, PART)
        loads.append(pltpu.make_async_copy(w_up.at[:, at], v_up.at[c], wsem.at[1 + 2 * c]))
        loads.append(pltpu.make_async_copy(w_down.at[at, :], v_down.at[c], wsem.at[2 + 2 * c]))

    @pl.when(step == 0)
    def _():
        for load in loads:
            load.start()
        for load in loads:
            load.wait()
        terms[...] = jnp.zeros_like(terms)

    gain1, bias1, gain2, bias2 = (x[...].reshape(1, -1) for x in (g1, b1, g2, b2))

    def chain(half, first):
        r = slice(half * HALF, (half + 1) * HALF)
        unit1, scale1 = normalize(inputs[r, :].astype(F32) + dot(mix_ref[r, :], v_out[...]))
        n1 = unit1 * gain1 + bias1
        n1_low = n1.astype(BF16)
        normed[r, :] = n1_low
        yield
        total = n1
        for c in range(parts):
            at = slice(c * PART, (c + 1) * PART)
            up = dot(n1_low, v_up[c])
            share = 0.5 * (1.0 + lax.erf(up * 0.7071067811865476))
            active = (up * share).astype(BF16)
            act[r, at] = active
            slope[r, at] = share + up * (jnp.exp(-0.5 * up * up) * 0.3989422804014327)
            total = total + dot(active, v_down[c])
        yield
        unit2, scale2 = normalize(total)
        out[r, :] = (unit2 * gain2 + bias2).astype(BF16)
        grad = cot[r, :].astype(F32)
        terms[2:3, :] += column_sums(grad * unit2)
        terms[3:4, :] += column_sums(grad)
        d_total = normalize_back(grad, gain2, unit2, scale2)
        low = d_total.astype(BF16)
        ddown[r, :] = low
        yield
        for c in range(parts):
            at = slice(c * PART, (c + 1) * PART)
            d_up = (dot(low, v_down[c], NT) * slope[r, at]).astype(BF16)
            dup[r, at] = d_up
            d_total = d_total + dot(d_up, v_up[c], NT)
        yield
        terms[0:1, :] += column_sums(d_total * unit1)
        terms[1:2, :] += column_sums(d_total)
        d_first = normalize_back(d_total, gain1, unit1, scale1)
        dres[r, :] = d_first
        low = d_first.astype(BF16)
        dout[r, :] = low
        dmix[r, :] = dot(low, v_out[...], NT).astype(BF16)

    ahead, behind = chain(0, True), chain(1, False)
    next(ahead)
    for _ in range(4):
        next(ahead, None)
        next(behind)
    next(behind, None)

    @pl.when(step == 0)
    def _():
        edge[0] = dmix[:16, :]

    @pl.when(step == pl.num_programs(0) - 1)
    def _():
        edge[1] = dmix[ROWS - 16 :, :]


def dense(mixture, inputs, cot, gains, w_out, w_up, w_down):
    total, width = mixture.shape
    wide = w_up.shape[1]
    parts = wide // PART
    row = pl.BlockSpec((ROWS, width), lambda i: (i, 0))
    long_row = pl.BlockSpec((ROWS, wide), lambda i: (i, 0))
    shape = jax.ShapeDtypeStruct
    return pl.pallas_call(
        dense_kernel,
        grid=(total // ROWS,),
        in_specs=[row, row, row] + [pl.BlockSpec((width,), lambda i: (0,))] * 4 + [pl.BlockSpec(memory_space=pl.ANY)] * 3,
        out_specs=[row, long_row, long_row, row, row, row, row, row]
        + [pl.BlockSpec((DENSE_TERMS, width), lambda i: (0, 0)), pl.BlockSpec((2, 16, width), lambda i: (0, 0, 0))],
        out_shape=[
            shape((total, width), BF16),
            shape((total, wide), BF16),
            shape((total, wide), BF16),
            shape((total, width), BF16),
            shape((total, width), BF16),
            shape((total, width), BF16),
            shape((total, width), BF16),
            shape((total, width), F32),
            shape((DENSE_TERMS, width), F32),
            shape((2, 16, width), BF16),
        ],
        scratch_shapes=[
            VMEM((width, width), BF16),
            VMEM((parts, width, PART), BF16),
            VMEM((parts, PART, width), BF16),
            VMEM((ROWS, wide), F32),
            pltpu.SemaphoreType.DMA((1 + 2 * parts,)),
        ],
        compiler_params=pltpu.CompilerParams(vmem_limit_bytes=62 * 2**20),
        name="dense",
    )(mixture, inputs, cot, *gains, w_out, w_up, w_down)


def back_f_kernel(lens, queries, dmix, kern, km, car, kms, cars, dq, part, parts):
    info = doc_ranges(lens, dq.shape[0])
    parts[...] = jnp.zeros_like(parts)
    ones = head_ones(GROUP).astype(BF16)

    def body(doc, size, start, inside):
        rows = pl.ds(start, size)
        zero = jnp.zeros((), BF16)
        marks = stacked(joint(km) if doc == 0 else kms[doc - 1])
        carried = stacked(joint(car) if doc == 0 else cars[doc - 1])
        datt = dmix[rows, :]
        kernel = jnp.where(inside, kern[rows, :], zero)
        d_carried = side_of(dot(kernel, datt, TN), GROUP)
        d_kernel = dot(datt, carried, NT)
        wide = kernel.astype(F32)
        weighed = wide * d_kernel
        high = weighed.astype(BF16)
        low = (weighed - high.astype(F32)).astype(BF16)
        inner = dot(high, ones) + dot(low, ones)
        d_scores = (weighed - wide * inner).astype(BF16)
        d_queries = dot(d_scores, marks) * 0.125
        d_marks = side_of(dot(d_scores, queries[rows, :], TN), GROUP) * 0.125
        if doc == 0:
            dq[...] = d_queries.astype(BF16)
            write_pairs(part, TOP, d_carried.astype(BF16))
            write_pairs(part, slice(LMK, 2 * LMK), d_marks.astype(BF16))
        else:
            dq[rows, :] = jnp.where(inside, d_queries.astype(BF16), dq[rows, :])
            parts[0, doc - 1] = d_carried
            parts[1, doc - 1] = d_marks

    for_docs(info, dq.shape[0], body)


def back_f(lens, joined, dmix, kern, km, car, kms, cars):
    total, width = dmix.shape
    groups = width // GROUP
    col = pl.BlockSpec((total, GROUP), lambda g: (0, g))
    mark, marks = LONG_SPEC, SMALL_SPEC
    return pl.pallas_call(
        back_f_kernel,
        grid=(groups,),
        in_specs=[pl.BlockSpec(memory_space=pltpu.SMEM), col, col, col, mark, mark, half_spec(1), marks],
        out_specs=[
            col,
            pl.BlockSpec((2, 2 * LMK, PAIR), lambda g: (g, 0, 0)),
            pl.BlockSpec((2, SMALL, None, LMK, GROUP), lambda g: (0, 0, g, 0, 0)),
        ],
        out_shape=[
            jax.ShapeDtypeStruct((total, width), BF16),
            jax.ShapeDtypeStruct((PAIRS, 2 * LMK, PAIR), BF16),
            jax.ShapeDtypeStruct((2, SMALL, groups, LMK, GROUP), F32),
        ],
        compiler_params=pltpu.CompilerParams(vmem_limit_bytes=62 * 2**20),
        name="back_f",
    )(lens, joined, dmix, kern, km, car, kms, cars)


def back_b_kernel(lens, keys, values, halo, exps, local, stat, sc, along, scs, alongs, qm, qms, taps, dmix, dhalo, dk, dv, part, parts, dtaps, pad, dpad, acc, dval, tap_rows):
    total = keys.shape[0]
    info = doc_ranges(lens, total)
    group = pl.program_id(0)
    parts[...] = jnp.zeros_like(parts)

    def body(doc, size, start, inside):
        rows = pl.ds(start, size)
        scaled = stacked(joint(sc) if doc == 0 else scs[doc - 1])
        marks = stacked(joint(qm) if doc == 0 else qms[doc - 1])
        wide = jnp.where(inside, exps[rows, :].astype(F32), 0.0)
        if doc == 0:
            top = jnp.concatenate([local[0, LMK : LMK + 1], local[1, LMK : LMK + 1]], axis=1)
            wide = wide * jnp.exp(top - joint(stat)[0:1, :])
        shift = joint(along)[0:1, :] if doc == 0 else alongs[doc - 1, 0:1, :]
        d_values = dot(wide.astype(BF16), scaled)
        reach = dot(values[rows, :], scaled, NT)
        d_scores = (wide * (reach - shift)).astype(BF16)
        d_keys = dot(d_scores, marks) * 0.125
        d_marks = side_of(dot(d_scores, keys[rows, :], TN), GROUP) * 0.125
        if doc == 0:
            dk[...] = d_keys.astype(BF16)
            dval[...] = d_values
            write_pairs(part, TOP, d_marks)
        else:
            dk[rows, :] = jnp.where(inside, d_keys.astype(BF16), dk[rows, :])
            dval[rows, :] = jnp.where(inside, d_values, dval[rows, :])
            parts[doc - 1] = d_marks

    for_docs(info, total, body)
    padded_rows(halo[0], values, halo[1], pad)
    padded_rows(dhalo[0], dmix, dhalo[1], dpad)
    tap_rows[...] = widened(taps, True)
    tape = bands(tap_rows, group)
    acc[...] = jnp.zeros_like(acc)

    def conv(doc, start, inside):
        zero = jnp.zeros((), BF16)
        rows = pl.ds(start, BLK)
        here = inside[16 : 16 + BLK]
        out = head_rows(dot(tape, jnp.where(inside, dpad[pl.ds(start, TOEP), :], zero)))
        dval[rows, :] = dval[rows, :] + jnp.where(here, out, 0.0)
        window = jnp.where(inside, pad[pl.ds(start, TOEP), :], zero)
        mine = jnp.where(here, dmix[rows, :], zero)
        lanes = lax.broadcasted_iota(jnp.int32, (BLK, GROUP), 1) // LMK
        spread = jnp.concatenate([jnp.where(lanes == i, mine, zero) for i in range(GROUP // LMK)], axis=0)
        acc[:, :TOEP] = acc[:, :TOEP] + dot(spread, window, NT)

    doc_windows(info, total, conv)
    dv[...] = dval[...].astype(BF16)
    rows = lax.broadcasted_iota(jnp.int32, (BLK, BLK), 0)
    lanes = lax.broadcasted_iota(jnp.int32, (BLK, BLK), 1)
    reverse = jnp.where(rows + lanes == BLK - 1, 1.0, 0.0).astype(F32)
    for i in range(GROUP // LMK):
        square = dot(reverse, acc[i * BLK : (i + 1) * BLK, :], precision=HIGHEST)
        turned = pltpu.roll(square, 0, 1, stride=1, stride_axis=0)
        dtaps[0, i : i + 1, :] = jnp.sum(turned, axis=0, keepdims=True)


def back_b(lens, joined, halo, exps, local, stat, sc, along, scs, alongs, qm, qms, taps, dmix, dhalo):
    total, width = dmix.shape
    groups = width // GROUP
    heads = GROUP // LMK
    col = pl.BlockSpec((total, GROUP), lambda g: (0, g))
    mark, marks = LONG_SPEC, SMALL_SPEC
    edge = pl.BlockSpec((2, 16, GROUP), lambda g: (0, 0, g))
    return pl.pallas_call(
        back_b_kernel,
        grid=(groups,),
        in_specs=[
            pl.BlockSpec(memory_space=pltpu.SMEM),
            pl.BlockSpec((total, GROUP), lambda g: (0, groups + g)),
            pl.BlockSpec((total, GROUP), lambda g: (0, 2 * groups + g)),
            edge,
            col,
            pl.BlockSpec((2, LMK + 8, PAIR), lambda g: (g, 0, 0)),
            ROW_SPEC,
            mark,
            ROW_SPEC,
            marks,
            SMALL_ROW_SPEC,
            mark,
            half_spec(0),
            pl.BlockSpec(taps.shape, lambda g: (0, 0)),
            col,
            edge,
        ],
        out_specs=[col, col, mark, marks, pl.BlockSpec((1, heads, 256), lambda g: (g, 0, 0))],
        out_shape=[
            jax.ShapeDtypeStruct((total, width), BF16),
            jax.ShapeDtypeStruct((total, width), BF16),
            jax.ShapeDtypeStruct((PAIRS, LMK, PAIR), F32),
            jax.ShapeDtypeStruct((SMALL, groups, LMK, GROUP), F32),
            jax.ShapeDtypeStruct((groups, heads, 256), F32),
        ],
        scratch_shapes=[VMEM((total + 32, GROUP), BF16), VMEM((total + 32, GROUP), BF16), VMEM((heads * BLK, 256), F32), VMEM((total, GROUP), F32), VMEM((taps.shape[0], 256), F32)],
        compiler_params=pltpu.CompilerParams(vmem_limit_bytes=62 * 2**20),
        name="back_b",
    )(lens, joined, joined, halo, exps, local, stat, sc, along, scs, alongs, qm, qms, taps, dmix, dhalo)


class Ring:
    def __init__(self, count):
        self.count = count
        self.me = lax.axis_index("seq")
        self.row = lax.axis_index("row")
        self.steps = range(1, count)

    def ahead(self, k):
        return lax.rem(self.me + k, self.count)

    def enter(self, others=()):
        barrier = pltpu.get_barrier_semaphore()
        for to in [(self.ahead(k), self.row) for k in self.steps] + list(others):
            pl.semaphore_signal(barrier, inc=1, device_id=to, device_id_type=MESH)
        pl.semaphore_wait(barrier, self.count - 1 + len(others))

    def copy(self, src, dst, send, recv, to):
        return pltpu.make_async_remote_copy(src_ref=src, dst_ref=dst, send_sem=send, recv_sem=recv, device_id=(to, self.row), device_id_type=MESH)

    def scatter(self, pieces, landing, send, recv, first, owners):
        for k in self.steps:
            to = self.ahead(k)

            @pl.when((to >= first) & (to < first + owners))
            def _():
                self.copy(pieces(to - first), landing.at[k - 1], send.at[k - 1], recv.at[k - 1], to).start()

        def arrived():
            for k in self.steps:
                self.copy(pieces(0), landing.at[k - 1], send.at[k - 1], recv.at[k - 1], self.ahead(k)).wait_recv()

        def sent():
            for k in self.steps:
                to = self.ahead(k)

                @pl.when((to >= first) & (to < first + owners))
                def _():
                    self.copy(pieces(to - first), landing.at[k - 1], send.at[k - 1], recv.at[k - 1], to).wait_send()

        return arrived, sent

    def share(self, held, send, recv, first):
        piece = self.me - first
        for k in self.steps:
            self.copy(held.at[piece], held.at[piece], send.at[k - 1], recv.at[piece], self.ahead(k)).start()

    def share_sent(self, held, send, recv, first):
        piece = self.me - first
        for k in self.steps:
            self.copy(held.at[piece], held.at[piece], send.at[k - 1], recv.at[piece], self.ahead(k)).wait_send()

    def shared(self, held, send, recv, first, owners):
        for p in range(owners):

            @pl.when(self.me != first + p)
            def _():
                self.copy(held.at[p], held.at[p], send.at[0], recv.at[p], self.ahead(1)).wait_recv()


    def edges_start(self, here, landing, send, recv):
        @pl.when(self.me > 0)
        def _():
            self.copy(here.at[0], landing.at[1], send.at[0], recv.at[1], self.me - 1).start()

        @pl.when(self.me < self.count - 1)
        def _():
            self.copy(here.at[1], landing.at[0], send.at[1], recv.at[0], self.me + 1).start()

    def edges_wait(self, here, landing, send, recv, out):
        out[...] = jnp.zeros_like(out)

        @pl.when(self.me > 0)
        def _():
            done = self.copy(here.at[0], landing.at[0], send.at[0], recv.at[0], self.me - 1)
            done.wait_recv()
            done.wait_send()
            out[0] = landing[0]

        @pl.when(self.me < self.count - 1)
        def _():
            done = self.copy(here.at[1], landing.at[1], send.at[1], recv.at[1], self.me + 1)
            done.wait_recv()
            done.wait_send()
            out[1] = landing[1]


OWNERS = 8
DMA = pltpu.SemaphoreType.DMA
SAVES = 3 * NS_ITERS + 2
CASES = SMALL * GROUPS
EARLY = 2


def ends(ring):
    return (ring.me == 0) | (ring.me == ring.count - 1)


def owner_of_pair(ring):
    return (ring.me >= 1) & (ring.me <= PAIRS)


def pair_of(ring):
    return jnp.clip(ring.me - 1, 0, PAIRS - 1)


def remote_params(cid):
    return pltpu.CompilerParams(collective_id=cid, has_side_effects=True, vmem_limit_bytes=62 * 2**20)


def in_vmem(n):
    return [pl.BlockSpec(memory_space=VMEM)] * n


ANY_SPEC = pl.BlockSpec(memory_space=pl.ANY)


def small_forward(doc, at, qms, kms, held, invs):
    def save(i, j, value):
        held[at, j, i] = value

    inverse = inverse_forward([qms[doc, g] for g in range(GROUPS)], [kms[doc, g] for g in range(GROUPS)], save, GROUP)
    for g in range(GROUPS):
        invs[at, g] = inverse[g]


def marks_kernel(count, part, counts, edge, small, qm, km, halo, saved, invs, landing, held, hland, sheld, ss, rs, gs, gr, es, er, hs):
    ring = Ring(count)
    ring.enter()
    ring.edges_start(edge, hland, es, er)
    each_ = LMK // OWNERS
    arrived, sent = ring.scatter(lambda o: part.at[pl.ds(pl.multiple_of(o * each_, each_), each_), :], landing, ss, rs, 0, OWNERS)
    keep = [pltpu.make_async_copy(sheld.at[d], saved.at[d], hs.at[d]) for d in range(EARLY)]

    def early(d):
        @pl.when(ends(ring))
        def _():
            small_forward(d, d, small.at[0], small.at[1], sheld, invs)
            keep[d].start()

    early(0)

    @pl.when(ring.me < OWNERS)
    def _():
        arrived()
        at = pl.ds(pl.multiple_of(ring.me * each_, each_), each_)
        total = part[at, :]
        for k in ring.steps:
            total = total + landing[k - 1]
        total = total / counts[0, at, 0:1]
        half = total.shape[1] // 2
        held[ring.me, 0:each_, :] = total[:, :half].astype(BF16)
        held[ring.me, each_ : 2 * each_, :] = total[:, half:].astype(BF16)
        ring.share(held, gs, gr, 0)

    for d in range(1, EARLY):
        early(d)
    ring.shared(held, gs, gr, 0, OWNERS)
    wide = [held[o].astype(F32) for o in range(OWNERS)]
    query = jnp.concatenate([w[:each_] for w in wide], axis=0).astype(BF16)
    key = jnp.concatenate([w[each_:] for w in wide], axis=0).astype(BF16)
    for p in range(PAIRS):
        qm[p] = query[:, p * PAIR : (p + 1) * PAIR]
        km[p] = key[:, p * PAIR : (p + 1) * PAIR]
    ring.edges_wait(edge, hland, es, er, halo)
    sent()

    @pl.when(ring.me < OWNERS)
    def _():
        ring.share_sent(held, gs, gr, 0)

    @pl.when(ends(ring))
    def _():
        for copy in keep:
            copy.wait()


def all_marks(count, part, counts, edge, small):
    width = part.shape[1]
    each_ = LMK // OWNERS
    return pl.pallas_call(
        functools.partial(marks_kernel, count),
        in_specs=in_vmem(4),
        out_specs=in_vmem(3) + [ANY_SPEC] + in_vmem(1),
        out_shape=[jax.ShapeDtypeStruct((PAIRS, LMK, PAIR), BF16)] * 2
        + [
            jax.ShapeDtypeStruct(edge.shape, BF16),
            jax.ShapeDtypeStruct((EARLY, GROUPS, SAVES, LMK, GROUP), F32),
            jax.ShapeDtypeStruct((EARLY, GROUPS, LMK, GROUP), F32),
        ],
        scratch_shapes=[
            VMEM((count - 1, each_, width), F32),
            VMEM((OWNERS, 2 * each_, width // 2), BF16),
            VMEM(edge.shape, BF16),
            VMEM((EARLY, GROUPS, SAVES, LMK, GROUP), F32),
            DMA((count - 1,)),
            DMA((count - 1,)),
            DMA((count - 1,)),
            DMA((OWNERS,)),
            DMA((2,)),
            DMA((2,)),
            DMA((EARLY,)),
        ],
        compiler_params=remote_params(1),
        name="all_marks",
    )(part, counts, edge, small)


def carry_kernel(count, part, qm, km, small, wsm, stsm, invs, car, stat, saved, inv, mixed, cars, saveds, inv2, mixeds, landing, cheld, sheld, sk, ss, rs, cs, cr, ts, tr, hs):
    ring = Ring(count)
    ring.enter()
    arrived, sent = ring.scatter(lambda p: part.at[p], landing, ss, rs, 1, PAIRS)
    keep = pltpu.make_async_copy(sk, saveds, hs.at[0])

    @pl.when(owner_of_pair(ring))
    def _():
        pair = pair_of(ring)

        def save(i, j, value):
            saved[i] = value

        inverse = inverse_forward([qm[pair]], [km[pair]], save, PAIR)[0]
        inv[...] = inverse
        arrived()
        pieces = [part[pair]] + [landing[k - 1] for k in ring.steps]
        top = pieces[0][LMK : LMK + 1]
        for piece in pieces[1:]:
            top = jnp.maximum(top, piece[LMK : LMK + 1])
        weighted = jnp.zeros((LMK, PAIR), F32)
        total = jnp.zeros((1, PAIR), F32)
        for piece in pieces:
            share = jnp.exp(piece[LMK : LMK + 1] - top)
            weighted = weighted + piece[:LMK] * column_of(share, PAIR)
            total = total + piece[LMK + 1 : LMK + 2] * share
        mean = weighted / column_of(total, PAIR)
        mixed[...] = mean
        cheld[pair] = mul(inverse, mean, PAIR).astype(BF16)
        sheld[pair] = jnp.concatenate([top, total, jnp.zeros((6, PAIR), F32)], axis=0)
        ring.share(cheld, cs, cr, 1)
        ring.share(sheld, ts, tr, 1)

    @pl.when(ends(ring))
    def _():
        @pl.loop(0, SMALL - EARLY)
        def _(d):
            small_forward(d + EARLY, d, small.at[0], small.at[1], sk, inv2)

        keep.start()

        def finish(doc, inverse):
            for g in range(GROUPS):
                total = jnp.maximum(stsm[doc, g, 1:2, :], 1e-30)
                mean = wsm[doc, g] / column_of(total, GROUP)
                mixeds[doc, g] = mean
                cars[doc, g] = mul(inverse[g], mean, GROUP).astype(BF16)

        for d in range(SMALL):
            finish(d, [invs[d, g] if d < EARLY else inv2[d - EARLY, g] for g in range(GROUPS)])

    ring.shared(cheld, cs, cr, 1, PAIRS)
    ring.shared(sheld, ts, tr, 1, PAIRS)
    car[...] = cheld[...]
    stat[...] = sheld[...]
    sent()

    @pl.when(owner_of_pair(ring))
    def _():
        ring.share_sent(cheld, cs, cr, 1)
        ring.share_sent(sheld, ts, tr, 1)

    @pl.when(ends(ring))
    def _():
        keep.wait()


def carry(count, part, qm, km, small, wsm, stsm, invs):
    late = SMALL - EARLY
    return pl.pallas_call(
        functools.partial(carry_kernel, count),
        in_specs=in_vmem(7),
        out_specs=in_vmem(6) + [ANY_SPEC] + in_vmem(2),
        out_shape=[
            jax.ShapeDtypeStruct((PAIRS, LMK, PAIR), BF16),
            jax.ShapeDtypeStruct((PAIRS, 8, PAIR), F32),
            jax.ShapeDtypeStruct((SAVES, LMK, PAIR), F32),
            jax.ShapeDtypeStruct((LMK, PAIR), F32),
            jax.ShapeDtypeStruct((LMK, PAIR), F32),
            jax.ShapeDtypeStruct((SMALL, GROUPS, LMK, GROUP), BF16),
            jax.ShapeDtypeStruct((late, GROUPS, SAVES, LMK, GROUP), F32),
            jax.ShapeDtypeStruct((late, GROUPS, LMK, GROUP), F32),
            jax.ShapeDtypeStruct((SMALL, GROUPS, LMK, GROUP), F32),
        ],
        scratch_shapes=[
            VMEM((count - 1, LMK + 8, PAIR), F32),
            VMEM((PAIRS, LMK, PAIR), BF16),
            VMEM((PAIRS, 8, PAIR), F32),
            VMEM((late, GROUPS, SAVES, LMK, GROUP), F32),
            DMA((count - 1,)),
            DMA((count - 1,)),
            DMA((count - 1,)),
            DMA((PAIRS,)),
            DMA((count - 1,)),
            DMA((PAIRS,)),
            DMA((1,)),
        ],
        compiler_params=remote_params(2),
        name="carry",
    )(part, qm, km, small, wsm, stsm, invs)


def spread_grad(d_carried, inverse, mixed, total, width):
    d_mixed = mul(flipped(inverse, width), d_carried, width)
    scaled = (d_mixed / column_of(total, width)).astype(BF16)
    along = row_of(scaled.astype(F32) * mixed, width)
    return scaled, along


def spread_kernel(count, part, stat, inv, mixed, smallf, stsm, invs, inv2, mixeds, edge, sc, along, dtot, scs, alongs, halo, landing, sheld, aheld, hland, ss, rs, cs, cr, ts, tr, es, er):
    ring = Ring(count)
    ring.enter()
    arrived, sent = ring.scatter(lambda p: part.at[p], landing, ss, rs, 1, PAIRS)
    ring.edges_start(edge, hland, es, er)

    @pl.when(owner_of_pair(ring))
    def _():
        pair = pair_of(ring)
        arrived()
        total = part[pair].astype(F32)
        for k in ring.steps:
            total = total + landing[k - 1].astype(F32)
        dtot[...] = total
        scaled, reach = spread_grad(total[:LMK], inv[...], mixed[...], stat[pair, 1:2, :], PAIR)
        sheld[pair] = scaled
        aheld[pair] = reach
        ring.share(sheld, cs, cr, 1)
        ring.share(aheld, ts, tr, 1)

    @pl.when(ends(ring))
    def _():
        for d in range(SMALL):
            for g in range(GROUPS):
                total = jnp.maximum(stsm[d, g, 1:2, :], 1e-30)
                inverse = invs[d, g] if d < EARLY else inv2[d - EARLY, g]
                scaled, reach = spread_grad(smallf[0, d, g], inverse, mixeds[d, g], total, GROUP)
                scs[d, g] = scaled
                alongs[d, g] = reach

    ring.shared(sheld, cs, cr, 1, PAIRS)
    ring.shared(aheld, ts, tr, 1, PAIRS)
    sc[...] = sheld[...]
    along[...] = aheld[...]
    ring.edges_wait(edge, hland, es, er, halo)
    sent()

    @pl.when(owner_of_pair(ring))
    def _():
        ring.share_sent(sheld, cs, cr, 1)
        ring.share_sent(aheld, ts, tr, 1)


def spread(count, part, stat, inv, mixed, smallf, stsm, invs, inv2, mixeds, edge):
    return pl.pallas_call(
        functools.partial(spread_kernel, count),
        in_specs=in_vmem(10),
        out_specs=in_vmem(6),
        out_shape=[
            jax.ShapeDtypeStruct((PAIRS, LMK, PAIR), BF16),
            jax.ShapeDtypeStruct((PAIRS, 8, PAIR), F32),
            jax.ShapeDtypeStruct((2 * LMK, PAIR), F32),
            jax.ShapeDtypeStruct((SMALL, GROUPS, LMK, GROUP), BF16),
            jax.ShapeDtypeStruct((SMALL, GROUPS, 8, GROUP), F32),
            jax.ShapeDtypeStruct(edge.shape, BF16),
        ],
        scratch_shapes=[
            VMEM((count - 1, 2 * LMK, PAIR), BF16),
            VMEM((PAIRS, LMK, PAIR), BF16),
            VMEM((PAIRS, 8, PAIR), F32),
            VMEM(edge.shape, BF16),
            DMA((count - 1,)),
            DMA((count - 1,)),
            DMA((count - 1,)),
            DMA((PAIRS,)),
            DMA((count - 1,)),
            DMA((PAIRS,)),
            DMA((2,)),
            DMA((2,)),
        ],
        compiler_params=remote_params(3),
        name="spread",
    )(part, stat, inv, mixed, smallf, stsm, invs, inv2, mixeds, edge)


UNIT = 256
ACROSS = UNIT // 2
TURNS = (0, 1, 3, 5, 7, 9, 11, 13, 14)


class Sums:
    STEPS = 9

    def __init__(self, count, own, out, r0, r1, r2, r3, osem, ss, rs):
        self.count = count
        self.own, self.out, self.r0, self.r1, self.r2, self.r3 = own, out, r0, r1, r2, r3
        self.osem, self.ss, self.rs = osem, ss, rs
        s_ax, r_ax = lax.axis_index("seq"), lax.axis_index("row")
        z, x, y, c = s_ax // 2, lax.rem(s_ax, 2), r_ax // 2, lax.rem(r_ax, 2)
        x1, y1 = x + (1 - c) * (1 - 2 * x), y + c * (1 - 2 * y)
        x2, y2 = x + c * (1 - 2 * x), y + (1 - c) * (1 - 2 * y)
        self.z = z
        self.core = (s_ax, y * 2 + (1 - c))
        self.first = (z * 2 + x1, y1 * 2 + c)
        self.second = (z * 2 + x2, y2 * 2 + c)
        self.line = [(lax.rem(z + k, 4) * 2 + x, r_ax) for k in (1, 2, 3)]
        self.others = [self.core, self.first, self.second] + self.line
        self.b1 = x * (1 - c) + y * c
        self.b2 = y * (1 - c) + x * c
        self.mine, self.theirs = c, 1 - c
        self.fly = (self.core, self.first, self.second) + tuple(self.line) + tuple(self.line) + (self.second, self.first, self.core)

    def rows(self, start, size):
        return pl.ds(pl.multiple_of(start, 16), size)

    def copies(self, u):
        out, line = self.out, [lax.rem(self.z + k, 4) for k in (1, 2, 3)]
        base1, base2 = self.b1 * 384, self.b1 * 384 + self.b2 * 192
        last = self.r2.at[u, self.rows(self.z * 48, 48), :]
        place = out.at[u, self.mine, self.rows(base2 + self.z * 48, 48), :]
        pairs = [
            (self.own.at[u, self.theirs], self.r0.at[u]),
            (self.r0.at[u, self.rows((1 - self.b1) * 384, 384), :], self.r1.at[u]),
            (self.r1.at[u, self.rows((1 - self.b2) * 192, 192), :], self.r2.at[u]),
        ]
        pairs += [(self.r2.at[u, self.rows(line[k] * 48, 48), :], self.r3.at[u, k]) for k in range(3)]
        pairs += [(last, place)] * 3
        for region in (out.at[u, self.mine, self.rows(base2, 192), :], out.at[u, self.mine, self.rows(base1, 384), :], out.at[u, self.mine]):
            pairs.append((region, region))
        return pairs

    def copy(self, u, k):
        src, dst = self.copies(u)[k]
        return pltpu.make_async_remote_copy(src_ref=src, dst_ref=dst, send_sem=self.ss.at[u, k], recv_sem=self.rs.at[u, k], device_id=self.fly[k], device_id_type=MESH)

    def keep(self, u):
        src, dst = self.copies(u)[6]
        return pltpu.make_async_copy(src, dst, self.osem.at[u])

    def add(self, u, here, start, there, size):
        @pl.loop(0, size, step=192)
        def _(t):
            q = self.rows(t, 192)
            here[u, q, :] = (here[u, q, :].astype(F32) + there(self.rows(start + t, 192)).astype(F32)).astype(BF16)

    def advance(self, u, s):
        if s == 0:
            self.copy(u, 0).start()
        elif s == 1:
            self.copy(u, 0).wait_recv()
            self.add(u, self.r0, 0, lambda q: self.own[u, self.mine, q, :], 768)
            self.copy(u, 1).start()
        elif s == 2:
            self.copy(u, 1).wait_recv()
            self.add(u, self.r1, self.b1 * 384, lambda q: self.r0[u, q, :], 384)
            self.copy(u, 2).start()
        elif s == 3:
            self.copy(u, 2).wait_recv()
            self.add(u, self.r2, self.b2 * 192, lambda q: self.r1[u, q, :], 192)
            for k in range(3):
                self.copy(u, 3 + k).start()
        elif s == 4:
            for k in range(3):
                self.copy(u, 3 + k).wait_recv()
            total = self.r2[u, self.rows(self.z * 48, 48), :].astype(F32)
            for k in range(3):
                total = total + self.r3[u, k].astype(F32)
            self.r2[u, self.rows(self.z * 48, 48), :] = total.astype(BF16)
            self.keep(u).start()
            for k in range(3):
                self.copy(u, 6 + k).start()
        elif s == 5:
            for k in range(3):
                self.copy(u, 6 + k).wait_recv()
            self.keep(u).wait()
            self.copy(u, 9).start()
        elif s in (6, 7):
            self.copy(u, s + 3).wait_recv()
            self.copy(u, s + 4).start()
        else:
            self.copy(u, 11).wait_recv()

    def taus(self):
        return self.count + TURNS[-1]

    def step(self, tau, steps):
        for s in steps:
            u = tau - TURNS[s]

            @pl.when((u >= 0) & (u < self.count))
            def _():
                self.advance(jnp.clip(u, 0, self.count - 1), s)

    def finish(self):
        @pl.loop(0, self.count)
        def _(u):
            for k in range(12):
                self.copy(u, k).wait_send()


def small_all(values, smr, sss, srs, sums, k):
    z = sums.z
    s_ax, r_ax = lax.axis_index("seq"), lax.axis_index("row")
    x = lax.rem(s_ax, 2)
    partners = [sums.core, sums.first, sums.second, (lax.rem(z + 2, 4) * 2 + x, r_ax), ((z + 1 - 2 * lax.rem(z, 2)) * 2 + x, r_ax)]

    def copy(i):
        return pltpu.make_async_remote_copy(src_ref=smr.at[i], dst_ref=smr.at[i + 6], send_sem=sss.at[i], recv_sem=srs.at[i], device_id=partners[i], device_id_type=MESH)

    if k == 0:
        terms, taps = values
        smr[0] = jnp.zeros(smr.shape[1:], F32)
        smr[0, 0:4, :] = terms[0:4, :]
        for g in range(GROUPS):
            smr[0, 8:12, g * GROUP : (g + 1) * GROUP] = taps[g]
    else:
        copy(k - 1).wait_recv()
        smr[k] = smr[k - 1] + smr[k + 5]
    if k < 5:
        copy(k).start()
    else:
        for i in range(5):
            copy(i).wait_send()


MARK_TAUS = NS_ITERS * SMALL


def marks_backward(ring, tau, arrived, part, dtot, saved, mixed, qm, km, counts, smallb, smallf, save_a, save_b, mixeds, marks, landing, held, dsums, keep, da, dk, kt, la, lk, lt, cs, cr, hs):
    owner, end = owner_of_pair(ring), ends(ring)
    pair = pair_of(ring)
    last = 3 * NS_ITERS + 1
    doc, turn = jnp.minimum(tau // NS_ITERS, SMALL - 1), lax.rem(tau, NS_ITERS)
    back = NS_ITERS - 1 - turn

    @pl.when(owner & (tau == 0))
    def _():
        la[...] = mul_nt(dtot[:LMK], mixed[...], PAIR)
        lk[...] = jnp.zeros_like(lk)
        lt[...] = flipped(saved[last], PAIR)

    @pl.when(owner & (tau < NS_ITERS))
    def _():
        a, b = backward_step([la[...]], [lk[...]], [lt[...]], [saved[3 * back]], [saved[3 * back + 1]], [saved[3 * back + 2]], PAIR)
        la[...] = a[0]
        lk[...] = b[0]

    @pl.when(owner & (tau == NS_ITERS - 1))
    def _():
        d_scores = backward_end(la[...], lk[...], saved[last], saved[0], PAIR) * 0.125
        d_query = mul(d_scores, km[pair].astype(F32), PAIR)
        d_key = mul(flipped(d_scores, PAIR), qm[pair].astype(F32), PAIR)
        arrived()
        total = part[pair]
        for k in ring.steps:
            total = total + landing[k - 1]
        held[pair, :LMK, :] = ((d_query + total) / counts[0, :, 0:1]).astype(BF16)
        held[pair, LMK:, :] = ((d_key + dtot[LMK:]) / counts[0, :, 0:1]).astype(BF16)
        ring.share(held, cs, cr, 1)

    work = end & (tau < MARK_TAUS)

    @pl.when(work & (turn == 0))
    def _():
        @pl.when(doc < EARLY)
        def _():
            copy = pltpu.make_async_copy(save_a.at[jnp.minimum(doc, EARLY - 1)], keep, hs.at[0])
            copy.start()
            copy.wait()

        @pl.when(doc >= EARLY)
        def _():
            copy = pltpu.make_async_copy(save_b.at[jnp.maximum(doc - EARLY, 0)], keep, hs.at[0])
            copy.start()
            copy.wait()

        for g in range(GROUPS):
            da[g] = mul_nt(smallf[0, doc, g], mixeds[doc, g], GROUP)
            dk[g] = jnp.zeros((LMK, GROUP), F32)
            kt[g] = flipped(keep[g, last], GROUP)

    @pl.when(work)
    def _():
        rows = range(GROUPS)
        iterates = [[keep[g, 3 * back + i] for g in rows] for i in range(3)]
        a, b = backward_step([da[g] for g in rows], [dk[g] for g in rows], [kt[g] for g in rows], *iterates, GROUP)
        for g in rows:
            da[g] = a[g]
            dk[g] = b[g]

    @pl.when(work & (turn == NS_ITERS - 1))
    def _():
        for g in range(GROUPS):
            d_scores = backward_end(da[g], dk[g], keep[g, last], keep[g, 0], GROUP) * 0.125
            d_query = mul(d_scores, marks[1, doc, g].astype(F32), GROUP)
            d_key = mul(flipped(d_scores, GROUP), marks[0, doc, g].astype(F32), GROUP)
            size = counts[1 + doc, :, 0:1]
            dsums[doc, g, :LMK, :] = ((d_query + smallb[doc, g]) / size).astype(BF16)
            dsums[doc, g, LMK:, :] = ((d_key + smallf[1, doc, g]) / size).astype(BF16)


N_MARKS = 13
MARKS_SPECS = in_vmem(9) + [ANY_SPEC] * 2 + in_vmem(2)
N_WORK = 12


def marks_work(count):
    return [
        VMEM((count - 1, LMK, PAIR), F32),
        VMEM((PAIRS, 2 * LMK, PAIR), BF16),
        VMEM((SMALL, GROUPS, 2 * LMK, GROUP), BF16),
        VMEM((GROUPS, SAVES, LMK, GROUP), F32),
        VMEM((GROUPS, LMK, GROUP), F32),
        VMEM((GROUPS, LMK, GROUP), F32),
        VMEM((GROUPS, LMK, GROUP), F32),
        VMEM((LMK, PAIR), F32),
        VMEM((LMK, PAIR), F32),
        VMEM((LMK, PAIR), F32),
        DMA((count - 1,)),
        DMA((PAIRS,)),
        DMA((1,)),
        DMA((count - 1,)),
        DMA((count - 1,)),
    ]


def finish_marks(ring, held, cs, cr, sent):
    sent()

    @pl.when(owner_of_pair(ring))
    def _():
        ring.share_sent(held, cs, cr, 1)


def sums_kernel(count, *refs):
    args, (dsum, dsums_out), work = refs[:N_MARKS], refs[N_MARKS : N_MARKS + 2], refs[N_MARKS + 2 :]
    (landing, held, dsums), rest, (ss, rs) = work[:3], work[3:13], work[13:]
    cs, cr = rest[7], rest[8]
    ring = Ring(count)
    ring.enter()
    arrived, sent = ring.scatter(lambda p: args[0].at[p], landing, ss, rs, 1, PAIRS)
    dsums[...] = jnp.zeros_like(dsums)

    @pl.loop(0, MARK_TAUS)
    def _(tau):
        marks_backward(ring, tau, arrived, *args, landing, held, dsums, *rest)

    ring.shared(held, cs, cr, 1, PAIRS)
    dsum[...] = held[...]
    dsums_out[...] = dsums[...]
    finish_marks(ring, held, cs, cr, sent)


def mark_sums(count, *args):
    shape = jax.ShapeDtypeStruct
    return pl.pallas_call(
        functools.partial(sums_kernel, count),
        in_specs=MARKS_SPECS,
        out_specs=in_vmem(2),
        out_shape=[shape((PAIRS, 2 * LMK, PAIR), BF16), shape((SMALL, GROUPS, 2 * LMK, GROUP), BF16)],
        scratch_shapes=marks_work(count),
        compiler_params=remote_params(4),
        name="mark_sums",
    )(*args)


BLOCKS = 3 * GROUPS


FIRST = (0, 12, 24, 27, 36)


def finale_kernel(count, *refs):
    args, refs = refs[:N_MARKS], refs[N_MARKS:]
    (lens, inputs, dq, dk, dv, w, ddown, act, normed, dup, mixture, dout, *sm), refs = refs[:14], refs[14:]
    (out, dx, osm), refs = refs[:3], refs[3:]
    work, refs = refs[:15], refs[15:]
    (own, r0, r1, r2, r3, dj, flip, left, right, member, table, smr, wide), refs = refs[:13], refs[13:]
    osem, gs, gr, sss, srs, jsem, fsem, bsem, wsem = refs
    (landing, held, dsums), rest, (ss, rs) = work[:3], work[3:13], work[13:]
    cs, cr = rest[7], rest[8]
    total = inputs.shape[0]
    ring = Ring(count)
    before = FIRST[3]
    sums = Sums(FIRST[4], own, out, r0, r1, r2, r3, osem, gs, gr)
    lefts, rights = (ddown, normed, mixture, inputs), (act, dup, dout)

    def fetch_left(i):
        return pltpu.make_async_copy(lefts[i], left, fsem.at[0])

    def fetch_right(i, u):
        columns = pl.ds(pl.multiple_of((u - FIRST[i]) * UNIT, 128), UNIT)
        return pltpu.make_async_copy(rights[i].at[:, columns], right.at[lax.rem(u, 2)], bsem.at[lax.rem(u, 2)])

    fetch_left(0).start()
    fetch_right(0, 0).start()
    joined = [pltpu.make_async_copy(src, dj.at[:, pl.ds(i * GROUPS * GROUP, GROUPS * GROUP)], jsem.at[i]) for i, src in enumerate((dq, dk, dv))]
    for copy in joined:
        copy.start()
    ring.enter(sums.others)
    arrived, sent = ring.scatter(lambda p: args[0].at[p], landing, ss, rs, 1, PAIRS)
    dsums[...] = jnp.zeros_like(dsums)
    weight = pltpu.make_async_copy(w, wide, wsem.at[0])
    weight.start()

    def keep(u, grad):
        own[u, 0] = grad[:, :ACROSS]
        own[u, 1] = grad[:, ACROSS:]

    def make(tau):
        for i in range(4):

            @pl.when(tau == FIRST[i])
            def _():
                fetch_left(i).wait()
                flip[...] = jnp.transpose(left[...])
                if i < 3:
                    fetch_left(i + 1).start()

        for i in range(3):

            @pl.when((tau + 1 >= FIRST[i]) & (tau + 1 < FIRST[i + 1]))
            def _():
                fetch_right(i, jnp.clip(tau + 1, FIRST[i], FIRST[i + 1] - 1)).start()

        @pl.when(tau < before)
        def _():
            u = jnp.minimum(tau, before - 1)
            pltpu.make_async_copy(act.at[:, pl.ds(0, UNIT)], right.at[lax.rem(u, 2)], bsem.at[lax.rem(u, 2)]).wait()
            keep(u, dot(flip[...], right[lax.rem(u, 2)]).astype(BF16))

        @pl.when(tau == before)
        def _():
            ring.shared(held, cs, cr, 1, PAIRS)
            for half in range(2):
                for g in range(GROUPS):
                    at = slice(half * LMK, (half + 1) * LMK)
                    table[half * GROUPS + g, :LMK, :PAIR] = held[2 * g, at, :]
                    table[half * GROUPS + g, :LMK, PAIR:] = held[2 * g + 1, at, :]
                    for d in range(SMALL):
                        table[half * GROUPS + g, (d + 1) * LMK : (d + 2) * LMK, :] = dsums[d, g, at, :]

        @pl.when((tau >= before) & (tau < FIRST[4]))
        def _():
            b = jnp.clip(tau - before, 0, BLOCKS - 1)
            columns = pl.ds(pl.multiple_of(b * GROUP, 128), GROUP)

            @pl.when(b < 2 * GROUPS)
            def _():
                from_marks = dot(member[...], table[jnp.minimum(b, 2 * GROUPS - 1)])
                dj[:, columns] = (dj[:, columns].astype(F32) + from_marks).astype(BF16)

            keep(before + b, dot(flip[...], dj[:, columns]).astype(BF16))

    @pl.loop(0, sums.taus())
    def _(tau):
        sums.step(tau, range(8, 0, -1))
        make(tau)
        sums.step(tau, (0,))
        for k in range(6):

            @pl.when(tau == 4 * k + 3)
            def _():
                small_all(sm, smr, sss, srs, sums, k)

        marks_backward(ring, tau, arrived, *args, landing, held, dsums, *rest)

        @pl.when(tau == MARK_TAUS)
        def _():
            low, high = slot_bounds(lens, total, (1, DOCS * LMK), 1)
            rows = lax.broadcasted_iota(jnp.int32, (total, DOCS * LMK), 0)
            member[...] = jnp.where((rows >= low) & (rows < high), 1.0, 0.0).astype(BF16)
            for copy in joined:
                copy.wait()

        for k in range(GROUPS):

            @pl.when(tau == FIRST[4] + 2 * k + 1)
            def _():
                if k == 0:
                    weight.wait()
                columns = slice(k * GROUP, (k + 1) * GROUP)
                dx[:, columns] = dot(dj[...], wide[columns, :], NT)

    finish_marks(ring, held, cs, cr, sent)
    sums.finish()
    osm[...] = smr[5]


def finale(count, marks_args, lens, inputs, dq, dk, dv, w, ddown, act, normed, dup, mixture, dout, terms, dtaps):
    n = FIRST[4]
    total, depth = inputs.shape
    width = w.shape[1]
    shape = jax.ShapeDtypeStruct
    return pl.pallas_call(
        functools.partial(finale_kernel, count),
        in_specs=MARKS_SPECS + [pl.BlockSpec(memory_space=pltpu.SMEM)] + [ANY_SPEC] * 11 + in_vmem(2),
        out_specs=[ANY_SPEC] + in_vmem(2),
        out_shape=[shape((n, 2, 768, ACROSS), BF16), shape((total, depth), F32), shape((16, depth), F32)],
        scratch_shapes=marks_work(count)
        + [
            VMEM((n, 2, 768, ACROSS), BF16),
            VMEM((n, 768, ACROSS), BF16),
            VMEM((n, 384, ACROSS), BF16),
            VMEM((n, 192, ACROSS), BF16),
            VMEM((n, 3, 48, ACROSS), BF16),
            VMEM((total, width), BF16),
            VMEM((depth, total), BF16),
            VMEM((total, depth), BF16),
            VMEM((2, total, UNIT), BF16),
            VMEM((total, DOCS * LMK), BF16),
            VMEM((2 * GROUPS, DOCS * LMK, GROUP), BF16),
            VMEM((11, 16, depth), F32),
            VMEM(w.shape, BF16),
            DMA((n,)),
            DMA((n, 12)),
            DMA((n, 12)),
            DMA((5,)),
            DMA((5,)),
            DMA((3,)),
            DMA((1,)),
            DMA((2,)),
            DMA((1,)),
        ],
        compiler_params=pltpu.CompilerParams(collective_id=5, has_side_effects=True, vmem_limit_bytes=62 * 2**20),
        name="finale",
    )(*marks_args, lens, inputs, dq, dk, dv, w, ddown, act, normed, dup, mixture, dout, terms, dtaps)


TRIPLE = 3


def widen_kernel(units, dx, residual, little, gd, gu, go, gq, grad, g1, b1, g2, b2, gtaps):
    i = pl.program_id(0)

    @pl.when(i == 0)
    def _():
        for k, ref in enumerate((g1, b1, g2, b2)):
            ref[...] = little[k, :]
        heads = GROUP // LMK
        for h in range(gtaps.shape[0]):
            row = little[8 + h % heads : 9 + h % heads, h // heads * GROUP : (h // heads + 1) * GROUP]
            gtaps[h : h + 1, :] = pltpu.roll(row, GROUP - BLK + 1, 1)[:, : gtaps.shape[1]]

    value = [jnp.concatenate([units[k, 0], units[k, 1]], axis=1).astype(F32) for k in range(TRIPLE)]

    @pl.when(i < 4)
    def _():
        for k in range(TRIPLE):
            gd[k * UNIT : (k + 1) * UNIT, :] = jnp.transpose(value[k])

    for ref, first, end in ((gu, 4, 8), (go, 8, 9), (gq, 9, 12)):

        @pl.when((i >= first) & (i < end))
        def _():
            for k in range(TRIPLE):
                ref[:, k * UNIT : (k + 1) * UNIT] = value[k]

    @pl.when(i < 8)
    def _():
        grad[...] = residual[...] + dx[...]


def widen(units, dx, residual, little, taps):
    n, _, side, half = units.shape
    shape = jax.ShapeDtypeStruct
    total, depth = dx.shape

    def place(first, last, down):
        def index(i):
            b = jnp.clip(i, first, last) - first
            return (b, 0) if down else (0, b)

        return pl.BlockSpec((side, side), index)

    part = pl.BlockSpec((total // 8, depth), lambda i: (jnp.minimum(i, 7), 0))
    return pl.pallas_call(
        widen_kernel,
        grid=(n // TRIPLE,),
        in_specs=[pl.BlockSpec((TRIPLE, 2, side, half), lambda i: (i, 0, 0, 0)), part, part, pl.BlockSpec(little.shape, lambda i: (0, 0))],
        out_specs=[place(0, 3, True), place(4, 7, False), place(8, 8, True), place(9, 11, False), part] + [pl.BlockSpec((depth,), lambda i: (0,))] * 4 + [pl.BlockSpec(taps, lambda i: (0, 0))],
        out_shape=[shape((4 * side, side), F32), shape((side, 4 * side), F32), shape((side, side), F32), shape((side, 3 * side), F32), shape(dx.shape, F32)] + [shape((depth,), F32)] * 4 + [shape(taps, F32)],
        compiler_params=pltpu.CompilerParams(vmem_limit_bytes=62 * 2**20),
        name="widen",
    )(units, dx, residual, little)


def member_of(doc_lengths, total):
    low, high = slot_bounds(doc_lengths, total, (1, DOCS * LMK), 1)
    rows = jnp.arange(total, dtype=jnp.int32)[:, None]
    return ((rows >= low) & (rows < high)).astype(BF16)


def over_all(*grads):
    out = []
    for g in grads:
        part = lax.psum_scatter(g.astype(F32).reshape(lax.axis_size(("seq", "row")), -1), ("seq", "row"), scatter_dimension=0, tiled=True)
        out.append(lax.all_gather(part.astype(BF16), ("seq", "row"), axis=0, tiled=True).reshape(g.shape))
    return out


def on_device(
    tokens,
    doc_lengths,
    w_qkv,
    w_out,
    conv_taps,
    norm1_gain,
    norm1_bias,
    w_up,
    w_down,
    norm2_gain,
    norm2_bias,
    cotangent,
):
    model_width = tokens.shape[2]
    head_count, tap_count = conv_taps.shape
    rim = (tap_count - 1) // 2
    count = lax.axis_size("seq")
    wide = count == 8 and lax.axis_size("row") == 4
    inputs = tokens[0]
    joined, slot_sums, small, edge, counts = project(doc_lengths, inputs, w_qkv)
    qm, km, halo, save_a, invs = all_marks(count, slot_sums, counts, edge, small)
    exps, part, wsm, stsm = mix(doc_lengths, joined, qm, small)
    carried, stat, saved, inv, mixed, cars, save_b, inv2, mixeds = carry(count, part, qm, km, small, wsm, stsm, invs)
    kernel_b, mixture_b = attend(doc_lengths, joined, halo, conv_taps, km, carried, small, cars)
    gains = (norm1_gain, norm1_bias, norm2_gain, norm2_bias)
    result, activated, delta_up, delta_down, normed1_b, delta_output, delta_mix, delta_residual1, norm_sums, delta_edge = dense(
        mixture_b, inputs, cotangent[0], gains, w_out, w_up, w_down
    )
    dq, part_f, small_f = back_f(doc_lengths, joined, delta_mix, kernel_b, km, carried, small, cars)
    scaled, along, dtot, scs, alongs, delta_halo = spread(count, part_f, stat, inv, mixed, small_f, stsm, invs, inv2, mixeds, delta_edge)
    dk, dv, part_b, small_b, dtaps = back_b(
        doc_lengths, joined, halo, exps, part, stat, scaled, along, scs, alongs, qm, small, conv_taps, delta_mix, delta_halo
    )
    marks_args = (part_b, dtot, saved, mixed, qm, km, counts, small_b, small_f, save_a, save_b, mixeds, small)
    if wide:
        units, from_joined, tsm = finale(
            count, marks_args, doc_lengths, inputs, dq, dk, dv, w_qkv, delta_down, activated, normed1_b, delta_up, mixture_b, delta_output, norm_sums, dtaps
        )
        total_down, total_up, total_output, total_joined, delta_inputs, *norms, total_taps = widen(units, from_joined, delta_residual1, tsm, conv_taps.shape)
    else:
        dsum, dsums = mark_sums(count, *marks_args)
        long_sums = dsum.reshape(PAIRS, 2, LMK, PAIR).transpose(2, 1, 0, 3).reshape(LMK, 2 * model_width)
        small_sums = dsums.reshape(SMALL, GROUPS, 2, LMK, GROUP).transpose(0, 3, 2, 1, 4).reshape(SMALL * LMK, 2 * model_width)
        from_marks = jnp.dot(member_of(doc_lengths, inputs.shape[0]), jnp.concatenate([long_sums, small_sums], axis=0), preferred_element_type=F32)
        delta_joined = jnp.concatenate([dq, dk, dv], axis=1) + jnp.pad(from_marks, ((0, 0), (0, model_width)))
        delta_joined = delta_joined.astype(BF16)
        grad_down = jnp.dot(activated.T, delta_down, preferred_element_type=F32)
        grad_up = jnp.dot(normed1_b.T, delta_up, preferred_element_type=F32)
        grad_output = jnp.dot(mixture_b.T, delta_output, preferred_element_type=F32)
        grad_joined = jnp.dot(inputs.T, delta_joined, preferred_element_type=F32)
        total_down, total_up, total_output, total_joined = over_all(grad_down, grad_up, grad_output, grad_joined)
        taps = dtaps.reshape(head_count, GROUP)[:, BLK - 1 : BLK - 1 + tap_count]
        norms, total_taps = lax.psum((norm_sums[:4], taps), ("seq", "row"))
        delta_inputs = delta_residual1 + dot(delta_joined, w_qkv, NT)
    return (
        result[None],
        delta_inputs[None],
        total_joined.astype(F32),
        total_output.astype(F32),
        total_taps,
        norms[0],
        norms[1],
        total_up.astype(F32),
        total_down.astype(F32),
        norms[2],
        norms[3],
    )


def solution(mesh):
    return jax.shard_map(
        on_device,
        mesh=mesh,
        in_specs=(
            P("row", "seq", None),
            P("row", None),
            P(),
            P(),
            P(),
            P(),
            P(),
            P(),
            P(),
            P(),
            P(),
            P("row", "seq", None),
        ),
        out_specs=(
            P("row", "seq", None),
            P("row", "seq", None),
            P(),
            P(),
            P(),
            P(),
            P(),
            P(),
            P(),
            P(),
            P(),
        ),
        check_vma=False,
    )
```

```python
import functools

import jax
import jax.numpy as jnp
from jax import lax
from jax.experimental import pallas as pl
from jax.experimental.pallas import tpu as pltpu
from jax.sharding import PartitionSpec as P

MESH = pl.DeviceIdType.MESH

LMK = 64
NS_ITERS = 6
DOCS = 4


HIGHEST = lax.Precision.HIGHEST
EPSILON = 1e-05
BIG_NEGATIVE = -1e30


F32, BF16 = jnp.float32, jnp.bfloat16
GROUP = 256
PAIR = 128
PAIRS = 6
SMALL = DOCS - 1
GROUPS = 3
WINDOW = 256
VMEM = pltpu.VMEM


def dot(a, b, dims=((1,), (0,)), precision=None):
    return lax.dot_general(a, b, (dims, ((), ())), preferred_element_type=F32, precision=precision)


NT, TN = ((1,), (1,)), ((0,), (0,))


def head_mask(width):
    rows = lax.broadcasted_iota(jnp.int32, (width, width), 0)
    lanes = lax.broadcasted_iota(jnp.int32, (width, width), 1)
    return (rows // LMK) == (lanes // LMK)


def blocks_of(side, width):
    tiled = jnp.concatenate([side] * (width // LMK), axis=0)
    return jnp.where(head_mask(width), tiled, jnp.zeros_like(tiled))


def side_of(full, width):
    full = jnp.where(head_mask(width), full, 0.0)
    return sum(full[i * LMK : (i + 1) * LMK] for i in range(width // LMK))


def flipped(side, width):
    return side_of(jnp.transpose(blocks_of(side, width)), width)


def head_ones(width):
    return jnp.where(head_mask(width), 1.0, 0.0).astype(F32)


def column_of(row, width):
    slots = lax.broadcasted_iota(jnp.int32, (LMK, width), 0)
    lanes = lax.broadcasted_iota(jnp.int32, (LMK, width), 1)
    picked = jnp.where(slots == lanes % LMK, jnp.broadcast_to(row, (LMK, width)), 0.0)
    return dot(picked, head_ones(width), precision=HIGHEST)


def row_of(side, width):
    return dot(jnp.ones((8, width), F32), blocks_of(side, width), NT, precision=HIGHEST)


def halves(x):
    high = x.astype(BF16)
    return high, (x - high.astype(F32)).astype(BF16)


def product3(a, b, dims, width):
    high, low = halves(a)
    b_high, b_low = halves(b)
    rows = a.shape[0]
    both = dot(jnp.concatenate([high, low], axis=0), blocks_of(b_high, width), dims)
    return both[:rows] + both[rows:] + dot(high, blocks_of(b_low, width), dims)


def mul(a, b, width):
    return product3(a, b, ((1,), (0,)), width)


def mul_nt(a, b, width):
    return product3(a, b, NT, width)


def each(f, *lists):
    return [f(*items) for items in zip(*lists)]


def side_eye(width):
    slots = lax.broadcasted_iota(jnp.int32, (LMK, width), 0)
    lanes = lax.broadcasted_iota(jnp.int32, (LMK, width), 1)
    return jnp.where(slots == lanes % LMK, 1.0, 0.0).astype(F32)


def head_total(side, width):
    columns = jnp.broadcast_to(jnp.sum(side, axis=0, keepdims=True), (8, width))
    return dot(columns, head_ones(width), precision=HIGHEST)[:1]


def head_max(scores, width):
    out = []
    for i in range(width // PAIR):
        part = scores[:, i * PAIR : (i + 1) * PAIR]
        left = lax.broadcasted_iota(jnp.int32, part.shape, 1) < LMK
        low = jnp.max(jnp.where(left, part, BIG_NEGATIVE), axis=1, keepdims=True)
        high = jnp.max(jnp.where(left, BIG_NEGATIVE, part), axis=1, keepdims=True)
        out.append(jnp.where(left, low, high))
    return out[0] if len(out) == 1 else jnp.concatenate(out, axis=1)


def inverse_forward(qm, km, save, width):
    ones = head_ones(width)

    def begin(q, k):
        scores = dot(q, blocks_of(k, width), NT) * 0.125
        exponent = jnp.exp(scores - head_max(scores, width))
        return exponent / dot(exponent, ones, precision=HIGHEST)

    kernel_a = each(begin, qm, km)
    approx = each(lambda a: flipped(a, width) / head_total(a * a, width), kernel_a)
    eye = side_eye(width)
    for j, a in enumerate(kernel_a):
        save(3 * NS_ITERS + 1, j, a)

    def sweep(i, approx):
        product = each(lambda a, x: mul(a, x, width), kernel_a, approx)
        square = each(lambda p: mul(p, p, width), product)
        cube = each(lambda s, p: mul(s, p, width), square, product)
        poly = each(lambda p, s, c: 3.25 * eye - 3.75 * p + 1.75 * s - 0.25 * c, product, square, cube)
        for j in range(len(approx)):
            save(3 * i, j, approx[j])
            save(3 * i + 1, j, product[j])
            save(3 * i + 2, j, poly[j])
        return tuple(each(lambda x, q: mul(x, q, width), approx, poly))

    approx = lax.fori_loop(0, NS_ITERS, sweep, tuple(approx))
    for j, x in enumerate(approx):
        save(3 * NS_ITERS, j, x)
    return list(approx)


def backward_step(d_approx, d_kernel, kernel_at, approx, product, poly, width):
    product_t = each(lambda p: flipped(p, width), product)
    d_poly = each(lambda x, d: mul(flipped(x, width), d, width), approx, d_approx)
    d_next = each(lambda d, q: mul_nt(d, q, width), d_approx, poly)
    right = each(lambda d, p: mul_nt(d, p, width), d_poly, product)
    left = each(lambda p, d: mul(p, d, width), product_t, d_poly)
    both = each(lambda r, x: r + x, right, left)
    third = each(lambda r, p: mul_nt(r, p, width), right, product)
    fourth = each(lambda p, b: mul(p, b, width), product_t, both)
    d_product = each(lambda d, b, t, f: -3.75 * d + 1.75 * b - 0.25 * (t + f), d_poly, both, third, fourth)
    d_kernel = each(lambda k, d, x: k + mul_nt(d, x, width), d_kernel, d_product, approx)
    d_approx = each(lambda n, a, d: n + mul(a, d, width), d_next, kernel_at, d_product)
    return d_approx, d_kernel


def backward_end(d_approx, d_kernel, kernel_a, first, width):
    scale = head_total(kernel_a * kernel_a, width)
    d_scale = -head_total(d_approx * first, width) / scale
    d_kernel = d_kernel + flipped(d_approx, width) / scale + 2.0 * kernel_a * d_scale
    inner = dot(d_kernel * kernel_a, head_ones(width), precision=HIGHEST)
    return kernel_a * (d_kernel - inner)


def stacked(side):
    return blocks_of(side, GROUP)


def doc_table(lens, total):
    shard_start = lax.axis_index("seq") * total
    lengths = [lens[0, i] for i in range(DOCS)]
    starts = [-shard_start]
    for i in range(DOCS - 1):
        starts.append(starts[i] + lengths[i])
    best, size, start = jnp.int32(0), lengths[0], starts[0]
    for i in range(1, DOCS):
        more = lengths[i] > size
        best, size, start = jnp.where(more, i, best), jnp.where(more, lengths[i], size), jnp.where(more, starts[i], start)
    sizes, begins = [size], [start]
    for i in range(DOCS - 1):
        later = best <= i
        sizes.append(jnp.where(later, lengths[i + 1], lengths[i]))
        begins.append(jnp.where(later, starts[i + 1], starts[i]))
    return sizes, begins


def doc_ranges(lens, total):
    sizes, begins = doc_table(lens, total)
    info = []
    for size, begin in zip(sizes, begins):
        info += [jnp.clip(begin, 0, total), jnp.clip(begin + size, 0, total)]
    return info + [begins[0], begins[0] + sizes[0]]


def slot_bounds(lens, total, shape, axis):
    sizes, begins = doc_table(lens, total)
    slot = lax.broadcasted_iota(jnp.int32, shape, axis)
    doc, within = slot // LMK, slot % LMK
    size, begin = jnp.full(shape, sizes[0]), jnp.full(shape, begins[0])
    for d in range(1, DOCS):
        size, begin = jnp.where(doc == d, sizes[d], size), jnp.where(doc == d, begins[d], begin)
    return begin + (within * size + LMK - 1) // LMK, begin + ((within + 1) * size + LMK - 1) // LMK


def project_kernel(lens, inputs, weight, joined, sums, small, edge, counts):
    total = inputs.shape[0]
    block = pl.program_id(0)
    out = dot(inputs[...], weight[...]).astype(BF16)
    joined[...] = out

    @pl.when(block < 2)
    def _():
        low, high = slot_bounds(lens, total, (DOCS * LMK, 1), 0)
        rows = lax.broadcasted_iota(jnp.int32, (DOCS * LMK, total), 1)
        member = jnp.where((rows >= low) & (rows < high), 1.0, 0.0).astype(BF16)
        slot_sums = dot(member, out)
        size = (high - low).astype(F32)
        sums[...] = slot_sums[:LMK]
        marks = (slot_sums[LMK:] / size[LMK:]).astype(BF16)
        for g in range(GROUPS):
            small[0, :, g] = marks[:, g * GROUP : (g + 1) * GROUP].reshape(SMALL, LMK, GROUP)
        counts[...] = jnp.broadcast_to(size, (DOCS * LMK, PAIR)).reshape(DOCS, LMK, PAIR)

    @pl.when(block == 2)
    def _():
        edge[0] = out[:16]
        edge[1] = out[total - 16 :]


def project(lens, inputs, weight):
    total, depth = inputs.shape
    width = weight.shape[1]
    third = GROUPS * GROUP

    return pl.pallas_call(
        project_kernel,
        grid=(width // third,),
        in_specs=[
            pl.BlockSpec(memory_space=pltpu.SMEM),
            pl.BlockSpec((total, depth), lambda j: (0, 0)),
            pl.BlockSpec((depth, third), lambda j: (0, j)),
        ],
        out_specs=[
            pl.BlockSpec((total, third), lambda j: (0, j)),
            pl.BlockSpec((LMK, third), lambda j: (0, jnp.minimum(j, 1))),
            pl.BlockSpec((1, SMALL, GROUPS, LMK, GROUP), lambda j: (jnp.minimum(j, 1), 0, 0, 0, 0)),
            pl.BlockSpec((2, 16, third), lambda j: (0, 0, 0)),
            pl.BlockSpec((DOCS, LMK, PAIR), lambda j: (0, 0, 0)),
        ],
        out_shape=[
            jax.ShapeDtypeStruct((total, width), BF16),
            jax.ShapeDtypeStruct((LMK, 2 * third), F32),
            jax.ShapeDtypeStruct((2, SMALL, GROUPS, LMK, GROUP), BF16),
            jax.ShapeDtypeStruct((2, 16, third), BF16),
            jax.ShapeDtypeStruct((DOCS, LMK, PAIR), F32),
        ],
        compiler_params=pltpu.CompilerParams(vmem_limit_bytes=62 * 2**20),
        name="project",
    )(lens, inputs, weight)


def joint(ref):
    return jnp.concatenate([ref[0], ref[1]], axis=1)


def write_pairs(ref, at, value):
    ref[0, at, :] = value[:, :PAIR]
    ref[1, at, :] = value[:, PAIR:]


LONG_SPEC = pl.BlockSpec((2, LMK, PAIR), lambda g: (g, 0, 0))
ROW_SPEC = pl.BlockSpec((2, 8, PAIR), lambda g: (g, 0, 0))
SMALL_SPEC = pl.BlockSpec((SMALL, None, LMK, GROUP), lambda g: (0, g, 0, 0))
SMALL_ROW_SPEC = pl.BlockSpec((SMALL, None, 8, GROUP), lambda g: (0, g, 0, 0))
TOP = slice(0, LMK)


def half_spec(half):
    return pl.BlockSpec((None, SMALL, None, LMK, GROUP), lambda g: (half, 0, g, 0, 0))


def for_docs(info, total, body):
    def inside(doc, size, start):
        rows = lax.broadcasted_iota(jnp.int32, (size, 1), 0) + start
        return (rows >= info[2 * doc]) & (rows < info[2 * doc + 1])

    body(0, total, 0, inside(0, total, 0))
    for doc in range(1, DOCS):
        low, high = info[2 * doc], info[2 * doc + 1]
        start = jnp.minimum(low // 16 * 16, total - WINDOW)

        @pl.when((high > low) & (high - start <= WINDOW))
        def _():
            at = pl.multiple_of(start, 16)
            body(doc, WINDOW, at, inside(doc, WINDOW, at))

        @pl.when(high - start > WINDOW)
        def _():
            body(doc, total, 0, inside(doc, total, 0))


def mix_kernel(lens, keys, values, qm, qms, exps, part, parts, stats):
    info = doc_ranges(lens, exps.shape[0])
    parts[...] = jnp.zeros_like(parts)
    stats[...] = jnp.zeros_like(stats)
    part[...] = jnp.zeros_like(part)

    def body(doc, size, start, inside):
        rows = pl.ds(start, size)
        marks = stacked(joint(qm) if doc == 0 else qms[doc - 1])
        scores = jnp.where(inside, dot(keys[rows, :], marks, NT) * 0.125, BIG_NEGATIVE)
        top = jnp.max(scores, axis=0, keepdims=True)
        wide = jnp.exp(scores - top)
        narrow = wide.astype(BF16)
        weighted = side_of(dot(narrow, values[rows, :], TN), GROUP)
        total = jnp.sum(wide, axis=0, keepdims=True)
        if doc == 0:
            exps[...] = narrow
            write_pairs(part, TOP, weighted)
            write_pairs(part, slice(LMK, LMK + 1), top)
            write_pairs(part, slice(LMK + 1, LMK + 2), total)
        else:
            exps[rows, :] = jnp.where(inside, narrow, exps[rows, :])
            parts[doc - 1] = weighted
            stats[doc - 1, 0:1, :] = top
            stats[doc - 1, 1:2, :] = total

    for_docs(info, exps.shape[0], body)


def mix(lens, joined, qm, qms):
    total, width = joined.shape[0], joined.shape[1] // 3
    groups = width // GROUP
    return pl.pallas_call(
        mix_kernel,
        grid=(groups,),
        in_specs=[
            pl.BlockSpec(memory_space=pltpu.SMEM),
            pl.BlockSpec((total, GROUP), lambda g: (0, groups + g)),
            pl.BlockSpec((total, GROUP), lambda g: (0, 2 * groups + g)),
            LONG_SPEC,
            half_spec(0),
        ],
        out_specs=[
            pl.BlockSpec((total, GROUP), lambda g: (0, g)),
            pl.BlockSpec((2, LMK + 8, PAIR), lambda g: (g, 0, 0)),
            SMALL_SPEC,
            SMALL_ROW_SPEC,
        ],
        out_shape=[
            jax.ShapeDtypeStruct((total, width), BF16),
            jax.ShapeDtypeStruct((PAIRS, LMK + 8, PAIR), F32),
            jax.ShapeDtypeStruct((SMALL, groups, LMK, GROUP), F32),
            jax.ShapeDtypeStruct((SMALL, groups, 8, GROUP), F32),
        ],
        compiler_params=pltpu.CompilerParams(vmem_limit_bytes=62 * 2**20),
        name="mix",
    )(lens, joined, joined, qm, qms)


TOEP = 160
BLK = 128


def widened(taps, backward):
    count = taps.shape[1]
    rows = lax.broadcasted_iota(jnp.int32, (count, 256), 0)
    lanes = lax.broadcasted_iota(jnp.int32, (count, 256), 1)
    place = rows + lanes == count - 1 if backward else rows == lanes
    return dot(taps[...], jnp.where(place, 1.0, 0.0).astype(F32), precision=HIGHEST)


def band(taps):
    wide = jnp.broadcast_to(taps, (BLK, 256))
    return pltpu.roll(wide, 0, 1, stride=1, stride_axis=0)[:, :TOEP].astype(BF16)


def bands(taps, group):
    heads = GROUP // LMK
    return jnp.concatenate([band(taps[pl.ds(group * heads + i, 1), :]) for i in range(heads)], axis=0)


def head_rows(stack):
    lanes = lax.broadcasted_iota(jnp.int32, (BLK, GROUP), 1) // LMK
    out = stack[:BLK]
    for i in range(1, GROUP // LMK):
        out = jnp.where(lanes == i, stack[i * BLK : (i + 1) * BLK], out)
    return out


def padded_rows(before, here, after, pad):
    total = here.shape[0]
    pad[0:16, :] = before
    pad[16 : total + 16, :] = here[...]
    pad[total + 16 : total + 32, :] = after


def doc_windows(info, total, body):
    def member(doc, start):
        rows = lax.broadcasted_iota(jnp.int32, (TOEP, 1), 0) + start - 16
        low, high = (info[8], info[9]) if doc == 0 else (info[2 * doc], info[2 * doc + 1])
        return (rows >= low) & (rows < high)

    for doc in range(DOCS):
        low, high = info[2 * doc], info[2 * doc + 1]

        @pl.loop(low // BLK, jnp.where(high > low, (high + BLK - 1) // BLK, low // BLK))
        def _(b):
            start = pl.multiple_of(b * BLK, BLK)
            body(doc, start, member(doc, start))


def attend_kernel(lens, queries, values, halo, taps, km, car, kms, cars, kern, mixture, pad, att, tap_rows):
    total = queries.shape[0]
    info = doc_ranges(lens, total)
    group = pl.program_id(0)
    ones = head_ones(GROUP).astype(BF16)

    def body(doc, size, start, inside):
        rows = pl.ds(start, size)
        marks = stacked(joint(km) if doc == 0 else kms[doc - 1])
        scores = dot(queries[rows, :], marks, NT) * 0.125
        exponent = jnp.exp(scores - head_max(scores, GROUP))
        kernel = (exponent / dot(exponent.astype(BF16), ones)).astype(BF16)
        carried = stacked(joint(car) if doc == 0 else cars[doc - 1])
        attended = dot(kernel, carried)
        if doc == 0:
            kern[...] = kernel
            att[...] = attended
        else:
            kern[rows, :] = jnp.where(inside, kernel, kern[rows, :])
            att[rows, :] = jnp.where(inside, attended, att[rows, :])

    for_docs(info, total, body)
    padded_rows(halo[0], values, halo[1], pad)
    tap_rows[...] = widened(taps, False)
    tape = bands(tap_rows, group)

    def conv(doc, start, inside):
        window = jnp.where(inside, pad[pl.ds(start, TOEP), :], jnp.zeros((), BF16))
        out = head_rows(dot(tape, window))
        rows = pl.ds(start, BLK)
        here = inside[16 : 16 + BLK]
        new = (att[rows, :] + out).astype(BF16)
        if doc == 0:
            mixture[rows, :] = new
        else:
            mixture[rows, :] = jnp.where(here, new, mixture[rows, :])

    doc_windows(info, total, conv)


def attend(lens, joined, halo, taps, km, car, kms, cars):
    total, width = joined.shape[0], joined.shape[1] // 3
    groups = width // GROUP
    col = pl.BlockSpec((total, GROUP), lambda g: (0, g))
    mark, marks = LONG_SPEC, SMALL_SPEC
    return pl.pallas_call(
        attend_kernel,
        grid=(groups,),
        in_specs=[
            pl.BlockSpec(memory_space=pltpu.SMEM),
            col,
            pl.BlockSpec((total, GROUP), lambda g: (0, 2 * groups + g)),
            pl.BlockSpec((2, 16, GROUP), lambda g: (0, 0, g)),
            pl.BlockSpec(taps.shape, lambda g: (0, 0)),
            mark,
            mark,
            half_spec(1),
            marks,
        ],
        out_specs=[col, col],
        out_shape=[jax.ShapeDtypeStruct((total, width), BF16)] * 2,
        scratch_shapes=[VMEM((total + 32, GROUP), BF16), VMEM((total, GROUP), F32), VMEM((taps.shape[0], 256), F32)],
        compiler_params=pltpu.CompilerParams(vmem_limit_bytes=62 * 2**20),
        name="attend",
    )(lens, joined, joined, halo, taps, km, car, kms, cars)


ROWS = 512
HALF = 256
PART = 1536
DENSE_TERMS = 8


def normalize(x):
    average = jnp.mean(x, axis=-1, keepdims=True)
    centered = x - average
    scale = lax.rsqrt(jnp.mean(centered * centered, axis=-1, keepdims=True) + EPSILON)
    return centered * scale, scale


def normalize_back(grad, gain, unit, scale):
    n = grad * gain
    return scale * (n - jnp.mean(n, axis=-1, keepdims=True) - unit * jnp.mean(n * unit, axis=-1, keepdims=True))


def column_sums(x):
    return jnp.sum(x, axis=0, keepdims=True)


def dense_kernel(mix_ref, inputs, cot, g1, b1, g2, b2, w_out, w_up, w_down, out, act, dup, ddown, normed, dout, dmix, dres, terms, edge, v_out, v_up, v_down, slope, wsem):
    step = pl.program_id(0)
    parts = w_up.shape[1] // PART
    loads = [pltpu.make_async_copy(w_out, v_out, wsem.at[0])]
    for c in range(parts):
        at = pl.ds(c * PART, PART)
        loads.append(pltpu.make_async_copy(w_up.at[:, at], v_up.at[c], wsem.at[1 + 2 * c]))
        loads.append(pltpu.make_async_copy(w_down.at[at, :], v_down.at[c], wsem.at[2 + 2 * c]))

    @pl.when(step == 0)
    def _():
        for load in loads:
            load.start()
        for load in loads:
            load.wait()
        terms[...] = jnp.zeros_like(terms)

    gain1, bias1, gain2, bias2 = (x[...].reshape(1, -1) for x in (g1, b1, g2, b2))

    def chain(half, first):
        r = slice(half * HALF, (half + 1) * HALF)
        unit1, scale1 = normalize(inputs[r, :].astype(F32) + dot(mix_ref[r, :], v_out[...]))
        n1 = unit1 * gain1 + bias1
        n1_low = n1.astype(BF16)
        normed[r, :] = n1_low
        yield
        total = n1
        for c in range(parts):
            at = slice(c * PART, (c + 1) * PART)
            up = dot(n1_low, v_up[c])
            share = 0.5 * (1.0 + lax.erf(up * 0.7071067811865476))
            active = (up * share).astype(BF16)
            act[r, at] = active
            slope[r, at] = share + up * (jnp.exp(-0.5 * up * up) * 0.3989422804014327)
            total = total + dot(active, v_down[c])
        yield
        unit2, scale2 = normalize(total)
        out[r, :] = (unit2 * gain2 + bias2).astype(BF16)
        grad = cot[r, :].astype(F32)
        terms[2:3, :] += column_sums(grad * unit2)
        terms[3:4, :] += column_sums(grad)
        d_total = normalize_back(grad, gain2, unit2, scale2)
        low = d_total.astype(BF16)
        ddown[r, :] = low
        yield
        for c in range(parts):
            at = slice(c * PART, (c + 1) * PART)
            d_up = (dot(low, v_down[c], NT) * slope[r, at]).astype(BF16)
            dup[r, at] = d_up
            d_total = d_total + dot(d_up, v_up[c], NT)
        yield
        terms[0:1, :] += column_sums(d_total * unit1)
        terms[1:2, :] += column_sums(d_total)
        d_first = normalize_back(d_total, gain1, unit1, scale1)
        dres[r, :] = d_first
        low = d_first.astype(BF16)
        dout[r, :] = low
        dmix[r, :] = dot(low, v_out[...], NT).astype(BF16)

    ahead, behind = chain(0, True), chain(1, False)
    next(ahead)
    for _ in range(4):
        next(ahead, None)
        next(behind)
    next(behind, None)

    @pl.when(step == 0)
    def _():
        edge[0] = dmix[:16, :]

    @pl.when(step == pl.num_programs(0) - 1)
    def _():
        edge[1] = dmix[ROWS - 16 :, :]


def dense(mixture, inputs, cot, gains, w_out, w_up, w_down):
    total, width = mixture.shape
    wide = w_up.shape[1]
    parts = wide // PART
    row = pl.BlockSpec((ROWS, width), lambda i: (i, 0))
    long_row = pl.BlockSpec((ROWS, wide), lambda i: (i, 0))
    shape = jax.ShapeDtypeStruct
    return pl.pallas_call(
        dense_kernel,
        grid=(total // ROWS,),
        in_specs=[row, row, row] + [pl.BlockSpec((width,), lambda i: (0,))] * 4 + [pl.BlockSpec(memory_space=pl.ANY)] * 3,
        out_specs=[row, long_row, long_row, row, row, row, row, row]
        + [pl.BlockSpec((DENSE_TERMS, width), lambda i: (0, 0)), pl.BlockSpec((2, 16, width), lambda i: (0, 0, 0))],
        out_shape=[
            shape((total, width), BF16),
            shape((total, wide), BF16),
            shape((total, wide), BF16),
            shape((total, width), BF16),
            shape((total, width), BF16),
            shape((total, width), BF16),
            shape((total, width), BF16),
            shape((total, width), F32),
            shape((DENSE_TERMS, width), F32),
            shape((2, 16, width), BF16),
        ],
        scratch_shapes=[
            VMEM((width, width), BF16),
            VMEM((parts, width, PART), BF16),
            VMEM((parts, PART, width), BF16),
            VMEM((ROWS, wide), F32),
            pltpu.SemaphoreType.DMA((1 + 2 * parts,)),
        ],
        compiler_params=pltpu.CompilerParams(vmem_limit_bytes=62 * 2**20),
        name="dense",
    )(mixture, inputs, cot, *gains, w_out, w_up, w_down)


def back_f_kernel(lens, queries, dmix, kern, km, car, kms, cars, dq, part, parts):
    info = doc_ranges(lens, dq.shape[0])
    parts[...] = jnp.zeros_like(parts)
    ones = head_ones(GROUP).astype(BF16)

    def body(doc, size, start, inside):
        rows = pl.ds(start, size)
        zero = jnp.zeros((), BF16)
        marks = stacked(joint(km) if doc == 0 else kms[doc - 1])
        carried = stacked(joint(car) if doc == 0 else cars[doc - 1])
        datt = dmix[rows, :]
        kernel = jnp.where(inside, kern[rows, :], zero)
        d_carried = side_of(dot(kernel, datt, TN), GROUP)
        d_kernel = dot(datt, carried, NT)
        wide = kernel.astype(F32)
        weighed = wide * d_kernel
        high = weighed.astype(BF16)
        low = (weighed - high.astype(F32)).astype(BF16)
        inner = dot(high, ones) + dot(low, ones)
        d_scores = (weighed - wide * inner).astype(BF16)
        d_queries = dot(d_scores, marks) * 0.125
        d_marks = side_of(dot(d_scores, queries[rows, :], TN), GROUP) * 0.125
        if doc == 0:
            dq[...] = d_queries.astype(BF16)
            write_pairs(part, TOP, d_carried.astype(BF16))
            write_pairs(part, slice(LMK, 2 * LMK), d_marks.astype(BF16))
        else:
            dq[rows, :] = jnp.where(inside, d_queries.astype(BF16), dq[rows, :])
            parts[0, doc - 1] = d_carried
            parts[1, doc - 1] = d_marks

    for_docs(info, dq.shape[0], body)


def back_f(lens, joined, dmix, kern, km, car, kms, cars):
    total, width = dmix.shape
    groups = width // GROUP
    col = pl.BlockSpec((total, GROUP), lambda g: (0, g))
    mark, marks = LONG_SPEC, SMALL_SPEC
    return pl.pallas_call(
        back_f_kernel,
        grid=(groups,),
        in_specs=[pl.BlockSpec(memory_space=pltpu.SMEM), col, col, col, mark, mark, half_spec(1), marks],
        out_specs=[
            col,
            pl.BlockSpec((2, 2 * LMK, PAIR), lambda g: (g, 0, 0)),
            pl.BlockSpec((2, SMALL, None, LMK, GROUP), lambda g: (0, 0, g, 0, 0)),
        ],
        out_shape=[
            jax.ShapeDtypeStruct((total, width), BF16),
            jax.ShapeDtypeStruct((PAIRS, 2 * LMK, PAIR), BF16),
            jax.ShapeDtypeStruct((2, SMALL, groups, LMK, GROUP), F32),
        ],
        compiler_params=pltpu.CompilerParams(vmem_limit_bytes=62 * 2**20),
        name="back_f",
    )(lens, joined, dmix, kern, km, car, kms, cars)


def back_b_kernel(lens, keys, values, halo, exps, local, stat, sc, along, scs, alongs, qm, qms, taps, dmix, dhalo, dk, dv, part, parts, dtaps, pad, dpad, acc, dval, tap_rows):
    total = keys.shape[0]
    info = doc_ranges(lens, total)
    group = pl.program_id(0)
    parts[...] = jnp.zeros_like(parts)

    def body(doc, size, start, inside):
        rows = pl.ds(start, size)
        scaled = stacked(joint(sc) if doc == 0 else scs[doc - 1])
        marks = stacked(joint(qm) if doc == 0 else qms[doc - 1])
        wide = jnp.where(inside, exps[rows, :].astype(F32), 0.0)
        if doc == 0:
            top = jnp.concatenate([local[0, LMK : LMK + 1], local[1, LMK : LMK + 1]], axis=1)
            wide = wide * jnp.exp(top - joint(stat)[0:1, :])
        shift = joint(along)[0:1, :] if doc == 0 else alongs[doc - 1, 0:1, :]
        d_values = dot(wide.astype(BF16), scaled)
        reach = dot(values[rows, :], scaled, NT)
        d_scores = (wide * (reach - shift)).astype(BF16)
        d_keys = dot(d_scores, marks) * 0.125
        d_marks = side_of(dot(d_scores, keys[rows, :], TN), GROUP) * 0.125
        if doc == 0:
            dk[...] = d_keys.astype(BF16)
            dval[...] = d_values
            write_pairs(part, TOP, d_marks)
        else:
            dk[rows, :] = jnp.where(inside, d_keys.astype(BF16), dk[rows, :])
            dval[rows, :] = jnp.where(inside, d_values, dval[rows, :])
            parts[doc - 1] = d_marks

    for_docs(info, total, body)
    padded_rows(halo[0], values, halo[1], pad)
    padded_rows(dhalo[0], dmix, dhalo[1], dpad)
    tap_rows[...] = widened(taps, True)
    tape = bands(tap_rows, group)
    acc[...] = jnp.zeros_like(acc)

    def conv(doc, start, inside):
        zero = jnp.zeros((), BF16)
        rows = pl.ds(start, BLK)
        here = inside[16 : 16 + BLK]
        out = head_rows(dot(tape, jnp.where(inside, dpad[pl.ds(start, TOEP), :], zero)))
        dval[rows, :] = dval[rows, :] + jnp.where(here, out, 0.0)
        window = jnp.where(inside, pad[pl.ds(start, TOEP), :], zero)
        mine = jnp.where(here, dmix[rows, :], zero)
        lanes = lax.broadcasted_iota(jnp.int32, (BLK, GROUP), 1) // LMK
        spread = jnp.concatenate([jnp.where(lanes == i, mine, zero) for i in range(GROUP // LMK)], axis=0)
        acc[:, :TOEP] = acc[:, :TOEP] + dot(spread, window, NT)

    doc_windows(info, total, conv)
    dv[...] = dval[...].astype(BF16)
    rows = lax.broadcasted_iota(jnp.int32, (BLK, BLK), 0)
    lanes = lax.broadcasted_iota(jnp.int32, (BLK, BLK), 1)
    reverse = jnp.where(rows + lanes == BLK - 1, 1.0, 0.0).astype(F32)
    for i in range(GROUP // LMK):
        square = dot(reverse, acc[i * BLK : (i + 1) * BLK, :], precision=HIGHEST)
        turned = pltpu.roll(square, 0, 1, stride=1, stride_axis=0)
        dtaps[0, i : i + 1, :] = jnp.sum(turned, axis=0, keepdims=True)


def back_b(lens, joined, halo, exps, local, stat, sc, along, scs, alongs, qm, qms, taps, dmix, dhalo):
    total, width = dmix.shape
    groups = width // GROUP
    heads = GROUP // LMK
    col = pl.BlockSpec((total, GROUP), lambda g: (0, g))
    mark, marks = LONG_SPEC, SMALL_SPEC
    edge = pl.BlockSpec((2, 16, GROUP), lambda g: (0, 0, g))
    return pl.pallas_call(
        back_b_kernel,
        grid=(groups,),
        in_specs=[
            pl.BlockSpec(memory_space=pltpu.SMEM),
            pl.BlockSpec((total, GROUP), lambda g: (0, groups + g)),
            pl.BlockSpec((total, GROUP), lambda g: (0, 2 * groups + g)),
            edge,
            col,
            pl.BlockSpec((2, LMK + 8, PAIR), lambda g: (g, 0, 0)),
            ROW_SPEC,
            mark,
            ROW_SPEC,
            marks,
            SMALL_ROW_SPEC,
            mark,
            half_spec(0),
            pl.BlockSpec(taps.shape, lambda g: (0, 0)),
            col,
            edge,
        ],
        out_specs=[col, col, mark, marks, pl.BlockSpec((1, heads, 256), lambda g: (g, 0, 0))],
        out_shape=[
            jax.ShapeDtypeStruct((total, width), BF16),
            jax.ShapeDtypeStruct((total, width), BF16),
            jax.ShapeDtypeStruct((PAIRS, LMK, PAIR), F32),
            jax.ShapeDtypeStruct((SMALL, groups, LMK, GROUP), F32),
            jax.ShapeDtypeStruct((groups, heads, 256), F32),
        ],
        scratch_shapes=[VMEM((total + 32, GROUP), BF16), VMEM((total + 32, GROUP), BF16), VMEM((heads * BLK, 256), F32), VMEM((total, GROUP), F32), VMEM((taps.shape[0], 256), F32)],
        compiler_params=pltpu.CompilerParams(vmem_limit_bytes=62 * 2**20),
        name="back_b",
    )(lens, joined, joined, halo, exps, local, stat, sc, along, scs, alongs, qm, qms, taps, dmix, dhalo)


class Ring:
    def __init__(self, count):
        self.count = count
        self.me = lax.axis_index("seq")
        self.row = lax.axis_index("row")
        self.steps = range(1, count)

    def ahead(self, k):
        return lax.rem(self.me + k, self.count)

    def enter(self, others=()):
        barrier = pltpu.get_barrier_semaphore()
        for to in [(self.ahead(k), self.row) for k in self.steps] + list(others):
            pl.semaphore_signal(barrier, inc=1, device_id=to, device_id_type=MESH)
        pl.semaphore_wait(barrier, self.count - 1 + len(others))

    def copy(self, src, dst, send, recv, to):
        return pltpu.make_async_remote_copy(src_ref=src, dst_ref=dst, send_sem=send, recv_sem=recv, device_id=(to, self.row), device_id_type=MESH)

    def scatter(self, pieces, landing, send, recv, first, owners):
        for k in self.steps:
            to = self.ahead(k)

            @pl.when((to >= first) & (to < first + owners))
            def _():
                self.copy(pieces(to - first), landing.at[k - 1], send.at[k - 1], recv.at[k - 1], to).start()

        def arrived():
            for k in self.steps:
                self.copy(pieces(0), landing.at[k - 1], send.at[k - 1], recv.at[k - 1], self.ahead(k)).wait_recv()

        def sent():
            for k in self.steps:
                to = self.ahead(k)

                @pl.when((to >= first) & (to < first + owners))
                def _():
                    self.copy(pieces(to - first), landing.at[k - 1], send.at[k - 1], recv.at[k - 1], to).wait_send()

        return arrived, sent

    def share(self, held, send, recv, first):
        piece = self.me - first
        for k in self.steps:
            self.copy(held.at[piece], held.at[piece], send.at[k - 1], recv.at[piece], self.ahead(k)).start()

    def share_sent(self, held, send, recv, first):
        piece = self.me - first
        for k in self.steps:
            self.copy(held.at[piece], held.at[piece], send.at[k - 1], recv.at[piece], self.ahead(k)).wait_send()

    def shared(self, held, send, recv, first, owners):
        for p in range(owners):

            @pl.when(self.me != first + p)
            def _():
                self.copy(held.at[p], held.at[p], send.at[0], recv.at[p], self.ahead(1)).wait_recv()


    def edges_start(self, here, landing, send, recv):
        @pl.when(self.me > 0)
        def _():
            self.copy(here.at[0], landing.at[1], send.at[0], recv.at[1], self.me - 1).start()

        @pl.when(self.me < self.count - 1)
        def _():
            self.copy(here.at[1], landing.at[0], send.at[1], recv.at[0], self.me + 1).start()

    def edges_wait(self, here, landing, send, recv, out):
        out[...] = jnp.zeros_like(out)

        @pl.when(self.me > 0)
        def _():
            done = self.copy(here.at[0], landing.at[0], send.at[0], recv.at[0], self.me - 1)
            done.wait_recv()
            done.wait_send()
            out[0] = landing[0]

        @pl.when(self.me < self.count - 1)
        def _():
            done = self.copy(here.at[1], landing.at[1], send.at[1], recv.at[1], self.me + 1)
            done.wait_recv()
            done.wait_send()
            out[1] = landing[1]


OWNERS = 8
DMA = pltpu.SemaphoreType.DMA
SAVES = 3 * NS_ITERS + 2
CASES = SMALL * GROUPS
EARLY = 2


def ends(ring):
    return (ring.me == 0) | (ring.me == ring.count - 1)


def owner_of_pair(ring):
    return (ring.me >= 1) & (ring.me <= PAIRS)


def pair_of(ring):
    return jnp.clip(ring.me - 1, 0, PAIRS - 1)


def remote_params(cid):
    return pltpu.CompilerParams(collective_id=cid, has_side_effects=True, vmem_limit_bytes=62 * 2**20)


def in_vmem(n):
    return [pl.BlockSpec(memory_space=VMEM)] * n


ANY_SPEC = pl.BlockSpec(memory_space=pl.ANY)


def small_forward(doc, at, qms, kms, held, invs):
    def save(i, j, value):
        held[at, j, i] = value

    inverse = inverse_forward([qms[doc, g] for g in range(GROUPS)], [kms[doc, g] for g in range(GROUPS)], save, GROUP)
    for g in range(GROUPS):
        invs[at, g] = inverse[g]


def marks_kernel(count, part, counts, edge, small, qm, km, halo, saved, invs, landing, held, hland, sheld, ss, rs, gs, gr, es, er, hs):
    ring = Ring(count)
    ring.enter()
    ring.edges_start(edge, hland, es, er)
    each_ = LMK // OWNERS
    arrived, sent = ring.scatter(lambda o: part.at[pl.ds(pl.multiple_of(o * each_, each_), each_), :], landing, ss, rs, 0, OWNERS)
    keep = [pltpu.make_async_copy(sheld.at[d], saved.at[d], hs.at[d]) for d in range(EARLY)]

    def early(d):
        @pl.when(ends(ring))
        def _():
            small_forward(d, d, small.at[0], small.at[1], sheld, invs)
            keep[d].start()

    early(0)

    @pl.when(ring.me < OWNERS)
    def _():
        arrived()
        at = pl.ds(pl.multiple_of(ring.me * each_, each_), each_)
        total = part[at, :]
        for k in ring.steps:
            total = total + landing[k - 1]
        total = total / counts[0, at, 0:1]
        half = total.shape[1] // 2
        held[ring.me, 0:each_, :] = total[:, :half].astype(BF16)
        held[ring.me, each_ : 2 * each_, :] = total[:, half:].astype(BF16)
        ring.share(held, gs, gr, 0)

    for d in range(1, EARLY):
        early(d)
    ring.shared(held, gs, gr, 0, OWNERS)
    wide = [held[o].astype(F32) for o in range(OWNERS)]
    query = jnp.concatenate([w[:each_] for w in wide], axis=0).astype(BF16)
    key = jnp.concatenate([w[each_:] for w in wide], axis=0).astype(BF16)
    for p in range(PAIRS):
        qm[p] = query[:, p * PAIR : (p + 1) * PAIR]
        km[p] = key[:, p * PAIR : (p + 1) * PAIR]
    ring.edges_wait(edge, hland, es, er, halo)
    sent()

    @pl.when(ring.me < OWNERS)
    def _():
        ring.share_sent(held, gs, gr, 0)

    @pl.when(ends(ring))
    def _():
        for copy in keep:
            copy.wait()


def all_marks(count, part, counts, edge, small):
    width = part.shape[1]
    each_ = LMK // OWNERS
    return pl.pallas_call(
        functools.partial(marks_kernel, count),
        in_specs=in_vmem(4),
        out_specs=in_vmem(3) + [ANY_SPEC] + in_vmem(1),
        out_shape=[jax.ShapeDtypeStruct((PAIRS, LMK, PAIR), BF16)] * 2
        + [
            jax.ShapeDtypeStruct(edge.shape, BF16),
            jax.ShapeDtypeStruct((EARLY, GROUPS, SAVES, LMK, GROUP), F32),
            jax.ShapeDtypeStruct((EARLY, GROUPS, LMK, GROUP), F32),
        ],
        scratch_shapes=[
            VMEM((count - 1, each_, width), F32),
            VMEM((OWNERS, 2 * each_, width // 2), BF16),
            VMEM(edge.shape, BF16),
            VMEM((EARLY, GROUPS, SAVES, LMK, GROUP), F32),
            DMA((count - 1,)),
            DMA((count - 1,)),
            DMA((count - 1,)),
            DMA((OWNERS,)),
            DMA((2,)),
            DMA((2,)),
            DMA((EARLY,)),
        ],
        compiler_params=remote_params(1),
        name="all_marks",
    )(part, counts, edge, small)


def carry_kernel(count, part, qm, km, small, wsm, stsm, invs, car, stat, saved, inv, mixed, cars, saveds, inv2, mixeds, landing, cheld, sheld, sk, ss, rs, cs, cr, ts, tr, hs):
    ring = Ring(count)
    ring.enter()
    arrived, sent = ring.scatter(lambda p: part.at[p], landing, ss, rs, 1, PAIRS)
    keep = pltpu.make_async_copy(sk, saveds, hs.at[0])

    @pl.when(owner_of_pair(ring))
    def _():
        pair = pair_of(ring)

        def save(i, j, value):
            saved[i] = value

        inverse = inverse_forward([qm[pair]], [km[pair]], save, PAIR)[0]
        inv[...] = inverse
        arrived()
        pieces = [part[pair]] + [landing[k - 1] for k in ring.steps]
        top = pieces[0][LMK : LMK + 1]
        for piece in pieces[1:]:
            top = jnp.maximum(top, piece[LMK : LMK + 1])
        weighted = jnp.zeros((LMK, PAIR), F32)
        total = jnp.zeros((1, PAIR), F32)
        for piece in pieces:
            share = jnp.exp(piece[LMK : LMK + 1] - top)
            weighted = weighted + piece[:LMK] * column_of(share, PAIR)
            total = total + piece[LMK + 1 : LMK + 2] * share
        mean = weighted / column_of(total, PAIR)
        mixed[...] = mean
        cheld[pair] = mul(inverse, mean, PAIR).astype(BF16)
        sheld[pair] = jnp.concatenate([top, total, jnp.zeros((6, PAIR), F32)], axis=0)
        ring.share(cheld, cs, cr, 1)
        ring.share(sheld, ts, tr, 1)

    @pl.when(ends(ring))
    def _():
        @pl.loop(0, SMALL - EARLY)
        def _(d):
            small_forward(d + EARLY, d, small.at[0], small.at[1], sk, inv2)

        keep.start()

        def finish(doc, inverse):
            for g in range(GROUPS):
                total = jnp.maximum(stsm[doc, g, 1:2, :], 1e-30)
                mean = wsm[doc, g] / column_of(total, GROUP)
                mixeds[doc, g] = mean
                cars[doc, g] = mul(inverse[g], mean, GROUP).astype(BF16)

        for d in range(SMALL):
            finish(d, [invs[d, g] if d < EARLY else inv2[d - EARLY, g] for g in range(GROUPS)])

    ring.shared(cheld, cs, cr, 1, PAIRS)
    ring.shared(sheld, ts, tr, 1, PAIRS)
    car[...] = cheld[...]
    stat[...] = sheld[...]
    sent()

    @pl.when(owner_of_pair(ring))
    def _():
        ring.share_sent(cheld, cs, cr, 1)
        ring.share_sent(sheld, ts, tr, 1)

    @pl.when(ends(ring))
    def _():
        keep.wait()


def carry(count, part, qm, km, small, wsm, stsm, invs):
    late = SMALL - EARLY
    return pl.pallas_call(
        functools.partial(carry_kernel, count),
        in_specs=in_vmem(7),
        out_specs=in_vmem(6) + [ANY_SPEC] + in_vmem(2),
        out_shape=[
            jax.ShapeDtypeStruct((PAIRS, LMK, PAIR), BF16),
            jax.ShapeDtypeStruct((PAIRS, 8, PAIR), F32),
            jax.ShapeDtypeStruct((SAVES, LMK, PAIR), F32),
            jax.ShapeDtypeStruct((LMK, PAIR), F32),
            jax.ShapeDtypeStruct((LMK, PAIR), F32),
            jax.ShapeDtypeStruct((SMALL, GROUPS, LMK, GROUP), BF16),
            jax.ShapeDtypeStruct((late, GROUPS, SAVES, LMK, GROUP), F32),
            jax.ShapeDtypeStruct((late, GROUPS, LMK, GROUP), F32),
            jax.ShapeDtypeStruct((SMALL, GROUPS, LMK, GROUP), F32),
        ],
        scratch_shapes=[
            VMEM((count - 1, LMK + 8, PAIR), F32),
            VMEM((PAIRS, LMK, PAIR), BF16),
            VMEM((PAIRS, 8, PAIR), F32),
            VMEM((late, GROUPS, SAVES, LMK, GROUP), F32),
            DMA((count - 1,)),
            DMA((count - 1,)),
            DMA((count - 1,)),
            DMA((PAIRS,)),
            DMA((count - 1,)),
            DMA((PAIRS,)),
            DMA((1,)),
        ],
        compiler_params=remote_params(2),
        name="carry",
    )(part, qm, km, small, wsm, stsm, invs)


def spread_grad(d_carried, inverse, mixed, total, width):
    d_mixed = mul(flipped(inverse, width), d_carried, width)
    scaled = (d_mixed / column_of(total, width)).astype(BF16)
    along = row_of(scaled.astype(F32) * mixed, width)
    return scaled, along


def spread_kernel(count, part, stat, inv, mixed, smallf, stsm, invs, inv2, mixeds, edge, sc, along, dtot, scs, alongs, halo, landing, sheld, aheld, hland, ss, rs, cs, cr, ts, tr, es, er):
    ring = Ring(count)
    ring.enter()
    arrived, sent = ring.scatter(lambda p: part.at[p], landing, ss, rs, 1, PAIRS)
    ring.edges_start(edge, hland, es, er)

    @pl.when(owner_of_pair(ring))
    def _():
        pair = pair_of(ring)
        arrived()
        total = part[pair].astype(F32)
        for k in ring.steps:
            total = total + landing[k - 1].astype(F32)
        dtot[...] = total
        scaled, reach = spread_grad(total[:LMK], inv[...], mixed[...], stat[pair, 1:2, :], PAIR)
        sheld[pair] = scaled
        aheld[pair] = reach
        ring.share(sheld, cs, cr, 1)
        ring.share(aheld, ts, tr, 1)

    @pl.when(ends(ring))
    def _():
        for d in range(SMALL):
            for g in range(GROUPS):
                total = jnp.maximum(stsm[d, g, 1:2, :], 1e-30)
                inverse = invs[d, g] if d < EARLY else inv2[d - EARLY, g]
                scaled, reach = spread_grad(smallf[0, d, g], inverse, mixeds[d, g], total, GROUP)
                scs[d, g] = scaled
                alongs[d, g] = reach

    ring.shared(sheld, cs, cr, 1, PAIRS)
    ring.shared(aheld, ts, tr, 1, PAIRS)
    sc[...] = sheld[...]
    along[...] = aheld[...]
    ring.edges_wait(edge, hland, es, er, halo)
    sent()

    @pl.when(owner_of_pair(ring))
    def _():
        ring.share_sent(sheld, cs, cr, 1)
        ring.share_sent(aheld, ts, tr, 1)


def spread(count, part, stat, inv, mixed, smallf, stsm, invs, inv2, mixeds, edge):
    return pl.pallas_call(
        functools.partial(spread_kernel, count),
        in_specs=in_vmem(10),
        out_specs=in_vmem(6),
        out_shape=[
            jax.ShapeDtypeStruct((PAIRS, LMK, PAIR), BF16),
            jax.ShapeDtypeStruct((PAIRS, 8, PAIR), F32),
            jax.ShapeDtypeStruct((2 * LMK, PAIR), F32),
            jax.ShapeDtypeStruct((SMALL, GROUPS, LMK, GROUP), BF16),
            jax.ShapeDtypeStruct((SMALL, GROUPS, 8, GROUP), F32),
            jax.ShapeDtypeStruct(edge.shape, BF16),
        ],
        scratch_shapes=[
            VMEM((count - 1, 2 * LMK, PAIR), BF16),
            VMEM((PAIRS, LMK, PAIR), BF16),
            VMEM((PAIRS, 8, PAIR), F32),
            VMEM(edge.shape, BF16),
            DMA((count - 1,)),
            DMA((count - 1,)),
            DMA((count - 1,)),
            DMA((PAIRS,)),
            DMA((count - 1,)),
            DMA((PAIRS,)),
            DMA((2,)),
            DMA((2,)),
        ],
        compiler_params=remote_params(3),
        name="spread",
    )(part, stat, inv, mixed, smallf, stsm, invs, inv2, mixeds, edge)


UNIT = 256
ACROSS = UNIT // 2
TURNS = (0, 1, 3, 5, 7, 9, 11, 13, 14)


class Sums:
    STEPS = 9

    def __init__(self, count, own, out, r0, r1, r2, r3, osem, ss, rs):
        self.count = count
        self.own, self.out, self.r0, self.r1, self.r2, self.r3 = own, out, r0, r1, r2, r3
        self.osem, self.ss, self.rs = osem, ss, rs
        s_ax, r_ax = lax.axis_index("seq"), lax.axis_index("row")
        z, x, y, c = s_ax // 2, lax.rem(s_ax, 2), r_ax // 2, lax.rem(r_ax, 2)
        x1, y1 = x + (1 - c) * (1 - 2 * x), y + c * (1 - 2 * y)
        x2, y2 = x + c * (1 - 2 * x), y + (1 - c) * (1 - 2 * y)
        self.z = z
        self.core = (s_ax, y * 2 + (1 - c))
        self.first = (z * 2 + x1, y1 * 2 + c)
        self.second = (z * 2 + x2, y2 * 2 + c)
        self.line = [(lax.rem(z + k, 4) * 2 + x, r_ax) for k in (1, 2, 3)]
        self.others = [self.core, self.first, self.second] + self.line
        self.b1 = x * (1 - c) + y * c
        self.b2 = y * (1 - c) + x * c
        self.mine, self.theirs = c, 1 - c
        self.fly = (self.core, self.first, self.second) + tuple(self.line) + tuple(self.line) + (self.second, self.first, self.core)

    def rows(self, start, size):
        return pl.ds(pl.multiple_of(start, 16), size)

    def copies(self, u):
        out, line = self.out, [lax.rem(self.z + k, 4) for k in (1, 2, 3)]
        base1, base2 = self.b1 * 384, self.b1 * 384 + self.b2 * 192
        last = self.r2.at[u, self.rows(self.z * 48, 48), :]
        place = out.at[u, self.mine, self.rows(base2 + self.z * 48, 48), :]
        pairs = [
            (self.own.at[u, self.theirs], self.r0.at[u]),
            (self.r0.at[u, self.rows((1 - self.b1) * 384, 384), :], self.r1.at[u]),
            (self.r1.at[u, self.rows((1 - self.b2) * 192, 192), :], self.r2.at[u]),
        ]
        pairs += [(self.r2.at[u, self.rows(line[k] * 48, 48), :], self.r3.at[u, k]) for k in range(3)]
        pairs += [(last, place)] * 3
        for region in (out.at[u, self.mine, self.rows(base2, 192), :], out.at[u, self.mine, self.rows(base1, 384), :], out.at[u, self.mine]):
            pairs.append((region, region))
        return pairs

    def copy(self, u, k):
        src, dst = self.copies(u)[k]
        return pltpu.make_async_remote_copy(src_ref=src, dst_ref=dst, send_sem=self.ss.at[u, k], recv_sem=self.rs.at[u, k], device_id=self.fly[k], device_id_type=MESH)

    def keep(self, u):
        src, dst = self.copies(u)[6]
        return pltpu.make_async_copy(src, dst, self.osem.at[u])

    def add(self, u, here, start, there, size):
        @pl.loop(0, size, step=192)
        def _(t):
            q = self.rows(t, 192)
            here[u, q, :] = (here[u, q, :].astype(F32) + there(self.rows(start + t, 192)).astype(F32)).astype(BF16)

    def advance(self, u, s):
        if s == 0:
            self.copy(u, 0).start()
        elif s == 1:
            self.copy(u, 0).wait_recv()
            self.add(u, self.r0, 0, lambda q: self.own[u, self.mine, q, :], 768)
            self.copy(u, 1).start()
        elif s == 2:
            self.copy(u, 1).wait_recv()
            self.add(u, self.r1, self.b1 * 384, lambda q: self.r0[u, q, :], 384)
            self.copy(u, 2).start()
        elif s == 3:
            self.copy(u, 2).wait_recv()
            self.add(u, self.r2, self.b2 * 192, lambda q: self.r1[u, q, :], 192)
            for k in range(3):
                self.copy(u, 3 + k).start()
        elif s == 4:
            for k in range(3):
                self.copy(u, 3 + k).wait_recv()
            total = self.r2[u, self.rows(self.z * 48, 48), :].astype(F32)
            for k in range(3):
                total = total + self.r3[u, k].astype(F32)
            self.r2[u, self.rows(self.z * 48, 48), :] = total.astype(BF16)
            self.keep(u).start()
            for k in range(3):
                self.copy(u, 6 + k).start()
        elif s == 5:
            for k in range(3):
                self.copy(u, 6 + k).wait_recv()
            self.keep(u).wait()
            self.copy(u, 9).start()
        elif s in (6, 7):
            self.copy(u, s + 3).wait_recv()
            self.copy(u, s + 4).start()
        else:
            self.copy(u, 11).wait_recv()

    def taus(self):
        return self.count + TURNS[-1]

    def step(self, tau, steps):
        for s in steps:
            u = tau - TURNS[s]

            @pl.when((u >= 0) & (u < self.count))
            def _():
                self.advance(jnp.clip(u, 0, self.count - 1), s)

    def finish(self):
        @pl.loop(0, self.count)
        def _(u):
            for k in range(12):
                self.copy(u, k).wait_send()


def small_all(values, smr, sss, srs, sums, k):
    z = sums.z
    s_ax, r_ax = lax.axis_index("seq"), lax.axis_index("row")
    x = lax.rem(s_ax, 2)
    partners = [sums.core, sums.first, sums.second, (lax.rem(z + 2, 4) * 2 + x, r_ax), ((z + 1 - 2 * lax.rem(z, 2)) * 2 + x, r_ax)]

    def copy(i):
        return pltpu.make_async_remote_copy(src_ref=smr.at[i], dst_ref=smr.at[i + 6], send_sem=sss.at[i], recv_sem=srs.at[i], device_id=partners[i], device_id_type=MESH)

    if k == 0:
        terms, taps = values
        smr[0] = jnp.zeros(smr.shape[1:], F32)
        smr[0, 0:4, :] = terms[0:4, :]
        for g in range(GROUPS):
            smr[0, 8:12, g * GROUP : (g + 1) * GROUP] = taps[g]
    else:
        copy(k - 1).wait_recv()
        smr[k] = smr[k - 1] + smr[k + 5]
    if k < 5:
        copy(k).start()
    else:
        for i in range(5):
            copy(i).wait_send()


MARK_TAUS = NS_ITERS * SMALL


def marks_backward(ring, tau, arrived, part, dtot, saved, mixed, qm, km, counts, smallb, smallf, save_a, save_b, mixeds, marks, landing, held, dsums, keep, da, dk, kt, la, lk, lt, cs, cr, hs):
    owner, end = owner_of_pair(ring), ends(ring)
    pair = pair_of(ring)
    last = 3 * NS_ITERS + 1
    doc, turn = jnp.minimum(tau // NS_ITERS, SMALL - 1), lax.rem(tau, NS_ITERS)
    back = NS_ITERS - 1 - turn

    @pl.when(owner & (tau == 0))
    def _():
        la[...] = mul_nt(dtot[:LMK], mixed[...], PAIR)
        lk[...] = jnp.zeros_like(lk)
        lt[...] = flipped(saved[last], PAIR)

    @pl.when(owner & (tau < NS_ITERS))
    def _():
        a, b = backward_step([la[...]], [lk[...]], [lt[...]], [saved[3 * back]], [saved[3 * back + 1]], [saved[3 * back + 2]], PAIR)
        la[...] = a[0]
        lk[...] = b[0]

    @pl.when(owner & (tau == NS_ITERS - 1))
    def _():
        d_scores = backward_end(la[...], lk[...], saved[last], saved[0], PAIR) * 0.125
        d_query = mul(d_scores, km[pair].astype(F32), PAIR)
        d_key = mul(flipped(d_scores, PAIR), qm[pair].astype(F32), PAIR)
        arrived()
        total = part[pair]
        for k in ring.steps:
            total = total + landing[k - 1]
        held[pair, :LMK, :] = ((d_query + total) / counts[0, :, 0:1]).astype(BF16)
        held[pair, LMK:, :] = ((d_key + dtot[LMK:]) / counts[0, :, 0:1]).astype(BF16)
        ring.share(held, cs, cr, 1)

    work = end & (tau < MARK_TAUS)

    @pl.when(work & (turn == 0))
    def _():
        @pl.when(doc < EARLY)
        def _():
            copy = pltpu.make_async_copy(save_a.at[jnp.minimum(doc, EARLY - 1)], keep, hs.at[0])
            copy.start()
            copy.wait()

        @pl.when(doc >= EARLY)
        def _():
            copy = pltpu.make_async_copy(save_b.at[jnp.maximum(doc - EARLY, 0)], keep, hs.at[0])
            copy.start()
            copy.wait()

        for g in range(GROUPS):
            da[g] = mul_nt(smallf[0, doc, g], mixeds[doc, g], GROUP)
            dk[g] = jnp.zeros((LMK, GROUP), F32)
            kt[g] = flipped(keep[g, last], GROUP)

    @pl.when(work)
    def _():
        rows = range(GROUPS)
        iterates = [[keep[g, 3 * back + i] for g in rows] for i in range(3)]
        a, b = backward_step([da[g] for g in rows], [dk[g] for g in rows], [kt[g] for g in rows], *iterates, GROUP)
        for g in rows:
            da[g] = a[g]
            dk[g] = b[g]

    @pl.when(work & (turn == NS_ITERS - 1))
    def _():
        for g in range(GROUPS):
            d_scores = backward_end(da[g], dk[g], keep[g, last], keep[g, 0], GROUP) * 0.125
            d_query = mul(d_scores, marks[1, doc, g].astype(F32), GROUP)
            d_key = mul(flipped(d_scores, GROUP), marks[0, doc, g].astype(F32), GROUP)
            size = counts[1 + doc, :, 0:1]
            dsums[doc, g, :LMK, :] = ((d_query + smallb[doc, g]) / size).astype(BF16)
            dsums[doc, g, LMK:, :] = ((d_key + smallf[1, doc, g]) / size).astype(BF16)


N_MARKS = 13
MARKS_SPECS = in_vmem(9) + [ANY_SPEC] * 2 + in_vmem(2)
N_WORK = 12


def marks_work(count):
    return [
        VMEM((count - 1, LMK, PAIR), F32),
        VMEM((PAIRS, 2 * LMK, PAIR), BF16),
        VMEM((SMALL, GROUPS, 2 * LMK, GROUP), BF16),
        VMEM((GROUPS, SAVES, LMK, GROUP), F32),
        VMEM((GROUPS, LMK, GROUP), F32),
        VMEM((GROUPS, LMK, GROUP), F32),
        VMEM((GROUPS, LMK, GROUP), F32),
        VMEM((LMK, PAIR), F32),
        VMEM((LMK, PAIR), F32),
        VMEM((LMK, PAIR), F32),
        DMA((count - 1,)),
        DMA((PAIRS,)),
        DMA((1,)),
        DMA((count - 1,)),
        DMA((count - 1,)),
    ]


def finish_marks(ring, held, cs, cr, sent):
    sent()

    @pl.when(owner_of_pair(ring))
    def _():
        ring.share_sent(held, cs, cr, 1)


def sums_kernel(count, *refs):
    args, (dsum, dsums_out), work = refs[:N_MARKS], refs[N_MARKS : N_MARKS + 2], refs[N_MARKS + 2 :]
    (landing, held, dsums), rest, (ss, rs) = work[:3], work[3:13], work[13:]
    cs, cr = rest[7], rest[8]
    ring = Ring(count)
    ring.enter()
    arrived, sent = ring.scatter(lambda p: args[0].at[p], landing, ss, rs, 1, PAIRS)
    dsums[...] = jnp.zeros_like(dsums)

    @pl.loop(0, MARK_TAUS)
    def _(tau):
        marks_backward(ring, tau, arrived, *args, landing, held, dsums, *rest)

    ring.shared(held, cs, cr, 1, PAIRS)
    dsum[...] = held[...]
    dsums_out[...] = dsums[...]
    finish_marks(ring, held, cs, cr, sent)


def mark_sums(count, *args):
    shape = jax.ShapeDtypeStruct
    return pl.pallas_call(
        functools.partial(sums_kernel, count),
        in_specs=MARKS_SPECS,
        out_specs=in_vmem(2),
        out_shape=[shape((PAIRS, 2 * LMK, PAIR), BF16), shape((SMALL, GROUPS, 2 * LMK, GROUP), BF16)],
        scratch_shapes=marks_work(count),
        compiler_params=remote_params(4),
        name="mark_sums",
    )(*args)


BLOCKS = 3 * GROUPS


FIRST = (0, 12, 24, 27, 36)


def finale_kernel(count, *refs):
    args, refs = refs[:N_MARKS], refs[N_MARKS:]
    (lens, inputs, dq, dk, dv, w, ddown, act, normed, dup, mixture, dout, *sm), refs = refs[:14], refs[14:]
    (out, dx, osm), refs = refs[:3], refs[3:]
    work, refs = refs[:15], refs[15:]
    (own, r0, r1, r2, r3, dj, flip, left, right, member, table, smr, wide), refs = refs[:13], refs[13:]
    osem, gs, gr, sss, srs, jsem, fsem, bsem, wsem = refs
    (landing, held, dsums), rest, (ss, rs) = work[:3], work[3:13], work[13:]
    cs, cr = rest[7], rest[8]
    total = inputs.shape[0]
    ring = Ring(count)
    before = FIRST[3]
    sums = Sums(FIRST[4], own, out, r0, r1, r2, r3, osem, gs, gr)
    lefts, rights = (ddown, normed, mixture, inputs), (act, dup, dout)

    def fetch_left(i):
        return pltpu.make_async_copy(lefts[i], left, fsem.at[0])

    def fetch_right(i, u):
        columns = pl.ds(pl.multiple_of((u - FIRST[i]) * UNIT, 128), UNIT)
        return pltpu.make_async_copy(rights[i].at[:, columns], right.at[lax.rem(u, 2)], bsem.at[lax.rem(u, 2)])

    fetch_left(0).start()
    fetch_right(0, 0).start()
    joined = [pltpu.make_async_copy(src, dj.at[:, pl.ds(i * GROUPS * GROUP, GROUPS * GROUP)], jsem.at[i]) for i, src in enumerate((dq, dk, dv))]
    for copy in joined:
        copy.start()
    ring.enter(sums.others)
    arrived, sent = ring.scatter(lambda p: args[0].at[p], landing, ss, rs, 1, PAIRS)
    dsums[...] = jnp.zeros_like(dsums)
    weight = pltpu.make_async_copy(w, wide, wsem.at[0])
    weight.start()

    def keep(u, grad):
        own[u, 0] = grad[:, :ACROSS]
        own[u, 1] = grad[:, ACROSS:]

    def make(tau):
        for i in range(4):

            @pl.when(tau == FIRST[i])
            def _():
                fetch_left(i).wait()
                flip[...] = jnp.transpose(left[...])
                if i < 3:
                    fetch_left(i + 1).start()

        for i in range(3):

            @pl.when((tau + 1 >= FIRST[i]) & (tau + 1 < FIRST[i + 1]))
            def _():
                fetch_right(i, jnp.clip(tau + 1, FIRST[i], FIRST[i + 1] - 1)).start()

        @pl.when(tau < before)
        def _():
            u = jnp.minimum(tau, before - 1)
            pltpu.make_async_copy(act.at[:, pl.ds(0, UNIT)], right.at[lax.rem(u, 2)], bsem.at[lax.rem(u, 2)]).wait()
            keep(u, dot(flip[...], right[lax.rem(u, 2)]).astype(BF16))

        @pl.when(tau == before)
        def _():
            ring.shared(held, cs, cr, 1, PAIRS)
            for half in range(2):
                for g in range(GROUPS):
                    at = slice(half * LMK, (half + 1) * LMK)
                    table[half * GROUPS + g, :LMK, :PAIR] = held[2 * g, at, :]
                    table[half * GROUPS + g, :LMK, PAIR:] = held[2 * g + 1, at, :]
                    for d in range(SMALL):
                        table[half * GROUPS + g, (d + 1) * LMK : (d + 2) * LMK, :] = dsums[d, g, at, :]

        @pl.when((tau >= before) & (tau < FIRST[4]))
        def _():
            b = jnp.clip(tau - before, 0, BLOCKS - 1)
            columns = pl.ds(pl.multiple_of(b * GROUP, 128), GROUP)

            @pl.when(b < 2 * GROUPS)
            def _():
                from_marks = dot(member[...], table[jnp.minimum(b, 2 * GROUPS - 1)])
                dj[:, columns] = (dj[:, columns].astype(F32) + from_marks).astype(BF16)

            keep(before + b, dot(flip[...], dj[:, columns]).astype(BF16))

    @pl.loop(0, sums.taus())
    def _(tau):
        sums.step(tau, range(8, 0, -1))
        make(tau)
        sums.step(tau, (0,))
        for k in range(6):

            @pl.when(tau == 4 * k + 3)
            def _():
                small_all(sm, smr, sss, srs, sums, k)

        marks_backward(ring, tau, arrived, *args, landing, held, dsums, *rest)

        @pl.when(tau == MARK_TAUS)
        def _():
            low, high = slot_bounds(lens, total, (1, DOCS * LMK), 1)
            rows = lax.broadcasted_iota(jnp.int32, (total, DOCS * LMK), 0)
            member[...] = jnp.where((rows >= low) & (rows < high), 1.0, 0.0).astype(BF16)
            for copy in joined:
                copy.wait()

        for k in range(GROUPS):

            @pl.when(tau == FIRST[4] + 2 * k + 1)
            def _():
                if k == 0:
                    weight.wait()
                columns = slice(k * GROUP, (k + 1) * GROUP)
                dx[:, columns] = dot(dj[...], wide[columns, :], NT)

    finish_marks(ring, held, cs, cr, sent)
    sums.finish()
    osm[...] = smr[5]


def finale(count, marks_args, lens, inputs, dq, dk, dv, w, ddown, act, normed, dup, mixture, dout, terms, dtaps):
    n = FIRST[4]
    total, depth = inputs.shape
    width = w.shape[1]
    shape = jax.ShapeDtypeStruct
    return pl.pallas_call(
        functools.partial(finale_kernel, count),
        in_specs=MARKS_SPECS + [pl.BlockSpec(memory_space=pltpu.SMEM)] + [ANY_SPEC] * 11 + in_vmem(2),
        out_specs=[ANY_SPEC] + in_vmem(2),
        out_shape=[shape((n, 2, 768, ACROSS), BF16), shape((total, depth), F32), shape((16, depth), F32)],
        scratch_shapes=marks_work(count)
        + [
            VMEM((n, 2, 768, ACROSS), BF16),
            VMEM((n, 768, ACROSS), BF16),
            VMEM((n, 384, ACROSS), BF16),
            VMEM((n, 192, ACROSS), BF16),
            VMEM((n, 3, 48, ACROSS), BF16),
            VMEM((total, width), BF16),
            VMEM((depth, total), BF16),
            VMEM((total, depth), BF16),
            VMEM((2, total, UNIT), BF16),
            VMEM((total, DOCS * LMK), BF16),
            VMEM((2 * GROUPS, DOCS * LMK, GROUP), BF16),
            VMEM((11, 16, depth), F32),
            VMEM(w.shape, BF16),
            DMA((n,)),
            DMA((n, 12)),
            DMA((n, 12)),
            DMA((5,)),
            DMA((5,)),
            DMA((3,)),
            DMA((1,)),
            DMA((2,)),
            DMA((1,)),
        ],
        compiler_params=pltpu.CompilerParams(collective_id=5, has_side_effects=True, vmem_limit_bytes=62 * 2**20),
        name="finale",
    )(*marks_args, lens, inputs, dq, dk, dv, w, ddown, act, normed, dup, mixture, dout, terms, dtaps)


TRIPLE = 3


def widen_kernel(units, dx, residual, little, gd, gu, go, gq, grad, g1, b1, g2, b2, gtaps):
    i = pl.program_id(0)

    @pl.when(i == 0)
    def _():
        for k, ref in enumerate((g1, b1, g2, b2)):
            ref[...] = little[k, :]
        heads = GROUP // LMK
        for h in range(gtaps.shape[0]):
            row = little[8 + h % heads : 9 + h % heads, h // heads * GROUP : (h // heads + 1) * GROUP]
            gtaps[h : h + 1, :] = pltpu.roll(row, GROUP - BLK + 1, 1)[:, : gtaps.shape[1]]

    value = [jnp.concatenate([units[k, 0], units[k, 1]], axis=1).astype(F32) for k in range(TRIPLE)]

    @pl.when(i < 4)
    def _():
        for k in range(TRIPLE):
            gd[k * UNIT : (k + 1) * UNIT, :] = jnp.transpose(value[k])

    for ref, first, end in ((gu, 4, 8), (go, 8, 9), (gq, 9, 12)):

        @pl.when((i >= first) & (i < end))
        def _():
            for k in range(TRIPLE):
                ref[:, k * UNIT : (k + 1) * UNIT] = value[k]

    @pl.when(i < 8)
    def _():
        grad[...] = residual[...] + dx[...]


def widen(units, dx, residual, little, taps):
    n, _, side, half = units.shape
    shape = jax.ShapeDtypeStruct
    total, depth = dx.shape

    def place(first, last, down):
        def index(i):
            b = jnp.clip(i, first, last) - first
            return (b, 0) if down else (0, b)

        return pl.BlockSpec((side, side), index)

    part = pl.BlockSpec((total // 8, depth), lambda i: (jnp.minimum(i, 7), 0))
    return pl.pallas_call(
        widen_kernel,
        grid=(n // TRIPLE,),
        in_specs=[pl.BlockSpec((TRIPLE, 2, side, half), lambda i: (i, 0, 0, 0)), part, part, pl.BlockSpec(little.shape, lambda i: (0, 0))],
        out_specs=[place(0, 3, True), place(4, 7, False), place(8, 8, True), place(9, 11, False), part] + [pl.BlockSpec((depth,), lambda i: (0,))] * 4 + [pl.BlockSpec(taps, lambda i: (0, 0))],
        out_shape=[shape((4 * side, side), F32), shape((side, 4 * side), F32), shape((side, side), F32), shape((side, 3 * side), F32), shape(dx.shape, F32)] + [shape((depth,), F32)] * 4 + [shape(taps, F32)],
        compiler_params=pltpu.CompilerParams(vmem_limit_bytes=62 * 2**20),
        name="widen",
    )(units, dx, residual, little)


def member_of(doc_lengths, total):
    low, high = slot_bounds(doc_lengths, total, (1, DOCS * LMK), 1)
    rows = jnp.arange(total, dtype=jnp.int32)[:, None]
    return ((rows >= low) & (rows < high)).astype(BF16)


def over_all(*grads):
    out = []
    for g in grads:
        part = lax.psum_scatter(g.astype(F32).reshape(lax.axis_size(("seq", "row")), -1), ("seq", "row"), scatter_dimension=0, tiled=True)
        out.append(lax.all_gather(part.astype(BF16), ("seq", "row"), axis=0, tiled=True).reshape(g.shape))
    return out


def on_device(
    tokens,
    doc_lengths,
    w_qkv,
    w_out,
    conv_taps,
    norm1_gain,
    norm1_bias,
    w_up,
    w_down,
    norm2_gain,
    norm2_bias,
    cotangent,
):
    model_width = tokens.shape[2]
    head_count, tap_count = conv_taps.shape
    rim = (tap_count - 1) // 2
    count = lax.axis_size("seq")
    wide = count == 8 and lax.axis_size("row") == 4
    inputs = tokens[0]
    joined, slot_sums, small, edge, counts = project(doc_lengths, inputs, w_qkv)
    qm, km, halo, save_a, invs = all_marks(count, slot_sums, counts, edge, small)
    exps, part, wsm, stsm = mix(doc_lengths, joined, qm, small)
    carried, stat, saved, inv, mixed, cars, save_b, inv2, mixeds = carry(count, part, qm, km, small, wsm, stsm, invs)
    kernel_b, mixture_b = attend(doc_lengths, joined, halo, conv_taps, km, carried, small, cars)
    gains = (norm1_gain, norm1_bias, norm2_gain, norm2_bias)
    result, activated, delta_up, delta_down, normed1_b, delta_output, delta_mix, delta_residual1, norm_sums, delta_edge = dense(
        mixture_b, inputs, cotangent[0], gains, w_out, w_up, w_down
    )
    dq, part_f, small_f = back_f(doc_lengths, joined, delta_mix, kernel_b, km, carried, small, cars)
    scaled, along, dtot, scs, alongs, delta_halo = spread(count, part_f, stat, inv, mixed, small_f, stsm, invs, inv2, mixeds, delta_edge)
    dk, dv, part_b, small_b, dtaps = back_b(
        doc_lengths, joined, halo, exps, part, stat, scaled, along, scs, alongs, qm, small, conv_taps, delta_mix, delta_halo
    )
    marks_args = (part_b, dtot, saved, mixed, qm, km, counts, small_b, small_f, save_a, save_b, mixeds, small)
    if wide:
        units, from_joined, tsm = finale(
            count, marks_args, doc_lengths, inputs, dq, dk, dv, w_qkv, delta_down, activated, normed1_b, delta_up, mixture_b, delta_output, norm_sums, dtaps
        )
        total_down, total_up, total_output, total_joined, delta_inputs, *norms, total_taps = widen(units, from_joined, delta_residual1, tsm, conv_taps.shape)
    else:
        dsum, dsums = mark_sums(count, *marks_args)
        long_sums = dsum.reshape(PAIRS, 2, LMK, PAIR).transpose(2, 1, 0, 3).reshape(LMK, 2 * model_width)
        small_sums = dsums.reshape(SMALL, GROUPS, 2, LMK, GROUP).transpose(0, 3, 2, 1, 4).reshape(SMALL * LMK, 2 * model_width)
        from_marks = jnp.dot(member_of(doc_lengths, inputs.shape[0]), jnp.concatenate([long_sums, small_sums], axis=0), preferred_element_type=F32)
        delta_joined = jnp.concatenate([dq, dk, dv], axis=1) + jnp.pad(from_marks, ((0, 0), (0, model_width)))
        delta_joined = delta_joined.astype(BF16)
        grad_down = jnp.dot(activated.T, delta_down, preferred_element_type=F32)
        grad_up = jnp.dot(normed1_b.T, delta_up, preferred_element_type=F32)
        grad_output = jnp.dot(mixture_b.T, delta_output, preferred_element_type=F32)
        grad_joined = jnp.dot(inputs.T, delta_joined, preferred_element_type=F32)
        total_down, total_up, total_output, total_joined = over_all(grad_down, grad_up, grad_output, grad_joined)
        taps = dtaps.reshape(head_count, GROUP)[:, BLK - 1 : BLK - 1 + tap_count]
        norms, total_taps = lax.psum((norm_sums[:4], taps), ("seq", "row"))
        delta_inputs = delta_residual1 + dot(delta_joined, w_qkv, NT)
    return (
        result[None],
        delta_inputs[None],
        total_joined.astype(F32),
        total_output.astype(F32),
        total_taps,
        norms[0],
        norms[1],
        total_up.astype(F32),
        total_down.astype(F32),
        norms[2],
        norms[3],
    )


def solution(mesh):
    return jax.shard_map(
        on_device,
        mesh=mesh,
        in_specs=(
            P("row", "seq", None),
            P("row", None),
            P(),
            P(),
            P(),
            P(),
            P(),
            P(),
            P(),
            P(),
            P(),
            P("row", "seq", None),
        ),
        out_specs=(
            P("row", "seq", None),
            P("row", "seq", None),
            P(),
            P(),
            P(),
            P(),
            P(),
            P(),
            P(),
            P(),
            P(),
        ),
        check_vma=False,
    )
```

```python
import functools

import jax
import jax.numpy as jnp
from jax import lax
from jax.experimental import pallas as pl
from jax.experimental.pallas import tpu as pltpu
from jax.sharding import PartitionSpec as P

MESH = pl.DeviceIdType.MESH

LMK = 64
NS_ITERS = 6
DOCS = 4


HIGHEST = lax.Precision.HIGHEST
EPSILON = 1e-05
BIG_NEGATIVE = -1e30


F32, BF16 = jnp.float32, jnp.bfloat16
GROUP = 256
PAIR = 128
PAIRS = 6
SMALL = DOCS - 1
GROUPS = 3
WINDOW = 256
VMEM = pltpu.VMEM


def dot(a, b, dims=((1,), (0,)), precision=None):
    return lax.dot_general(a, b, (dims, ((), ())), preferred_element_type=F32, precision=precision)


NT, TN = ((1,), (1,)), ((0,), (0,))


def head_mask(width):
    rows = lax.broadcasted_iota(jnp.int32, (width, width), 0)
    lanes = lax.broadcasted_iota(jnp.int32, (width, width), 1)
    return (rows // LMK) == (lanes // LMK)


def blocks_of(side, width):
    tiled = jnp.concatenate([side] * (width // LMK), axis=0)
    return jnp.where(head_mask(width), tiled, jnp.zeros_like(tiled))


def side_of(full, width):
    full = jnp.where(head_mask(width), full, 0.0)
    return sum(full[i * LMK : (i + 1) * LMK] for i in range(width // LMK))


def flipped(side, width):
    return side_of(jnp.transpose(blocks_of(side, width)), width)


def head_ones(width):
    return jnp.where(head_mask(width), 1.0, 0.0).astype(F32)


def column_of(row, width):
    slots = lax.broadcasted_iota(jnp.int32, (LMK, width), 0)
    lanes = lax.broadcasted_iota(jnp.int32, (LMK, width), 1)
    picked = jnp.where(slots == lanes % LMK, jnp.broadcast_to(row, (LMK, width)), 0.0)
    return dot(picked, head_ones(width), precision=HIGHEST)


def row_of(side, width):
    return dot(jnp.ones((8, width), F32), blocks_of(side, width), NT, precision=HIGHEST)


def halves(x):
    high = x.astype(BF16)
    return high, (x - high.astype(F32)).astype(BF16)


def product3(a, b, dims, width):
    high, low = halves(a)
    b_high, b_low = halves(b)
    rows = a.shape[0]
    both = dot(jnp.concatenate([high, low], axis=0), blocks_of(b_high, width), dims)
    return both[:rows] + both[rows:] + dot(high, blocks_of(b_low, width), dims)


def mul(a, b, width):
    return product3(a, b, ((1,), (0,)), width)


def mul_nt(a, b, width):
    return product3(a, b, NT, width)


def each(f, *lists):
    return [f(*items) for items in zip(*lists)]


def side_eye(width):
    slots = lax.broadcasted_iota(jnp.int32, (LMK, width), 0)
    lanes = lax.broadcasted_iota(jnp.int32, (LMK, width), 1)
    return jnp.where(slots == lanes % LMK, 1.0, 0.0).astype(F32)


def head_total(side, width):
    columns = jnp.broadcast_to(jnp.sum(side, axis=0, keepdims=True), (8, width))
    return dot(columns, head_ones(width), precision=HIGHEST)[:1]


def head_max(scores, width):
    out = []
    for i in range(width // PAIR):
        part = scores[:, i * PAIR : (i + 1) * PAIR]
        left = lax.broadcasted_iota(jnp.int32, part.shape, 1) < LMK
        low = jnp.max(jnp.where(left, part, BIG_NEGATIVE), axis=1, keepdims=True)
        high = jnp.max(jnp.where(left, BIG_NEGATIVE, part), axis=1, keepdims=True)
        out.append(jnp.where(left, low, high))
    return out[0] if len(out) == 1 else jnp.concatenate(out, axis=1)


def inverse_forward(qm, km, save, width):
    ones = head_ones(width)

    def begin(q, k):
        scores = dot(q, blocks_of(k, width), NT) * 0.125
        exponent = jnp.exp(scores - head_max(scores, width))
        return exponent / dot(exponent, ones, precision=HIGHEST)

    kernel_a = each(begin, qm, km)
    approx = each(lambda a: flipped(a, width) / head_total(a * a, width), kernel_a)
    eye = side_eye(width)
    for j, a in enumerate(kernel_a):
        save(3 * NS_ITERS + 1, j, a)

    def sweep(i, approx):
        product = each(lambda a, x: mul(a, x, width), kernel_a, approx)
        square = each(lambda p: mul(p, p, width), product)
        cube = each(lambda s, p: mul(s, p, width), square, product)
        poly = each(lambda p, s, c: 3.25 * eye - 3.75 * p + 1.75 * s - 0.25 * c, product, square, cube)
        for j in range(len(approx)):
            save(3 * i, j, approx[j])
            save(3 * i + 1, j, product[j])
            save(3 * i + 2, j, poly[j])
        return tuple(each(lambda x, q: mul(x, q, width), approx, poly))

    approx = lax.fori_loop(0, NS_ITERS, sweep, tuple(approx))
    for j, x in enumerate(approx):
        save(3 * NS_ITERS, j, x)
    return list(approx)


def backward_step(d_approx, d_kernel, kernel_at, approx, product, poly, width):
    product_t = each(lambda p: flipped(p, width), product)
    d_poly = each(lambda x, d: mul(flipped(x, width), d, width), approx, d_approx)
    d_next = each(lambda d, q: mul_nt(d, q, width), d_approx, poly)
    right = each(lambda d, p: mul_nt(d, p, width), d_poly, product)
    left = each(lambda p, d: mul(p, d, width), product_t, d_poly)
    both = each(lambda r, x: r + x, right, left)
    third = each(lambda r, p: mul_nt(r, p, width), right, product)
    fourth = each(lambda p, b: mul(p, b, width), product_t, both)
    d_product = each(lambda d, b, t, f: -3.75 * d + 1.75 * b - 0.25 * (t + f), d_poly, both, third, fourth)
    d_kernel = each(lambda k, d, x: k + mul_nt(d, x, width), d_kernel, d_product, approx)
    d_approx = each(lambda n, a, d: n + mul(a, d, width), d_next, kernel_at, d_product)
    return d_approx, d_kernel


def backward_end(d_approx, d_kernel, kernel_a, first, width):
    scale = head_total(kernel_a * kernel_a, width)
    d_scale = -head_total(d_approx * first, width) / scale
    d_kernel = d_kernel + flipped(d_approx, width) / scale + 2.0 * kernel_a * d_scale
    inner = dot(d_kernel * kernel_a, head_ones(width), precision=HIGHEST)
    return kernel_a * (d_kernel - inner)


def stacked(side):
    return blocks_of(side, GROUP)


def doc_table(lens, total):
    shard_start = lax.axis_index("seq") * total
    lengths = [lens[0, i] for i in range(DOCS)]
    starts = [-shard_start]
    for i in range(DOCS - 1):
        starts.append(starts[i] + lengths[i])
    best, size, start = jnp.int32(0), lengths[0], starts[0]
    for i in range(1, DOCS):
        more = lengths[i] > size
        best, size, start = jnp.where(more, i, best), jnp.where(more, lengths[i], size), jnp.where(more, starts[i], start)
    sizes, begins = [size], [start]
    for i in range(DOCS - 1):
        later = best <= i
        sizes.append(jnp.where(later, lengths[i + 1], lengths[i]))
        begins.append(jnp.where(later, starts[i + 1], starts[i]))
    return sizes, begins


def doc_ranges(lens, total):
    sizes, begins = doc_table(lens, total)
    info = []
    for size, begin in zip(sizes, begins):
        info += [jnp.clip(begin, 0, total), jnp.clip(begin + size, 0, total)]
    return info + [begins[0], begins[0] + sizes[0]]


def slot_bounds(lens, total, shape, axis):
    sizes, begins = doc_table(lens, total)
    slot = lax.broadcasted_iota(jnp.int32, shape, axis)
    doc, within = slot // LMK, slot % LMK
    size, begin = jnp.full(shape, sizes[0]), jnp.full(shape, begins[0])
    for d in range(1, DOCS):
        size, begin = jnp.where(doc == d, sizes[d], size), jnp.where(doc == d, begins[d], begin)
    return begin + (within * size + LMK - 1) // LMK, begin + ((within + 1) * size + LMK - 1) // LMK


def project_kernel(lens, inputs, weight, joined, sums, small, edge, counts):
    total = inputs.shape[0]
    block = pl.program_id(0)
    out = dot(inputs[...], weight[...]).astype(BF16)
    joined[...] = out

    @pl.when(block < 2)
    def _():
        low, high = slot_bounds(lens, total, (DOCS * LMK, 1), 0)
        rows = lax.broadcasted_iota(jnp.int32, (DOCS * LMK, total), 1)
        member = jnp.where((rows >= low) & (rows < high), 1.0, 0.0).astype(BF16)
        slot_sums = dot(member, out)
        size = (high - low).astype(F32)
        sums[...] = slot_sums[:LMK]
        marks = (slot_sums[LMK:] / size[LMK:]).astype(BF16)
        for g in range(GROUPS):
            small[0, :, g] = marks[:, g * GROUP : (g + 1) * GROUP].reshape(SMALL, LMK, GROUP)
        counts[...] = jnp.broadcast_to(size, (DOCS * LMK, PAIR)).reshape(DOCS, LMK, PAIR)

    @pl.when(block == 2)
    def _():
        edge[0] = out[:16]
        edge[1] = out[total - 16 :]


def project(lens, inputs, weight):
    total, depth = inputs.shape
    width = weight.shape[1]
    third = GROUPS * GROUP

    return pl.pallas_call(
        project_kernel,
        grid=(width // third,),
        in_specs=[
            pl.BlockSpec(memory_space=pltpu.SMEM),
            pl.BlockSpec((total, depth), lambda j: (0, 0)),
            pl.BlockSpec((depth, third), lambda j: (0, j)),
        ],
        out_specs=[
            pl.BlockSpec((total, third), lambda j: (0, j)),
            pl.BlockSpec((LMK, third), lambda j: (0, jnp.minimum(j, 1))),
            pl.BlockSpec((1, SMALL, GROUPS, LMK, GROUP), lambda j: (jnp.minimum(j, 1), 0, 0, 0, 0)),
            pl.BlockSpec((2, 16, third), lambda j: (0, 0, 0)),
            pl.BlockSpec((DOCS, LMK, PAIR), lambda j: (0, 0, 0)),
        ],
        out_shape=[
            jax.ShapeDtypeStruct((total, width), BF16),
            jax.ShapeDtypeStruct((LMK, 2 * third), F32),
            jax.ShapeDtypeStruct((2, SMALL, GROUPS, LMK, GROUP), BF16),
            jax.ShapeDtypeStruct((2, 16, third), BF16),
            jax.ShapeDtypeStruct((DOCS, LMK, PAIR), F32),
        ],
        compiler_params=pltpu.CompilerParams(vmem_limit_bytes=62 * 2**20),
        name="project",
    )(lens, inputs, weight)


def joint(ref):
    return jnp.concatenate([ref[0], ref[1]], axis=1)


def write_pairs(ref, at, value):
    ref[0, at, :] = value[:, :PAIR]
    ref[1, at, :] = value[:, PAIR:]


LONG_SPEC = pl.BlockSpec((2, LMK, PAIR), lambda g: (g, 0, 0))
ROW_SPEC = pl.BlockSpec((2, 8, PAIR), lambda g: (g, 0, 0))
SMALL_SPEC = pl.BlockSpec((SMALL, None, LMK, GROUP), lambda g: (0, g, 0, 0))
SMALL_ROW_SPEC = pl.BlockSpec((SMALL, None, 8, GROUP), lambda g: (0, g, 0, 0))
TOP = slice(0, LMK)


def half_spec(half):
    return pl.BlockSpec((None, SMALL, None, LMK, GROUP), lambda g: (half, 0, g, 0, 0))


def for_docs(info, total, body):
    def inside(doc, size, start):
        rows = lax.broadcasted_iota(jnp.int32, (size, 1), 0) + start
        return (rows >= info[2 * doc]) & (rows < info[2 * doc + 1])

    body(0, total, 0, inside(0, total, 0))
    for doc in range(1, DOCS):
        low, high = info[2 * doc], info[2 * doc + 1]
        start = jnp.minimum(low // 16 * 16, total - WINDOW)

        @pl.when((high > low) & (high - start <= WINDOW))
        def _():
            at = pl.multiple_of(start, 16)
            body(doc, WINDOW, at, inside(doc, WINDOW, at))

        @pl.when(high - start > WINDOW)
        def _():
            body(doc, total, 0, inside(doc, total, 0))


def mix_kernel(lens, keys, values, qm, qms, exps, part, parts, stats):
    info = doc_ranges(lens, exps.shape[0])
    parts[...] = jnp.zeros_like(parts)
    stats[...] = jnp.zeros_like(stats)
    part[...] = jnp.zeros_like(part)

    def body(doc, size, start, inside):
        rows = pl.ds(start, size)
        marks = stacked(joint(qm) if doc == 0 else qms[doc - 1])
        scores = jnp.where(inside, dot(keys[rows, :], marks, NT) * 0.125, BIG_NEGATIVE)
        top = jnp.max(scores, axis=0, keepdims=True)
        wide = jnp.exp(scores - top)
        narrow = wide.astype(BF16)
        weighted = side_of(dot(narrow, values[rows, :], TN), GROUP)
        total = jnp.sum(wide, axis=0, keepdims=True)
        if doc == 0:
            exps[...] = narrow
            write_pairs(part, TOP, weighted)
            write_pairs(part, slice(LMK, LMK + 1), top)
            write_pairs(part, slice(LMK + 1, LMK + 2), total)
        else:
            exps[rows, :] = jnp.where(inside, narrow, exps[rows, :])
            parts[doc - 1] = weighted
            stats[doc - 1, 0:1, :] = top
            stats[doc - 1, 1:2, :] = total

    for_docs(info, exps.shape[0], body)


def mix(lens, joined, qm, qms):
    total, width = joined.shape[0], joined.shape[1] // 3
    groups = width // GROUP
    return pl.pallas_call(
        mix_kernel,
        grid=(groups,),
        in_specs=[
            pl.BlockSpec(memory_space=pltpu.SMEM),
            pl.BlockSpec((total, GROUP), lambda g: (0, groups + g)),
            pl.BlockSpec((total, GROUP), lambda g: (0, 2 * groups + g)),
            LONG_SPEC,
            half_spec(0),
        ],
        out_specs=[
            pl.BlockSpec((total, GROUP), lambda g: (0, g)),
            pl.BlockSpec((2, LMK + 8, PAIR), lambda g: (g, 0, 0)),
            SMALL_SPEC,
            SMALL_ROW_SPEC,
        ],
        out_shape=[
            jax.ShapeDtypeStruct((total, width), BF16),
            jax.ShapeDtypeStruct((PAIRS, LMK + 8, PAIR), F32),
            jax.ShapeDtypeStruct((SMALL, groups, LMK, GROUP), F32),
            jax.ShapeDtypeStruct((SMALL, groups, 8, GROUP), F32),
        ],
        compiler_params=pltpu.CompilerParams(vmem_limit_bytes=62 * 2**20),
        name="mix",
    )(lens, joined, joined, qm, qms)


TOEP = 160
BLK = 128


def widened(taps, backward):
    count = taps.shape[1]
    rows = lax.broadcasted_iota(jnp.int32, (count, 256), 0)
    lanes = lax.broadcasted_iota(jnp.int32, (count, 256), 1)
    place = rows + lanes == count - 1 if backward else rows == lanes
    return dot(taps[...], jnp.where(place, 1.0, 0.0).astype(F32), precision=HIGHEST)


def band(taps):
    wide = jnp.broadcast_to(taps, (BLK, 256))
    return pltpu.roll(wide, 0, 1, stride=1, stride_axis=0)[:, :TOEP].astype(BF16)


def bands(taps, group):
    heads = GROUP // LMK
    return jnp.concatenate([band(taps[pl.ds(group * heads + i, 1), :]) for i in range(heads)], axis=0)


def head_rows(stack):
    lanes = lax.broadcasted_iota(jnp.int32, (BLK, GROUP), 1) // LMK
    out = stack[:BLK]
    for i in range(1, GROUP // LMK):
        out = jnp.where(lanes == i, stack[i * BLK : (i + 1) * BLK], out)
    return out


def padded_rows(before, here, after, pad):
    total = here.shape[0]
    pad[0:16, :] = before
    pad[16 : total + 16, :] = here[...]
    pad[total + 16 : total + 32, :] = after


def doc_windows(info, total, body):
    def member(doc, start):
        rows = lax.broadcasted_iota(jnp.int32, (TOEP, 1), 0) + start - 16
        low, high = (info[8], info[9]) if doc == 0 else (info[2 * doc], info[2 * doc + 1])
        return (rows >= low) & (rows < high)

    for doc in range(DOCS):
        low, high = info[2 * doc], info[2 * doc + 1]

        @pl.loop(low // BLK, jnp.where(high > low, (high + BLK - 1) // BLK, low // BLK))
        def _(b):
            start = pl.multiple_of(b * BLK, BLK)
            body(doc, start, member(doc, start))


def attend_kernel(lens, queries, values, halo, taps, km, car, kms, cars, kern, mixture, pad, att, tap_rows):
    total = queries.shape[0]
    info = doc_ranges(lens, total)
    group = pl.program_id(0)
    ones = head_ones(GROUP).astype(BF16)

    def body(doc, size, start, inside):
        rows = pl.ds(start, size)
        marks = stacked(joint(km) if doc == 0 else kms[doc - 1])
        scores = dot(queries[rows, :], marks, NT) * 0.125
        exponent = jnp.exp(scores - head_max(scores, GROUP))
        kernel = (exponent / dot(exponent.astype(BF16), ones)).astype(BF16)
        carried = stacked(joint(car) if doc == 0 else cars[doc - 1])
        attended = dot(kernel, carried)
        if doc == 0:
            kern[...] = kernel
            att[...] = attended
        else:
            kern[rows, :] = jnp.where(inside, kernel, kern[rows, :])
            att[rows, :] = jnp.where(inside, attended, att[rows, :])

    for_docs(info, total, body)
    padded_rows(halo[0], values, halo[1], pad)
    tap_rows[...] = widened(taps, False)
    tape = bands(tap_rows, group)

    def conv(doc, start, inside):
        window = jnp.where(inside, pad[pl.ds(start, TOEP), :], jnp.zeros((), BF16))
        out = head_rows(dot(tape, window))
        rows = pl.ds(start, BLK)
        here = inside[16 : 16 + BLK]
        new = (att[rows, :] + out).astype(BF16)
        if doc == 0:
            mixture[rows, :] = new
        else:
            mixture[rows, :] = jnp.where(here, new, mixture[rows, :])

    doc_windows(info, total, conv)


def attend(lens, joined, halo, taps, km, car, kms, cars):
    total, width = joined.shape[0], joined.shape[1] // 3
    groups = width // GROUP
    col = pl.BlockSpec((total, GROUP), lambda g: (0, g))
    mark, marks = LONG_SPEC, SMALL_SPEC
    return pl.pallas_call(
        attend_kernel,
        grid=(groups,),
        in_specs=[
            pl.BlockSpec(memory_space=pltpu.SMEM),
            col,
            pl.BlockSpec((total, GROUP), lambda g: (0, 2 * groups + g)),
            pl.BlockSpec((2, 16, GROUP), lambda g: (0, 0, g)),
            pl.BlockSpec(taps.shape, lambda g: (0, 0)),
            mark,
            mark,
            half_spec(1),
            marks,
        ],
        out_specs=[col, col],
        out_shape=[jax.ShapeDtypeStruct((total, width), BF16)] * 2,
        scratch_shapes=[VMEM((total + 32, GROUP), BF16), VMEM((total, GROUP), F32), VMEM((taps.shape[0], 256), F32)],
        compiler_params=pltpu.CompilerParams(vmem_limit_bytes=62 * 2**20),
        name="attend",
    )(lens, joined, joined, halo, taps, km, car, kms, cars)


ROWS = 512
HALF = 256
PART = 1536
DENSE_TERMS = 8


def normalize(x):
    average = jnp.mean(x, axis=-1, keepdims=True)
    centered = x - average
    scale = lax.rsqrt(jnp.mean(centered * centered, axis=-1, keepdims=True) + EPSILON)
    return centered * scale, scale


def normalize_back(grad, gain, unit, scale):
    n = grad * gain
    return scale * (n - jnp.mean(n, axis=-1, keepdims=True) - unit * jnp.mean(n * unit, axis=-1, keepdims=True))


def column_sums(x):
    return jnp.sum(x, axis=0, keepdims=True)


def dense_kernel(mix_ref, inputs, cot, g1, b1, g2, b2, w_out, w_up, w_down, out, act, dup, ddown, normed, dout, dmix, dres, terms, edge, v_out, v_up, v_down, slope, wsem):
    step = pl.program_id(0)
    parts = w_up.shape[1] // PART
    loads = [pltpu.make_async_copy(w_out, v_out, wsem.at[0])]
    for c in range(parts):
        at = pl.ds(c * PART, PART)
        loads.append(pltpu.make_async_copy(w_up.at[:, at], v_up.at[c], wsem.at[1 + 2 * c]))
        loads.append(pltpu.make_async_copy(w_down.at[at, :], v_down.at[c], wsem.at[2 + 2 * c]))

    @pl.when(step == 0)
    def _():
        for load in loads:
            load.start()
        for load in loads:
            load.wait()
        terms[...] = jnp.zeros_like(terms)

    gain1, bias1, gain2, bias2 = (x[...].reshape(1, -1) for x in (g1, b1, g2, b2))

    def chain(half, first):
        r = slice(half * HALF, (half + 1) * HALF)
        unit1, scale1 = normalize(inputs[r, :].astype(F32) + dot(mix_ref[r, :], v_out[...]))
        n1 = unit1 * gain1 + bias1
        n1_low = n1.astype(BF16)
        normed[r, :] = n1_low
        yield
        total = n1
        for c in range(parts):
            at = slice(c * PART, (c + 1) * PART)
            up = dot(n1_low, v_up[c])
            share = 0.5 * (1.0 + lax.erf(up * 0.7071067811865476))
            active = (up * share).astype(BF16)
            act[r, at] = active
            slope[r, at] = share + up * (jnp.exp(-0.5 * up * up) * 0.3989422804014327)
            total = total + dot(active, v_down[c])
        yield
        unit2, scale2 = normalize(total)
        out[r, :] = (unit2 * gain2 + bias2).astype(BF16)
        grad = cot[r, :].astype(F32)
        terms[2:3, :] += column_sums(grad * unit2)
        terms[3:4, :] += column_sums(grad)
        d_total = normalize_back(grad, gain2, unit2, scale2)
        low = d_total.astype(BF16)
        ddown[r, :] = low
        yield
        for c in range(parts):
            at = slice(c * PART, (c + 1) * PART)
            d_up = (dot(low, v_down[c], NT) * slope[r, at]).astype(BF16)
            dup[r, at] = d_up
            d_total = d_total + dot(d_up, v_up[c], NT)
        yield
        terms[0:1, :] += column_sums(d_total * unit1)
        terms[1:2, :] += column_sums(d_total)
        d_first = normalize_back(d_total, gain1, unit1, scale1)
        dres[r, :] = d_first
        low = d_first.astype(BF16)
        dout[r, :] = low
        dmix[r, :] = dot(low, v_out[...], NT).astype(BF16)

    ahead, behind = chain(0, True), chain(1, False)
    next(ahead)
    for _ in range(4):
        next(ahead, None)
        next(behind)
    next(behind, None)

    @pl.when(step == 0)
    def _():
        edge[0] = dmix[:16, :]

    @pl.when(step == pl.num_programs(0) - 1)
    def _():
        edge[1] = dmix[ROWS - 16 :, :]


def dense(mixture, inputs, cot, gains, w_out, w_up, w_down):
    total, width = mixture.shape
    wide = w_up.shape[1]
    parts = wide // PART
    row = pl.BlockSpec((ROWS, width), lambda i: (i, 0))
    long_row = pl.BlockSpec((ROWS, wide), lambda i: (i, 0))
    shape = jax.ShapeDtypeStruct
    return pl.pallas_call(
        dense_kernel,
        grid=(total // ROWS,),
        in_specs=[row, row, row] + [pl.BlockSpec((width,), lambda i: (0,))] * 4 + [pl.BlockSpec(memory_space=pl.ANY)] * 3,
        out_specs=[row, long_row, long_row, row, row, row, row, row]
        + [pl.BlockSpec((DENSE_TERMS, width), lambda i: (0, 0)), pl.BlockSpec((2, 16, width), lambda i: (0, 0, 0))],
        out_shape=[
            shape((total, width), BF16),
            shape((total, wide), BF16),
            shape((total, wide), BF16),
            shape((total, width), BF16),
            shape((total, width), BF16),
            shape((total, width), BF16),
            shape((total, width), BF16),
            shape((total, width), F32),
            shape((DENSE_TERMS, width), F32),
            shape((2, 16, width), BF16),
        ],
        scratch_shapes=[
            VMEM((width, width), BF16),
            VMEM((parts, width, PART), BF16),
            VMEM((parts, PART, width), BF16),
            VMEM((ROWS, wide), F32),
            pltpu.SemaphoreType.DMA((1 + 2 * parts,)),
        ],
        compiler_params=pltpu.CompilerParams(vmem_limit_bytes=62 * 2**20),
        name="dense",
    )(mixture, inputs, cot, *gains, w_out, w_up, w_down)


def back_f_kernel(lens, queries, dmix, kern, km, car, kms, cars, dq, part, parts):
    info = doc_ranges(lens, dq.shape[0])
    parts[...] = jnp.zeros_like(parts)
    ones = head_ones(GROUP).astype(BF16)

    def body(doc, size, start, inside):
        rows = pl.ds(start, size)
        zero = jnp.zeros((), BF16)
        marks = stacked(joint(km) if doc == 0 else kms[doc - 1])
        carried = stacked(joint(car) if doc == 0 else cars[doc - 1])
        datt = dmix[rows, :]
        kernel = jnp.where(inside, kern[rows, :], zero)
        d_carried = side_of(dot(kernel, datt, TN), GROUP)
        d_kernel = dot(datt, carried, NT)
        wide = kernel.astype(F32)
        weighed = wide * d_kernel
        high = weighed.astype(BF16)
        low = (weighed - high.astype(F32)).astype(BF16)
        inner = dot(high, ones) + dot(low, ones)
        d_scores = (weighed - wide * inner).astype(BF16)
        d_queries = dot(d_scores, marks) * 0.125
        d_marks = side_of(dot(d_scores, queries[rows, :], TN), GROUP) * 0.125
        if doc == 0:
            dq[...] = d_queries.astype(BF16)
            write_pairs(part, TOP, d_carried.astype(BF16))
            write_pairs(part, slice(LMK, 2 * LMK), d_marks.astype(BF16))
        else:
            dq[rows, :] = jnp.where(inside, d_queries.astype(BF16), dq[rows, :])
            parts[0, doc - 1] = d_carried
            parts[1, doc - 1] = d_marks

    for_docs(info, dq.shape[0], body)


def back_f(lens, joined, dmix, kern, km, car, kms, cars):
    total, width = dmix.shape
    groups = width // GROUP
    col = pl.BlockSpec((total, GROUP), lambda g: (0, g))
    mark, marks = LONG_SPEC, SMALL_SPEC
    return pl.pallas_call(
        back_f_kernel,
        grid=(groups,),
        in_specs=[pl.BlockSpec(memory_space=pltpu.SMEM), col, col, col, mark, mark, half_spec(1), marks],
        out_specs=[
            col,
            pl.BlockSpec((2, 2 * LMK, PAIR), lambda g: (g, 0, 0)),
            pl.BlockSpec((2, SMALL, None, LMK, GROUP), lambda g: (0, 0, g, 0, 0)),
        ],
        out_shape=[
            jax.ShapeDtypeStruct((total, width), BF16),
            jax.ShapeDtypeStruct((PAIRS, 2 * LMK, PAIR), BF16),
            jax.ShapeDtypeStruct((2, SMALL, groups, LMK, GROUP), F32),
        ],
        compiler_params=pltpu.CompilerParams(vmem_limit_bytes=62 * 2**20),
        name="back_f",
    )(lens, joined, dmix, kern, km, car, kms, cars)


def back_b_kernel(lens, keys, values, halo, exps, local, stat, sc, along, scs, alongs, qm, qms, taps, dmix, dhalo, dk, dv, part, parts, dtaps, pad, dpad, acc, dval, tap_rows):
    total = keys.shape[0]
    info = doc_ranges(lens, total)
    group = pl.program_id(0)
    parts[...] = jnp.zeros_like(parts)

    def body(doc, size, start, inside):
        rows = pl.ds(start, size)
        scaled = stacked(joint(sc) if doc == 0 else scs[doc - 1])
        marks = stacked(joint(qm) if doc == 0 else qms[doc - 1])
        wide = jnp.where(inside, exps[rows, :].astype(F32), 0.0)
        if doc == 0:
            top = jnp.concatenate([local[0, LMK : LMK + 1], local[1, LMK : LMK + 1]], axis=1)
            wide = wide * jnp.exp(top - joint(stat)[0:1, :])
        shift = joint(along)[0:1, :] if doc == 0 else alongs[doc - 1, 0:1, :]
        d_values = dot(wide.astype(BF16), scaled)
        reach = dot(values[rows, :], scaled, NT)
        d_scores = (wide * (reach - shift)).astype(BF16)
        d_keys = dot(d_scores, marks) * 0.125
        d_marks = side_of(dot(d_scores, keys[rows, :], TN), GROUP) * 0.125
        if doc == 0:
            dk[...] = d_keys.astype(BF16)
            dval[...] = d_values
            write_pairs(part, TOP, d_marks)
        else:
            dk[rows, :] = jnp.where(inside, d_keys.astype(BF16), dk[rows, :])
            dval[rows, :] = jnp.where(inside, d_values, dval[rows, :])
            parts[doc - 1] = d_marks

    for_docs(info, total, body)
    padded_rows(halo[0], values, halo[1], pad)
    padded_rows(dhalo[0], dmix, dhalo[1], dpad)
    tap_rows[...] = widened(taps, True)
    tape = bands(tap_rows, group)
    acc[...] = jnp.zeros_like(acc)

    def conv(doc, start, inside):
        zero = jnp.zeros((), BF16)
        rows = pl.ds(start, BLK)
        here = inside[16 : 16 + BLK]
        out = head_rows(dot(tape, jnp.where(inside, dpad[pl.ds(start, TOEP), :], zero)))
        dval[rows, :] = dval[rows, :] + jnp.where(here, out, 0.0)
        window = jnp.where(inside, pad[pl.ds(start, TOEP), :], zero)
        mine = jnp.where(here, dmix[rows, :], zero)
        lanes = lax.broadcasted_iota(jnp.int32, (BLK, GROUP), 1) // LMK
        spread = jnp.concatenate([jnp.where(lanes == i, mine, zero) for i in range(GROUP // LMK)], axis=0)
        acc[:, :TOEP] = acc[:, :TOEP] + dot(spread, window, NT)

    doc_windows(info, total, conv)
    dv[...] = dval[...].astype(BF16)
    rows = lax.broadcasted_iota(jnp.int32, (BLK, BLK), 0)
    lanes = lax.broadcasted_iota(jnp.int32, (BLK, BLK), 1)
    reverse = jnp.where(rows + lanes == BLK - 1, 1.0, 0.0).astype(F32)
    for i in range(GROUP // LMK):
        square = dot(reverse, acc[i * BLK : (i + 1) * BLK, :], precision=HIGHEST)
        turned = pltpu.roll(square, 0, 1, stride=1, stride_axis=0)
        dtaps[0, i : i + 1, :] = jnp.sum(turned, axis=0, keepdims=True)


def back_b(lens, joined, halo, exps, local, stat, sc, along, scs, alongs, qm, qms, taps, dmix, dhalo):
    total, width = dmix.shape
    groups = width // GROUP
    heads = GROUP // LMK
    col = pl.BlockSpec((total, GROUP), lambda g: (0, g))
    mark, marks = LONG_SPEC, SMALL_SPEC
    edge = pl.BlockSpec((2, 16, GROUP), lambda g: (0, 0, g))
    return pl.pallas_call(
        back_b_kernel,
        grid=(groups,),
        in_specs=[
            pl.BlockSpec(memory_space=pltpu.SMEM),
            pl.BlockSpec((total, GROUP), lambda g: (0, groups + g)),
            pl.BlockSpec((total, GROUP), lambda g: (0, 2 * groups + g)),
            edge,
            col,
            pl.BlockSpec((2, LMK + 8, PAIR), lambda g: (g, 0, 0)),
            ROW_SPEC,
            mark,
            ROW_SPEC,
            marks,
            SMALL_ROW_SPEC,
            mark,
            half_spec(0),
            pl.BlockSpec(taps.shape, lambda g: (0, 0)),
            col,
            edge,
        ],
        out_specs=[col, col, mark, marks, pl.BlockSpec((1, heads, 256), lambda g: (g, 0, 0))],
        out_shape=[
            jax.ShapeDtypeStruct((total, width), BF16),
            jax.ShapeDtypeStruct((total, width), BF16),
            jax.ShapeDtypeStruct((PAIRS, LMK, PAIR), F32),
            jax.ShapeDtypeStruct((SMALL, groups, LMK, GROUP), F32),
            jax.ShapeDtypeStruct((groups, heads, 256), F32),
        ],
        scratch_shapes=[VMEM((total + 32, GROUP), BF16), VMEM((total + 32, GROUP), BF16), VMEM((heads * BLK, 256), F32), VMEM((total, GROUP), F32), VMEM((taps.shape[0], 256), F32)],
        compiler_params=pltpu.CompilerParams(vmem_limit_bytes=62 * 2**20),
        name="back_b",
    )(lens, joined, joined, halo, exps, local, stat, sc, along, scs, alongs, qm, qms, taps, dmix, dhalo)


class Ring:
    def __init__(self, count):
        self.count = count
        self.me = lax.axis_index("seq")
        self.row = lax.axis_index("row")
        self.steps = range(1, count)

    def ahead(self, k):
        return lax.rem(self.me + k, self.count)

    def enter(self, others=()):
        barrier = pltpu.get_barrier_semaphore()
        for to in [(self.ahead(k), self.row) for k in self.steps] + list(others):
            pl.semaphore_signal(barrier, inc=1, device_id=to, device_id_type=MESH)
        pl.semaphore_wait(barrier, self.count - 1 + len(others))

    def copy(self, src, dst, send, recv, to):
        return pltpu.make_async_remote_copy(src_ref=src, dst_ref=dst, send_sem=send, recv_sem=recv, device_id=(to, self.row), device_id_type=MESH)

    def scatter(self, pieces, landing, send, recv, first, owners):
        for k in self.steps:
            to = self.ahead(k)

            @pl.when((to >= first) & (to < first + owners))
            def _():
                self.copy(pieces(to - first), landing.at[k - 1], send.at[k - 1], recv.at[k - 1], to).start()

        def arrived():
            for k in self.steps:
                self.copy(pieces(0), landing.at[k - 1], send.at[k - 1], recv.at[k - 1], self.ahead(k)).wait_recv()

        def sent():
            for k in self.steps:
                to = self.ahead(k)

                @pl.when((to >= first) & (to < first + owners))
                def _():
                    self.copy(pieces(to - first), landing.at[k - 1], send.at[k - 1], recv.at[k - 1], to).wait_send()

        return arrived, sent

    def share(self, held, send, recv, first):
        piece = self.me - first
        for k in self.steps:
            self.copy(held.at[piece], held.at[piece], send.at[k - 1], recv.at[piece], self.ahead(k)).start()

    def share_sent(self, held, send, recv, first):
        piece = self.me - first
        for k in self.steps:
            self.copy(held.at[piece], held.at[piece], send.at[k - 1], recv.at[piece], self.ahead(k)).wait_send()

    def shared(self, held, send, recv, first, owners):
        for p in range(owners):

            @pl.when(self.me != first + p)
            def _():
                self.copy(held.at[p], held.at[p], send.at[0], recv.at[p], self.ahead(1)).wait_recv()


    def edges_start(self, here, landing, send, recv):
        @pl.when(self.me > 0)
        def _():
            self.copy(here.at[0], landing.at[1], send.at[0], recv.at[1], self.me - 1).start()

        @pl.when(self.me < self.count - 1)
        def _():
            self.copy(here.at[1], landing.at[0], send.at[1], recv.at[0], self.me + 1).start()

    def edges_wait(self, here, landing, send, recv, out):
        out[...] = jnp.zeros_like(out)

        @pl.when(self.me > 0)
        def _():
            done = self.copy(here.at[0], landing.at[0], send.at[0], recv.at[0], self.me - 1)
            done.wait_recv()
            done.wait_send()
            out[0] = landing[0]

        @pl.when(self.me < self.count - 1)
        def _():
            done = self.copy(here.at[1], landing.at[1], send.at[1], recv.at[1], self.me + 1)
            done.wait_recv()
            done.wait_send()
            out[1] = landing[1]


OWNERS = 8
DMA = pltpu.SemaphoreType.DMA
SAVES = 3 * NS_ITERS + 2
CASES = SMALL * GROUPS
EARLY = 2


def ends(ring):
    return (ring.me == 0) | (ring.me == ring.count - 1)


def owner_of_pair(ring):
    return (ring.me >= 1) & (ring.me <= PAIRS)


def pair_of(ring):
    return jnp.clip(ring.me - 1, 0, PAIRS - 1)


def remote_params(cid):
    return pltpu.CompilerParams(collective_id=cid, has_side_effects=True, vmem_limit_bytes=62 * 2**20)


def in_vmem(n):
    return [pl.BlockSpec(memory_space=VMEM)] * n


ANY_SPEC = pl.BlockSpec(memory_space=pl.ANY)


def small_forward(doc, at, qms, kms, held, invs):
    def save(i, j, value):
        held[at, j, i] = value

    inverse = inverse_forward([qms[doc, g] for g in range(GROUPS)], [kms[doc, g] for g in range(GROUPS)], save, GROUP)
    for g in range(GROUPS):
        invs[at, g] = inverse[g]


def marks_kernel(count, part, counts, edge, small, qm, km, halo, saved, invs, landing, held, hland, sheld, ss, rs, gs, gr, es, er, hs):
    ring = Ring(count)
    ring.enter()
    ring.edges_start(edge, hland, es, er)
    each_ = LMK // OWNERS
    arrived, sent = ring.scatter(lambda o: part.at[pl.ds(pl.multiple_of(o * each_, each_), each_), :], landing, ss, rs, 0, OWNERS)
    keep = [pltpu.make_async_copy(sheld.at[d], saved.at[d], hs.at[d]) for d in range(EARLY)]

    def early(d):
        @pl.when(ends(ring))
        def _():
            small_forward(d, d, small.at[0], small.at[1], sheld, invs)
            keep[d].start()

    early(0)

    @pl.when(ring.me < OWNERS)
    def _():
        arrived()
        at = pl.ds(pl.multiple_of(ring.me * each_, each_), each_)
        total = part[at, :]
        for k in ring.steps:
            total = total + landing[k - 1]
        total = total / counts[0, at, 0:1]
        half = total.shape[1] // 2
        held[ring.me, 0:each_, :] = total[:, :half].astype(BF16)
        held[ring.me, each_ : 2 * each_, :] = total[:, half:].astype(BF16)
        ring.share(held, gs, gr, 0)

    for d in range(1, EARLY):
        early(d)
    ring.shared(held, gs, gr, 0, OWNERS)
    wide = [held[o].astype(F32) for o in range(OWNERS)]
    query = jnp.concatenate([w[:each_] for w in wide], axis=0).astype(BF16)
    key = jnp.concatenate([w[each_:] for w in wide], axis=0).astype(BF16)
    for p in range(PAIRS):
        qm[p] = query[:, p * PAIR : (p + 1) * PAIR]
        km[p] = key[:, p * PAIR : (p + 1) * PAIR]
    ring.edges_wait(edge, hland, es, er, halo)
    sent()

    @pl.when(ring.me < OWNERS)
    def _():
        ring.share_sent(held, gs, gr, 0)

    @pl.when(ends(ring))
    def _():
        for copy in keep:
            copy.wait()


def all_marks(count, part, counts, edge, small):
    width = part.shape[1]
    each_ = LMK // OWNERS
    return pl.pallas_call(
        functools.partial(marks_kernel, count),
        in_specs=in_vmem(4),
        out_specs=in_vmem(3) + [ANY_SPEC] + in_vmem(1),
        out_shape=[jax.ShapeDtypeStruct((PAIRS, LMK, PAIR), BF16)] * 2
        + [
            jax.ShapeDtypeStruct(edge.shape, BF16),
            jax.ShapeDtypeStruct((EARLY, GROUPS, SAVES, LMK, GROUP), F32),
            jax.ShapeDtypeStruct((EARLY, GROUPS, LMK, GROUP), F32),
        ],
        scratch_shapes=[
            VMEM((count - 1, each_, width), F32),
            VMEM((OWNERS, 2 * each_, width // 2), BF16),
            VMEM(edge.shape, BF16),
            VMEM((EARLY, GROUPS, SAVES, LMK, GROUP), F32),
            DMA((count - 1,)),
            DMA((count - 1,)),
            DMA((count - 1,)),
            DMA((OWNERS,)),
            DMA((2,)),
            DMA((2,)),
            DMA((EARLY,)),
        ],
        compiler_params=remote_params(1),
        name="all_marks",
    )(part, counts, edge, small)


def carry_kernel(count, part, qm, km, small, wsm, stsm, invs, car, stat, saved, inv, mixed, cars, saveds, inv2, mixeds, landing, cheld, sheld, sk, ss, rs, cs, cr, ts, tr, hs):
    ring = Ring(count)
    ring.enter()
    arrived, sent = ring.scatter(lambda p: part.at[p], landing, ss, rs, 1, PAIRS)
    keep = pltpu.make_async_copy(sk, saveds, hs.at[0])

    @pl.when(owner_of_pair(ring))
    def _():
        pair = pair_of(ring)

        def save(i, j, value):
            saved[i] = value

        inverse = inverse_forward([qm[pair]], [km[pair]], save, PAIR)[0]
        inv[...] = inverse
        arrived()
        pieces = [part[pair]] + [landing[k - 1] for k in ring.steps]
        top = pieces[0][LMK : LMK + 1]
        for piece in pieces[1:]:
            top = jnp.maximum(top, piece[LMK : LMK + 1])
        weighted = jnp.zeros((LMK, PAIR), F32)
        total = jnp.zeros((1, PAIR), F32)
        for piece in pieces:
            share = jnp.exp(piece[LMK : LMK + 1] - top)
            weighted = weighted + piece[:LMK] * column_of(share, PAIR)
            total = total + piece[LMK + 1 : LMK + 2] * share
        mean = weighted / column_of(total, PAIR)
        mixed[...] = mean
        cheld[pair] = mul(inverse, mean, PAIR).astype(BF16)
        sheld[pair] = jnp.concatenate([top, total, jnp.zeros((6, PAIR), F32)], axis=0)
        ring.share(cheld, cs, cr, 1)
        ring.share(sheld, ts, tr, 1)

    @pl.when(ends(ring))
    def _():
        @pl.loop(0, SMALL - EARLY)
        def _(d):
            small_forward(d + EARLY, d, small.at[0], small.at[1], sk, inv2)

        keep.start()

        def finish(doc, inverse):
            for g in range(GROUPS):
                total = jnp.maximum(stsm[doc, g, 1:2, :], 1e-30)
                mean = wsm[doc, g] / column_of(total, GROUP)
                mixeds[doc, g] = mean
                cars[doc, g] = mul(inverse[g], mean, GROUP).astype(BF16)

        for d in range(SMALL):
            finish(d, [invs[d, g] if d < EARLY else inv2[d - EARLY, g] for g in range(GROUPS)])

    ring.shared(cheld, cs, cr, 1, PAIRS)
    ring.shared(sheld, ts, tr, 1, PAIRS)
    car[...] = cheld[...]
    stat[...] = sheld[...]
    sent()

    @pl.when(owner_of_pair(ring))
    def _():
        ring.share_sent(cheld, cs, cr, 1)
        ring.share_sent(sheld, ts, tr, 1)

    @pl.when(ends(ring))
    def _():
        keep.wait()


def carry(count, part, qm, km, small, wsm, stsm, invs):
    late = SMALL - EARLY
    return pl.pallas_call(
        functools.partial(carry_kernel, count),
        in_specs=in_vmem(7),
        out_specs=in_vmem(6) + [ANY_SPEC] + in_vmem(2),
        out_shape=[
            jax.ShapeDtypeStruct((PAIRS, LMK, PAIR), BF16),
            jax.ShapeDtypeStruct((PAIRS, 8, PAIR), F32),
            jax.ShapeDtypeStruct((SAVES, LMK, PAIR), F32),
            jax.ShapeDtypeStruct((LMK, PAIR), F32),
            jax.ShapeDtypeStruct((LMK, PAIR), F32),
            jax.ShapeDtypeStruct((SMALL, GROUPS, LMK, GROUP), BF16),
            jax.ShapeDtypeStruct((late, GROUPS, SAVES, LMK, GROUP), F32),
            jax.ShapeDtypeStruct((late, GROUPS, LMK, GROUP), F32),
            jax.ShapeDtypeStruct((SMALL, GROUPS, LMK, GROUP), F32),
        ],
        scratch_shapes=[
            VMEM((count - 1, LMK + 8, PAIR), F32),
            VMEM((PAIRS, LMK, PAIR), BF16),
            VMEM((PAIRS, 8, PAIR), F32),
            VMEM((late, GROUPS, SAVES, LMK, GROUP), F32),
            DMA((count - 1,)),
            DMA((count - 1,)),
            DMA((count - 1,)),
            DMA((PAIRS,)),
            DMA((count - 1,)),
            DMA((PAIRS,)),
            DMA((1,)),
        ],
        compiler_params=remote_params(2),
        name="carry",
    )(part, qm, km, small, wsm, stsm, invs)


def spread_grad(d_carried, inverse, mixed, total, width):
    d_mixed = mul(flipped(inverse, width), d_carried, width)
    scaled = (d_mixed / column_of(total, width)).astype(BF16)
    along = row_of(scaled.astype(F32) * mixed, width)
    return scaled, along


def spread_kernel(count, part, stat, inv, mixed, smallf, stsm, invs, inv2, mixeds, edge, sc, along, dtot, scs, alongs, halo, landing, sheld, aheld, hland, ss, rs, cs, cr, ts, tr, es, er):
    ring = Ring(count)
    ring.enter()
    arrived, sent = ring.scatter(lambda p: part.at[p], landing, ss, rs, 1, PAIRS)
    ring.edges_start(edge, hland, es, er)

    @pl.when(owner_of_pair(ring))
    def _():
        pair = pair_of(ring)
        arrived()
        total = part[pair].astype(F32)
        for k in ring.steps:
            total = total + landing[k - 1].astype(F32)
        dtot[...] = total
        scaled, reach = spread_grad(total[:LMK], inv[...], mixed[...], stat[pair, 1:2, :], PAIR)
        sheld[pair] = scaled
        aheld[pair] = reach
        ring.share(sheld, cs, cr, 1)
        ring.share(aheld, ts, tr, 1)

    @pl.when(ends(ring))
    def _():
        for d in range(SMALL):
            for g in range(GROUPS):
                total = jnp.maximum(stsm[d, g, 1:2, :], 1e-30)
                inverse = invs[d, g] if d < EARLY else inv2[d - EARLY, g]
                scaled, reach = spread_grad(smallf[0, d, g], inverse, mixeds[d, g], total, GROUP)
                scs[d, g] = scaled
                alongs[d, g] = reach

    ring.shared(sheld, cs, cr, 1, PAIRS)
    ring.shared(aheld, ts, tr, 1, PAIRS)
    sc[...] = sheld[...]
    along[...] = aheld[...]
    ring.edges_wait(edge, hland, es, er, halo)
    sent()

    @pl.when(owner_of_pair(ring))
    def _():
        ring.share_sent(sheld, cs, cr, 1)
        ring.share_sent(aheld, ts, tr, 1)


def spread(count, part, stat, inv, mixed, smallf, stsm, invs, inv2, mixeds, edge):
    return pl.pallas_call(
        functools.partial(spread_kernel, count),
        in_specs=in_vmem(10),
        out_specs=in_vmem(6),
        out_shape=[
            jax.ShapeDtypeStruct((PAIRS, LMK, PAIR), BF16),
            jax.ShapeDtypeStruct((PAIRS, 8, PAIR), F32),
            jax.ShapeDtypeStruct((2 * LMK, PAIR), F32),
            jax.ShapeDtypeStruct((SMALL, GROUPS, LMK, GROUP), BF16),
            jax.ShapeDtypeStruct((SMALL, GROUPS, 8, GROUP), F32),
            jax.ShapeDtypeStruct(edge.shape, BF16),
        ],
        scratch_shapes=[
            VMEM((count - 1, 2 * LMK, PAIR), BF16),
            VMEM((PAIRS, LMK, PAIR), BF16),
            VMEM((PAIRS, 8, PAIR), F32),
            VMEM(edge.shape, BF16),
            DMA((count - 1,)),
            DMA((count - 1,)),
            DMA((count - 1,)),
            DMA((PAIRS,)),
            DMA((count - 1,)),
            DMA((PAIRS,)),
            DMA((2,)),
            DMA((2,)),
        ],
        compiler_params=remote_params(3),
        name="spread",
    )(part, stat, inv, mixed, smallf, stsm, invs, inv2, mixeds, edge)


UNIT = 256
ACROSS = UNIT // 2
TURNS = (0, 1, 3, 5, 7, 9, 11, 13, 14)


class Sums:
    STEPS = 9

    def __init__(self, count, own, out, r0, r1, r2, r3, osem, ss, rs):
        self.count = count
        self.own, self.out, self.r0, self.r1, self.r2, self.r3 = own, out, r0, r1, r2, r3
        self.osem, self.ss, self.rs = osem, ss, rs
        s_ax, r_ax = lax.axis_index("seq"), lax.axis_index("row")
        z, x, y, c = s_ax // 2, lax.rem(s_ax, 2), r_ax // 2, lax.rem(r_ax, 2)
        x1, y1 = x + (1 - c) * (1 - 2 * x), y + c * (1 - 2 * y)
        x2, y2 = x + c * (1 - 2 * x), y + (1 - c) * (1 - 2 * y)
        self.z = z
        self.core = (s_ax, y * 2 + (1 - c))
        self.first = (z * 2 + x1, y1 * 2 + c)
        self.second = (z * 2 + x2, y2 * 2 + c)
        self.line = [(lax.rem(z + k, 4) * 2 + x, r_ax) for k in (1, 2, 3)]
        self.others = [self.core, self.first, self.second] + self.line
        self.b1 = x * (1 - c) + y * c
        self.b2 = y * (1 - c) + x * c
        self.mine, self.theirs = c, 1 - c
        self.fly = (self.core, self.first, self.second) + tuple(self.line) + tuple(self.line) + (self.second, self.first, self.core)

    def rows(self, start, size):
        return pl.ds(pl.multiple_of(start, 16), size)

    def copies(self, u):
        out, line = self.out, [lax.rem(self.z + k, 4) for k in (1, 2, 3)]
        base1, base2 = self.b1 * 384, self.b1 * 384 + self.b2 * 192
        last = self.r2.at[u, self.rows(self.z * 48, 48), :]
        place = out.at[u, self.mine, self.rows(base2 + self.z * 48, 48), :]
        pairs = [
            (self.own.at[u, self.theirs], self.r0.at[u]),
            (self.r0.at[u, self.rows((1 - self.b1) * 384, 384), :], self.r1.at[u]),
            (self.r1.at[u, self.rows((1 - self.b2) * 192, 192), :], self.r2.at[u]),
        ]
        pairs += [(self.r2.at[u, self.rows(line[k] * 48, 48), :], self.r3.at[u, k]) for k in range(3)]
        pairs += [(last, place)] * 3
        for region in (out.at[u, self.mine, self.rows(base2, 192), :], out.at[u, self.mine, self.rows(base1, 384), :], out.at[u, self.mine]):
            pairs.append((region, region))
        return pairs

    def copy(self, u, k):
        src, dst = self.copies(u)[k]
        return pltpu.make_async_remote_copy(src_ref=src, dst_ref=dst, send_sem=self.ss.at[u, k], recv_sem=self.rs.at[u, k], device_id=self.fly[k], device_id_type=MESH)

    def keep(self, u):
        src, dst = self.copies(u)[6]
        return pltpu.make_async_copy(src, dst, self.osem.at[u])

    def add(self, u, here, start, there, size):
        piece = min(size, 384)

        @pl.loop(0, size, step=piece)
        def _(t):
            q = self.rows(t, piece)
            here[u, q, :] = (here[u, q, :].astype(F32) + there(self.rows(start + t, piece)).astype(F32)).astype(BF16)

    def advance(self, u, s):
        if s == 0:
            self.copy(u, 0).start()
        elif s == 1:
            self.copy(u, 0).wait_recv()
            self.add(u, self.r0, 0, lambda q: self.own[u, self.mine, q, :], 768)
            self.copy(u, 1).start()
        elif s == 2:
            self.copy(u, 1).wait_recv()
            self.add(u, self.r1, self.b1 * 384, lambda q: self.r0[u, q, :], 384)
            self.copy(u, 2).start()
        elif s == 3:
            self.copy(u, 2).wait_recv()
            self.add(u, self.r2, self.b2 * 192, lambda q: self.r1[u, q, :], 192)
            for k in range(3):
                self.copy(u, 3 + k).start()
        elif s == 4:
            for k in range(3):
                self.copy(u, 3 + k).wait_recv()
            total = self.r2[u, self.rows(self.z * 48, 48), :].astype(F32)
            for k in range(3):
                total = total + self.r3[u, k].astype(F32)
            self.r2[u, self.rows(self.z * 48, 48), :] = total.astype(BF16)
            self.keep(u).start()
            for k in range(3):
                self.copy(u, 6 + k).start()
        elif s == 5:
            for k in range(3):
                self.copy(u, 6 + k).wait_recv()
            self.keep(u).wait()
            self.copy(u, 9).start()
        elif s in (6, 7):
            self.copy(u, s + 3).wait_recv()
            self.copy(u, s + 4).start()
        else:
            self.copy(u, 11).wait_recv()

    def taus(self):
        return self.count + TURNS[-1]

    def step(self, tau, steps):
        for s in steps:
            u = tau - TURNS[s]

            @pl.when((u >= 0) & (u < self.count))
            def _():
                self.advance(jnp.clip(u, 0, self.count - 1), s)

    def finish(self):
        @pl.loop(0, self.count)
        def _(u):
            for k in range(12):
                self.copy(u, k).wait_send()


def small_all(values, smr, sss, srs, sums, k):
    z = sums.z
    s_ax, r_ax = lax.axis_index("seq"), lax.axis_index("row")
    x = lax.rem(s_ax, 2)
    partners = [sums.core, sums.first, sums.second, (lax.rem(z + 2, 4) * 2 + x, r_ax), ((z + 1 - 2 * lax.rem(z, 2)) * 2 + x, r_ax)]

    def copy(i):
        return pltpu.make_async_remote_copy(src_ref=smr.at[i], dst_ref=smr.at[i + 6], send_sem=sss.at[i], recv_sem=srs.at[i], device_id=partners[i], device_id_type=MESH)

    if k == 0:
        terms, taps = values
        smr[0] = jnp.zeros(smr.shape[1:], F32)
        smr[0, 0:4, :] = terms[0:4, :]
        for g in range(GROUPS):
            smr[0, 8:12, g * GROUP : (g + 1) * GROUP] = taps[g]
    else:
        copy(k - 1).wait_recv()
        smr[k] = smr[k - 1] + smr[k + 5]
    if k < 5:
        copy(k).start()
    else:
        for i in range(5):
            copy(i).wait_send()


MARK_TAUS = NS_ITERS * SMALL


def marks_backward(ring, tau, arrived, part, dtot, saved, mixed, qm, km, counts, smallb, smallf, save_a, save_b, mixeds, marks, landing, held, dsums, keep, da, dk, kt, la, lk, lt, cs, cr, hs):
    owner, end = owner_of_pair(ring), ends(ring)
    pair = pair_of(ring)
    last = 3 * NS_ITERS + 1
    doc, turn = jnp.minimum(tau // NS_ITERS, SMALL - 1), lax.rem(tau, NS_ITERS)
    back = NS_ITERS - 1 - turn

    @pl.when(owner & (tau == 0))
    def _():
        la[...] = mul_nt(dtot[:LMK], mixed[...], PAIR)
        lk[...] = jnp.zeros_like(lk)
        lt[...] = flipped(saved[last], PAIR)

    @pl.when(owner & (tau < NS_ITERS))
    def _():
        a, b = backward_step([la[...]], [lk[...]], [lt[...]], [saved[3 * back]], [saved[3 * back + 1]], [saved[3 * back + 2]], PAIR)
        la[...] = a[0]
        lk[...] = b[0]

    @pl.when(owner & (tau == NS_ITERS - 1))
    def _():
        d_scores = backward_end(la[...], lk[...], saved[last], saved[0], PAIR) * 0.125
        d_query = mul(d_scores, km[pair].astype(F32), PAIR)
        d_key = mul(flipped(d_scores, PAIR), qm[pair].astype(F32), PAIR)
        arrived()
        total = part[pair]
        for k in ring.steps:
            total = total + landing[k - 1]
        held[pair, :LMK, :] = ((d_query + total) / counts[0, :, 0:1]).astype(BF16)
        held[pair, LMK:, :] = ((d_key + dtot[LMK:]) / counts[0, :, 0:1]).astype(BF16)
        ring.share(held, cs, cr, 1)

    work = end & (tau < MARK_TAUS)

    @pl.when(work & (turn == 0))
    def _():
        @pl.when(doc < EARLY)
        def _():
            copy = pltpu.make_async_copy(save_a.at[jnp.minimum(doc, EARLY - 1)], keep, hs.at[0])
            copy.start()
            copy.wait()

        @pl.when(doc >= EARLY)
        def _():
            copy = pltpu.make_async_copy(save_b.at[jnp.maximum(doc - EARLY, 0)], keep, hs.at[0])
            copy.start()
            copy.wait()

        for g in range(GROUPS):
            da[g] = mul_nt(smallf[0, doc, g], mixeds[doc, g], GROUP)
            dk[g] = jnp.zeros((LMK, GROUP), F32)
            kt[g] = flipped(keep[g, last], GROUP)

    @pl.when(work)
    def _():
        rows = range(GROUPS)
        iterates = [[keep[g, 3 * back + i] for g in rows] for i in range(3)]
        a, b = backward_step([da[g] for g in rows], [dk[g] for g in rows], [kt[g] for g in rows], *iterates, GROUP)
        for g in rows:
            da[g] = a[g]
            dk[g] = b[g]

    @pl.when(work & (turn == NS_ITERS - 1))
    def _():
        for g in range(GROUPS):
            d_scores = backward_end(da[g], dk[g], keep[g, last], keep[g, 0], GROUP) * 0.125
            d_query = mul(d_scores, marks[1, doc, g].astype(F32), GROUP)
            d_key = mul(flipped(d_scores, GROUP), marks[0, doc, g].astype(F32), GROUP)
            size = counts[1 + doc, :, 0:1]
            dsums[doc, g, :LMK, :] = ((d_query + smallb[doc, g]) / size).astype(BF16)
            dsums[doc, g, LMK:, :] = ((d_key + smallf[1, doc, g]) / size).astype(BF16)


N_MARKS = 13
MARKS_SPECS = in_vmem(9) + [ANY_SPEC] * 2 + in_vmem(2)
N_WORK = 12


def marks_work(count):
    return [
        VMEM((count - 1, LMK, PAIR), F32),
        VMEM((PAIRS, 2 * LMK, PAIR), BF16),
        VMEM((SMALL, GROUPS, 2 * LMK, GROUP), BF16),
        VMEM((GROUPS, SAVES, LMK, GROUP), F32),
        VMEM((GROUPS, LMK, GROUP), F32),
        VMEM((GROUPS, LMK, GROUP), F32),
        VMEM((GROUPS, LMK, GROUP), F32),
        VMEM((LMK, PAIR), F32),
        VMEM((LMK, PAIR), F32),
        VMEM((LMK, PAIR), F32),
        DMA((count - 1,)),
        DMA((PAIRS,)),
        DMA((1,)),
        DMA((count - 1,)),
        DMA((count - 1,)),
    ]


def finish_marks(ring, held, cs, cr, sent):
    sent()

    @pl.when(owner_of_pair(ring))
    def _():
        ring.share_sent(held, cs, cr, 1)


def sums_kernel(count, *refs):
    args, (dsum, dsums_out), work = refs[:N_MARKS], refs[N_MARKS : N_MARKS + 2], refs[N_MARKS + 2 :]
    (landing, held, dsums), rest, (ss, rs) = work[:3], work[3:13], work[13:]
    cs, cr = rest[7], rest[8]
    ring = Ring(count)
    ring.enter()
    arrived, sent = ring.scatter(lambda p: args[0].at[p], landing, ss, rs, 1, PAIRS)
    dsums[...] = jnp.zeros_like(dsums)

    @pl.loop(0, MARK_TAUS)
    def _(tau):
        marks_backward(ring, tau, arrived, *args, landing, held, dsums, *rest)

    ring.shared(held, cs, cr, 1, PAIRS)
    dsum[...] = held[...]
    dsums_out[...] = dsums[...]
    finish_marks(ring, held, cs, cr, sent)


def mark_sums(count, *args):
    shape = jax.ShapeDtypeStruct
    return pl.pallas_call(
        functools.partial(sums_kernel, count),
        in_specs=MARKS_SPECS,
        out_specs=in_vmem(2),
        out_shape=[shape((PAIRS, 2 * LMK, PAIR), BF16), shape((SMALL, GROUPS, 2 * LMK, GROUP), BF16)],
        scratch_shapes=marks_work(count),
        compiler_params=remote_params(4),
        name="mark_sums",
    )(*args)


BLOCKS = 3 * GROUPS


FIRST = (0, 12, 24, 27, 36)


def finale_kernel(count, *refs):
    args, refs = refs[:N_MARKS], refs[N_MARKS:]
    (lens, inputs, dq, dk, dv, w, ddown, act, normed, dup, mixture, dout, *sm), refs = refs[:14], refs[14:]
    (out, dx, osm), refs = refs[:3], refs[3:]
    work, refs = refs[:15], refs[15:]
    (own, r0, r1, r2, r3, dj, flip, left, right, member, table, smr, wide), refs = refs[:13], refs[13:]
    osem, gs, gr, sss, srs, jsem, fsem, bsem, wsem = refs
    (landing, held, dsums), rest, (ss, rs) = work[:3], work[3:13], work[13:]
    cs, cr = rest[7], rest[8]
    total = inputs.shape[0]
    ring = Ring(count)
    before = FIRST[3]
    sums = Sums(FIRST[4], own, out, r0, r1, r2, r3, osem, gs, gr)
    lefts, rights = (ddown, normed, mixture, inputs), (act, dup, dout)

    def fetch_left(i):
        return pltpu.make_async_copy(lefts[i], left, fsem.at[0])

    def fetch_right(i, u):
        columns = pl.ds(pl.multiple_of((u - FIRST[i]) * UNIT, 128), UNIT)
        return pltpu.make_async_copy(rights[i].at[:, columns], right.at[lax.rem(u, 2)], bsem.at[lax.rem(u, 2)])

    fetch_left(0).start()
    fetch_right(0, 0).start()
    joined = [pltpu.make_async_copy(src, dj.at[:, pl.ds(i * GROUPS * GROUP, GROUPS * GROUP)], jsem.at[i]) for i, src in enumerate((dq, dk, dv))]
    for copy in joined:
        copy.start()
    ring.enter(sums.others)
    arrived, sent = ring.scatter(lambda p: args[0].at[p], landing, ss, rs, 1, PAIRS)
    dsums[...] = jnp.zeros_like(dsums)
    weight = pltpu.make_async_copy(w, wide, wsem.at[0])
    weight.start()

    def keep(u, grad):
        own[u, 0] = grad[:, :ACROSS]
        own[u, 1] = grad[:, ACROSS:]

    def make(tau):
        for i in range(4):

            @pl.when(tau == FIRST[i])
            def _():
                fetch_left(i).wait()
                flip[...] = jnp.transpose(left[...])
                if i < 3:
                    fetch_left(i + 1).start()

        for i in range(3):

            @pl.when((tau + 1 >= FIRST[i]) & (tau + 1 < FIRST[i + 1]))
            def _():
                fetch_right(i, jnp.clip(tau + 1, FIRST[i], FIRST[i + 1] - 1)).start()

        @pl.when(tau < before)
        def _():
            u = jnp.minimum(tau, before - 1)
            pltpu.make_async_copy(act.at[:, pl.ds(0, UNIT)], right.at[lax.rem(u, 2)], bsem.at[lax.rem(u, 2)]).wait()
            keep(u, dot(flip[...], right[lax.rem(u, 2)]).astype(BF16))

        @pl.when(tau == before)
        def _():
            ring.shared(held, cs, cr, 1, PAIRS)
            for half in range(2):
                for g in range(GROUPS):
                    at = slice(half * LMK, (half + 1) * LMK)
                    table[half * GROUPS + g, :LMK, :PAIR] = held[2 * g, at, :]
                    table[half * GROUPS + g, :LMK, PAIR:] = held[2 * g + 1, at, :]
                    for d in range(SMALL):
                        table[half * GROUPS + g, (d + 1) * LMK : (d + 2) * LMK, :] = dsums[d, g, at, :]

        @pl.when((tau >= before) & (tau < FIRST[4]))
        def _():
            b = jnp.clip(tau - before, 0, BLOCKS - 1)
            columns = pl.ds(pl.multiple_of(b * GROUP, 128), GROUP)

            @pl.when(b < 2 * GROUPS)
            def _():
                from_marks = dot(member[...], table[jnp.minimum(b, 2 * GROUPS - 1)])
                dj[:, columns] = (dj[:, columns].astype(F32) + from_marks).astype(BF16)

            keep(before + b, dot(flip[...], dj[:, columns]).astype(BF16))

    @pl.loop(0, sums.taus())
    def _(tau):
        sums.step(tau, range(8, 0, -1))
        make(tau)
        sums.step(tau, (0,))
        for k in range(6):

            @pl.when(tau == 4 * k + 3)
            def _():
                small_all(sm, smr, sss, srs, sums, k)

        marks_backward(ring, tau, arrived, *args, landing, held, dsums, *rest)

        @pl.when(tau == MARK_TAUS)
        def _():
            low, high = slot_bounds(lens, total, (1, DOCS * LMK), 1)
            rows = lax.broadcasted_iota(jnp.int32, (total, DOCS * LMK), 0)
            member[...] = jnp.where((rows >= low) & (rows < high), 1.0, 0.0).astype(BF16)
            for copy in joined:
                copy.wait()

        for k in range(GROUPS):

            @pl.when(tau == FIRST[4] + 2 * k + 1)
            def _():
                if k == 0:
                    weight.wait()
                columns = slice(k * GROUP, (k + 1) * GROUP)
                dx[:, columns] = dot(dj[...], wide[columns, :], NT)

    finish_marks(ring, held, cs, cr, sent)
    sums.finish()
    osm[...] = smr[5]


def finale(count, marks_args, lens, inputs, dq, dk, dv, w, ddown, act, normed, dup, mixture, dout, terms, dtaps):
    n = FIRST[4]
    total, depth = inputs.shape
    width = w.shape[1]
    shape = jax.ShapeDtypeStruct
    return pl.pallas_call(
        functools.partial(finale_kernel, count),
        in_specs=MARKS_SPECS + [pl.BlockSpec(memory_space=pltpu.SMEM)] + [ANY_SPEC] * 11 + in_vmem(2),
        out_specs=[ANY_SPEC] + in_vmem(2),
        out_shape=[shape((n, 2, 768, ACROSS), BF16), shape((total, depth), F32), shape((16, depth), F32)],
        scratch_shapes=marks_work(count)
        + [
            VMEM((n, 2, 768, ACROSS), BF16),
            VMEM((n, 768, ACROSS), BF16),
            VMEM((n, 384, ACROSS), BF16),
            VMEM((n, 192, ACROSS), BF16),
            VMEM((n, 3, 48, ACROSS), BF16),
            VMEM((total, width), BF16),
            VMEM((depth, total), BF16),
            VMEM((total, depth), BF16),
            VMEM((2, total, UNIT), BF16),
            VMEM((total, DOCS * LMK), BF16),
            VMEM((2 * GROUPS, DOCS * LMK, GROUP), BF16),
            VMEM((11, 16, depth), F32),
            VMEM(w.shape, BF16),
            DMA((n,)),
            DMA((n, 12)),
            DMA((n, 12)),
            DMA((5,)),
            DMA((5,)),
            DMA((3,)),
            DMA((1,)),
            DMA((2,)),
            DMA((1,)),
        ],
        compiler_params=pltpu.CompilerParams(collective_id=5, has_side_effects=True, vmem_limit_bytes=62 * 2**20),
        name="finale",
    )(*marks_args, lens, inputs, dq, dk, dv, w, ddown, act, normed, dup, mixture, dout, terms, dtaps)


TRIPLE = 3


def widen_kernel(units, dx, residual, little, gd, gu, go, gq, grad, g1, b1, g2, b2, gtaps):
    i = pl.program_id(0)

    @pl.when(i == 0)
    def _():
        for k, ref in enumerate((g1, b1, g2, b2)):
            ref[...] = little[k, :]
        heads = GROUP // LMK
        for h in range(gtaps.shape[0]):
            row = little[8 + h % heads : 9 + h % heads, h // heads * GROUP : (h // heads + 1) * GROUP]
            gtaps[h : h + 1, :] = pltpu.roll(row, GROUP - BLK + 1, 1)[:, : gtaps.shape[1]]

    value = [jnp.concatenate([units[k, 0], units[k, 1]], axis=1).astype(F32) for k in range(TRIPLE)]

    @pl.when(i < 4)
    def _():
        for k in range(TRIPLE):
            gd[k * UNIT : (k + 1) * UNIT, :] = jnp.transpose(value[k])

    for ref, first, end in ((gu, 4, 8), (go, 8, 9), (gq, 9, 12)):

        @pl.when((i >= first) & (i < end))
        def _():
            for k in range(TRIPLE):
                ref[:, k * UNIT : (k + 1) * UNIT] = value[k]

    @pl.when(i < 8)
    def _():
        grad[...] = residual[...] + dx[...]


def widen(units, dx, residual, little, taps):
    n, _, side, half = units.shape
    shape = jax.ShapeDtypeStruct
    total, depth = dx.shape

    def place(first, last, down):
        def index(i):
            b = jnp.clip(i, first, last) - first
            return (b, 0) if down else (0, b)

        return pl.BlockSpec((side, side), index)

    part = pl.BlockSpec((total // 8, depth), lambda i: (jnp.minimum(i, 7), 0))
    return pl.pallas_call(
        widen_kernel,
        grid=(n // TRIPLE,),
        in_specs=[pl.BlockSpec((TRIPLE, 2, side, half), lambda i: (i, 0, 0, 0)), part, part, pl.BlockSpec(little.shape, lambda i: (0, 0))],
        out_specs=[place(0, 3, True), place(4, 7, False), place(8, 8, True), place(9, 11, False), part] + [pl.BlockSpec((depth,), lambda i: (0,))] * 4 + [pl.BlockSpec(taps, lambda i: (0, 0))],
        out_shape=[shape((4 * side, side), F32), shape((side, 4 * side), F32), shape((side, side), F32), shape((side, 3 * side), F32), shape(dx.shape, F32)] + [shape((depth,), F32)] * 4 + [shape(taps, F32)],
        compiler_params=pltpu.CompilerParams(vmem_limit_bytes=62 * 2**20),
        name="widen",
    )(units, dx, residual, little)


def member_of(doc_lengths, total):
    low, high = slot_bounds(doc_lengths, total, (1, DOCS * LMK), 1)
    rows = jnp.arange(total, dtype=jnp.int32)[:, None]
    return ((rows >= low) & (rows < high)).astype(BF16)


def over_all(*grads):
    out = []
    for g in grads:
        part = lax.psum_scatter(g.astype(F32).reshape(lax.axis_size(("seq", "row")), -1), ("seq", "row"), scatter_dimension=0, tiled=True)
        out.append(lax.all_gather(part.astype(BF16), ("seq", "row"), axis=0, tiled=True).reshape(g.shape))
    return out


def on_device(
    tokens,
    doc_lengths,
    w_qkv,
    w_out,
    conv_taps,
    norm1_gain,
    norm1_bias,
    w_up,
    w_down,
    norm2_gain,
    norm2_bias,
    cotangent,
):
    model_width = tokens.shape[2]
    head_count, tap_count = conv_taps.shape
    rim = (tap_count - 1) // 2
    count = lax.axis_size("seq")
    wide = count == 8 and lax.axis_size("row") == 4
    inputs = tokens[0]
    joined, slot_sums, small, edge, counts = project(doc_lengths, inputs, w_qkv)
    qm, km, halo, save_a, invs = all_marks(count, slot_sums, counts, edge, small)
    exps, part, wsm, stsm = mix(doc_lengths, joined, qm, small)
    carried, stat, saved, inv, mixed, cars, save_b, inv2, mixeds = carry(count, part, qm, km, small, wsm, stsm, invs)
    kernel_b, mixture_b = attend(doc_lengths, joined, halo, conv_taps, km, carried, small, cars)
    gains = (norm1_gain, norm1_bias, norm2_gain, norm2_bias)
    result, activated, delta_up, delta_down, normed1_b, delta_output, delta_mix, delta_residual1, norm_sums, delta_edge = dense(
        mixture_b, inputs, cotangent[0], gains, w_out, w_up, w_down
    )
    dq, part_f, small_f = back_f(doc_lengths, joined, delta_mix, kernel_b, km, carried, small, cars)
    scaled, along, dtot, scs, alongs, delta_halo = spread(count, part_f, stat, inv, mixed, small_f, stsm, invs, inv2, mixeds, delta_edge)
    dk, dv, part_b, small_b, dtaps = back_b(
        doc_lengths, joined, halo, exps, part, stat, scaled, along, scs, alongs, qm, small, conv_taps, delta_mix, delta_halo
    )
    marks_args = (part_b, dtot, saved, mixed, qm, km, counts, small_b, small_f, save_a, save_b, mixeds, small)
    if wide:
        units, from_joined, tsm = finale(
            count, marks_args, doc_lengths, inputs, dq, dk, dv, w_qkv, delta_down, activated, normed1_b, delta_up, mixture_b, delta_output, norm_sums, dtaps
        )
        total_down, total_up, total_output, total_joined, delta_inputs, *norms, total_taps = widen(units, from_joined, delta_residual1, tsm, conv_taps.shape)
    else:
        dsum, dsums = mark_sums(count, *marks_args)
        long_sums = dsum.reshape(PAIRS, 2, LMK, PAIR).transpose(2, 1, 0, 3).reshape(LMK, 2 * model_width)
        small_sums = dsums.reshape(SMALL, GROUPS, 2, LMK, GROUP).transpose(0, 3, 2, 1, 4).reshape(SMALL * LMK, 2 * model_width)
        from_marks = jnp.dot(member_of(doc_lengths, inputs.shape[0]), jnp.concatenate([long_sums, small_sums], axis=0), preferred_element_type=F32)
        delta_joined = jnp.concatenate([dq, dk, dv], axis=1) + jnp.pad(from_marks, ((0, 0), (0, model_width)))
        delta_joined = delta_joined.astype(BF16)
        grad_down = jnp.dot(activated.T, delta_down, preferred_element_type=F32)
        grad_up = jnp.dot(normed1_b.T, delta_up, preferred_element_type=F32)
        grad_output = jnp.dot(mixture_b.T, delta_output, preferred_element_type=F32)
        grad_joined = jnp.dot(inputs.T, delta_joined, preferred_element_type=F32)
        total_down, total_up, total_output, total_joined = over_all(grad_down, grad_up, grad_output, grad_joined)
        taps = dtaps.reshape(head_count, GROUP)[:, BLK - 1 : BLK - 1 + tap_count]
        norms, total_taps = lax.psum((norm_sums[:4], taps), ("seq", "row"))
        delta_inputs = delta_residual1 + dot(delta_joined, w_qkv, NT)
    return (
        result[None],
        delta_inputs[None],
        total_joined.astype(F32),
        total_output.astype(F32),
        total_taps,
        norms[0],
        norms[1],
        total_up.astype(F32),
        total_down.astype(F32),
        norms[2],
        norms[3],
    )


def solution(mesh):
    return jax.shard_map(
        on_device,
        mesh=mesh,
        in_specs=(
            P("row", "seq", None),
            P("row", None),
            P(),
            P(),
            P(),
            P(),
            P(),
            P(),
            P(),
            P(),
            P(),
            P("row", "seq", None),
        ),
        out_specs=(
            P("row", "seq", None),
            P("row", "seq", None),
            P(),
            P(),
            P(),
            P(),
            P(),
            P(),
            P(),
            P(),
            P(),
        ),
        check_vma=False,
    )
```
